32 devices in a mesh: dom: 4 (over y, core), sub: 8 (over z, x).
Axes of the slice: x: 2, y: 2, z: 4, core: 2. Of those that a mesh axis runs over, the one named last changes fastest.
Arguments:
- node_feat: bfloat16 [304, 16384], P(None, ('dom', 'sub')), may hold values from -6 to 6
- node_pos: bfloat16 [3, 16384], P(None, ('dom', 'sub')), may hold values from -4 to 4
- node_cot: bfloat16 [304, 16384], P(None, ('dom', 'sub')), may hold values from -6 to 6
- mesh_senders: int32 [98304], P(('dom', 'sub')), may hold values from 0 to 1535
- edge_mask: int32 [98304], P(('dom', 'sub')), may hold values 0 or 1
- halo_up: int32 [16384], P(('dom', 'sub')), may hold values from 0 to 511
- halo_down: int32 [16384], P(('dom', 'sub')), may hold values from 0 to 511
- contact_rows: int32 [65536], P(('dom', 'sub')), may hold values from 0 to 511
- contact_dst: int32 [65536], P(('dom', 'sub')), may hold values from 0 to 511
- contact_mask: int32 [65536], P(('dom', 'sub')), may hold values from 0 to 1, as said below
- w_one: bfloat16 [128, 128], replicated, may hold values from -0.5 to 0.5
- b_one: float32 [128], replicated, may hold values from -3 to 3
- w_dist: float32 [128], replicated, may hold values from -3 to 3
- w_two: bfloat16 [144, 128], replicated, may hold values from -0.5 to 0.5
- w_scal: bfloat16 [64, 64], replicated, may hold values from -0.75 to 0.75
- w_vec: bfloat16 [32, 32], replicated, may hold values from -1 to 1
- w_ten: bfloat16 [16, 16], replicated, may hold values from -1.5 to 1.5
Outputs:
- node_out: bfloat16 [304, 16384], P(None, ('dom', 'sub'))
- grad_one: float32 [128, 128], replicated
- grad_bias: float32 [128], replicated
- grad_dist: float32 [128], replicated
- grad_two: float32 [144, 128], replicated
- grad_scal: float32 [64, 64], replicated
- grad_vec: float32 [32, 32], replicated
- grad_ten: float32 [16, 16], replicated
The draws below stay inside these ranges and needn't reach their ends.
Inputs may be any that keep to these rules, and one draw needn't show every extreme that they name: `mesh_senders`: below 512 an own node, then the block from the previous and the block from the next sub-partition. `contact_rows`: entry p * 2048 + c * 64 + k names a row of partition c. `contact_mask`: in every draw some partition has all 2048 contact slots live; partitions differ in how many are.
All inputs are finite; a program needn't handle non-finite values. No bound on the sum of `edge_mask` on one device may be relied on, other than what follows from the above.
Results may differ from the reference program's by a relative error of at most 0.0059.
Values may be sent and summed in bfloat16 or wider, within the bound.
No kernel may reach another device: no remote copies, remote signals or barrier semaphores. Data moves between devices by JAX's collectives and lax.ppermute only.
A program may use at most 128 MiB of HBM per device.

```python
import math
import jax
import jax.numpy as jnp
from jax import lax

CS = 64
CV = 32
CT = 16
HID = 128
DEGREE = 6
NODE_DEV = 512
HALO = 512
CON_DEV = 2048
CAP = 64
FEAT = 304
GATES = 144
EDGE_DEV = 3072
NODES = 16384
N_SUB = 8
DEVICES = 32


def draw_contact_mask(key, part):
    key = jax.random.fold_in(key, 7)
    level_key, pick_key, slot_key = jax.random.split(key, 3)
    levels = jax.random.randint(level_key, (DEVICES,), 1, 9)
    chosen = jax.random.randint(pick_key, (), 0, DEVICES)
    levels = jnp.where(jnp.arange(DEVICES) == chosen, 8, levels)
    slot_rolls = jax.random.randint(slot_key, (DEVICES, CON_DEV), 0, 8)
    return (slot_rolls < levels[:, None]).astype(jnp.int32).reshape(DEVICES * CON_DEV)


def place_ends(entries, own_key, least, largest):
    longest = entries.shape.index(max(entries.shape))
    spots = []
    for shift in (0, 1):
        where = [jax.random.randint(jax.random.fold_in(own_key, axis), (), 0, length) for axis, length in enumerate(entries.shape)]
        where[longest] = (where[longest] + shift) % entries.shape[longest]
        spots.append(tuple(where))
    return entries.at[spots[0]].set(least).at[spots[1]].set(largest)


def steps_of(rng, shape, pieces, smallest, largest):
    factor_of = 1.0
    for axis_at, parts in pieces:
        draws = jax.random.uniform(jax.random.fold_in(jax.random.fold_in(rng, 6), axis_at), (parts,), jnp.float32, smallest / len(pieces), largest / len(pieces))
        factor_of = factor_of * jnp.repeat(jnp.exp(draws), shape[axis_at] // parts).reshape((-1,) + (1,) * (len(shape) - 1 - axis_at))
    return factor_of


def gaussian(own_key, shape, spread, most, cuts=(), held_as=jnp.bfloat16):
    array = spread * jax.random.normal(own_key, shape, jnp.float32)
    if cuts:
        array = array * steps_of(own_key, shape, cuts, -0.22, 0.18)
    return jnp.clip(array, -most, most).astype(held_as)


def setup_inputs(seed: int = 0) -> dict:
    seeds = jax.random.split(jax.random.key(seed), 18)
    node_feat = gaussian(seeds[0], (FEAT, NODES), 1.0, 6.0, ((1, 32),))
    node_pos = gaussian(seeds[1], (3, NODES), 0.5, 4.0, ((1, 32),))
    node_cot = gaussian(seeds[2], (FEAT, NODES), 1.0, 6.0, ((1, 32),))
    mesh_senders = place_ends(jax.random.randint(seeds[3], (DEVICES * EDGE_DEV,), 0, NODE_DEV + 2 * HALO), jax.random.fold_in(seeds[3], 1), 0, (NODE_DEV + 2 * HALO) - 1).astype(jnp.int32)
    edge_mask = place_ends((jax.random.randint(seeds[4], (DEVICES * EDGE_DEV,), 0, 8) < 7).astype(jnp.int32), jax.random.fold_in(seeds[4], 1), 0, 1)
    halo_up = place_ends(jax.random.randint(seeds[5], (DEVICES * HALO,), 0, NODE_DEV), jax.random.fold_in(seeds[5], 1), 0, NODE_DEV - 1).astype(jnp.int32)
    halo_down = place_ends(jax.random.randint(seeds[6], (DEVICES * HALO,), 0, NODE_DEV), jax.random.fold_in(seeds[6], 1), 0, NODE_DEV - 1).astype(jnp.int32)
    contact_rows = place_ends(jax.random.randint(seeds[7], (DEVICES * CON_DEV,), 0, NODE_DEV), jax.random.fold_in(seeds[7], 1), 0, NODE_DEV - 1).astype(jnp.int32)
    contact_dst = place_ends(jax.random.randint(seeds[8], (DEVICES * CON_DEV,), 0, NODE_DEV), jax.random.fold_in(seeds[8], 1), 0, NODE_DEV - 1).astype(jnp.int32)
    contact_mask = draw_contact_mask(jax.random.fold_in(seeds[17], 71), 0)
    w_one = gaussian(seeds[10], (HID, 2 * CS), (2 * CS) ** -0.5, 0.5)
    b_one = gaussian(seeds[11], (HID,), 0.5, 3.0, (), jnp.float32)
    w_dist = gaussian(seeds[12], (HID,), 0.5, 3.0, (), jnp.float32)
    w_two = gaussian(seeds[13], (GATES, HID), HID ** -0.5, 0.5)
    w_scal = gaussian(seeds[14], (CS, CS), CS ** -0.5, 0.75)
    w_vec = gaussian(seeds[15], (CV, CV), CV ** -0.5, 1.0)
    w_ten = gaussian(seeds[16], (CT, CT), CT ** -0.5, 1.5)
    return dict(node_feat=node_feat, node_pos=node_pos, node_cot=node_cot, mesh_senders=mesh_senders, edge_mask=edge_mask, halo_up=halo_up, halo_down=halo_down, contact_rows=contact_rows, contact_dst=contact_dst, contact_mask=contact_mask, w_one=w_one, b_one=b_one, w_dist=w_dist, w_two=w_two, w_scal=w_scal, w_vec=w_vec, w_ten=w_ten)


def matmul(lhs_matrix, rhs_matrix):
    return jnp.dot(lhs_matrix.astype(jnp.float32), rhs_matrix.astype(jnp.float32), preferred_element_type=jnp.float32)

def contract(lhs_matrix, rhs_matrix, contracted):
    return lax.dot_general(lhs_matrix.astype(jnp.float32), rhs_matrix.astype(jnp.float32), (contracted, ((), ())), preferred_element_type=jnp.float32)

def edge_block(totals, feat_own, pos_own, source_table, source_pos, back_rows, edge_weights, senders, receivers, live_mask):
    aggregate, grad_one, grad_bias, grad_dist, grad_two = totals
    w_one, b_one, w_dist, w_two = edge_weights
    edge_count = senders.shape[0]
    source = jnp.take(source_table, senders, axis=1)
    scal_send = source[:CS]
    scal_recv = jnp.take(feat_own[:CS], receivers, axis=1)
    inputs = jnp.concatenate([scal_recv, scal_send], 0)
    offset = jnp.take(source_pos, senders, axis=1).astype(jnp.float32) - jnp.take(pos_own, receivers, axis=1).astype(jnp.float32)
    distance = lax.optimization_barrier(jnp.sum(offset * offset, 0))
    linear = matmul(w_one, inputs) + b_one[:, None] + w_dist[:, None] * distance[None]
    squashed = jax.nn.sigmoid(linear)
    hidden = (linear * squashed).astype(jnp.bfloat16)
    gate_values = matmul(w_two, hidden) * live_mask[None]
    gate_scal = gate_values[:CS]
    gate_vec = gate_values[CS:CS + CV]
    gate_dir = gate_values[CS + CV:CS + 2 * CV]
    gate_ten = gate_values[CS + 2 * CV:]
    send_scal = scal_send.astype(jnp.float32)
    send_vec = source[CS:CS + 3 * CV].astype(jnp.float32).reshape(3, CV, edge_count)
    send_ten = source[CS + 3 * CV:].astype(jnp.float32).reshape(9, CT, edge_count)
    message = jnp.concatenate([gate_scal * send_scal, (gate_vec[None] * send_vec + gate_dir[None] * offset[:, None]).reshape(3 * CV, edge_count), (gate_ten[None] * send_ten).reshape(9 * CT, edge_count)], 0)
    aggregate = aggregate.at[:, receivers].add(message)
    back_edge = jnp.take(back_rows, receivers, axis=1).astype(jnp.float32)
    back_vec = back_edge[CS:CS + 3 * CV].reshape(3, CV, edge_count)
    back_ten = back_edge[CS + 3 * CV:].reshape(9, CT, edge_count)
    dgates = jnp.concatenate([back_edge[:CS] * send_scal, lax.optimization_barrier(jnp.sum(back_vec * send_vec, 0)), lax.optimization_barrier(jnp.sum(back_vec * offset[:, None], 0)), lax.optimization_barrier(jnp.sum(back_ten * send_ten, 0))], 0)
    dgates = (dgates * live_mask[None]).astype(jnp.bfloat16)
    grad_two = grad_two + contract(dgates, hidden, ((1,), (1,)))
    hidden_grad = contract(w_two, dgates, ((0,), (0,)))
    linear_grad = (hidden_grad * squashed * (1.0 + linear * (1.0 - squashed))).astype(jnp.bfloat16)
    grad_one = grad_one + contract(linear_grad, inputs, ((1,), (1,)))
    grad_float = linear_grad.astype(jnp.float32)
    grad_bias = grad_bias + lax.optimization_barrier(jnp.sum(grad_float, 1))
    grad_dist = grad_dist + lax.optimization_barrier(jnp.sum(grad_float * distance[None], 1))
    return (aggregate, grad_one, grad_bias, grad_dist, grad_two)

def mix_channels(weight, field, form):
    return jnp.einsum(form, weight.astype(jnp.float32), field.astype(jnp.float32), preferred_element_type=jnp.float32)

def node_update(feat_own, agg_rows, w_scal, w_vec, w_ten):
    node_count = feat_own.shape[1]
    feat_float = feat_own.astype(jnp.float32)
    out_scal = feat_float[:CS] + matmul(w_scal, agg_rows[:CS])
    out_vec = feat_float[CS:CS + 3 * CV] + mix_channels(w_vec, agg_rows[CS:CS + 3 * CV].reshape(3, CV, node_count), 'cd,kdn->kcn').reshape(3 * CV, node_count)
    out_ten = feat_float[CS + 3 * CV:] + mix_channels(w_ten, agg_rows[CS + 3 * CV:].reshape(9, CT, node_count), 'cd,kdn->kcn').reshape(9 * CT, node_count)
    return jnp.concatenate([out_scal, out_vec, out_ten], 0).astype(jnp.bfloat16)

def node_backward(cotangent, w_scal, w_vec, w_ten):
    node_count = cotangent.shape[1]
    back_scal = contract(w_scal, cotangent[:CS], ((0,), (0,)))
    back_vec = mix_channels(w_vec, cotangent[CS:CS + 3 * CV].reshape(3, CV, node_count), 'cd,kcn->kdn').reshape(3 * CV, node_count)
    back_ten = mix_channels(w_ten, cotangent[CS + 3 * CV:].reshape(9, CT, node_count), 'cd,kcn->kdn').reshape(9 * CT, node_count)
    return jnp.concatenate([back_scal, back_vec, back_ten], 0).astype(jnp.bfloat16)

def node_grads(cotangent, agg_rows):
    node_count = cotangent.shape[1]
    grad_scal = contract(cotangent[:CS], agg_rows[:CS], ((1,), (1,)))
    grad_vec = mix_channels(cotangent[CS:CS + 3 * CV].reshape(3, CV, node_count), agg_rows[CS:CS + 3 * CV].reshape(3, CV, node_count), 'kcn,kdn->cd')
    grad_ten = mix_channels(cotangent[CS + 3 * CV:].reshape(9, CT, node_count), agg_rows[CS + 3 * CV:].reshape(9, CT, node_count), 'kcn,kdn->cd')
    return (grad_scal, grad_vec, grad_ten)

def reference(node_feat, node_pos, node_cot, mesh_senders, edge_mask, halo_up, halo_down, contact_rows, contact_dst, contact_mask, w_one, b_one, w_dist, w_two, w_scal, w_vec, w_ten):

    def one_part(partition):
        dom_index = partition // N_SUB
        sub_index = partition % N_SUB
        lower_part = dom_index * N_SUB + (sub_index + N_SUB - 1) % N_SUB
        upper_part = dom_index * N_SUB + (sub_index + 1) % N_SUB
        own_cols = partition * NODE_DEV + jnp.arange(NODE_DEV, dtype=jnp.int32)
        low_cols = lax.dynamic_slice_in_dim(halo_up, lower_part * HALO, HALO) + lower_part * NODE_DEV
        high_cols = lax.dynamic_slice_in_dim(halo_down, upper_part * HALO, HALO) + upper_part * NODE_DEV
        asked_cols = lax.dynamic_slice_in_dim(contact_rows, partition * CON_DEV, CON_DEV) + jnp.arange(CON_DEV, dtype=jnp.int32) // CAP * NODE_DEV
        columns = jnp.concatenate([own_cols, low_cols, high_cols, asked_cols]).astype(jnp.int32)
        source_table = jnp.take(node_feat, columns, axis=1)
        source_pos = jnp.take(node_pos, columns, axis=1)
        feat_own = source_table[:, :NODE_DEV]
        pos_own = source_pos[:, :NODE_DEV]
        cotangent = lax.dynamic_slice_in_dim(node_cot, partition * NODE_DEV, NODE_DEV, 1)
        senders = jnp.concatenate([lax.dynamic_slice_in_dim(mesh_senders, partition * EDGE_DEV, EDGE_DEV), NODE_DEV + 2 * HALO + jnp.arange(CON_DEV, dtype=jnp.int32)]).astype(jnp.int32)
        receivers = jnp.concatenate([jnp.arange(EDGE_DEV, dtype=jnp.int32) // DEGREE, lax.dynamic_slice_in_dim(contact_dst, partition * CON_DEV, CON_DEV)]).astype(jnp.int32)
        live_mask = jnp.concatenate([lax.dynamic_slice_in_dim(edge_mask, partition * EDGE_DEV, EDGE_DEV), lax.dynamic_slice_in_dim(contact_mask, partition * CON_DEV, CON_DEV)]).astype(jnp.float32)
        back_rows = node_backward(cotangent, w_scal, w_vec, w_ten)
        initial = (jnp.zeros((FEAT, NODE_DEV), jnp.float32), jnp.zeros((HID, 2 * CS), jnp.float32), jnp.zeros((HID,), jnp.float32), jnp.zeros((HID,), jnp.float32), jnp.zeros((GATES, HID), jnp.float32))
        aggregate, grad_one, grad_bias, grad_dist, grad_two = edge_block(initial, feat_own, pos_own, source_table, source_pos, back_rows, (w_one, b_one, w_dist, w_two), senders, receivers, live_mask)
        agg_rows = aggregate.astype(jnp.bfloat16)
        updated = node_update(feat_own, agg_rows, w_scal, w_vec, w_ten)
        grad_scal, grad_vec, grad_ten = node_grads(cotangent, agg_rows)
        return (updated, (grad_one, grad_bias, grad_dist, grad_two, grad_scal, grad_vec, grad_ten))
    outputs, gradients = lax.map(one_part, jnp.arange(DEVICES, dtype=jnp.int32))
    node_out = jnp.transpose(outputs, (1, 0, 2)).reshape(FEAT, DEVICES * NODE_DEV)
    grad_scale = 1.0 / math.sqrt(DEVICES * EDGE_DEV)
    summed = [lax.optimization_barrier(jnp.sum(member, 0)) * grad_scale for member in gradients]
    return (node_out, summed[0], summed[1], summed[2], summed[3], summed[4], summed[5], summed[6])
```

```python
import functools
import math

import jax
import jax.numpy as jnp
from jax import lax
from jax.experimental import pallas as pl
from jax.experimental.pallas import tpu as pltpu
from jax.sharding import PartitionSpec as P

CS = 64
CV = 32
CT = 16
HID = 128
DEGREE = 6
GATES = 144
FEAT = CS + 3 * CV + 9 * CT
ROWS = 320
LANES = 128
CHUNK = 512
VMEM_BYTES = 48 * 1024 * 1024


def dot(lhs, rhs, lhs_dim=1, rhs_dim=0):
    return lax.dot_general(
        lhs, rhs, (((lhs_dim,), (rhs_dim,)), ((), ())), preferred_element_type=jnp.float32
    )


def one_hot(code, width):
    rows = lax.broadcasted_iota(jnp.int32, (width, code.shape[1]), 0)
    return jnp.where(rows == code, 1.0, 0.0).astype(jnp.bfloat16)


def split_index(index):
    high = index // 128
    return high.astype(jnp.bfloat16), (index - high * 128).astype(jnp.bfloat16)


def join_index(table, row):
    pair = table[row : row + 2].astype(jnp.float32)
    return (pair[0:1] * 128.0 + pair[1:2]).astype(jnp.int32)


def table_kernel(feat_ref, pos_ref, up_ref, down_ref, table_ref):
    node_count = feat_ref.shape[1]
    table_ref[:FEAT] = feat_ref[...]
    rows = lax.broadcasted_iota(jnp.int32, (ROWS - FEAT, node_count), 0)
    pos = pos_ref[...].astype(jnp.float32)
    tail = jnp.zeros((ROWS - FEAT, node_count), jnp.float32)
    for k in range(3):
        tail = jnp.where(rows == k, pos[k : k + 1], tail)
    for k, index_ref in ((3, up_ref), (5, down_ref)):
        index = index_ref[...]
        high = index >> 7
        tail = jnp.where(rows == k, high.astype(jnp.float32), tail)
        tail = jnp.where(rows == k + 1, (index - (high << 7)).astype(jnp.float32), tail)
    table_ref[FEAT:] = tail.astype(jnp.bfloat16)


def contact_gather_kernel(slot, table_ref, wanted_ref, out_ref):
    node_count = table_ref.shape[1]
    parts = LANES // slot
    height = out_ref.shape[1]
    per_chunk = CHUNK // slot
    for chunk in range(wanted_ref.shape[0]):
        hot = one_hot(wanted_ref[chunk], node_count)
        rows = dot(table_ref[...], hot).astype(jnp.bfloat16)
        if parts * height > ROWS:
            rows = jnp.concatenate(
                [rows, jnp.zeros((parts * height - ROWS, CHUNK), jnp.bfloat16)], 0
            )
        for peer in range(per_chunk):
            out_ref[chunk * per_chunk + peer] = jnp.concatenate(
                [
                    rows[part * height : (part + 1) * height, peer * slot : (peer + 1) * slot]
                    for part in range(parts)
                ],
                1,
            )


def edge_math(src, recv_linear, scal_recv, pos_recv, back, live, weights):
    w_send, w_dist, w_two, w_two_t = weights
    edges = src.shape[1]
    send_scal = src[:CS].astype(jnp.bfloat16)
    offset = src[FEAT : FEAT + 3] - pos_recv
    if live is not None:
        offset = offset * live
    distance = jnp.sum(offset * offset, 0, keepdims=True)
    linear = recv_linear + dot(w_send, send_scal) + w_dist * distance
    squashed = 0.5 * jnp.tanh(0.5 * linear) + 0.5
    hidden = (linear * squashed).astype(jnp.bfloat16)
    gates = dot(w_two, hidden)
    gate_vec = gates[CS : CS + CV]
    gate_dir = gates[CS + CV : CS + 2 * CV]
    gate_ten = gates[CS + 2 * CV :]
    message = [gates[:CS] * src[:CS]]
    vec_part = jnp.zeros((CV, edges), jnp.float32)
    dir_part = jnp.zeros((CV, edges), jnp.float32)
    for k in range(3):
        rows = slice(CS + k * CV, CS + (k + 1) * CV)
        message.append(gate_vec * src[rows] + gate_dir * offset[k : k + 1])
        vec_part = vec_part + back[rows] * src[rows]
        dir_part = dir_part + back[rows] * offset[k : k + 1]
    ten_part = jnp.zeros((CT, edges), jnp.float32)
    for m in range(9):
        rows = slice(CS + 3 * CV + m * CT, CS + 3 * CV + (m + 1) * CT)
        message.append(gate_ten * src[rows])
        ten_part = ten_part + back[rows] * src[rows]
    message = jnp.concatenate(message, 0)
    dgates = jnp.concatenate([back[:CS] * src[:CS], vec_part, dir_part, ten_part], 0).astype(
        jnp.bfloat16
    )
    hidden_grad = dot(w_two_t, dgates)
    linear_grad = (hidden_grad * squashed * (1.0 + linear * (1.0 - squashed))).astype(jnp.bfloat16)
    rows = lax.broadcasted_iota(jnp.int32, (16, edges), 0)
    coarse = distance.astype(jnp.bfloat16).astype(jnp.float32)
    extra = jnp.where(
        rows == 0, 1.0, jnp.where(rows == 1, coarse, jnp.where(rows == 2, distance - coarse, 0.0))
    ).astype(jnp.bfloat16)
    inputs = jnp.concatenate([scal_recv, send_scal], 0)
    grads = (
        dot(linear_grad, inputs, 1, 1),
        dot(dgates, hidden, 1, 1),
        dot(extra, linear_grad, 1, 1),
    )
    return message, grads


def block_diagonal(block_ref, w_scal, w_vec, w_ten):
    block_ref[...] = jnp.zeros_like(block_ref)
    block_ref[:CS, :CS] = w_scal[...]
    for k in range(3):
        rows = slice(CS + k * CV, CS + (k + 1) * CV)
        block_ref[rows, rows] = w_vec[...]
    for m in range(9):
        rows = slice(CS + 3 * CV + m * CT, CS + 3 * CV + (m + 1) * CT)
        block_ref[rows, rows] = w_ten[...]


def mesh_kernel(
    table_ref,
    low_ref,
    high_ref,
    code_ref,
    cot_ref,
    w_one_ref,
    b_one_ref,
    w_dist_ref,
    w_two_ref,
    w_scal_ref,
    w_vec_ref,
    w_ten_ref,
    agg_ref,
    back_ref,
    grad_one_ref,
    grad_two_ref,
    extra_ref,
    source_ref,
    block_ref,
):
    node_count = table_ref.shape[1]
    source_ref[:, :node_count] = table_ref[...]
    low = low_ref[...]
    high = high_ref[...]
    source_ref[:, node_count : 2 * node_count] = dot(
        low, one_hot(join_index(low, FEAT + 3), node_count)
    ).astype(jnp.bfloat16)
    source_ref[:, 2 * node_count :] = dot(
        high, one_hot(join_index(high, FEAT + 5), node_count)
    ).astype(jnp.bfloat16)
    block_diagonal(block_ref, w_scal_ref, w_vec_ref, w_ten_ref)
    back_ref[...] = dot(block_ref[...], cot_ref[...], 0, 0).astype(jnp.bfloat16)
    w_one = w_one_ref[...]
    w_two = w_two_ref[...]
    scal_recv = table_ref[:CS]
    recv_linear = dot(w_one[:, :CS], scal_recv) + b_one_ref[...]
    weights = (w_one[:, CS:], w_dist_ref[...], w_two, w_two.T)
    pos_recv = table_ref[FEAT:].astype(jnp.float32)[:3]
    grad_one_ref[...] = jnp.zeros_like(grad_one_ref)
    grad_two_ref[...] = jnp.zeros_like(grad_two_ref)
    extra_ref[...] = jnp.zeros_like(extra_ref)
    agg_ref[...] = jnp.zeros_like(agg_ref)
    for step in range(DEGREE):
        code = code_ref[step]
        src = dot(source_ref[...], one_hot(code, 3 * node_count))
        live = jnp.where(code >= 0, 1.0, 0.0)
        back = back_ref[...].astype(jnp.float32)
        message, grads = edge_math(src, recv_linear, scal_recv, pos_recv, back, live, weights)
        agg_ref[...] += message
        grad_one_ref[...] += grads[0]
        grad_two_ref[...] += grads[1]
        extra_ref[...] += grads[2]


def contact_kernel(
    slot,
    grad_scale,
    reply_ref,
    code_ref,
    table_ref,
    back_ref,
    agg_in_ref,
    one_in_ref,
    two_in_ref,
    extra_in_ref,
    cot_ref,
    w_one_ref,
    b_one_ref,
    w_dist_ref,
    w_two_ref,
    w_scal_ref,
    w_vec_ref,
    w_ten_ref,
    out_ref,
    packed_ref,
    agg_ref,
    receive_ref,
    block_ref,
):
    node_count = table_ref.shape[1]
    parts = LANES // slot
    per_chunk = CHUNK // slot
    receive_ref[:CS] = table_ref[:CS]
    receive_ref[CS : CS + 16] = table_ref[FEAT:]
    receive_ref[CS + 16 :] = back_ref[...]
    w_one = w_one_ref[...]
    w_two = w_two_ref[...]
    weights = (w_one[:, CS:], w_dist_ref[...], w_two, w_two.T)
    agg_ref[...] = agg_in_ref[...]
    grad_one = one_in_ref[...]
    grad_two = two_in_ref[...]
    extra = extra_in_ref[...]
    for chunk in range(code_ref.shape[0]):
        blocks = [reply_ref[chunk * per_chunk + peer] for peer in range(per_chunk)]
        src = jnp.concatenate(
            [
                jnp.concatenate(
                    [block[:, part * slot : (part + 1) * slot] for block in blocks], 1
                )
                for part in range(parts)
            ],
            0,
        )[:ROWS].astype(jnp.float32)
        hot = one_hot(code_ref[chunk], node_count)
        recv = dot(receive_ref[...], hot)
        scal_recv = recv[:CS].astype(jnp.bfloat16)
        recv_linear = dot(w_one[:, :CS], scal_recv) + b_one_ref[...]
        message, grads = edge_math(
            src, recv_linear, scal_recv, recv[CS : CS + 3], recv[CS + 16 :], None, weights
        )
        agg_ref[...] += dot(message.astype(jnp.bfloat16), hot, 1, 1)
        grad_one = grad_one + grads[0]
        grad_two = grad_two + grads[1]
        extra = extra + grads[2]
    block_diagonal(block_ref, w_scal_ref, w_vec_ref, w_ten_ref)
    agg_rows = agg_ref[...].astype(jnp.bfloat16)
    out_ref[...] = (
        table_ref[:FEAT].astype(jnp.float32) + dot(block_ref[...], agg_rows)
    ).astype(jnp.bfloat16)
    cot = cot_ref[...]
    packed_ref[:HID] = grad_one * grad_scale
    packed_ref[HID : HID + GATES] = grad_two * grad_scale
    low = HID + GATES
    packed_ref[low : low + CS] = jnp.zeros((CS, LANES), jnp.float32)
    packed_ref[low : low + CS, :CS] = dot(cot[:CS], agg_rows[:CS], 1, 1) * grad_scale
    grad_vec = jnp.zeros((CV, CV), jnp.float32)
    for k in range(3):
        rows = slice(CS + k * CV, CS + (k + 1) * CV)
        grad_vec = grad_vec + dot(cot[rows], agg_rows[rows], 1, 1)
    packed_ref[low : low + CV, CS : CS + CV] = grad_vec * grad_scale
    grad_ten = jnp.zeros((CT, CT), jnp.float32)
    for m in range(9):
        rows = slice(CS + 3 * CV + m * CT, CS + 3 * CV + (m + 1) * CT)
        grad_ten = grad_ten + dot(cot[rows], agg_rows[rows], 1, 1)
    packed_ref[low : low + CT, CS + CV : CS + CV + CT] = grad_ten * grad_scale
    packed_ref[low + CS : low + CS + 8] = extra[:8] * grad_scale


def call(kernel, out_shape, scratch=()):
    return pl.pallas_call(
        kernel,
        out_shape=out_shape,
        scratch_shapes=list(scratch),
        compiler_params=pltpu.CompilerParams(vmem_limit_bytes=VMEM_BYTES),
    )


def shaped(shape, dtype):
    return jax.ShapeDtypeStruct(shape, dtype)


def from_behind(shard, axis, by):
    peers = lax.axis_size(axis)
    return lax.ppermute(shard, axis, [(i, (i + by) % peers) for i in range(peers)])


def on_device(
    node_feat,
    node_pos,
    node_cot,
    mesh_senders,
    edge_mask,
    halo_up,
    halo_down,
    contact_rows,
    contact_dst,
    contact_mask,
    w_one,
    b_one,
    w_dist,
    w_two,
    w_scal,
    w_vec,
    w_ten,
):
    f32, bf16 = jnp.float32, jnp.bfloat16
    node_count = node_feat.shape[1]
    contact_count = contact_rows.shape[0]
    device_count = lax.axis_size("dom") * lax.axis_size("sub")
    slot = contact_count // device_count
    chunks = contact_count // CHUNK
    parts = LANES // slot
    height = -(-ROWS // (parts * 16)) * 16
    grad_scale = 1.0 / math.sqrt(device_count * node_count * DEGREE)
    wanted = lax.all_to_all(
        contact_rows.reshape(device_count, slot),
        ("dom", "sub"),
        split_axis=0,
        concat_axis=0,
        tiled=True,
    ).reshape(chunks, 1, CHUNK)
    table = call(table_kernel, shaped((ROWS, node_count), bf16))(
        node_feat, node_pos, halo_up[None], halo_down[None]
    )
    low = from_behind(table, "sub", 1)
    high = from_behind(table, "sub", -1)
    replies = call(
        functools.partial(contact_gather_kernel, slot), shaped((device_count, height, LANES), bf16)
    )(table, wanted)
    replies = lax.all_to_all(
        replies, ("dom", "sub"), split_axis=0, concat_axis=0, tiled=True
    )
    mesh_code = (
        jnp.where(edge_mask != 0, mesh_senders, -1)
        .reshape(node_count, DEGREE)
        .T.reshape(DEGREE, 1, node_count)
    )
    contact_code = jnp.where(contact_mask != 0, contact_dst, -1).reshape(chunks, 1, CHUNK)
    weights = (w_one, b_one[:, None], w_dist[:, None], w_two, w_scal, w_vec, w_ten)
    agg, back, grad_one, grad_two, extra = call(
        mesh_kernel,
        (
            shaped((FEAT, node_count), f32),
            shaped((FEAT, node_count), bf16),
            shaped((HID, 2 * CS), f32),
            shaped((GATES, HID), f32),
            shaped((16, HID), f32),
        ),
        (
            pltpu.VMEM((ROWS, 3 * node_count), bf16),
            pltpu.VMEM((FEAT, FEAT), bf16),
        ),
    )(table, low, high, mesh_code, node_cot, *weights)
    packed_rows = HID + GATES + CS + 8
    node_out, packed = call(
        functools.partial(contact_kernel, slot, grad_scale),
        (shaped((FEAT, node_count), bf16), shaped((packed_rows, LANES), f32)),
        (
            pltpu.VMEM((FEAT, node_count), f32),
            pltpu.VMEM((CS + 16 + FEAT, node_count), bf16),
            pltpu.VMEM((FEAT, FEAT), bf16),
        ),
    )(
        replies,
        contact_code,
        table,
        back,
        agg,
        grad_one,
        grad_two,
        extra,
        node_cot,
        *weights,
    )
    packed = lax.psum(packed, ("dom", "sub"))
    base = HID + GATES
    return (
        node_out,
        packed[:HID],
        packed[base + CS],
        packed[base + CS + 1] + packed[base + CS + 2],
        packed[HID:base],
        packed[base : base + CS, :CS],
        packed[base : base + CV, CS : CS + CV],
        packed[base : base + CT, CS + CV : CS + CV + CT],
    )


def solution(mesh):
    along = P(("dom", "sub"))
    columns = P(None, ("dom", "sub"))
    in_specs = (columns,) * 3 + (along,) * 7 + (P(),) * 7
    out_specs = (columns,) + (P(),) * 7
    return jax.shard_map(
        on_device, mesh=mesh, in_specs=in_specs, out_specs=out_specs, check_vma=False
    )
```

```python
import functools
import math

import jax
import jax.numpy as jnp
from jax import lax
from jax.experimental import pallas as pl
from jax.experimental.pallas import tpu as pltpu
from jax.sharding import PartitionSpec as P

CS = 64
CV = 32
CT = 16
HID = 128
DEGREE = 6
GATES = 144
FEAT = CS + 3 * CV + 9 * CT
ROWS = 320
LANES = 128
CHUNK = 512
VMEM_BYTES = 48 * 1024 * 1024


def dot(lhs, rhs, lhs_dim=1, rhs_dim=0):
    return lax.dot_general(
        lhs, rhs, (((lhs_dim,), (rhs_dim,)), ((), ())), preferred_element_type=jnp.float32
    )


def one_hot(code, width):
    rows = lax.broadcasted_iota(jnp.int32, (width, code.shape[1]), 0)
    return jnp.where(rows == code, 1.0, 0.0).astype(jnp.bfloat16)


def join_index(table, row):
    pair = table[row : row + 2].astype(jnp.float32)
    return (pair[0:1] * 128.0 + pair[1:2]).astype(jnp.int32)


def table_kernel(feat_ref, pos_ref, up_ref, down_ref, table_ref, up_scr, down_scr, sems):
    node_count = table_ref.shape[1]
    copies = [
        pltpu.make_async_copy(up_ref, up_scr, sems.at[0]),
        pltpu.make_async_copy(down_ref, down_scr, sems.at[1]),
        pltpu.make_async_copy(feat_ref, table_ref.at[:FEAT], sems.at[2]),
    ]
    for copy in copies:
        copy.start()
    rows = lax.broadcasted_iota(jnp.int32, (ROWS - FEAT, node_count), 0)
    pos = pos_ref[...].astype(jnp.float32)
    tail = jnp.zeros((ROWS - FEAT, node_count), jnp.float32)
    for k in range(3):
        tail = jnp.where(rows == k, pos[k : k + 1], tail)
    copies[0].wait()
    copies[1].wait()
    for k, index_ref in ((3, up_scr), (5, down_scr)):
        index = index_ref[...]
        high = index >> 7
        tail = jnp.where(rows == k, high.astype(jnp.float32), tail)
        tail = jnp.where(rows == k + 1, (index - (high << 7)).astype(jnp.float32), tail)
    table_ref[FEAT:] = tail.astype(jnp.bfloat16)
    copies[2].wait()


def contact_gather_kernel(slot, table_ref, wanted_ref, low_ref, high_ref, out_ref):
    node_count = table_ref.shape[1]
    parts = LANES // slot
    height = out_ref.shape[1]
    per_chunk = CHUNK // slot
    for chunk in range(wanted_ref.shape[0] // per_chunk):
        wanted = [wanted_ref[chunk * per_chunk + peer] for peer in range(per_chunk)]
        hot = one_hot(jnp.concatenate(wanted, 1), node_count)
        rows = dot(table_ref[...], hot).astype(jnp.bfloat16)
        if parts * height > ROWS:
            rows = jnp.concatenate(
                [rows, jnp.zeros((parts * height - ROWS, CHUNK), jnp.bfloat16)], 0
            )
        for peer in range(per_chunk):
            out_ref[chunk * per_chunk + peer] = jnp.concatenate(
                [
                    rows[part * height : (part + 1) * height, peer * slot : (peer + 1) * slot]
                    for part in range(parts)
                ],
                1,
            )


def edge_math(src, recv_linear, scal_recv, pos_recv, back, live, weights):
    w_send, w_dist, w_two, w_two_t = weights
    edges = src.shape[1]
    send_scal = src[:CS].astype(jnp.bfloat16)
    offset = src[FEAT : FEAT + 3] - pos_recv
    if live is not None:
        offset = offset * live
    distance = jnp.sum(offset * offset, 0, keepdims=True)
    linear = recv_linear + dot(w_send, send_scal) + w_dist * distance
    squashed = 0.5 * jnp.tanh(0.5 * linear) + 0.5
    hidden = (linear * squashed).astype(jnp.bfloat16)
    gates = dot(w_two, hidden)
    gate_vec = gates[CS : CS + CV]
    gate_dir = gates[CS + CV : CS + 2 * CV]
    gate_ten = gates[CS + 2 * CV :]
    message = [gates[:CS] * src[:CS]]
    vec_part = jnp.zeros((CV, edges), jnp.float32)
    dir_part = jnp.zeros((CV, edges), jnp.float32)
    for k in range(3):
        rows = slice(CS + k * CV, CS + (k + 1) * CV)
        message.append(gate_vec * src[rows] + gate_dir * offset[k : k + 1])
        vec_part = vec_part + back[rows] * src[rows]
        dir_part = dir_part + back[rows] * offset[k : k + 1]
    ten_part = jnp.zeros((CT, edges), jnp.float32)
    for m in range(9):
        rows = slice(CS + 3 * CV + m * CT, CS + 3 * CV + (m + 1) * CT)
        message.append(gate_ten * src[rows])
        ten_part = ten_part + back[rows] * src[rows]
    message = jnp.concatenate(message, 0)
    dgates = jnp.concatenate([back[:CS] * src[:CS], vec_part, dir_part, ten_part], 0).astype(
        jnp.bfloat16
    )
    hidden_grad = dot(w_two_t, dgates)
    linear_grad = (hidden_grad * squashed * (1.0 + linear * (1.0 - squashed))).astype(jnp.bfloat16)
    rows = lax.broadcasted_iota(jnp.int32, (16, edges), 0)
    coarse = distance.astype(jnp.bfloat16).astype(jnp.float32)
    extra = jnp.where(
        rows == 0, 1.0, jnp.where(rows == 1, coarse, jnp.where(rows == 2, distance - coarse, 0.0))
    ).astype(jnp.bfloat16)
    inputs = jnp.concatenate([scal_recv, send_scal], 0)
    grads = (
        dot(linear_grad, inputs, 1, 1),
        dot(dgates, hidden, 1, 1),
        dot(extra, linear_grad, 1, 1),
    )
    return message, grads


def add_grads(grads_ref, grads):
    grads_ref[:HID] += grads[0]
    grads_ref[HID : HID + GATES] += grads[1]
    grads_ref[HID + GATES : HID + GATES + 16] += grads[2]


def block_diagonal(block_ref, w_scal, w_vec, w_ten):
    block_ref[...] = jnp.zeros_like(block_ref)
    block_ref[:CS, :CS] = w_scal[...]
    for k in range(3):
        rows = slice(CS + k * CV, CS + (k + 1) * CV)
        block_ref[rows, rows] = w_vec[...]
    for m in range(9):
        rows = slice(CS + 3 * CV + m * CT, CS + 3 * CV + (m + 1) * CT)
        block_ref[rows, rows] = w_ten[...]


def mesh_kernel(
    table_ref,
    low_ref,
    high_ref,
    code_ref,
    cot_ref,
    w_one_ref,
    b_one_ref,
    w_dist_ref,
    w_two_ref,
    w_scal_ref,
    w_vec_ref,
    w_ten_ref,
    agg_out_ref,
    grads_out_ref,
    agg_ref,
    grads_ref,
    back_ref,
    source_ref,
    block_ref,
    sems,
):
    node_count = table_ref.shape[1]
    source_ref[:, :node_count] = table_ref[...]
    low = low_ref[...]
    high = high_ref[...]
    source_ref[:, node_count : 2 * node_count] = dot(
        low, one_hot(join_index(low, FEAT + 3), node_count)
    ).astype(jnp.bfloat16)
    source_ref[:, 2 * node_count :] = dot(
        high, one_hot(join_index(high, FEAT + 5), node_count)
    ).astype(jnp.bfloat16)
    block_diagonal(block_ref, w_scal_ref, w_vec_ref, w_ten_ref)
    back_ref[...] = dot(block_ref[...], cot_ref[...], 0, 0).astype(jnp.bfloat16)
    w_one = w_one_ref[...]
    w_two = w_two_ref[...]
    scal_recv = table_ref[:CS]
    recv_linear = dot(w_one[:, :CS], scal_recv) + b_one_ref[...]
    weights = (w_one[:, CS:], w_dist_ref[...], w_two, w_two.T)
    pos_recv = table_ref[FEAT:].astype(jnp.float32)[:3]
    grads_ref[...] = jnp.zeros_like(grads_ref)
    agg_ref[...] = jnp.zeros_like(agg_ref)
    for step in range(DEGREE):
        code = code_ref[step]
        src = dot(source_ref[...], one_hot(code, 3 * node_count))
        live = jnp.where(code >= 0, 1.0, 0.0)
        back = back_ref[...].astype(jnp.float32)
        message, grads = edge_math(src, recv_linear, scal_recv, pos_recv, back, live, weights)
        agg_ref[...] += message
        add_grads(grads_ref, grads)
    copies = [
        pltpu.make_async_copy(agg_ref, agg_out_ref, sems.at[0]),
        pltpu.make_async_copy(grads_ref, grads_out_ref, sems.at[1]),
    ]
    for copy in copies:
        copy.start()
    for copy in copies:
        copy.wait()


def contact_kernel(
    slot,
    grad_scale,
    reply_ref,
    code_ref,
    table_ref,
    cot_ref,
    mesh_agg_ref,
    mesh_grads_ref,
    w_one_ref,
    b_one_ref,
    w_dist_ref,
    w_two_ref,
    w_scal_ref,
    w_vec_ref,
    w_ten_ref,
    out_ref,
    packed_ref,
    agg_ref,
    grads_ref,
    mesh_agg_scr,
    mesh_grads_scr,
    receive_ref,
    block_ref,
    sems,
):
    copies = [
        pltpu.make_async_copy(mesh_agg_ref, mesh_agg_scr, sems.at[0]),
        pltpu.make_async_copy(mesh_grads_ref, mesh_grads_scr, sems.at[1]),
    ]
    for copy in copies:
        copy.start()
    node_count = table_ref.shape[1]
    parts = LANES // slot
    per_chunk = CHUNK // slot
    block_diagonal(block_ref, w_scal_ref, w_vec_ref, w_ten_ref)
    receive_ref[:CS] = table_ref[:CS]
    receive_ref[CS : CS + 16] = table_ref[FEAT:]
    receive_ref[CS + 16 :] = dot(block_ref[...], cot_ref[...], 0, 0).astype(jnp.bfloat16)
    w_one = w_one_ref[...]
    w_two = w_two_ref[...]
    weights = (w_one[:, CS:], w_dist_ref[...], w_two, w_two.T)
    grads_ref[...] = jnp.zeros_like(grads_ref)
    agg_ref[...] = jnp.zeros_like(agg_ref)
    for chunk in range(code_ref.shape[0]):
        blocks = [reply_ref[chunk * per_chunk + peer] for peer in range(per_chunk)]
        src = jnp.concatenate(
            [
                jnp.concatenate(
                    [block[:, part * slot : (part + 1) * slot] for block in blocks], 1
                )
                for part in range(parts)
            ],
            0,
        )[:ROWS].astype(jnp.float32)
        hot = one_hot(code_ref[chunk], node_count)
        recv = dot(receive_ref[...], hot)
        scal_recv = recv[:CS].astype(jnp.bfloat16)
        recv_linear = dot(w_one[:, :CS], scal_recv) + b_one_ref[...]
        message, grads = edge_math(
            src, recv_linear, scal_recv, recv[CS : CS + 3], recv[CS + 16 :], None, weights
        )
        agg_ref[...] += dot(message.astype(jnp.bfloat16), hot, 1, 1)
        add_grads(grads_ref, grads)
    for copy in copies:
        copy.wait()
    agg_rows = (agg_ref[...] + mesh_agg_scr[...]).astype(jnp.bfloat16)
    out_ref[...] = (
        table_ref[:FEAT].astype(jnp.float32) + dot(block_ref[...], agg_rows)
    ).astype(jnp.bfloat16)
    cot = cot_ref[...]
    low = HID + GATES
    total = (grads_ref[: low + 16] + mesh_grads_scr[...]) * grad_scale
    node = jnp.concatenate(
        [
            dot(cot[:CS], agg_rows[:CS], 1, 1) * grad_scale,
            jnp.zeros((CS, LANES - CS), jnp.float32),
        ],
        1,
    )
    grads_ref[:low] = total[:low]
    grads_ref[low : low + CS] = node
    grad_vec = jnp.zeros((CV, CV), jnp.float32)
    for k in range(3):
        rows = slice(CS + k * CV, CS + (k + 1) * CV)
        grad_vec = grad_vec + dot(cot[rows], agg_rows[rows], 1, 1)
    grads_ref[low : low + CV, CS : CS + CV] = grad_vec * grad_scale
    grad_ten = jnp.zeros((CT, CT), jnp.float32)
    for m in range(9):
        rows = slice(CS + 3 * CV + m * CT, CS + 3 * CV + (m + 1) * CT)
        grad_ten = grad_ten + dot(cot[rows], agg_rows[rows], 1, 1)
    grads_ref[low : low + CT, CS + CV : CS + CV + CT] = grad_ten * grad_scale
    extra = total[low : low + 16]
    rows = lax.broadcasted_iota(jnp.int32, (16, LANES), 0)
    dist_row = extra[1:2] + extra[2:3]
    grads_ref[low + CS :] = jnp.where(rows == 1, dist_row, extra)
    packed = grads_ref[...].astype(jnp.bfloat16)
    packed_ref[...] = jnp.zeros_like(packed_ref)
    for block in range(packed.shape[0] // 16):
        packed_ref[block] = packed[block * 16 : (block + 1) * 16]


def sum_kernel(parts_ref, out_ref):
    total = jnp.sum(parts_ref[...].astype(jnp.float32), 0).astype(jnp.bfloat16)
    for peer in range(out_ref.shape[0]):
        out_ref[peer] = total


def unpack_kernel(blocks_ref, one_ref, bias_ref, dist_ref, two_ref, scal_ref, vec_ref, ten_ref):
    for block in range(HID // 16):
        one_ref[block * 16 : (block + 1) * 16] = blocks_ref[block].astype(jnp.float32)
    for block in range(GATES // 16):
        two_ref[block * 16 : (block + 1) * 16] = blocks_ref[HID // 16 + block].astype(jnp.float32)
    low = (HID + GATES) // 16
    for block in range(CS // 16):
        rows = blocks_ref[low + block].astype(jnp.float32)
        scal_ref[block * 16 : (block + 1) * 16] = rows[:, :CS]
        if block < CV // 16:
            vec_ref[block * 16 : (block + 1) * 16] = rows[:, CS : CS + CV]
        if block == 0:
            ten_ref[...] = rows[:, CS + CV : CS + CV + CT]
    extra = blocks_ref[low + CS // 16].astype(jnp.float32)
    bias_ref[...] = extra[0:1]
    dist_ref[...] = extra[1:2]


def call(kernel, out_shape, scratch=(), in_specs=None, out_specs=None):
    specs = {}
    if in_specs is not None:
        specs["in_specs"] = in_specs
    if out_specs is not None:
        specs["out_specs"] = out_specs
    return pl.pallas_call(
        kernel,
        out_shape=out_shape,
        scratch_shapes=list(scratch),
        compiler_params=pltpu.CompilerParams(vmem_limit_bytes=VMEM_BYTES),
        **specs,
    )


IN_VMEM = pl.BlockSpec(memory_space=pltpu.VMEM)
IN_HBM = pl.BlockSpec(memory_space=pltpu.HBM)
ANYWHERE = pl.BlockSpec(memory_space=pl.ANY)


def exchange(blocks):
    return lax.all_to_all(blocks, ("dom", "sub"), split_axis=0, concat_axis=0, tiled=True)


def shaped(shape, dtype):
    return jax.ShapeDtypeStruct(shape, dtype)


def from_behind(shard, axis, by):
    peers = lax.axis_size(axis)
    return lax.ppermute(shard, axis, [(i, (i + by) % peers) for i in range(peers)])


def on_device(
    node_feat,
    node_pos,
    node_cot,
    mesh_senders,
    edge_mask,
    halo_up,
    halo_down,
    contact_rows,
    contact_dst,
    contact_mask,
    w_one,
    b_one,
    w_dist,
    w_two,
    w_scal,
    w_vec,
    w_ten,
):
    f32, bf16 = jnp.float32, jnp.bfloat16
    node_count = node_feat.shape[1]
    contact_count = contact_rows.shape[0]
    device_count = lax.axis_size("dom") * lax.axis_size("sub")
    slot = contact_count // device_count
    chunks = contact_count // CHUNK
    parts = LANES // slot
    height = -(-ROWS // (parts * 16)) * 16
    grad_scale = 1.0 / math.sqrt(device_count * node_count * DEGREE)
    wanted = exchange(contact_rows.reshape(device_count, 1, slot))
    table = call(
        table_kernel,
        shaped((ROWS, node_count), bf16),
        (
            pltpu.VMEM((1, node_count), jnp.int32),
            pltpu.VMEM((1, node_count), jnp.int32),
            pltpu.SemaphoreType.DMA((3,)),
        ),
        in_specs=[IN_HBM, IN_VMEM, IN_HBM, IN_HBM],
        out_specs=IN_VMEM,
    )(node_feat, node_pos, halo_up[None], halo_down[None])
    low = from_behind(table, "sub", 1)
    high = from_behind(table, "sub", -1)
    replies = exchange(
        call(
            functools.partial(contact_gather_kernel, slot),
            shaped((device_count, height, LANES), bf16),
            in_specs=[IN_VMEM, IN_VMEM, ANYWHERE, ANYWHERE],
            out_specs=IN_VMEM,
        )(table, wanted, low, high)
    )
    mesh_code = (
        jnp.where(edge_mask != 0, mesh_senders, -1)
        .reshape(node_count, DEGREE)
        .T.reshape(DEGREE, 1, node_count)
    )
    contact_code = jnp.where(contact_mask != 0, contact_dst, -1).reshape(chunks, 1, CHUNK)
    weights = (w_one, b_one[:, None], w_dist[:, None], w_two, w_scal, w_vec, w_ten)
    mesh_rows = HID + GATES + 16
    mesh_agg, mesh_grads = call(
        mesh_kernel,
        (shaped((FEAT, node_count), f32), shaped((mesh_rows, LANES), f32)),
        (
            pltpu.VMEM((FEAT, node_count), f32),
            pltpu.VMEM((mesh_rows, LANES), f32),
            pltpu.VMEM((FEAT, node_count), bf16),
            pltpu.VMEM((ROWS, 3 * node_count), bf16),
            pltpu.VMEM((FEAT, FEAT), bf16),
            pltpu.SemaphoreType.DMA((2,)),
        ),
        in_specs=[IN_VMEM] * 12,
        out_specs=(IN_HBM, IN_HBM),
    )(table, low, high, mesh_code, node_cot, *weights)
    node_out, packed = call(
        functools.partial(contact_kernel, slot, grad_scale),
        (shaped((FEAT, node_count), bf16), shaped((device_count, 16, LANES), bf16)),
        (
            pltpu.VMEM((FEAT, node_count), f32),
            pltpu.VMEM((mesh_rows + CS, LANES), f32),
            pltpu.VMEM((FEAT, node_count), f32),
            pltpu.VMEM((mesh_rows, LANES), f32),
            pltpu.VMEM((CS + 16 + FEAT, node_count), bf16),
            pltpu.VMEM((FEAT, FEAT), bf16),
            pltpu.SemaphoreType.DMA((2,)),
        ),
        in_specs=[IN_VMEM] * 4 + [IN_HBM] * 2 + [IN_VMEM] * 7,
        out_specs=(IN_VMEM, IN_VMEM),
    )(replies, contact_code, table, node_cot, mesh_agg, mesh_grads, *weights)
    shares = call(sum_kernel, shaped((device_count, 16, LANES), bf16))(exchange(packed))
    one, bias, dist, two, scal, vec, ten = call(
        unpack_kernel,
        (
            shaped((HID, 2 * CS), f32),
            shaped((1, HID), f32),
            shaped((1, HID), f32),
            shaped((GATES, HID), f32),
            shaped((CS, CS), f32),
            shaped((CV, CV), f32),
            shaped((CT, CT), f32),
        ),
    )(exchange(shares))
    return node_out, one, bias[0], dist[0], two, scal, vec, ten


def solution(mesh):
    along = P(("dom", "sub"))
    columns = P(None, ("dom", "sub"))
    in_specs = (columns,) * 3 + (along,) * 7 + (P(),) * 7
    out_specs = (columns,) + (P(),) * 7
    return jax.shard_map(
        on_device, mesh=mesh, in_specs=in_specs, out_specs=out_specs, check_vma=False
    )
```

```python
import functools
import math

import jax
import jax.numpy as jnp
from jax import lax
from jax.experimental import pallas as pl
from jax.experimental.pallas import tpu as pltpu
from jax.sharding import PartitionSpec as P

CS = 64
CV = 32
CT = 16
HID = 128
DEGREE = 6
GATES = 144
FEAT = CS + 3 * CV + 9 * CT
ROWS = 320
LANES = 128
CHUNK = 512
VMEM_BYTES = 48 * 1024 * 1024


def dot(lhs, rhs, lhs_dim=1, rhs_dim=0):
    return lax.dot_general(
        lhs, rhs, (((lhs_dim,), (rhs_dim,)), ((), ())), preferred_element_type=jnp.float32
    )


def one_hot(code, width):
    rows = lax.broadcasted_iota(jnp.int32, (width, code.shape[1]), 0)
    return jnp.where(rows == code, 1.0, 0.0).astype(jnp.bfloat16)


def join_index(table, row):
    pair = table[row : row + 2].astype(jnp.float32)
    return (pair[0:1] * 128.0 + pair[1:2]).astype(jnp.int32)


def table_kernel(
    feat_ref,
    pos_ref,
    up_ref,
    down_ref,
    rows_ref,
    table_ref,
    request_ref,
    pos_scr,
    up_scr,
    down_scr,
    rows_scr,
    sems,
):
    node_count = table_ref.shape[1]
    copies = [
        pltpu.make_async_copy(rows_ref, rows_scr, sems.at[0]),
        pltpu.make_async_copy(feat_ref, table_ref.at[:FEAT], sems.at[1]),
        pltpu.make_async_copy(pos_ref, pos_scr, sems.at[2]),
        pltpu.make_async_copy(up_ref, up_scr, sems.at[3]),
        pltpu.make_async_copy(down_ref, down_scr, sems.at[4]),
    ]
    for copy in copies:
        copy.start()
    copies[0].wait()
    slot = request_ref.shape[2]
    parts = LANES // slot
    for row in range(rows_scr.shape[0]):
        line = rows_scr[row : row + 1]
        for part in range(parts):
            request_ref[row * parts + part] = line[:, part * slot : (part + 1) * slot]
    for copy in copies[2:]:
        copy.wait()
    rows = lax.broadcasted_iota(jnp.int32, (ROWS - FEAT, node_count), 0)
    pos = pos_scr[...].astype(jnp.float32)
    tail = jnp.zeros((ROWS - FEAT, node_count), jnp.float32)
    for k in range(3):
        tail = jnp.where(rows == k, pos[k : k + 1], tail)
    for k, index_ref in ((3, up_scr), (5, down_scr)):
        index = index_ref[...]
        high = index >> 7
        tail = jnp.where(rows == k, high.astype(jnp.float32), tail)
        tail = jnp.where(rows == k + 1, (index - (high << 7)).astype(jnp.float32), tail)
    table_ref[FEAT:] = tail.astype(jnp.bfloat16)
    copies[1].wait()


def contact_gather_kernel(slot, table_ref, wanted_ref, low_ref, high_ref, out_ref):
    node_count = table_ref.shape[1]
    parts = LANES // slot
    height = out_ref.shape[1]
    per_chunk = CHUNK // slot
    for chunk in range(wanted_ref.shape[0] // per_chunk):
        wanted = [wanted_ref[chunk * per_chunk + peer] for peer in range(per_chunk)]
        hot = one_hot(jnp.concatenate(wanted, 1), node_count)
        rows = dot(table_ref[...], hot).astype(jnp.bfloat16)
        if parts * height > ROWS:
            rows = jnp.concatenate(
                [rows, jnp.zeros((parts * height - ROWS, CHUNK), jnp.bfloat16)], 0
            )
        for peer in range(per_chunk):
            out_ref[chunk * per_chunk + peer] = jnp.concatenate(
                [
                    rows[part * height : (part + 1) * height, peer * slot : (peer + 1) * slot]
                    for part in range(parts)
                ],
                1,
            )


def edge_math(src, base, first, inputs, pos_recv, back, live, weights):
    w_dist, w_two, w_two_t = weights
    edges = src.shape[1]
    offset = src[FEAT : FEAT + 3] - pos_recv
    if live is not None:
        offset = offset * live
    distance = jnp.sum(offset * offset, 0, keepdims=True)
    linear = base + first + w_dist * distance
    squashed = 0.5 * jnp.tanh(0.5 * linear) + 0.5
    hidden = (linear * squashed).astype(jnp.bfloat16)
    gates = dot(w_two, hidden)
    gate_vec = gates[CS : CS + CV]
    gate_dir = gates[CS + CV : CS + 2 * CV]
    gate_ten = gates[CS + 2 * CV :]
    message = [gates[:CS] * src[:CS]]
    vec_part = jnp.zeros((CV, edges), jnp.float32)
    dir_part = jnp.zeros((CV, edges), jnp.float32)
    for k in range(3):
        rows = slice(CS + k * CV, CS + (k + 1) * CV)
        message.append(gate_vec * src[rows] + gate_dir * offset[k : k + 1])
        vec_part = vec_part + back[rows] * src[rows]
        dir_part = dir_part + back[rows] * offset[k : k + 1]
    ten_part = jnp.zeros((CT, edges), jnp.float32)
    for m in range(9):
        rows = slice(CS + 3 * CV + m * CT, CS + 3 * CV + (m + 1) * CT)
        message.append(gate_ten * src[rows])
        ten_part = ten_part + back[rows] * src[rows]
    message = jnp.concatenate(message, 0)
    dgates = jnp.concatenate([back[:CS] * src[:CS], vec_part, dir_part, ten_part], 0).astype(
        jnp.bfloat16
    )
    hidden_grad = dot(w_two_t, dgates)
    linear_grad = (hidden_grad * squashed * (1.0 + linear * (1.0 - squashed))).astype(jnp.bfloat16)
    rows = lax.broadcasted_iota(jnp.int32, (16, edges), 0)
    coarse = distance.astype(jnp.bfloat16).astype(jnp.float32)
    extra = jnp.where(
        rows == 0, 1.0, jnp.where(rows == 1, coarse, jnp.where(rows == 2, distance - coarse, 0.0))
    ).astype(jnp.bfloat16)
    grads = (
        dot(linear_grad, inputs, 1, 1),
        dot(dgates, hidden, 1, 1),
        dot(extra, linear_grad, 1, 1),
    )
    return message, grads


def add_grads(grads_ref, grads):
    grads_ref[:HID] += grads[0]
    grads_ref[HID : HID + GATES] += grads[1]
    grads_ref[HID + GATES : HID + GATES + 16] += grads[2]


def block_diagonal(block_ref, w_scal, w_vec, w_ten):
    block_ref[...] = jnp.zeros_like(block_ref)
    block_ref[:CS, :CS] = w_scal[...]
    for k in range(3):
        rows = slice(CS + k * CV, CS + (k + 1) * CV)
        block_ref[rows, rows] = w_vec[...]
    for m in range(9):
        rows = slice(CS + 3 * CV + m * CT, CS + 3 * CV + (m + 1) * CT)
        block_ref[rows, rows] = w_ten[...]


def mesh_kernel(
    table_ref,
    low_ref,
    high_ref,
    code_ref,
    cot_ref,
    w_one_ref,
    b_one_ref,
    w_dist_ref,
    w_two_ref,
    w_scal_ref,
    w_vec_ref,
    w_ten_ref,
    contact_ref,
    agg_out_ref,
    grads_out_ref,
    recv_out_ref,
    agg_ref,
    grads_ref,
    recv_ref,
    receive_ref,
    source_ref,
    block_ref,
    sems,
):
    node_count = table_ref.shape[1]
    source_ref[:, :node_count] = table_ref[...]
    low = low_ref[...]
    high = high_ref[...]
    source_ref[:, node_count : 2 * node_count] = dot(
        low, one_hot(join_index(low, FEAT + 3), node_count)
    ).astype(jnp.bfloat16)
    source_ref[:, 2 * node_count :] = dot(
        high, one_hot(join_index(high, FEAT + 5), node_count)
    ).astype(jnp.bfloat16)
    block_diagonal(block_ref, w_scal_ref, w_vec_ref, w_ten_ref)
    receive_ref[:FEAT] = dot(block_ref[...], cot_ref[...], 0, 0).astype(jnp.bfloat16)
    receive_ref[FEAT : FEAT + 16] = table_ref[FEAT:]
    receive_ref[FEAT + 16 :] = table_ref[:CS]
    w_one = w_one_ref[...]
    w_two = w_two_ref[...]
    scal_recv = table_ref[:CS]
    recv_linear = dot(w_one[:, :CS], scal_recv) + b_one_ref[...]
    weights = (w_dist_ref[...], w_two, w_two.T)
    pos_recv = table_ref[FEAT:].astype(jnp.float32)[:3]
    grads_ref[...] = jnp.zeros_like(grads_ref)
    agg_ref[...] = jnp.zeros_like(agg_ref)
    for step in range(DEGREE):
        code = code_ref[step]
        src = dot(source_ref[...], one_hot(code, 3 * node_count))
        live = jnp.where(code >= 0, 1.0, 0.0)
        back = receive_ref[:FEAT].astype(jnp.float32)
        scal_send = src[:CS].astype(jnp.bfloat16)
        inputs = jnp.concatenate([scal_recv, scal_send], 0)
        message, grads = edge_math(
            src, recv_linear, dot(w_one[:, CS:], scal_send), inputs, pos_recv, back, live, weights
        )
        agg_ref[...] += message
        add_grads(grads_ref, grads)
    for chunk in range(contact_ref.shape[0]):
        recv_ref[chunk] = dot(
            receive_ref[...], one_hot(contact_ref[chunk], node_count)
        ).astype(jnp.bfloat16)
    copies = [
        pltpu.make_async_copy(agg_ref, agg_out_ref, sems.at[0]),
        pltpu.make_async_copy(grads_ref, grads_out_ref, sems.at[1]),
        pltpu.make_async_copy(recv_ref, recv_out_ref, sems.at[2]),
    ]
    for copy in copies:
        copy.start()
    for copy in copies:
        copy.wait()


def contact_kernel(
    slot,
    grad_scale,
    reply_ref,
    cot_ref,
    b_one_ref,
    w_dist_ref,
    code_hbm,
    recv_hbm,
    mesh_agg_hbm,
    mesh_grads_hbm,
    w_one_hbm,
    w_two_hbm,
    agg_out_ref,
    packed_ref,
    code_ref,
    recv_ref,
    agg_ref,
    grads_ref,
    w_one_ref,
    w_two_ref,
    packed_scr,
    sems,
):
    chunks = code_ref.shape[0]
    sources = [(code_hbm, code_ref), (w_one_hbm, w_one_ref), (w_two_hbm, w_two_ref)]
    sources += [(recv_hbm.at[chunk], recv_ref.at[chunk]) for chunk in range(chunks)]
    sources += [(mesh_agg_hbm, agg_ref), (mesh_grads_hbm, grads_ref)]
    copies = [
        pltpu.make_async_copy(source, target, sems.at[at])
        for at, (source, target) in enumerate(sources)
    ]
    for copy in copies:
        copy.start()
    node_count = cot_ref.shape[1]
    parts = LANES // slot
    per_chunk = CHUNK // slot
    for copy in copies[:3]:
        copy.wait()
    w_one = w_one_ref[...]
    w_two = w_two_ref[...]
    weights = (w_dist_ref[...], w_two, w_two.T)
    for chunk in range(chunks):
        blocks = [reply_ref[chunk * per_chunk + peer] for peer in range(per_chunk)]
        src_rows = jnp.concatenate(
            [
                jnp.concatenate(
                    [block[:, part * slot : (part + 1) * slot] for block in blocks], 1
                )
                for part in range(parts)
            ],
            0,
        )[:ROWS]
        copies[3 + chunk].wait()
        recv = recv_ref[chunk]
        inputs = jnp.concatenate([recv[FEAT + 16 :], src_rows[:CS]], 0)
        message, grads = edge_math(
            src_rows.astype(jnp.float32),
            b_one_ref[...],
            dot(w_one, inputs),
            inputs,
            recv[FEAT : FEAT + 16].astype(jnp.float32)[:3],
            recv[:FEAT].astype(jnp.float32),
            None,
            weights,
        )
        scattered = dot(message.astype(jnp.bfloat16), one_hot(code_ref[chunk], node_count), 1, 1)
        if chunk == 0:
            for copy in copies[3 + chunks :]:
                copy.wait()
        agg_ref[...] += scattered
        add_grads(grads_ref, grads)
    agg_rows = agg_ref[...].astype(jnp.bfloat16)
    agg_out_ref[...] = agg_rows
    cot = cot_ref[...]
    low = HID + GATES
    packed_scr[:low] = grads_ref[:low] * grad_scale
    packed_scr[low : low + CS] = jnp.concatenate(
        [
            dot(cot[:CS], agg_rows[:CS], 1, 1) * grad_scale,
            jnp.zeros((CS, LANES - CS), jnp.float32),
        ],
        1,
    )
    grad_vec = jnp.zeros((CV, CV), jnp.float32)
    for k in range(3):
        rows = slice(CS + k * CV, CS + (k + 1) * CV)
        grad_vec = grad_vec + dot(cot[rows], agg_rows[rows], 1, 1)
    packed_scr[low : low + CV, CS : CS + CV] = grad_vec * grad_scale
    grad_ten = jnp.zeros((CT, CT), jnp.float32)
    for m in range(9):
        rows = slice(CS + 3 * CV + m * CT, CS + 3 * CV + (m + 1) * CT)
        grad_ten = grad_ten + dot(cot[rows], agg_rows[rows], 1, 1)
    packed_scr[low : low + CT, CS + CV : CS + CV + CT] = grad_ten * grad_scale
    extra = grads_ref[low:] * grad_scale
    rows = lax.broadcasted_iota(jnp.int32, (16, LANES), 0)
    packed_scr[low + CS :] = jnp.where(rows == 1, extra[1:2] + extra[2:3], extra)
    packed = packed_scr[...].astype(jnp.bfloat16)
    height = packed_ref.shape[1]
    for peer in range(packed_ref.shape[0]):
        for row in range(0, height, 16):
            at = peer * height + row
            if at < packed.shape[0]:
                packed_ref[peer, row : row + 16] = packed[at : at + 16]
            else:
                packed_ref[peer, row : row + 16] = jnp.zeros((16, LANES), jnp.bfloat16)


def update_kernel(table_ref, agg_ref, w_scal_ref, w_vec_ref, w_ten_ref, out_ref, block_ref):
    block_diagonal(block_ref, w_scal_ref, w_vec_ref, w_ten_ref)
    out_ref[...] = (
        table_ref[:FEAT].astype(jnp.float32) + dot(block_ref[...], agg_ref[...])
    ).astype(jnp.bfloat16)


def sum_kernel(parts_ref, out_ref):
    total = parts_ref[0].astype(jnp.float32)
    for peer in range(1, parts_ref.shape[0]):
        total = total + parts_ref[peer].astype(jnp.float32)
    total = total.astype(jnp.bfloat16)
    for peer in range(out_ref.shape[0]):
        out_ref[peer] = total


def unpack_kernel(blocks_ref, one_ref, bias_ref, dist_ref, two_ref, scal_ref, vec_ref, ten_ref):
    height = blocks_ref.shape[1]

    def rows_of(block):
        peer, row = divmod(block * 16, height)
        return blocks_ref[peer, row : row + 16].astype(jnp.float32)

    for block in range(HID // 16):
        one_ref[block * 16 : (block + 1) * 16] = rows_of(block)
    for block in range(GATES // 16):
        two_ref[block * 16 : (block + 1) * 16] = rows_of(HID // 16 + block)
    low = (HID + GATES) // 16
    for block in range(CS // 16):
        rows = rows_of(low + block)
        scal_ref[block * 16 : (block + 1) * 16] = rows[:, :CS]
        if block < CV // 16:
            vec_ref[block * 16 : (block + 1) * 16] = rows[:, CS : CS + CV]
        if block == 0:
            ten_ref[...] = rows[:, CS + CV : CS + CV + CT]
    extra = rows_of(low + CS // 16)
    bias_ref[...] = extra[0:1]
    dist_ref[...] = extra[1:2]


def call(kernel, out_shape, scratch=(), in_specs=None, out_specs=None):
    specs = {}
    if in_specs is not None:
        specs["in_specs"] = in_specs
    if out_specs is not None:
        specs["out_specs"] = out_specs
    return pl.pallas_call(
        kernel,
        out_shape=out_shape,
        scratch_shapes=list(scratch),
        compiler_params=pltpu.CompilerParams(vmem_limit_bytes=VMEM_BYTES),
        **specs,
    )


IN_VMEM = pl.BlockSpec(memory_space=pltpu.VMEM)
IN_HBM = pl.BlockSpec(memory_space=pltpu.HBM)
ANYWHERE = pl.BlockSpec(memory_space=pl.ANY)


def exchange(blocks, axes=("dom", "sub")):
    return lax.all_to_all(blocks, axes, split_axis=0, concat_axis=0, tiled=True)


def in_hbm(*arrays):
    return tuple(pltpu.with_memory_space_constraint(array, pltpu.HBM) for array in arrays)


def shaped(shape, dtype):
    return jax.ShapeDtypeStruct(shape, dtype)


def from_behind(shard, axis, by):
    peers = lax.axis_size(axis)
    return lax.ppermute(shard, axis, [(i, (i + by) % peers) for i in range(peers)])


def on_device(
    node_feat,
    node_pos,
    node_cot,
    mesh_senders,
    edge_mask,
    halo_up,
    halo_down,
    contact_rows,
    contact_dst,
    contact_mask,
    w_one,
    b_one,
    w_dist,
    w_two,
    w_scal,
    w_vec,
    w_ten,
):
    f32, bf16 = jnp.float32, jnp.bfloat16
    node_count = node_feat.shape[1]
    contact_count = contact_rows.shape[0]
    device_count = lax.axis_size("dom") * lax.axis_size("sub")
    slot = contact_count // device_count
    chunks = contact_count // CHUNK
    parts = LANES // slot
    height = -(-ROWS // (parts * 16)) * 16
    grad_scale = 1.0 / math.sqrt(device_count * node_count * DEGREE)
    table, requests = call(
        table_kernel,
        (
            shaped((ROWS, node_count), bf16),
            shaped((device_count, 1, slot), jnp.int32),
        ),
        (
            pltpu.VMEM((3, node_count), bf16),
            pltpu.VMEM((1, node_count), jnp.int32),
            pltpu.VMEM((1, node_count), jnp.int32),
            pltpu.VMEM((contact_count // LANES, LANES), jnp.int32),
            pltpu.SemaphoreType.DMA((5,)),
        ),
        in_specs=[IN_HBM] * 5,
        out_specs=(IN_VMEM, IN_VMEM),
    )(
        *in_hbm(
            node_feat,
            node_pos,
            halo_up[None],
            halo_down[None],
            contact_rows.reshape(contact_count // LANES, LANES),
        )
    )
    wanted = exchange(requests)
    low = from_behind(table, "sub", 1)
    high = from_behind(table, "sub", -1)
    replies = exchange(
        call(
            functools.partial(contact_gather_kernel, slot),
            shaped((device_count, height, LANES), bf16),
            in_specs=[IN_VMEM, IN_VMEM, ANYWHERE, ANYWHERE],
            out_specs=IN_VMEM,
        )(table, wanted, low, high)
    )
    mesh_code = (
        jnp.where(edge_mask != 0, mesh_senders, -1)
        .reshape(node_count, DEGREE)
        .T.reshape(DEGREE, 1, node_count)
    )
    contact_code = jnp.where(contact_mask != 0, contact_dst, -1).reshape(chunks, 1, CHUNK)
    b_column = b_one[:, None]
    dist_column = w_dist[:, None]
    mesh_rows = HID + GATES + 16
    recv_rows = FEAT + 16 + CS
    mesh_agg, mesh_grads, recv = call(
        mesh_kernel,
        (
            shaped((FEAT, node_count), f32),
            shaped((mesh_rows, LANES), f32),
            shaped((chunks, recv_rows, CHUNK), bf16),
        ),
        (
            pltpu.VMEM((FEAT, node_count), f32),
            pltpu.VMEM((mesh_rows, LANES), f32),
            pltpu.VMEM((chunks, recv_rows, CHUNK), bf16),
            pltpu.VMEM((recv_rows, node_count), bf16),
            pltpu.VMEM((ROWS, 3 * node_count), bf16),
            pltpu.VMEM((FEAT, FEAT), bf16),
            pltpu.SemaphoreType.DMA((3,)),
        ),
        in_specs=[IN_VMEM] * 13,
        out_specs=(IN_HBM, IN_HBM, IN_HBM),
    )(
        table,
        low,
        high,
        mesh_code,
        node_cot,
        w_one,
        b_column,
        dist_column,
        w_two,
        w_scal,
        w_vec,
        w_ten,
        contact_code,
    )
    dom_count = lax.axis_size("dom")
    sub_count = lax.axis_size("sub")
    packed_rows = mesh_rows + CS
    share = -(-packed_rows // (16 * dom_count)) * 16
    agg_rows, packed = call(
        functools.partial(contact_kernel, slot, grad_scale),
        (shaped((FEAT, node_count), bf16), shaped((dom_count, share, LANES), bf16)),
        (
            pltpu.VMEM((chunks, 1, CHUNK), jnp.int32),
            pltpu.VMEM((chunks, recv_rows, CHUNK), bf16),
            pltpu.VMEM((FEAT, node_count), f32),
            pltpu.VMEM((mesh_rows, LANES), f32),
            pltpu.VMEM((HID, 2 * CS), bf16),
            pltpu.VMEM((GATES, HID), bf16),
            pltpu.VMEM((packed_rows, LANES), f32),
            pltpu.SemaphoreType.DMA((chunks + 5,)),
        ),
        in_specs=[IN_VMEM] * 4 + [IN_HBM] * 6,
        out_specs=(IN_VMEM, IN_VMEM),
    )(
        replies,
        node_cot,
        b_column,
        dist_column,
        *in_hbm(contact_code, recv, mesh_agg, mesh_grads, w_one, w_two),
    )
    node_out = call(
        update_kernel,
        shaped((FEAT, node_count), bf16),
        (pltpu.VMEM((FEAT, FEAT), bf16),),
    )(table, agg_rows, w_scal, w_vec, w_ten)
    parts = exchange(packed, "dom")
    shares = call(sum_kernel, shaped((sub_count, share, LANES), bf16))(parts)
    parts = exchange(shares, "sub")
    shares = call(sum_kernel, shaped((dom_count, share, LANES), bf16))(parts)
    one, bias, dist, two, scal, vec, ten = call(
        unpack_kernel,
        (
            shaped((HID, 2 * CS), f32),
            shaped((1, HID), f32),
            shaped((1, HID), f32),
            shaped((GATES, HID), f32),
            shaped((CS, CS), f32),
            shaped((CV, CV), f32),
            shaped((CT, CT), f32),
        ),
    )(exchange(shares, "dom"))
    return node_out, one, bias[0], dist[0], two, scal, vec, ten


def solution(mesh):
    along = P(("dom", "sub"))
    columns = P(None, ("dom", "sub"))
    in_specs = (columns,) * 3 + (along,) * 7 + (P(),) * 7
    out_specs = (columns,) + (P(),) * 7
    return jax.shard_map(
        on_device, mesh=mesh, in_specs=in_specs, out_specs=out_specs, check_vma=False
    )
```

```python
import functools
import math

import jax
import jax.numpy as jnp
from jax import lax
from jax.experimental import pallas as pl
from jax.experimental.pallas import tpu as pltpu
from jax.sharding import Mesh
from jax.sharding import PartitionSpec as P

CS = 64
CV = 32
CT = 16
HID = 128
DEGREE = 6
GATES = 144
FEAT = CS + 3 * CV + 9 * CT
ROWS = 320
LANES = 128
PLANES = 4
PLAN = ((0, 1, 2, 3), (1, 0, 2, 3), (2, 3, 1, 0), (3, 2, 1, 0))
CHUNK = 512
VMEM_BYTES = 48 * 1024 * 1024


def dot(lhs, rhs, lhs_dim=1, rhs_dim=0):
    return lax.dot_general(
        lhs, rhs, (((lhs_dim,), (rhs_dim,)), ((), ())), preferred_element_type=jnp.float32
    )


def one_hot(code, width):
    rows = lax.broadcasted_iota(jnp.int32, (width, code.shape[1]), 0)
    return jnp.where(rows == code, 1.0, 0.0).astype(jnp.bfloat16)


def join_index(table, row):
    pair = table[row : row + 2].astype(jnp.float32)
    return (pair[0:1] * 128.0 + pair[1:2]).astype(jnp.int32)


def table_kernel(
    doms,
    feat_ref,
    pos_ref,
    up_ref,
    down_ref,
    rows_ref,
    table_ref,
    request_ref,
    pos_scr,
    up_scr,
    down_scr,
    rows_scr,
    sems,
):
    node_count = table_ref.shape[1]
    copies = [
        pltpu.make_async_copy(rows_ref, rows_scr, sems.at[0]),
        pltpu.make_async_copy(feat_ref, table_ref.at[:FEAT], sems.at[1]),
        pltpu.make_async_copy(pos_ref, pos_scr, sems.at[2]),
        pltpu.make_async_copy(up_ref, up_scr, sems.at[3]),
        pltpu.make_async_copy(down_ref, down_scr, sems.at[4]),
    ]
    for copy in copies:
        copy.start()
    copies[0].wait()
    slot = request_ref.shape[2]
    parts = LANES // slot
    across = request_ref.shape[0] // doms
    for row in range(rows_scr.shape[0]):
        line = rows_scr[row : row + 1]
        for part in range(parts):
            owner = row * parts + part
            plane = owner // across % PLANES
            peer = owner // (across * PLANES) * across + owner % across
            request_ref[peer, plane : plane + 1] = line[:, part * slot : (part + 1) * slot]
    for copy in copies[2:]:
        copy.wait()
    rows = lax.broadcasted_iota(jnp.int32, (ROWS - FEAT, node_count), 0)
    pos = pos_scr[...].astype(jnp.float32)
    tail = jnp.zeros((ROWS - FEAT, node_count), jnp.float32)
    for k in range(3):
        tail = jnp.where(rows == k, pos[k : k + 1], tail)
    for k, index_ref in ((3, up_scr), (5, down_scr)):
        index = index_ref[...]
        high = index >> 7
        tail = jnp.where(rows == k, high.astype(jnp.float32), tail)
        tail = jnp.where(rows == k + 1, (index - (high << 7)).astype(jnp.float32), tail)
    table_ref[FEAT:] = tail.astype(jnp.bfloat16)
    copies[1].wait()


def gather_pair(tables, planes, wanted_ref, out_ref):
    peers, _, slot = wanted_ref.shape
    per_chunk = CHUNK // slot
    for chunk in range(peers // per_chunk):
        at = range(chunk * per_chunk, (chunk + 1) * per_chunk)
        found = []
        for table, plane in zip(tables, planes):
            wanted = jnp.concatenate([wanted_ref[peer, pl.ds(plane, 1)] for peer in at], 1)
            found.append(dot(table, one_hot(wanted, table.shape[1])).astype(jnp.bfloat16))
        for place, peer in enumerate(at):
            lanes = slice(place * slot, (place + 1) * slot)
            out_ref[peer] = jnp.concatenate([rows[:, lanes] for rows in found], 1)


def near_gather_kernel(plan_ref, table_ref, below_ref, above_ref, wanted_ref, out_ref):
    near = lax.cond(
        plan_ref[1] > plan_ref[0], lambda: above_ref[...], lambda: below_ref[...]
    )
    gather_pair((table_ref[...], near), (plan_ref[0], plan_ref[1]), wanted_ref, out_ref)


def far_gather_kernel(
    plan_ref, below_ref, above_ref, far_ref, last_ref, wanted_ref, low_ref, high_ref, out_ref
):
    plane = plan_ref[0]
    inner = jnp.logical_and(plane > 0, plane < PLANES - 1)
    third = lax.cond(
        inner,
        lambda: lax.cond(plane == 1, lambda: above_ref[...], lambda: below_ref[...]),
        lambda: far_ref[...],
    )
    fourth = lax.cond(inner, lambda: far_ref[...], lambda: last_ref[...])
    gather_pair((third, fourth), (plan_ref[2], plan_ref[3]), wanted_ref, out_ref)


def edge_math(src, base, first, inputs, pos_recv, back, live, weights):
    w_dist, w_two, w_two_t = weights
    edges = src.shape[1]
    offset = src[FEAT : FEAT + 3] - pos_recv
    if live is not None:
        offset = offset * live
    distance = jnp.sum(offset * offset, 0, keepdims=True)
    linear = base + first + w_dist * distance
    squashed = 0.5 * jnp.tanh(0.5 * linear) + 0.5
    hidden = (linear * squashed).astype(jnp.bfloat16)
    gates = dot(w_two, hidden)
    gate_vec = gates[CS : CS + CV]
    gate_dir = gates[CS + CV : CS + 2 * CV]
    gate_ten = gates[CS + 2 * CV :]
    message = [gates[:CS] * src[:CS]]
    vec_part = jnp.zeros((CV, edges), jnp.float32)
    dir_part = jnp.zeros((CV, edges), jnp.float32)
    for k in range(3):
        rows = slice(CS + k * CV, CS + (k + 1) * CV)
        message.append(gate_vec * src[rows] + gate_dir * offset[k : k + 1])
        vec_part = vec_part + back[rows] * src[rows]
        dir_part = dir_part + back[rows] * offset[k : k + 1]
    ten_part = jnp.zeros((CT, edges), jnp.float32)
    for m in range(9):
        rows = slice(CS + 3 * CV + m * CT, CS + 3 * CV + (m + 1) * CT)
        message.append(gate_ten * src[rows])
        ten_part = ten_part + back[rows] * src[rows]
    message = jnp.concatenate(message, 0)
    dgates = jnp.concatenate([back[:CS] * src[:CS], vec_part, dir_part, ten_part], 0).astype(
        jnp.bfloat16
    )
    hidden_grad = dot(w_two_t, dgates)
    linear_grad = (hidden_grad * squashed * (1.0 + linear * (1.0 - squashed))).astype(jnp.bfloat16)
    rows = lax.broadcasted_iota(jnp.int32, (16, edges), 0)
    coarse = distance.astype(jnp.bfloat16).astype(jnp.float32)
    extra = jnp.where(
        rows == 0, 1.0, jnp.where(rows == 1, coarse, jnp.where(rows == 2, distance - coarse, 0.0))
    ).astype(jnp.bfloat16)
    grads = (
        dot(linear_grad, inputs, 1, 1),
        dot(dgates, hidden, 1, 1),
        dot(extra, linear_grad, 1, 1),
    )
    return message, grads


def add_grads(grads_ref, grads):
    grads_ref[:HID] += grads[0]
    grads_ref[HID : HID + GATES] += grads[1]
    grads_ref[HID + GATES : HID + GATES + 16] += grads[2]


def block_diagonal(block_ref, w_scal, w_vec, w_ten):
    block_ref[...] = jnp.zeros_like(block_ref)
    block_ref[:CS, :CS] = w_scal[...]
    for k in range(3):
        rows = slice(CS + k * CV, CS + (k + 1) * CV)
        block_ref[rows, rows] = w_vec[...]
    for m in range(9):
        rows = slice(CS + 3 * CV + m * CT, CS + 3 * CV + (m + 1) * CT)
        block_ref[rows, rows] = w_ten[...]


def mesh_kernel(
    table_ref,
    low_ref,
    high_ref,
    code_ref,
    cot_ref,
    w_one_ref,
    b_one_ref,
    w_dist_ref,
    w_two_ref,
    w_scal_ref,
    w_vec_ref,
    w_ten_ref,
    contact_ref,
    agg_out_ref,
    grads_out_ref,
    recv_out_ref,
    agg_ref,
    grads_ref,
    recv_ref,
    receive_ref,
    source_ref,
    block_ref,
    sems,
):
    node_count = table_ref.shape[1]
    source_ref[:, :node_count] = table_ref[...]
    low = low_ref[...]
    high = high_ref[...]
    source_ref[:, node_count : 2 * node_count] = dot(
        low, one_hot(join_index(low, FEAT + 3), node_count)
    ).astype(jnp.bfloat16)
    source_ref[:, 2 * node_count :] = dot(
        high, one_hot(join_index(high, FEAT + 5), node_count)
    ).astype(jnp.bfloat16)
    block_diagonal(block_ref, w_scal_ref, w_vec_ref, w_ten_ref)
    receive_ref[:FEAT] = dot(block_ref[...], cot_ref[...], 0, 0).astype(jnp.bfloat16)
    receive_ref[FEAT : FEAT + 16] = table_ref[FEAT:]
    receive_ref[FEAT + 16 :] = table_ref[:CS]
    w_one = w_one_ref[...]
    w_two = w_two_ref[...]
    scal_recv = table_ref[:CS]
    recv_linear = dot(w_one[:, :CS], scal_recv) + b_one_ref[...]
    weights = (w_dist_ref[...], w_two, w_two.T)
    pos_recv = table_ref[FEAT:].astype(jnp.float32)[:3]
    grads_ref[...] = jnp.zeros_like(grads_ref)
    agg_ref[...] = jnp.zeros_like(agg_ref)
    for step in range(DEGREE):
        code = code_ref[step]
        src = dot(source_ref[...], one_hot(code, 3 * node_count))
        live = jnp.where(code >= 0, 1.0, 0.0)
        back = receive_ref[:FEAT].astype(jnp.float32)
        scal_send = src[:CS].astype(jnp.bfloat16)
        inputs = jnp.concatenate([scal_recv, scal_send], 0)
        message, grads = edge_math(
            src, recv_linear, dot(w_one[:, CS:], scal_send), inputs, pos_recv, back, live, weights
        )
        agg_ref[...] += message
        add_grads(grads_ref, grads)
    for chunk in range(contact_ref.shape[0]):
        recv_ref[chunk] = dot(
            receive_ref[...], one_hot(contact_ref[chunk], node_count)
        ).astype(jnp.bfloat16)
    copies = [
        pltpu.make_async_copy(agg_ref, agg_out_ref, sems.at[0]),
        pltpu.make_async_copy(grads_ref, grads_out_ref, sems.at[1]),
        pltpu.make_async_copy(recv_ref, recv_out_ref, sems.at[2]),
    ]
    for copy in copies:
        copy.start()
    for copy in copies:
        copy.wait()


def contact_kernel(
    first,
    reply_ref,
    b_one_ref,
    w_dist_ref,
    code_hbm,
    recv_hbm,
    agg_hbm,
    grads_hbm,
    w_one_hbm,
    w_two_hbm,
    agg_out_ref,
    grads_out_ref,
    code_ref,
    recv_ref,
    agg_ref,
    grads_ref,
    w_one_ref,
    w_two_ref,
    sems,
):
    peers, _, lanes = reply_ref.shape
    chunks = recv_ref.shape[0]
    node_count = agg_ref.shape[1]
    sources = [(code_hbm, code_ref), (w_one_hbm, w_one_ref), (w_two_hbm, w_two_ref)]
    sources += [(recv_hbm.at[first + chunk], recv_ref.at[chunk]) for chunk in range(chunks)]
    sources += [(agg_hbm, agg_ref), (grads_hbm, grads_ref)]
    copies = [
        pltpu.make_async_copy(source, target, sems.at[at])
        for at, (source, target) in enumerate(sources)
    ]
    for copy in copies:
        copy.start()
    for copy in copies[:3]:
        copy.wait()
    w_one = w_one_ref[...]
    w_two = w_two_ref[...]
    weights = (w_dist_ref[...], w_two, w_two.T)
    per_chunk = peers // chunks
    for chunk in range(chunks):
        src_rows = jnp.concatenate(
            [reply_ref[chunk * per_chunk + peer] for peer in range(per_chunk)], 1
        )
        copies[3 + chunk].wait()
        recv = recv_ref[chunk]
        inputs = jnp.concatenate([recv[FEAT + 16 :], src_rows[:CS]], 0)
        message, grads = edge_math(
            src_rows.astype(jnp.float32),
            b_one_ref[...],
            dot(w_one, inputs),
            inputs,
            recv[FEAT : FEAT + 16].astype(jnp.float32)[:3],
            recv[:FEAT].astype(jnp.float32),
            None,
            weights,
        )
        hot = one_hot(code_ref[first + chunk], node_count)
        scattered = dot(message.astype(jnp.bfloat16), hot, 1, 1)
        if chunk == 0:
            for copy in copies[3 + chunks :]:
                copy.wait()
        agg_ref[...] += scattered
        add_grads(grads_ref, grads)


def near_contact_kernel(*refs):
    agg_out_ref, grads_out_ref = refs[9:11]
    agg_ref, grads_ref = refs[13:15]
    sems = refs[17]
    contact_kernel(0, *refs)
    copies = [
        pltpu.make_async_copy(agg_ref, agg_out_ref, sems.at[0]),
        pltpu.make_async_copy(grads_ref, grads_out_ref, sems.at[1]),
    ]
    for copy in copies:
        copy.start()
    for copy in copies:
        copy.wait()


def far_contact_kernel(grad_scale, first, *refs):
    cot_ref = refs[0]
    refs = refs[1:]
    agg_out_ref, packed_ref = refs[9:11]
    agg_ref, grads_ref = refs[13:15]
    packed_scr = refs[18]
    contact_kernel(first, *refs[:18])
    agg_rows = agg_ref[...].astype(jnp.bfloat16)
    agg_out_ref[...] = agg_rows
    cot = cot_ref[...]
    low = HID + GATES
    packed_scr[:low] = grads_ref[:low] * grad_scale
    packed_scr[low : low + CS] = jnp.concatenate(
        [
            dot(cot[:CS], agg_rows[:CS], 1, 1) * grad_scale,
            jnp.zeros((CS, LANES - CS), jnp.float32),
        ],
        1,
    )
    grad_vec = jnp.zeros((CV, CV), jnp.float32)
    for k in range(3):
        rows = slice(CS + k * CV, CS + (k + 1) * CV)
        grad_vec = grad_vec + dot(cot[rows], agg_rows[rows], 1, 1)
    packed_scr[low : low + CV, CS : CS + CV] = grad_vec * grad_scale
    grad_ten = jnp.zeros((CT, CT), jnp.float32)
    for m in range(9):
        rows = slice(CS + 3 * CV + m * CT, CS + 3 * CV + (m + 1) * CT)
        grad_ten = grad_ten + dot(cot[rows], agg_rows[rows], 1, 1)
    packed_scr[low : low + CT, CS + CV : CS + CV + CT] = grad_ten * grad_scale
    extra = grads_ref[low:] * grad_scale
    rows = lax.broadcasted_iota(jnp.int32, (16, LANES), 0)
    packed_scr[low + CS :] = jnp.where(rows == 1, extra[1:2] + extra[2:3], extra)
    packed = packed_scr[...].astype(jnp.bfloat16)
    height = packed_ref.shape[1]
    for peer in range(packed_ref.shape[0]):
        for row in range(0, height, 16):
            at = peer * height + row
            if at < packed.shape[0]:
                packed_ref[peer, row : row + 16] = packed[at : at + 16]
            else:
                packed_ref[peer, row : row + 16] = jnp.zeros((16, LANES), jnp.bfloat16)


def update_kernel(table_ref, agg_ref, w_scal_ref, w_vec_ref, w_ten_ref, out_ref, block_ref):
    block_diagonal(block_ref, w_scal_ref, w_vec_ref, w_ten_ref)
    out_ref[...] = (
        table_ref[:FEAT].astype(jnp.float32) + dot(block_ref[...], agg_ref[...])
    ).astype(jnp.bfloat16)


def sum_kernel(parts_ref, out_ref):
    total = parts_ref[0].astype(jnp.float32)
    for peer in range(1, parts_ref.shape[0]):
        total = total + parts_ref[peer].astype(jnp.float32)
    total = total.astype(jnp.bfloat16)
    for peer in range(out_ref.shape[0]):
        out_ref[peer] = total


def unpack_kernel(blocks_ref, one_ref, bias_ref, dist_ref, two_ref, scal_ref, vec_ref, ten_ref):
    height = blocks_ref.shape[1]

    def rows_of(block):
        peer, row = divmod(block * 16, height)
        return blocks_ref[peer, row : row + 16].astype(jnp.float32)

    for block in range(HID // 16):
        one_ref[block * 16 : (block + 1) * 16] = rows_of(block)
    for block in range(GATES // 16):
        two_ref[block * 16 : (block + 1) * 16] = rows_of(HID // 16 + block)
    low = (HID + GATES) // 16
    for block in range(CS // 16):
        rows = rows_of(low + block)
        scal_ref[block * 16 : (block + 1) * 16] = rows[:, :CS]
        if block < CV // 16:
            vec_ref[block * 16 : (block + 1) * 16] = rows[:, CS : CS + CV]
        if block == 0:
            ten_ref[...] = rows[:, CS + CV : CS + CV + CT]
    extra = rows_of(low + CS // 16)
    bias_ref[...] = extra[0:1]
    dist_ref[...] = extra[1:2]


def call(kernel, out_shape, scratch=(), in_specs=None, out_specs=None):
    specs = {}
    if in_specs is not None:
        specs["in_specs"] = in_specs
    if out_specs is not None:
        specs["out_specs"] = out_specs
    return pl.pallas_call(
        kernel,
        out_shape=out_shape,
        scratch_shapes=list(scratch),
        compiler_params=pltpu.CompilerParams(vmem_limit_bytes=VMEM_BYTES),
        **specs,
    )


IN_VMEM = pl.BlockSpec(memory_space=pltpu.VMEM)
IN_HBM = pl.BlockSpec(memory_space=pltpu.HBM)
IN_SMEM = pl.BlockSpec(memory_space=pltpu.SMEM)
ANYWHERE = pl.BlockSpec(memory_space=pl.ANY)


def exchange(blocks, axes=("dom", "z", "x")):
    return lax.all_to_all(blocks, axes, split_axis=0, concat_axis=0, tiled=True)


def in_hbm(*arrays):
    return tuple(pltpu.with_memory_space_constraint(array, pltpu.HBM) for array in arrays)


def shaped(shape, dtype):
    return jax.ShapeDtypeStruct(shape, dtype)


def from_behind(shard, axis, by):
    peers = lax.axis_size("z") * lax.axis_size("x")
    return lax.ppermute(shard, axis, [(i, (i + by) % peers) for i in range(peers)])


def planes_on(shard, pairs):
    return lax.ppermute(shard, "z", pairs)


def on_device(
    node_feat,
    node_pos,
    node_cot,
    mesh_senders,
    edge_mask,
    halo_up,
    halo_down,
    contact_rows,
    contact_dst,
    contact_mask,
    w_one,
    b_one,
    w_dist,
    w_two,
    w_scal,
    w_vec,
    w_ten,
):
    f32, bf16 = jnp.float32, jnp.bfloat16
    node_count = node_feat.shape[1]
    contact_count = contact_rows.shape[0]
    doms = lax.axis_size("dom")
    across = lax.axis_size("x")
    peers = doms * across
    device_count = peers * PLANES
    slot = contact_count // device_count
    chunks = contact_count // CHUNK
    grad_scale = 1.0 / math.sqrt(device_count * node_count * DEGREE)
    plane = lax.axis_index("z")
    plan = jnp.take(jnp.array(PLAN, jnp.int32), plane, axis=0)
    table, requests = call(
        functools.partial(table_kernel, doms),
        (
            shaped((ROWS, node_count), bf16),
            shaped((peers, PLANES, slot), jnp.int32),
        ),
        (
            pltpu.VMEM((3, node_count), bf16),
            pltpu.VMEM((1, node_count), jnp.int32),
            pltpu.VMEM((1, node_count), jnp.int32),
            pltpu.VMEM((contact_count // LANES, LANES), jnp.int32),
            pltpu.SemaphoreType.DMA((5,)),
        ),
        in_specs=[IN_HBM] * 5,
        out_specs=(IN_VMEM, IN_VMEM),
    )(
        *in_hbm(
            node_feat,
            node_pos,
            halo_up[None],
            halo_down[None],
            contact_rows.reshape(contact_count // LANES, LANES),
        )
    )
    below = planes_on(table, [(0, 1), (1, 2), (2, 3)])
    above = planes_on(table, [(1, 0), (2, 1), (3, 2)])
    wanted = exchange(requests, ("dom", "x"))
    below_two = planes_on(below, [(1, 2), (2, 3)])
    above_two = planes_on(above, [(2, 1), (1, 0)])
    far = jnp.where(plane < PLANES // 2, above_two, below_two)
    last = planes_on(far, [(2, 3), (1, 0)])
    low = from_behind(table, ("z", "x"), 1)
    high = from_behind(table, ("z", "x"), -1)
    reply_shape = shaped((peers, ROWS, 2 * slot), bf16)
    near_reply = exchange(
        call(
            near_gather_kernel,
            reply_shape,
            in_specs=[IN_SMEM] + [IN_VMEM] * 4,
            out_specs=IN_VMEM,
        )(plan, table, below, above, wanted),
        ("dom", "x"),
    )
    far_reply = exchange(
        call(
            far_gather_kernel,
            reply_shape,
            in_specs=[IN_SMEM] + [IN_VMEM] * 5 + [ANYWHERE] * 2,
            out_specs=IN_VMEM,
        )(plan, below, above, far, last, wanted, low, high),
        ("dom", "x"),
    )
    mesh_code = (
        jnp.where(edge_mask != 0, mesh_senders, -1)
        .reshape(node_count, DEGREE)
        .T.reshape(DEGREE, 1, node_count)
    )
    contact_code = (
        jnp.where(contact_mask != 0, contact_dst, -1)
        .reshape(doms, PLANES, across, slot)
        .transpose(1, 0, 2, 3)
        .reshape(PLANES, peers, slot)
    )
    ordered = jnp.zeros_like(contact_code)
    for at, order in enumerate(PLAN):
        ordered = jnp.where(plane == at, jnp.stack([contact_code[i] for i in order]), ordered)
    contact_code = (
        ordered.reshape(2, 2, peers, slot).transpose(0, 2, 1, 3).reshape(chunks, 1, CHUNK)
    )
    b_column = b_one[:, None]
    dist_column = w_dist[:, None]
    mesh_rows = HID + GATES + 16
    recv_rows = FEAT + 16 + CS
    mesh_agg, mesh_grads, recv = call(
        mesh_kernel,
        (
            shaped((FEAT, node_count), f32),
            shaped((mesh_rows, LANES), f32),
            shaped((chunks, recv_rows, CHUNK), bf16),
        ),
        (
            pltpu.VMEM((FEAT, node_count), f32),
            pltpu.VMEM((mesh_rows, LANES), f32),
            pltpu.VMEM((chunks, recv_rows, CHUNK), bf16),
            pltpu.VMEM((recv_rows, node_count), bf16),
            pltpu.VMEM((ROWS, 3 * node_count), bf16),
            pltpu.VMEM((FEAT, FEAT), bf16),
            pltpu.SemaphoreType.DMA((3,)),
        ),
        in_specs=[IN_VMEM] * 13,
        out_specs=(IN_HBM, IN_HBM, IN_HBM),
    )(
        table,
        low,
        high,
        mesh_code,
        node_cot,
        w_one,
        b_column,
        dist_column,
        w_two,
        w_scal,
        w_vec,
        w_ten,
        contact_code,
    )
    packed_rows = mesh_rows + CS
    half = chunks // 2
    contact_scratch = (
        pltpu.VMEM((chunks, 1, CHUNK), jnp.int32),
        pltpu.VMEM((half, recv_rows, CHUNK), bf16),
        pltpu.VMEM((FEAT, node_count), f32),
        pltpu.VMEM((mesh_rows, LANES), f32),
        pltpu.VMEM((HID, 2 * CS), bf16),
        pltpu.VMEM((GATES, HID), bf16),
        pltpu.SemaphoreType.DMA((half + 5,)),
    )
    near_agg, near_grads = call(
        near_contact_kernel,
        (shaped((FEAT, node_count), f32), shaped((mesh_rows, LANES), f32)),
        contact_scratch,
        in_specs=[IN_VMEM] * 3 + [IN_HBM] * 6,
        out_specs=(IN_HBM, IN_HBM),
    )(
        near_reply,
        b_column,
        dist_column,
        *in_hbm(contact_code, recv, mesh_agg, mesh_grads, w_one, w_two),
    )
    agg_rows, packed = call(
        functools.partial(far_contact_kernel, grad_scale, half),
        (shaped((FEAT, node_count), bf16), shaped((device_count, 16, LANES), bf16)),
        contact_scratch + (pltpu.VMEM((packed_rows, LANES), f32),),
        in_specs=[IN_VMEM] * 4 + [IN_HBM] * 6,
        out_specs=(IN_VMEM, IN_VMEM),
    )(
        node_cot,
        far_reply,
        b_column,
        dist_column,
        *in_hbm(contact_code, recv, near_agg, near_grads, w_one, w_two),
    )
    node_out = call(
        update_kernel,
        shaped((FEAT, node_count), bf16),
        (pltpu.VMEM((FEAT, FEAT), bf16),),
    )(table, agg_rows, w_scal, w_vec, w_ten)
    shares = call(sum_kernel, shaped((device_count, 16, LANES), bf16))(exchange(packed))
    one, bias, dist, two, scal, vec, ten = call(
        unpack_kernel,
        (
            shaped((HID, 2 * CS), f32),
            shaped((1, HID), f32),
            shaped((1, HID), f32),
            shaped((GATES, HID), f32),
            shaped((CS, CS), f32),
            shaped((CV, CV), f32),
            shaped((CT, CT), f32),
        ),
    )(exchange(shares))
    return node_out, one, bias[0], dist[0], two, scal, vec, ten


def solution(mesh):
    doms = mesh.shape["dom"]
    across = mesh.shape["sub"] // PLANES
    cut = Mesh(mesh.devices.reshape(doms, PLANES, across), ("dom", "z", "x"))
    along = P(("dom", "z", "x"))
    columns = P(None, ("dom", "z", "x"))
    in_specs = (columns,) * 3 + (along,) * 7 + (P(),) * 7
    out_specs = (columns,) + (P(),) * 7
    return jax.shard_map(
        on_device, mesh=cut, in_specs=in_specs, out_specs=out_specs, check_vma=False
    )
```

```python
import functools
import math

import jax
import jax.numpy as jnp
from jax import lax
from jax.experimental import pallas as pl
from jax.experimental.pallas import tpu as pltpu
from jax.sharding import Mesh
from jax.sharding import PartitionSpec as P

CS = 64
CV = 32
CT = 16
HID = 128
DEGREE = 6
GATES = 144
FEAT = CS + 3 * CV + 9 * CT
ROWS = 320
LANES = 128
PLANES = 4
PLAN = ((0, 1, 2, 3), (1, 0, 2, 3), (2, 3, 1, 0), (3, 2, 1, 0))
CHUNK = 512
VMEM_BYTES = 48 * 1024 * 1024


def dot(lhs, rhs, lhs_dim=1, rhs_dim=0):
    return lax.dot_general(
        lhs, rhs, (((lhs_dim,), (rhs_dim,)), ((), ())), preferred_element_type=jnp.float32
    )


def one_hot(code, width):
    rows = lax.broadcasted_iota(jnp.int32, (width, code.shape[1]), 0)
    return jnp.where(rows == code, 1.0, 0.0).astype(jnp.bfloat16)


def join_index(table, row):
    pair = table[row : row + 2].astype(jnp.float32)
    return (pair[0:1] * 128.0 + pair[1:2]).astype(jnp.int32)


def table_kernel(
    doms,
    feat_ref,
    pos_ref,
    up_ref,
    down_ref,
    rows_ref,
    table_ref,
    request_ref,
    pos_scr,
    up_scr,
    down_scr,
    rows_scr,
    sems,
):
    node_count = table_ref.shape[1]
    copies = [
        pltpu.make_async_copy(rows_ref, rows_scr, sems.at[0]),
        pltpu.make_async_copy(feat_ref, table_ref.at[:FEAT], sems.at[1]),
        pltpu.make_async_copy(pos_ref, pos_scr, sems.at[2]),
        pltpu.make_async_copy(up_ref, up_scr, sems.at[3]),
        pltpu.make_async_copy(down_ref, down_scr, sems.at[4]),
    ]
    for copy in copies:
        copy.start()
    copies[0].wait()
    slot = request_ref.shape[2] // PLANES
    parts = LANES // slot
    across = request_ref.shape[0] // doms
    for row in range(rows_scr.shape[0]):
        line = rows_scr[row : row + 1]
        for part in range(parts):
            owner = row * parts + part
            plane = owner // across % PLANES
            peer = owner // (across * PLANES) * across + owner % across
            request_ref[peer, :, plane * slot : (plane + 1) * slot] = line[
                :, part * slot : (part + 1) * slot
            ]
    for copy in copies[2:]:
        copy.wait()
    rows = lax.broadcasted_iota(jnp.int32, (ROWS - FEAT, node_count), 0)
    pos = pos_scr[...].astype(jnp.float32)
    tail = jnp.zeros((ROWS - FEAT, node_count), jnp.float32)
    for k in range(3):
        tail = jnp.where(rows == k, pos[k : k + 1], tail)
    for k, index_ref in ((3, up_scr), (5, down_scr)):
        index = index_ref[...]
        high = index >> 7
        tail = jnp.where(rows == k, high.astype(jnp.float32), tail)
        tail = jnp.where(rows == k + 1, (index - (high << 7)).astype(jnp.float32), tail)
    table_ref[FEAT:] = tail.astype(jnp.bfloat16)
    copies[1].wait()


def gather_pair(tables, planes, wanted_ref, out_ref):
    peers = wanted_ref.shape[0]
    slot = wanted_ref.shape[2] // PLANES
    per_chunk = CHUNK // slot
    for chunk in range(peers // per_chunk):
        at = range(chunk * per_chunk, (chunk + 1) * per_chunk)
        found = []
        for table, plane in zip(tables, planes):
            by_plane = [
                jnp.concatenate(
                    [wanted_ref[peer, :, i * slot : (i + 1) * slot] for peer in at], 1
                )
                for i in range(PLANES)
            ]
            wanted = by_plane[0]
            for i in range(1, PLANES):
                wanted = jnp.where(plane == i, by_plane[i], wanted)
            found.append(dot(table, one_hot(wanted, table.shape[1])).astype(jnp.bfloat16))
        for place, peer in enumerate(at):
            lanes = slice(place * slot, (place + 1) * slot)
            out_ref[peer] = jnp.concatenate([rows[:, lanes] for rows in found], 1)


def near_gather_kernel(plan_ref, table_ref, below_ref, above_ref, wanted_ref, out_ref):
    near = lax.cond(
        plan_ref[1] > plan_ref[0], lambda: above_ref[...], lambda: below_ref[...]
    )
    gather_pair((table_ref[...], near), (plan_ref[0], plan_ref[1]), wanted_ref, out_ref)


def far_gather_kernel(
    plan_ref, below_ref, above_ref, far_ref, last_ref, wanted_ref, after_ref, out_ref
):
    plane = plan_ref[0]
    inner = jnp.logical_and(plane > 0, plane < PLANES - 1)
    third = lax.cond(
        inner,
        lambda: lax.cond(plane == 1, lambda: above_ref[...], lambda: below_ref[...]),
        lambda: far_ref[...],
    )
    fourth = lax.cond(inner, lambda: far_ref[...], lambda: last_ref[...])
    gather_pair((third, fourth), (plan_ref[2], plan_ref[3]), wanted_ref, out_ref)


def edge_math(src, base, first, inputs, pos_recv, back, live, weights):
    w_dist, w_two, w_two_t = weights
    edges = src.shape[1]
    offset = src[FEAT : FEAT + 3] - pos_recv
    if live is not None:
        offset = offset * live
    distance = jnp.sum(offset * offset, 0, keepdims=True)
    linear = base + first + w_dist * distance
    squashed = 0.5 * jnp.tanh(0.5 * linear) + 0.5
    hidden = (linear * squashed).astype(jnp.bfloat16)
    gates = dot(w_two, hidden)
    gate_vec = gates[CS : CS + CV]
    gate_dir = gates[CS + CV : CS + 2 * CV]
    gate_ten = gates[CS + 2 * CV :]
    message = [gates[:CS] * src[:CS]]
    vec_part = jnp.zeros((CV, edges), jnp.float32)
    dir_part = jnp.zeros((CV, edges), jnp.float32)
    for k in range(3):
        rows = slice(CS + k * CV, CS + (k + 1) * CV)
        message.append(gate_vec * src[rows] + gate_dir * offset[k : k + 1])
        vec_part = vec_part + back[rows] * src[rows]
        dir_part = dir_part + back[rows] * offset[k : k + 1]
    ten_part = jnp.zeros((CT, edges), jnp.float32)
    for m in range(9):
        rows = slice(CS + 3 * CV + m * CT, CS + 3 * CV + (m + 1) * CT)
        message.append(gate_ten * src[rows])
        ten_part = ten_part + back[rows] * src[rows]
    message = jnp.concatenate(message, 0)
    dgates = jnp.concatenate([back[:CS] * src[:CS], vec_part, dir_part, ten_part], 0).astype(
        jnp.bfloat16
    )
    hidden_grad = dot(w_two_t, dgates)
    linear_grad = (hidden_grad * squashed * (1.0 + linear * (1.0 - squashed))).astype(jnp.bfloat16)
    rows = lax.broadcasted_iota(jnp.int32, (16, edges), 0)
    coarse = distance.astype(jnp.bfloat16).astype(jnp.float32)
    extra = jnp.where(
        rows == 0, 1.0, jnp.where(rows == 1, coarse, jnp.where(rows == 2, distance - coarse, 0.0))
    ).astype(jnp.bfloat16)
    grads = (
        dot(linear_grad, inputs, 1, 1),
        dot(dgates, hidden, 1, 1),
        dot(extra, linear_grad, 1, 1),
    )
    return message, grads


def add_grads(grads_ref, grads):
    grads_ref[:HID] += grads[0]
    grads_ref[HID : HID + GATES] += grads[1]
    grads_ref[HID + GATES : HID + GATES + 16] += grads[2]


def block_diagonal(block_ref, w_scal, w_vec, w_ten):
    block_ref[...] = jnp.zeros_like(block_ref)
    block_ref[:CS, :CS] = w_scal[...]
    for k in range(3):
        rows = slice(CS + k * CV, CS + (k + 1) * CV)
        block_ref[rows, rows] = w_vec[...]
    for m in range(9):
        rows = slice(CS + 3 * CV + m * CT, CS + 3 * CV + (m + 1) * CT)
        block_ref[rows, rows] = w_ten[...]


def mesh_kernel(
    table_ref,
    low_ref,
    high_ref,
    code_ref,
    cot_ref,
    w_one_ref,
    b_one_ref,
    w_dist_ref,
    w_two_ref,
    w_scal_ref,
    w_vec_ref,
    w_ten_ref,
    contact_ref,
    agg_out_ref,
    grads_out_ref,
    recv_out_ref,
    agg_ref,
    grads_ref,
    recv_ref,
    receive_ref,
    source_ref,
    block_ref,
    sems,
):
    node_count = table_ref.shape[1]
    source_ref[:, :node_count] = table_ref[...]
    low = low_ref[...]
    high = high_ref[...]
    source_ref[:, node_count : 2 * node_count] = dot(
        low, one_hot(join_index(low, FEAT + 3), node_count)
    ).astype(jnp.bfloat16)
    source_ref[:, 2 * node_count :] = dot(
        high, one_hot(join_index(high, FEAT + 5), node_count)
    ).astype(jnp.bfloat16)
    block_diagonal(block_ref, w_scal_ref, w_vec_ref, w_ten_ref)
    receive_ref[:FEAT] = dot(block_ref[...], cot_ref[...], 0, 0).astype(jnp.bfloat16)
    receive_ref[FEAT : FEAT + 16] = table_ref[FEAT:]
    receive_ref[FEAT + 16 :] = table_ref[:CS]
    w_one = w_one_ref[...]
    w_two = w_two_ref[...]
    scal_recv = table_ref[:CS]
    recv_linear = dot(w_one[:, :CS], scal_recv) + b_one_ref[...]
    weights = (w_dist_ref[...], w_two, w_two.T)
    pos_recv = table_ref[FEAT:].astype(jnp.float32)[:3]
    grads_ref[...] = jnp.zeros_like(grads_ref)
    agg_ref[...] = jnp.zeros_like(agg_ref)
    for step in range(DEGREE):
        code = code_ref[step]
        src = dot(source_ref[...], one_hot(code, 3 * node_count))
        live = jnp.where(code >= 0, 1.0, 0.0)
        back = receive_ref[:FEAT].astype(jnp.float32)
        scal_send = src[:CS].astype(jnp.bfloat16)
        inputs = jnp.concatenate([scal_recv, scal_send], 0)
        message, grads = edge_math(
            src, recv_linear, dot(w_one[:, CS:], scal_send), inputs, pos_recv, back, live, weights
        )
        agg_ref[...] += message
        add_grads(grads_ref, grads)
    for chunk in range(contact_ref.shape[0]):
        recv_ref[chunk] = dot(
            receive_ref[...], one_hot(contact_ref[chunk], node_count)
        ).astype(jnp.bfloat16)
    copies = [
        pltpu.make_async_copy(agg_ref, agg_out_ref, sems.at[0]),
        pltpu.make_async_copy(grads_ref, grads_out_ref, sems.at[1]),
        pltpu.make_async_copy(recv_ref, recv_out_ref, sems.at[2]),
    ]
    for copy in copies:
        copy.start()
    for copy in copies:
        copy.wait()


def contact_kernel(
    first,
    reply_ref,
    b_one_ref,
    w_dist_ref,
    code_hbm,
    recv_hbm,
    agg_hbm,
    grads_hbm,
    w_one_hbm,
    w_two_hbm,
    agg_out_ref,
    grads_out_ref,
    code_ref,
    recv_ref,
    agg_ref,
    grads_ref,
    w_one_ref,
    w_two_ref,
    sems,
):
    peers, _, lanes = reply_ref.shape
    chunks = recv_ref.shape[0]
    node_count = agg_ref.shape[1]
    sources = [(code_hbm, code_ref), (w_one_hbm, w_one_ref), (w_two_hbm, w_two_ref)]
    sources += [(recv_hbm.at[first + chunk], recv_ref.at[chunk]) for chunk in range(chunks)]
    sources += [(agg_hbm, agg_ref), (grads_hbm, grads_ref)]
    copies = [
        pltpu.make_async_copy(source, target, sems.at[at])
        for at, (source, target) in enumerate(sources)
    ]
    for copy in copies:
        copy.start()
    for copy in copies[:3]:
        copy.wait()
    w_one = w_one_ref[...]
    w_two = w_two_ref[...]
    weights = (w_dist_ref[...], w_two, w_two.T)
    per_chunk = peers // chunks
    for chunk in range(chunks):
        src_rows = jnp.concatenate(
            [reply_ref[chunk * per_chunk + peer] for peer in range(per_chunk)], 1
        )
        copies[3 + chunk].wait()
        recv = recv_ref[chunk]
        inputs = jnp.concatenate([recv[FEAT + 16 :], src_rows[:CS]], 0)
        message, grads = edge_math(
            src_rows.astype(jnp.float32),
            b_one_ref[...],
            dot(w_one, inputs),
            inputs,
            recv[FEAT : FEAT + 16].astype(jnp.float32)[:3],
            recv[:FEAT].astype(jnp.float32),
            None,
            weights,
        )
        hot = one_hot(code_ref[first + chunk], node_count)
        scattered = dot(message.astype(jnp.bfloat16), hot, 1, 1)
        if chunk == 0:
            for copy in copies[3 + chunks :]:
                copy.wait()
        agg_ref[...] += scattered
        add_grads(grads_ref, grads)


def near_contact_kernel(*refs):
    agg_out_ref, grads_out_ref = refs[9:11]
    agg_ref, grads_ref = refs[13:15]
    sems = refs[17]
    contact_kernel(0, *refs)
    copies = [
        pltpu.make_async_copy(agg_ref, agg_out_ref, sems.at[0]),
        pltpu.make_async_copy(grads_ref, grads_out_ref, sems.at[1]),
    ]
    for copy in copies:
        copy.start()
    for copy in copies:
        copy.wait()


def far_contact_kernel(grad_scale, first, *refs):
    cot_ref = refs[0]
    refs = refs[1:]
    agg_out_ref, packed_ref = refs[9:11]
    agg_ref, grads_ref = refs[13:15]
    packed_scr = refs[18]
    contact_kernel(first, *refs[:18])
    agg_rows = agg_ref[...].astype(jnp.bfloat16)
    agg_out_ref[...] = agg_rows
    cot = cot_ref[...]
    low = HID + GATES
    packed_scr[:low] = grads_ref[:low] * grad_scale
    packed_scr[low : low + CS] = jnp.concatenate(
        [
            dot(cot[:CS], agg_rows[:CS], 1, 1) * grad_scale,
            jnp.zeros((CS, LANES - CS), jnp.float32),
        ],
        1,
    )
    grad_vec = jnp.zeros((CV, CV), jnp.float32)
    for k in range(3):
        rows = slice(CS + k * CV, CS + (k + 1) * CV)
        grad_vec = grad_vec + dot(cot[rows], agg_rows[rows], 1, 1)
    packed_scr[low : low + CV, CS : CS + CV] = grad_vec * grad_scale
    grad_ten = jnp.zeros((CT, CT), jnp.float32)
    for m in range(9):
        rows = slice(CS + 3 * CV + m * CT, CS + 3 * CV + (m + 1) * CT)
        grad_ten = grad_ten + dot(cot[rows], agg_rows[rows], 1, 1)
    packed_scr[low : low + CT, CS + CV : CS + CV + CT] = grad_ten * grad_scale
    extra = grads_ref[low:] * grad_scale
    rows = lax.broadcasted_iota(jnp.int32, (16, LANES), 0)
    packed_scr[low + CS :] = jnp.where(rows == 1, extra[1:2] + extra[2:3], extra)
    packed = packed_scr[...].astype(jnp.bfloat16)
    height = packed_ref.shape[1]
    for peer in range(packed_ref.shape[0]):
        for row in range(0, height, 16):
            at = peer * height + row
            if at < packed.shape[0]:
                packed_ref[peer, row : row + 16] = packed[at : at + 16]
            else:
                packed_ref[peer, row : row + 16] = jnp.zeros((16, LANES), jnp.bfloat16)


def update_kernel(table_ref, agg_ref, w_scal_ref, w_vec_ref, w_ten_ref, out_ref, block_ref):
    block_diagonal(block_ref, w_scal_ref, w_vec_ref, w_ten_ref)
    out_ref[...] = (
        table_ref[:FEAT].astype(jnp.float32) + dot(block_ref[...], agg_ref[...])
    ).astype(jnp.bfloat16)


def sum_kernel(parts_ref, out_ref):
    total = parts_ref[0].astype(jnp.float32)
    for peer in range(1, parts_ref.shape[0]):
        total = total + parts_ref[peer].astype(jnp.float32)
    total = total.astype(jnp.bfloat16)
    for peer in range(out_ref.shape[0]):
        out_ref[peer] = total


def unpack_kernel(blocks_ref, one_ref, bias_ref, dist_ref, two_ref, scal_ref, vec_ref, ten_ref):
    height = blocks_ref.shape[1]

    def rows_of(block):
        peer, row = divmod(block * 16, height)
        return blocks_ref[peer, row : row + 16].astype(jnp.float32)

    for block in range(HID // 16):
        one_ref[block * 16 : (block + 1) * 16] = rows_of(block)
    for block in range(GATES // 16):
        two_ref[block * 16 : (block + 1) * 16] = rows_of(HID // 16 + block)
    low = (HID + GATES) // 16
    for block in range(CS // 16):
        rows = rows_of(low + block)
        scal_ref[block * 16 : (block + 1) * 16] = rows[:, :CS]
        if block < CV // 16:
            vec_ref[block * 16 : (block + 1) * 16] = rows[:, CS : CS + CV]
        if block == 0:
            ten_ref[...] = rows[:, CS + CV : CS + CV + CT]
    extra = rows_of(low + CS // 16)
    bias_ref[...] = extra[0:1]
    dist_ref[...] = extra[1:2]


def call(kernel, out_shape, scratch=(), in_specs=None, out_specs=None):
    specs = {}
    if in_specs is not None:
        specs["in_specs"] = in_specs
    if out_specs is not None:
        specs["out_specs"] = out_specs
    return pl.pallas_call(
        kernel,
        out_shape=out_shape,
        scratch_shapes=list(scratch),
        compiler_params=pltpu.CompilerParams(vmem_limit_bytes=VMEM_BYTES),
        **specs,
    )


IN_VMEM = pl.BlockSpec(memory_space=pltpu.VMEM)
IN_HBM = pl.BlockSpec(memory_space=pltpu.HBM)
IN_SMEM = pl.BlockSpec(memory_space=pltpu.SMEM)
ANYWHERE = pl.BlockSpec(memory_space=pl.ANY)


def exchange(blocks, axes=("dom", "z", "x")):
    return lax.all_to_all(blocks, axes, split_axis=0, concat_axis=0, tiled=True)


def in_hbm(*arrays):
    return tuple(pltpu.with_memory_space_constraint(array, pltpu.HBM) for array in arrays)


def shaped(shape, dtype):
    return jax.ShapeDtypeStruct(shape, dtype)


def from_behind(shard, axis, by):
    peers = lax.axis_size("z") * lax.axis_size("x")
    return lax.ppermute(shard, axis, [(i, (i + by) % peers) for i in range(peers)])


def planes_on(shard, pairs):
    return lax.ppermute(shard, "z", pairs)


def on_device(
    node_feat,
    node_pos,
    node_cot,
    mesh_senders,
    edge_mask,
    halo_up,
    halo_down,
    contact_rows,
    contact_dst,
    contact_mask,
    w_one,
    b_one,
    w_dist,
    w_two,
    w_scal,
    w_vec,
    w_ten,
):
    f32, bf16 = jnp.float32, jnp.bfloat16
    node_count = node_feat.shape[1]
    contact_count = contact_rows.shape[0]
    doms = lax.axis_size("dom")
    across = lax.axis_size("x")
    peers = doms * across
    device_count = peers * PLANES
    slot = contact_count // device_count
    chunks = contact_count // CHUNK
    grad_scale = 1.0 / math.sqrt(device_count * node_count * DEGREE)
    plane = lax.axis_index("z")
    plan = jnp.take(jnp.array(PLAN, jnp.int32), plane, axis=0)
    table, requests = call(
        functools.partial(table_kernel, doms),
        (
            shaped((ROWS, node_count), bf16),
            shaped((peers, 1, PLANES * slot), jnp.int32),
        ),
        (
            pltpu.VMEM((3, node_count), bf16),
            pltpu.VMEM((1, node_count), jnp.int32),
            pltpu.VMEM((1, node_count), jnp.int32),
            pltpu.VMEM((contact_count // LANES, LANES), jnp.int32),
            pltpu.SemaphoreType.DMA((5,)),
        ),
        in_specs=[IN_HBM] * 5,
        out_specs=(IN_VMEM, IN_VMEM),
    )(
        *in_hbm(
            node_feat,
            node_pos,
            halo_up[None],
            halo_down[None],
            contact_rows.reshape(contact_count // LANES, LANES),
        )
    )
    below = planes_on(table, [(0, 1), (1, 2), (2, 3)])
    above = planes_on(table, [(1, 0), (2, 1), (3, 2)])
    wanted = exchange(requests, ("dom", "x"))
    wanted, below, above, table_late = lax.optimization_barrier((wanted, below, above, table))
    below_two = planes_on(below, [(1, 2), (2, 3)])
    above_two = planes_on(above, [(2, 1), (1, 0)])
    far = jnp.where(plane < PLANES // 2, above_two, below_two)
    last = planes_on(far, [(2, 3), (1, 0)])
    low = from_behind(table_late, ("z", "x"), 1)
    high = from_behind(table_late, ("z", "x"), -1)
    reply_shape = shaped((peers, ROWS, 2 * slot), bf16)
    near_reply = exchange(
        call(
            near_gather_kernel,
            reply_shape,
            in_specs=[IN_SMEM] + [IN_VMEM] * 4,
            out_specs=IN_VMEM,
        )(plan, table, below, above, wanted),
        ("dom", "x"),
    )
    mesh_code = (
        jnp.where(edge_mask != 0, mesh_senders, -1)
        .reshape(node_count, DEGREE)
        .T.reshape(DEGREE, 1, node_count)
    )
    contact_code = (
        jnp.where(contact_mask != 0, contact_dst, -1)
        .reshape(doms, PLANES, across, slot)
        .transpose(1, 0, 2, 3)
        .reshape(PLANES, peers, slot)
    )
    ordered = jnp.zeros_like(contact_code)
    for at, order in enumerate(PLAN):
        ordered = jnp.where(plane == at, jnp.stack([contact_code[i] for i in order]), ordered)
    contact_code = (
        ordered.reshape(2, 2, peers, slot).transpose(0, 2, 1, 3).reshape(chunks, 1, CHUNK)
    )
    b_column = b_one[:, None]
    dist_column = w_dist[:, None]
    mesh_rows = HID + GATES + 16
    recv_rows = FEAT + 16 + CS
    mesh_agg, mesh_grads, recv = call(
        mesh_kernel,
        (
            pltpu.HBM((FEAT, node_count), f32),
            pltpu.HBM((mesh_rows, LANES), f32),
            pltpu.HBM((chunks, recv_rows, CHUNK), bf16),
        ),
        (
            pltpu.VMEM((FEAT, node_count), f32),
            pltpu.VMEM((mesh_rows, LANES), f32),
            pltpu.VMEM((chunks, recv_rows, CHUNK), bf16),
            pltpu.VMEM((recv_rows, node_count), bf16),
            pltpu.VMEM((ROWS, 3 * node_count), bf16),
            pltpu.VMEM((FEAT, FEAT), bf16),
            pltpu.SemaphoreType.DMA((3,)),
        ),
        in_specs=[IN_VMEM] * 13,
        out_specs=(IN_HBM, IN_HBM, IN_HBM),
    )(
        table,
        low,
        high,
        mesh_code,
        node_cot,
        w_one,
        b_column,
        dist_column,
        w_two,
        w_scal,
        w_vec,
        w_ten,
        contact_code,
    )
    far_reply = exchange(
        call(
            far_gather_kernel,
            reply_shape,
            in_specs=[IN_SMEM] + [IN_VMEM] * 5 + [IN_HBM],
            out_specs=IN_VMEM,
        )(plan, below, above, far, last, wanted, *in_hbm(mesh_grads)),
        ("dom", "x"),
    )
    packed_rows = mesh_rows + CS
    half = chunks // 2
    contact_scratch = (
        pltpu.VMEM((chunks, 1, CHUNK), jnp.int32),
        pltpu.VMEM((half, recv_rows, CHUNK), bf16),
        pltpu.VMEM((FEAT, node_count), f32),
        pltpu.VMEM((mesh_rows, LANES), f32),
        pltpu.VMEM((HID, 2 * CS), bf16),
        pltpu.VMEM((GATES, HID), bf16),
        pltpu.SemaphoreType.DMA((half + 5,)),
    )
    near_agg, near_grads = call(
        near_contact_kernel,
        (pltpu.HBM((FEAT, node_count), f32), pltpu.HBM((mesh_rows, LANES), f32)),
        contact_scratch,
        in_specs=[IN_VMEM] * 3 + [IN_HBM] * 6,
        out_specs=(IN_HBM, IN_HBM),
    )(
        near_reply,
        b_column,
        dist_column,
        *in_hbm(contact_code, recv, mesh_agg, mesh_grads, w_one, w_two),
    )
    agg_rows, packed = call(
        functools.partial(far_contact_kernel, grad_scale, half),
        (shaped((FEAT, node_count), bf16), shaped((device_count, 16, LANES), bf16)),
        contact_scratch + (pltpu.VMEM((packed_rows, LANES), f32),),
        in_specs=[IN_VMEM] * 4 + [IN_HBM] * 6,
        out_specs=(IN_VMEM, IN_VMEM),
    )(
        node_cot,
        far_reply,
        b_column,
        dist_column,
        *in_hbm(contact_code, recv, near_agg, near_grads, w_one, w_two),
    )
    node_out = call(
        update_kernel,
        shaped((FEAT, node_count), bf16),
        (pltpu.VMEM((FEAT, FEAT), bf16),),
    )(table, agg_rows, w_scal, w_vec, w_ten)
    shares = call(sum_kernel, shaped((device_count, 16, LANES), bf16))(exchange(packed))
    one, bias, dist, two, scal, vec, ten = call(
        unpack_kernel,
        (
            shaped((HID, 2 * CS), f32),
            shaped((1, HID), f32),
            shaped((1, HID), f32),
            shaped((GATES, HID), f32),
            shaped((CS, CS), f32),
            shaped((CV, CV), f32),
            shaped((CT, CT), f32),
        ),
    )(exchange(shares))
    return node_out, one, bias[0], dist[0], two, scal, vec, ten


def solution(mesh):
    doms = mesh.shape["dom"]
    across = mesh.shape["sub"] // PLANES
    cut = Mesh(mesh.devices.reshape(doms, PLANES, across), ("dom", "z", "x"))
    along = P(("dom", "z", "x"))
    columns = P(None, ("dom", "z", "x"))
    in_specs = (columns,) * 3 + (along,) * 7 + (P(),) * 7
    out_specs = (columns,) + (P(),) * 7
    return jax.shard_map(
        on_device, mesh=cut, in_specs=in_specs, out_specs=out_specs, check_vma=False
    )
```

```python
import functools
import math

import jax
import jax.numpy as jnp
from jax import lax
from jax.experimental import pallas as pl
from jax.experimental.pallas import tpu as pltpu
from jax.sharding import PartitionSpec as P

CS = 64
CV = 32
CT = 16
HID = 128
DEGREE = 6
GATES = 144
FEAT = CS + 3 * CV + 9 * CT
ROWS = 320
LANES = 128
CHUNK = 512
VMEM_BYTES = 48 * 1024 * 1024


def dot(lhs, rhs, lhs_dim=1, rhs_dim=0):
    return lax.dot_general(
        lhs, rhs, (((lhs_dim,), (rhs_dim,)), ((), ())), preferred_element_type=jnp.float32
    )


def one_hot(code, width):
    rows = lax.broadcasted_iota(jnp.int32, (width, code.shape[1]), 0)
    return jnp.where(rows == code, 1.0, 0.0).astype(jnp.bfloat16)


def join_index(table, row):
    pair = table[row : row + 2].astype(jnp.float32)
    return (pair[0:1] * 128.0 + pair[1:2]).astype(jnp.int32)


def table_kernel(
    feat_ref,
    pos_ref,
    up_ref,
    down_ref,
    rows_ref,
    table_ref,
    request_ref,
    pos_scr,
    up_scr,
    down_scr,
    rows_scr,
    sems,
):
    node_count = table_ref.shape[1]
    copies = [
        pltpu.make_async_copy(rows_ref, rows_scr, sems.at[0]),
        pltpu.make_async_copy(feat_ref, table_ref.at[:FEAT], sems.at[1]),
        pltpu.make_async_copy(pos_ref, pos_scr, sems.at[2]),
        pltpu.make_async_copy(up_ref, up_scr, sems.at[3]),
        pltpu.make_async_copy(down_ref, down_scr, sems.at[4]),
    ]
    for copy in copies:
        copy.start()
    copies[0].wait()
    slot = request_ref.shape[2]
    parts = LANES // slot
    for row in range(rows_scr.shape[0]):
        line = rows_scr[row : row + 1]
        for part in range(parts):
            request_ref[row * parts + part] = line[:, part * slot : (part + 1) * slot]
    for copy in copies[2:]:
        copy.wait()
    rows = lax.broadcasted_iota(jnp.int32, (ROWS - FEAT, node_count), 0)
    pos = pos_scr[...].astype(jnp.float32)
    tail = jnp.zeros((ROWS - FEAT, node_count), jnp.float32)
    for k in range(3):
        tail = jnp.where(rows == k, pos[k : k + 1], tail)
    for k, index_ref in ((3, up_scr), (5, down_scr)):
        index = index_ref[...]
        high = index >> 7
        tail = jnp.where(rows == k, high.astype(jnp.float32), tail)
        tail = jnp.where(rows == k + 1, (index - (high << 7)).astype(jnp.float32), tail)
    table_ref[FEAT:] = tail.astype(jnp.bfloat16)
    copies[1].wait()


def contact_gather_kernel(slot, table_ref, wanted_ref, out_ref):
    node_count = table_ref.shape[1]
    parts = LANES // slot
    height = out_ref.shape[1]
    per_chunk = CHUNK // slot
    for chunk in range(wanted_ref.shape[0] // per_chunk):
        wanted = [wanted_ref[chunk * per_chunk + peer] for peer in range(per_chunk)]
        hot = one_hot(jnp.concatenate(wanted, 1), node_count)
        rows = dot(table_ref[...], hot).astype(jnp.bfloat16)
        if parts * height > ROWS:
            rows = jnp.concatenate(
                [rows, jnp.zeros((parts * height - ROWS, CHUNK), jnp.bfloat16)], 0
            )
        for peer in range(per_chunk):
            out_ref[chunk * per_chunk + peer] = jnp.concatenate(
                [
                    rows[part * height : (part + 1) * height, peer * slot : (peer + 1) * slot]
                    for part in range(parts)
                ],
                1,
            )


def edge_math(src, base, first, inputs, pos_recv, back, live, weights):
    w_dist, w_two, w_two_t = weights
    edges = src.shape[1]
    offset = src[FEAT : FEAT + 3] - pos_recv
    if live is not None:
        offset = offset * live
    distance = jnp.sum(offset * offset, 0, keepdims=True)
    linear = base + first + w_dist * distance
    squashed = 0.5 * jnp.tanh(0.5 * linear) + 0.5
    hidden = (linear * squashed).astype(jnp.bfloat16)
    gates = dot(w_two, hidden)
    gate_vec = gates[CS : CS + CV]
    gate_dir = gates[CS + CV : CS + 2 * CV]
    gate_ten = gates[CS + 2 * CV :]
    message = [gates[:CS] * src[:CS]]
    vec_part = jnp.zeros((CV, edges), jnp.float32)
    dir_part = jnp.zeros((CV, edges), jnp.float32)
    for k in range(3):
        rows = slice(CS + k * CV, CS + (k + 1) * CV)
        message.append(gate_vec * src[rows] + gate_dir * offset[k : k + 1])
        vec_part = vec_part + back[rows] * src[rows]
        dir_part = dir_part + back[rows] * offset[k : k + 1]
    ten_part = jnp.zeros((CT, edges), jnp.float32)
    for m in range(9):
        rows = slice(CS + 3 * CV + m * CT, CS + 3 * CV + (m + 1) * CT)
        message.append(gate_ten * src[rows])
        ten_part = ten_part + back[rows] * src[rows]
    message = jnp.concatenate(message, 0)
    dgates = jnp.concatenate([back[:CS] * src[:CS], vec_part, dir_part, ten_part], 0).astype(
        jnp.bfloat16
    )
    hidden_grad = dot(w_two_t, dgates)
    linear_grad = (hidden_grad * squashed * (1.0 + linear * (1.0 - squashed))).astype(jnp.bfloat16)
    rows = lax.broadcasted_iota(jnp.int32, (16, edges), 0)
    coarse = distance.astype(jnp.bfloat16).astype(jnp.float32)
    extra = jnp.where(
        rows == 0, 1.0, jnp.where(rows == 1, coarse, jnp.where(rows == 2, distance - coarse, 0.0))
    ).astype(jnp.bfloat16)
    grads = (
        dot(linear_grad, inputs, 1, 1),
        dot(dgates, hidden, 1, 1),
        dot(extra, linear_grad, 1, 1),
    )
    return message, grads


def add_grads(grads_ref, grads):
    grads_ref[:HID] += grads[0]
    grads_ref[HID : HID + GATES] += grads[1]
    grads_ref[HID + GATES : HID + GATES + 16] += grads[2]


def block_diagonal(block_ref, w_scal, w_vec, w_ten):
    block_ref[...] = jnp.zeros_like(block_ref)
    block_ref[:CS, :CS] = w_scal[...]
    for k in range(3):
        rows = slice(CS + k * CV, CS + (k + 1) * CV)
        block_ref[rows, rows] = w_vec[...]
    for m in range(9):
        rows = slice(CS + 3 * CV + m * CT, CS + 3 * CV + (m + 1) * CT)
        block_ref[rows, rows] = w_ten[...]


def mesh_kernel(
    table_ref,
    low_ref,
    high_ref,
    code_ref,
    cot_ref,
    w_one_ref,
    b_one_ref,
    w_dist_ref,
    w_two_ref,
    w_scal_ref,
    w_vec_ref,
    w_ten_ref,
    contact_ref,
    agg_out_ref,
    grads_out_ref,
    recv_out_ref,
    agg_ref,
    grads_ref,
    recv_ref,
    receive_ref,
    source_ref,
    block_ref,
    sems,
):
    node_count = table_ref.shape[1]
    source_ref[:, :node_count] = table_ref[...]
    low = low_ref[...]
    high = high_ref[...]
    source_ref[:, node_count : 2 * node_count] = dot(
        low, one_hot(join_index(low, FEAT + 3), node_count)
    ).astype(jnp.bfloat16)
    source_ref[:, 2 * node_count :] = dot(
        high, one_hot(join_index(high, FEAT + 5), node_count)
    ).astype(jnp.bfloat16)
    block_diagonal(block_ref, w_scal_ref, w_vec_ref, w_ten_ref)
    receive_ref[:FEAT] = dot(block_ref[...], cot_ref[...], 0, 0).astype(jnp.bfloat16)
    receive_ref[FEAT : FEAT + 16] = table_ref[FEAT:]
    receive_ref[FEAT + 16 :] = table_ref[:CS]
    w_one = w_one_ref[...]
    w_two = w_two_ref[...]
    scal_recv = table_ref[:CS]
    recv_linear = dot(w_one[:, :CS], scal_recv) + b_one_ref[...]
    weights = (w_dist_ref[...], w_two, w_two.T)
    pos_recv = table_ref[FEAT:].astype(jnp.float32)[:3]
    grads_ref[...] = jnp.zeros_like(grads_ref)
    agg_ref[...] = jnp.zeros_like(agg_ref)
    for step in range(DEGREE):
        code = code_ref[step]
        src = dot(source_ref[...], one_hot(code, 3 * node_count))
        live = jnp.where(code >= 0, 1.0, 0.0)
        back = receive_ref[:FEAT].astype(jnp.float32)
        scal_send = src[:CS].astype(jnp.bfloat16)
        inputs = jnp.concatenate([scal_recv, scal_send], 0)
        message, grads = edge_math(
            src, recv_linear, dot(w_one[:, CS:], scal_send), inputs, pos_recv, back, live, weights
        )
        agg_ref[...] += message
        add_grads(grads_ref, grads)
    for chunk in range(contact_ref.shape[0]):
        recv_ref[chunk] = dot(
            receive_ref[...], one_hot(contact_ref[chunk], node_count)
        ).astype(jnp.bfloat16)
    copies = [
        pltpu.make_async_copy(agg_ref, agg_out_ref, sems.at[0]),
        pltpu.make_async_copy(grads_ref, grads_out_ref, sems.at[1]),
        pltpu.make_async_copy(recv_ref, recv_out_ref, sems.at[2]),
    ]
    for copy in copies:
        copy.start()
    for copy in copies:
        copy.wait()


def contact_kernel(
    slot,
    grad_scale,
    reply_ref,
    cot_ref,
    b_one_ref,
    w_dist_ref,
    code_hbm,
    recv_hbm,
    mesh_agg_hbm,
    mesh_grads_hbm,
    w_one_hbm,
    w_two_hbm,
    agg_out_ref,
    packed_ref,
    code_ref,
    recv_ref,
    agg_ref,
    grads_ref,
    w_one_ref,
    w_two_ref,
    packed_scr,
    sems,
):
    chunks = code_ref.shape[0]
    sources = [(code_hbm, code_ref), (w_one_hbm, w_one_ref), (w_two_hbm, w_two_ref)]
    sources += [(recv_hbm.at[chunk], recv_ref.at[chunk]) for chunk in range(chunks)]
    sources += [(mesh_agg_hbm, agg_ref), (mesh_grads_hbm, grads_ref)]
    copies = [
        pltpu.make_async_copy(source, target, sems.at[at])
        for at, (source, target) in enumerate(sources)
    ]
    for copy in copies:
        copy.start()
    node_count = cot_ref.shape[1]
    parts = LANES // slot
    per_chunk = CHUNK // slot
    for copy in copies[:3]:
        copy.wait()
    w_one = w_one_ref[...]
    w_two = w_two_ref[...]
    weights = (w_dist_ref[...], w_two, w_two.T)
    for chunk in range(chunks):
        blocks = [reply_ref[chunk * per_chunk + peer] for peer in range(per_chunk)]
        src_rows = jnp.concatenate(
            [
                jnp.concatenate(
                    [block[:, part * slot : (part + 1) * slot] for block in blocks], 1
                )
                for part in range(parts)
            ],
            0,
        )[:ROWS]
        copies[3 + chunk].wait()
        recv = recv_ref[chunk]
        inputs = jnp.concatenate([recv[FEAT + 16 :], src_rows[:CS]], 0)
        message, grads = edge_math(
            src_rows.astype(jnp.float32),
            b_one_ref[...],
            dot(w_one, inputs),
            inputs,
            recv[FEAT : FEAT + 16].astype(jnp.float32)[:3],
            recv[:FEAT].astype(jnp.float32),
            None,
            weights,
        )
        scattered = dot(message.astype(jnp.bfloat16), one_hot(code_ref[chunk], node_count), 1, 1)
        if chunk == 0:
            for copy in copies[3 + chunks :]:
                copy.wait()
        agg_ref[...] += scattered
        add_grads(grads_ref, grads)
    agg_rows = agg_ref[...].astype(jnp.bfloat16)
    agg_out_ref[...] = agg_rows
    cot = cot_ref[...]
    low = HID + GATES
    packed_scr[:low] = grads_ref[:low] * grad_scale
    packed_scr[low : low + CS] = jnp.concatenate(
        [
            dot(cot[:CS], agg_rows[:CS], 1, 1) * grad_scale,
            jnp.zeros((CS, LANES - CS), jnp.float32),
        ],
        1,
    )
    grad_vec = jnp.zeros((CV, CV), jnp.float32)
    for k in range(3):
        rows = slice(CS + k * CV, CS + (k + 1) * CV)
        grad_vec = grad_vec + dot(cot[rows], agg_rows[rows], 1, 1)
    packed_scr[low : low + CV, CS : CS + CV] = grad_vec * grad_scale
    grad_ten = jnp.zeros((CT, CT), jnp.float32)
    for m in range(9):
        rows = slice(CS + 3 * CV + m * CT, CS + 3 * CV + (m + 1) * CT)
        grad_ten = grad_ten + dot(cot[rows], agg_rows[rows], 1, 1)
    packed_scr[low : low + CT, CS + CV : CS + CV + CT] = grad_ten * grad_scale
    extra = grads_ref[low:] * grad_scale
    rows = lax.broadcasted_iota(jnp.int32, (16, LANES), 0)
    packed_scr[low + CS :] = jnp.where(rows == 1, extra[1:2] + extra[2:3], extra)
    packed = packed_scr[...].astype(jnp.bfloat16)
    height = packed_ref.shape[1]
    for peer in range(packed_ref.shape[0]):
        for row in range(0, height, 16):
            at = peer * height + row
            if at < packed.shape[0]:
                packed_ref[peer, row : row + 16] = packed[at : at + 16]
            else:
                packed_ref[peer, row : row + 16] = jnp.zeros((16, LANES), jnp.bfloat16)


def update_kernel(table_ref, agg_ref, w_scal_ref, w_vec_ref, w_ten_ref, out_ref, block_ref):
    block_diagonal(block_ref, w_scal_ref, w_vec_ref, w_ten_ref)
    out_ref[...] = (
        table_ref[:FEAT].astype(jnp.float32) + dot(block_ref[...], agg_ref[...])
    ).astype(jnp.bfloat16)


def sum_kernel(parts_ref, out_ref):
    total = parts_ref[0].astype(jnp.float32)
    for peer in range(1, parts_ref.shape[0]):
        total = total + parts_ref[peer].astype(jnp.float32)
    total = total.astype(jnp.bfloat16)
    for peer in range(out_ref.shape[0]):
        out_ref[peer] = total


def unpack_kernel(blocks_ref, one_ref, bias_ref, dist_ref, two_ref, scal_ref, vec_ref, ten_ref):
    height = blocks_ref.shape[1]

    def rows_of(block):
        peer, row = divmod(block * 16, height)
        return blocks_ref[peer, row : row + 16].astype(jnp.float32)

    for block in range(HID // 16):
        one_ref[block * 16 : (block + 1) * 16] = rows_of(block)
    for block in range(GATES // 16):
        two_ref[block * 16 : (block + 1) * 16] = rows_of(HID // 16 + block)
    low = (HID + GATES) // 16
    for block in range(CS // 16):
        rows = rows_of(low + block)
        scal_ref[block * 16 : (block + 1) * 16] = rows[:, :CS]
        if block < CV // 16:
            vec_ref[block * 16 : (block + 1) * 16] = rows[:, CS : CS + CV]
        if block == 0:
            ten_ref[...] = rows[:, CS + CV : CS + CV + CT]
    extra = rows_of(low + CS // 16)
    bias_ref[...] = extra[0:1]
    dist_ref[...] = extra[1:2]


def call(kernel, out_shape, scratch=(), in_specs=None, out_specs=None, cost_estimate=None):
    specs = {}
    if cost_estimate is not None:
        specs["cost_estimate"] = cost_estimate
    if in_specs is not None:
        specs["in_specs"] = in_specs
    if out_specs is not None:
        specs["out_specs"] = out_specs
    return pl.pallas_call(
        kernel,
        out_shape=out_shape,
        scratch_shapes=list(scratch),
        compiler_params=pltpu.CompilerParams(vmem_limit_bytes=VMEM_BYTES),
        **specs,
    )


IN_VMEM = pl.BlockSpec(memory_space=pltpu.VMEM)
IN_HBM = pl.BlockSpec(memory_space=pltpu.HBM)
ANYWHERE = pl.BlockSpec(memory_space=pl.ANY)


def exchange(blocks, axes=("dom", "sub")):
    return lax.all_to_all(blocks, axes, split_axis=0, concat_axis=0, tiled=True)


def in_hbm(*arrays):
    return tuple(pltpu.with_memory_space_constraint(array, pltpu.HBM) for array in arrays)


def shaped(shape, dtype):
    return jax.ShapeDtypeStruct(shape, dtype)


def from_behind(shard, axis, by):
    peers = lax.axis_size(axis)
    return lax.ppermute(shard, axis, [(i, (i + by) % peers) for i in range(peers)])


def on_device(
    node_feat,
    node_pos,
    node_cot,
    mesh_senders,
    edge_mask,
    halo_up,
    halo_down,
    contact_rows,
    contact_dst,
    contact_mask,
    w_one,
    b_one,
    w_dist,
    w_two,
    w_scal,
    w_vec,
    w_ten,
):
    f32, bf16 = jnp.float32, jnp.bfloat16
    node_count = node_feat.shape[1]
    contact_count = contact_rows.shape[0]
    device_count = lax.axis_size("dom") * lax.axis_size("sub")
    slot = contact_count // device_count
    chunks = contact_count // CHUNK
    parts = LANES // slot
    height = -(-ROWS // (parts * 16)) * 16
    grad_scale = 1.0 / math.sqrt(device_count * node_count * DEGREE)
    table, requests = call(
        table_kernel,
        (
            shaped((ROWS, node_count), bf16),
            shaped((device_count, 1, slot), jnp.int32),
        ),
        (
            pltpu.VMEM((3, node_count), bf16),
            pltpu.VMEM((1, node_count), jnp.int32),
            pltpu.VMEM((1, node_count), jnp.int32),
            pltpu.VMEM((contact_count // LANES, LANES), jnp.int32),
            pltpu.SemaphoreType.DMA((5,)),
        ),
        in_specs=[IN_HBM] * 5,
        out_specs=(IN_VMEM, IN_VMEM),
    )(
        *in_hbm(
            node_feat,
            node_pos,
            halo_up[None],
            halo_down[None],
            contact_rows.reshape(contact_count // LANES, LANES),
        )
    )
    wanted = exchange(requests)
    wanted, table_late = lax.optimization_barrier((wanted, table))
    low = from_behind(table_late, "sub", 1)
    high = from_behind(table_late, "sub", -1)
    replies = exchange(
        call(
            functools.partial(contact_gather_kernel, slot),
            shaped((device_count, height, LANES), bf16),
            in_specs=[IN_VMEM, IN_VMEM],
            out_specs=IN_VMEM,
        )(table, wanted)
    )
    mesh_code = (
        jnp.where(edge_mask != 0, mesh_senders, -1)
        .reshape(node_count, DEGREE)
        .T.reshape(DEGREE, 1, node_count)
    )
    contact_code = jnp.where(contact_mask != 0, contact_dst, -1).reshape(chunks, 1, CHUNK)
    b_column = b_one[:, None]
    dist_column = w_dist[:, None]
    mesh_rows = HID + GATES + 16
    recv_rows = FEAT + 16 + CS
    mesh_agg, mesh_grads, recv = call(
        mesh_kernel,
        (
            pltpu.HBM((FEAT, node_count), f32),
            pltpu.HBM((mesh_rows, LANES), f32),
            pltpu.HBM((chunks, recv_rows, CHUNK), bf16),
        ),
        (
            pltpu.VMEM((FEAT, node_count), f32),
            pltpu.VMEM((mesh_rows, LANES), f32),
            pltpu.VMEM((chunks, recv_rows, CHUNK), bf16),
            pltpu.VMEM((recv_rows, node_count), bf16),
            pltpu.VMEM((ROWS, 3 * node_count), bf16),
            pltpu.VMEM((FEAT, FEAT), bf16),
            pltpu.SemaphoreType.DMA((3,)),
        ),
        in_specs=[IN_VMEM] * 13,
        out_specs=(IN_HBM, IN_HBM, IN_HBM),
        cost_estimate=pl.CostEstimate(
            flops=40_000_000_000, bytes_accessed=8_000_000, transcendentals=400_000
        ),
    )(
        table,
        low,
        high,
        mesh_code,
        node_cot,
        w_one,
        b_column,
        dist_column,
        w_two,
        w_scal,
        w_vec,
        w_ten,
        contact_code,
    )
    packed_rows = mesh_rows + CS
    agg_rows, packed = call(
        functools.partial(contact_kernel, slot, grad_scale),
        (shaped((FEAT, node_count), bf16), shaped((device_count, 16, LANES), bf16)),
        (
            pltpu.VMEM((chunks, 1, CHUNK), jnp.int32),
            pltpu.VMEM((chunks, recv_rows, CHUNK), bf16),
            pltpu.VMEM((FEAT, node_count), f32),
            pltpu.VMEM((mesh_rows, LANES), f32),
            pltpu.VMEM((HID, 2 * CS), bf16),
            pltpu.VMEM((GATES, HID), bf16),
            pltpu.VMEM((packed_rows, LANES), f32),
            pltpu.SemaphoreType.DMA((chunks + 5,)),
        ),
        in_specs=[IN_VMEM] * 4 + [IN_HBM] * 6,
        out_specs=(IN_VMEM, IN_VMEM),
    )(
        replies,
        node_cot,
        b_column,
        dist_column,
        *in_hbm(contact_code, recv, mesh_agg, mesh_grads, w_one, w_two),
    )
    node_out = call(
        update_kernel,
        shaped((FEAT, node_count), bf16),
        (pltpu.VMEM((FEAT, FEAT), bf16),),
    )(table, agg_rows, w_scal, w_vec, w_ten)
    shares = call(sum_kernel, shaped((device_count, 16, LANES), bf16))(exchange(packed))
    one, bias, dist, two, scal, vec, ten = call(
        unpack_kernel,
        (
            shaped((HID, 2 * CS), f32),
            shaped((1, HID), f32),
            shaped((1, HID), f32),
            shaped((GATES, HID), f32),
            shaped((CS, CS), f32),
            shaped((CV, CV), f32),
            shaped((CT, CT), f32),
        ),
    )(exchange(shares))
    return node_out, one, bias[0], dist[0], two, scal, vec, ten


def solution(mesh):
    along = P(("dom", "sub"))
    columns = P(None, ("dom", "sub"))
    in_specs = (columns,) * 3 + (along,) * 7 + (P(),) * 7
    out_specs = (columns,) + (P(),) * 7
    return jax.shard_map(
        on_device, mesh=mesh, in_specs=in_specs, out_specs=out_specs, check_vma=False
    )
```

```python
import functools
import math

import jax
import jax.numpy as jnp
from jax import lax
from jax.experimental import pallas as pl
from jax.experimental.pallas import tpu as pltpu
from jax.sharding import PartitionSpec as P

CS = 64
CV = 32
CT = 16
HID = 128
DEGREE = 6
GATES = 144
FEAT = CS + 3 * CV + 9 * CT
ROWS = 320
LANES = 128
CHUNK = 512
VMEM_BYTES = 48 * 1024 * 1024


def dot(lhs, rhs, lhs_dim=1, rhs_dim=0):
    return lax.dot_general(
        lhs, rhs, (((lhs_dim,), (rhs_dim,)), ((), ())), preferred_element_type=jnp.float32
    )


def one_hot(code, width):
    rows = lax.broadcasted_iota(jnp.int32, (width, code.shape[1]), 0)
    return jnp.where(rows == code, 1.0, 0.0).astype(jnp.bfloat16)


def join_index(table, row):
    pair = table[row : row + 2].astype(jnp.float32)
    return (pair[0:1] * 128.0 + pair[1:2]).astype(jnp.int32)


def table_kernel(
    feat_ref,
    pos_ref,
    up_ref,
    down_ref,
    rows_ref,
    table_ref,
    request_ref,
    pos_scr,
    up_scr,
    down_scr,
    rows_scr,
    sems,
):
    node_count = table_ref.shape[1]
    copies = [
        pltpu.make_async_copy(rows_ref, rows_scr, sems.at[0]),
        pltpu.make_async_copy(feat_ref, table_ref.at[:FEAT], sems.at[1]),
        pltpu.make_async_copy(pos_ref, pos_scr, sems.at[2]),
        pltpu.make_async_copy(up_ref, up_scr, sems.at[3]),
        pltpu.make_async_copy(down_ref, down_scr, sems.at[4]),
    ]
    for copy in copies:
        copy.start()
    copies[0].wait()
    slot = request_ref.shape[2]
    parts = LANES // slot
    for row in range(rows_scr.shape[0]):
        line = rows_scr[row : row + 1]
        for part in range(parts):
            request_ref[row * parts + part] = line[:, part * slot : (part + 1) * slot]
    for copy in copies[2:]:
        copy.wait()
    rows = lax.broadcasted_iota(jnp.int32, (ROWS - FEAT, node_count), 0)
    pos = pos_scr[...].astype(jnp.float32)
    tail = jnp.zeros((ROWS - FEAT, node_count), jnp.float32)
    for k in range(3):
        tail = jnp.where(rows == k, pos[k : k + 1], tail)
    for k, index_ref in ((3, up_scr), (5, down_scr)):
        index = index_ref[...]
        high = index >> 7
        tail = jnp.where(rows == k, high.astype(jnp.float32), tail)
        tail = jnp.where(rows == k + 1, (index - (high << 7)).astype(jnp.float32), tail)
    table_ref[FEAT:] = tail.astype(jnp.bfloat16)
    copies[1].wait()


def contact_gather_kernel(first, half, table_ref, wanted_ref, out_ref):
    node_count = table_ref.shape[1]
    parts = LANES // half
    peers, height, _ = out_ref.shape
    per_chunk = CHUNK // half
    for chunk in range(peers // per_chunk):
        at = range(chunk * per_chunk, (chunk + 1) * per_chunk)
        wanted = jnp.concatenate([wanted_ref[peer, :, first : first + half] for peer in at], 1)
        rows = dot(table_ref[...], one_hot(wanted, node_count)).astype(jnp.bfloat16)
        if parts * height > ROWS:
            rows = jnp.concatenate(
                [rows, jnp.zeros((parts * height - ROWS, CHUNK), jnp.bfloat16)], 0
            )
        for place, peer in enumerate(at):
            out_ref[peer] = jnp.concatenate(
                [
                    rows[part * height : (part + 1) * height, place * half : (place + 1) * half]
                    for part in range(parts)
                ],
                1,
            )


def edge_math(src, base, first, inputs, pos_recv, back, live, weights):
    w_dist, w_two, w_two_t = weights
    edges = src.shape[1]
    offset = src[FEAT : FEAT + 3] - pos_recv
    if live is not None:
        offset = offset * live
    distance = jnp.sum(offset * offset, 0, keepdims=True)
    linear = base + first + w_dist * distance
    squashed = 0.5 * jnp.tanh(0.5 * linear) + 0.5
    hidden = (linear * squashed).astype(jnp.bfloat16)
    gates = dot(w_two, hidden)
    gate_vec = gates[CS : CS + CV]
    gate_dir = gates[CS + CV : CS + 2 * CV]
    gate_ten = gates[CS + 2 * CV :]
    message = [gates[:CS] * src[:CS]]
    vec_part = jnp.zeros((CV, edges), jnp.float32)
    dir_part = jnp.zeros((CV, edges), jnp.float32)
    for k in range(3):
        rows = slice(CS + k * CV, CS + (k + 1) * CV)
        message.append(gate_vec * src[rows] + gate_dir * offset[k : k + 1])
        vec_part = vec_part + back[rows] * src[rows]
        dir_part = dir_part + back[rows] * offset[k : k + 1]
    ten_part = jnp.zeros((CT, edges), jnp.float32)
    for m in range(9):
        rows = slice(CS + 3 * CV + m * CT, CS + 3 * CV + (m + 1) * CT)
        message.append(gate_ten * src[rows])
        ten_part = ten_part + back[rows] * src[rows]
    message = jnp.concatenate(message, 0)
    dgates = jnp.concatenate([back[:CS] * src[:CS], vec_part, dir_part, ten_part], 0).astype(
        jnp.bfloat16
    )
    hidden_grad = dot(w_two_t, dgates)
    linear_grad = (hidden_grad * squashed * (1.0 + linear * (1.0 - squashed))).astype(jnp.bfloat16)
    rows = lax.broadcasted_iota(jnp.int32, (16, edges), 0)
    coarse = distance.astype(jnp.bfloat16).astype(jnp.float32)
    extra = jnp.where(
        rows == 0, 1.0, jnp.where(rows == 1, coarse, jnp.where(rows == 2, distance - coarse, 0.0))
    ).astype(jnp.bfloat16)
    grads = (
        dot(linear_grad, inputs, 1, 1),
        dot(dgates, hidden, 1, 1),
        dot(extra, linear_grad, 1, 1),
    )
    return message, grads


def add_grads(grads_ref, grads):
    grads_ref[:HID] += grads[0]
    grads_ref[HID : HID + GATES] += grads[1]
    grads_ref[HID + GATES : HID + GATES + 16] += grads[2]


def block_diagonal(block_ref, w_scal, w_vec, w_ten):
    block_ref[...] = jnp.zeros_like(block_ref)
    block_ref[:CS, :CS] = w_scal[...]
    for k in range(3):
        rows = slice(CS + k * CV, CS + (k + 1) * CV)
        block_ref[rows, rows] = w_vec[...]
    for m in range(9):
        rows = slice(CS + 3 * CV + m * CT, CS + 3 * CV + (m + 1) * CT)
        block_ref[rows, rows] = w_ten[...]


def mesh_kernel(
    table_ref,
    low_ref,
    high_ref,
    code_ref,
    cot_ref,
    w_one_ref,
    b_one_ref,
    w_dist_ref,
    w_two_ref,
    w_scal_ref,
    w_vec_ref,
    w_ten_ref,
    contact_ref,
    agg_out_ref,
    grads_out_ref,
    recv_out_ref,
    agg_ref,
    grads_ref,
    recv_ref,
    receive_ref,
    source_ref,
    block_ref,
    sems,
):
    node_count = table_ref.shape[1]
    source_ref[:, :node_count] = table_ref[...]
    low = low_ref[...]
    high = high_ref[...]
    source_ref[:, node_count : 2 * node_count] = dot(
        low, one_hot(join_index(low, FEAT + 3), node_count)
    ).astype(jnp.bfloat16)
    source_ref[:, 2 * node_count :] = dot(
        high, one_hot(join_index(high, FEAT + 5), node_count)
    ).astype(jnp.bfloat16)
    block_diagonal(block_ref, w_scal_ref, w_vec_ref, w_ten_ref)
    receive_ref[:FEAT] = dot(block_ref[...], cot_ref[...], 0, 0).astype(jnp.bfloat16)
    receive_ref[FEAT : FEAT + 16] = table_ref[FEAT:]
    receive_ref[FEAT + 16 :] = table_ref[:CS]
    w_one = w_one_ref[...]
    w_two = w_two_ref[...]
    scal_recv = table_ref[:CS]
    recv_linear = dot(w_one[:, :CS], scal_recv) + b_one_ref[...]
    weights = (w_dist_ref[...], w_two, w_two.T)
    pos_recv = table_ref[FEAT:].astype(jnp.float32)[:3]
    grads_ref[...] = jnp.zeros_like(grads_ref)
    agg_ref[...] = jnp.zeros_like(agg_ref)
    for step in range(DEGREE):
        code = code_ref[step]
        src = dot(source_ref[...], one_hot(code, 3 * node_count))
        live = jnp.where(code >= 0, 1.0, 0.0)
        back = receive_ref[:FEAT].astype(jnp.float32)
        scal_send = src[:CS].astype(jnp.bfloat16)
        inputs = jnp.concatenate([scal_recv, scal_send], 0)
        message, grads = edge_math(
            src, recv_linear, dot(w_one[:, CS:], scal_send), inputs, pos_recv, back, live, weights
        )
        agg_ref[...] += message
        add_grads(grads_ref, grads)
    for chunk in range(contact_ref.shape[0]):
        recv_ref[chunk] = dot(
            receive_ref[...], one_hot(contact_ref[chunk], node_count)
        ).astype(jnp.bfloat16)
    copies = [
        pltpu.make_async_copy(agg_ref, agg_out_ref, sems.at[0]),
        pltpu.make_async_copy(grads_ref, grads_out_ref, sems.at[1]),
        pltpu.make_async_copy(recv_ref, recv_out_ref, sems.at[2]),
    ]
    for copy in copies:
        copy.start()
    for copy in copies:
        copy.wait()


def contact_kernel(
    first,
    reply_ref,
    b_one_ref,
    w_dist_ref,
    code_hbm,
    recv_hbm,
    agg_hbm,
    grads_hbm,
    w_one_hbm,
    w_two_hbm,
    agg_out_ref,
    grads_out_ref,
    code_ref,
    recv_ref,
    agg_ref,
    grads_ref,
    w_one_ref,
    w_two_ref,
    sems,
):
    chunks = recv_ref.shape[0]
    half = chunks * CHUNK // reply_ref.shape[0]
    parts = LANES // half
    node_count = agg_ref.shape[1]
    sources = [(code_hbm, code_ref), (w_one_hbm, w_one_ref), (w_two_hbm, w_two_ref)]
    sources += [(recv_hbm.at[first + chunk], recv_ref.at[chunk]) for chunk in range(chunks)]
    sources += [(agg_hbm, agg_ref), (grads_hbm, grads_ref)]
    copies = [
        pltpu.make_async_copy(source, target, sems.at[at])
        for at, (source, target) in enumerate(sources)
    ]
    for copy in copies:
        copy.start()
    for copy in copies[:3]:
        copy.wait()
    w_one = w_one_ref[...]
    w_two = w_two_ref[...]
    weights = (w_dist_ref[...], w_two, w_two.T)
    per_chunk = CHUNK // half
    for chunk in range(chunks):
        blocks = [reply_ref[chunk * per_chunk + peer] for peer in range(per_chunk)]
        src_rows = jnp.concatenate(
            [
                jnp.concatenate(
                    [block[:, part * half : (part + 1) * half] for block in blocks], 1
                )
                for part in range(parts)
            ],
            0,
        )[:ROWS]
        copies[3 + chunk].wait()
        recv = recv_ref[chunk]
        inputs = jnp.concatenate([recv[FEAT + 16 :], src_rows[:CS]], 0)
        message, grads = edge_math(
            src_rows.astype(jnp.float32),
            b_one_ref[...],
            dot(w_one, inputs),
            inputs,
            recv[FEAT : FEAT + 16].astype(jnp.float32)[:3],
            recv[:FEAT].astype(jnp.float32),
            None,
            weights,
        )
        hot = one_hot(code_ref[first + chunk], node_count)
        scattered = dot(message.astype(jnp.bfloat16), hot, 1, 1)
        if chunk == 0:
            for copy in copies[3 + chunks :]:
                copy.wait()
        agg_ref[...] += scattered
        add_grads(grads_ref, grads)


def near_contact_kernel(*refs):
    agg_out_ref, grads_out_ref = refs[9:11]
    agg_ref, grads_ref = refs[13:15]
    sems = refs[17]
    contact_kernel(0, *refs)
    copies = [
        pltpu.make_async_copy(agg_ref, agg_out_ref, sems.at[0]),
        pltpu.make_async_copy(grads_ref, grads_out_ref, sems.at[1]),
    ]
    for copy in copies:
        copy.start()
    for copy in copies:
        copy.wait()


def far_contact_kernel(grad_scale, first, *refs):
    cot_ref = refs[0]
    refs = refs[1:]
    agg_out_ref, packed_ref = refs[9:11]
    agg_ref, grads_ref = refs[13:15]
    packed_scr = refs[18]
    contact_kernel(first, *refs[:18])
    agg_rows = agg_ref[...].astype(jnp.bfloat16)
    agg_out_ref[...] = agg_rows
    cot = cot_ref[...]
    low = HID + GATES
    packed_scr[:low] = grads_ref[:low] * grad_scale
    packed_scr[low : low + CS] = jnp.concatenate(
        [
            dot(cot[:CS], agg_rows[:CS], 1, 1) * grad_scale,
            jnp.zeros((CS, LANES - CS), jnp.float32),
        ],
        1,
    )
    grad_vec = jnp.zeros((CV, CV), jnp.float32)
    for k in range(3):
        rows = slice(CS + k * CV, CS + (k + 1) * CV)
        grad_vec = grad_vec + dot(cot[rows], agg_rows[rows], 1, 1)
    packed_scr[low : low + CV, CS : CS + CV] = grad_vec * grad_scale
    grad_ten = jnp.zeros((CT, CT), jnp.float32)
    for m in range(9):
        rows = slice(CS + 3 * CV + m * CT, CS + 3 * CV + (m + 1) * CT)
        grad_ten = grad_ten + dot(cot[rows], agg_rows[rows], 1, 1)
    packed_scr[low : low + CT, CS + CV : CS + CV + CT] = grad_ten * grad_scale
    extra = grads_ref[low:] * grad_scale
    rows = lax.broadcasted_iota(jnp.int32, (16, LANES), 0)
    packed_scr[low + CS :] = jnp.where(rows == 1, extra[1:2] + extra[2:3], extra)
    packed = packed_scr[...].astype(jnp.bfloat16)
    height = packed_ref.shape[1]
    for peer in range(packed_ref.shape[0]):
        for row in range(0, height, 16):
            at = peer * height + row
            if at < packed.shape[0]:
                packed_ref[peer, row : row + 16] = packed[at : at + 16]
            else:
                packed_ref[peer, row : row + 16] = jnp.zeros((16, LANES), jnp.bfloat16)


def update_kernel(table_ref, agg_ref, w_scal_ref, w_vec_ref, w_ten_ref, out_ref, block_ref):
    block_diagonal(block_ref, w_scal_ref, w_vec_ref, w_ten_ref)
    out_ref[...] = (
        table_ref[:FEAT].astype(jnp.float32) + dot(block_ref[...], agg_ref[...])
    ).astype(jnp.bfloat16)


def sum_kernel(parts_ref, out_ref):
    total = parts_ref[0].astype(jnp.float32)
    for peer in range(1, parts_ref.shape[0]):
        total = total + parts_ref[peer].astype(jnp.float32)
    total = total.astype(jnp.bfloat16)
    for peer in range(out_ref.shape[0]):
        out_ref[peer] = total


def unpack_kernel(blocks_ref, one_ref, bias_ref, dist_ref, two_ref, scal_ref, vec_ref, ten_ref):
    height = blocks_ref.shape[1]

    def rows_of(block):
        peer, row = divmod(block * 16, height)
        return blocks_ref[peer, row : row + 16].astype(jnp.float32)

    for block in range(HID // 16):
        one_ref[block * 16 : (block + 1) * 16] = rows_of(block)
    for block in range(GATES // 16):
        two_ref[block * 16 : (block + 1) * 16] = rows_of(HID // 16 + block)
    low = (HID + GATES) // 16
    for block in range(CS // 16):
        rows = rows_of(low + block)
        scal_ref[block * 16 : (block + 1) * 16] = rows[:, :CS]
        if block < CV // 16:
            vec_ref[block * 16 : (block + 1) * 16] = rows[:, CS : CS + CV]
        if block == 0:
            ten_ref[...] = rows[:, CS + CV : CS + CV + CT]
    extra = rows_of(low + CS // 16)
    bias_ref[...] = extra[0:1]
    dist_ref[...] = extra[1:2]


def call(kernel, out_shape, scratch=(), in_specs=None, out_specs=None, cost_estimate=None):
    specs = {}
    if cost_estimate is not None:
        specs["cost_estimate"] = cost_estimate
    if in_specs is not None:
        specs["in_specs"] = in_specs
    if out_specs is not None:
        specs["out_specs"] = out_specs
    return pl.pallas_call(
        kernel,
        out_shape=out_shape,
        scratch_shapes=list(scratch),
        compiler_params=pltpu.CompilerParams(vmem_limit_bytes=VMEM_BYTES),
        **specs,
    )


IN_VMEM = pl.BlockSpec(memory_space=pltpu.VMEM)
IN_HBM = pl.BlockSpec(memory_space=pltpu.HBM)
ANYWHERE = pl.BlockSpec(memory_space=pl.ANY)


def exchange(blocks, axes=("dom", "sub")):
    return lax.all_to_all(blocks, axes, split_axis=0, concat_axis=0, tiled=True)


def in_hbm(*arrays):
    return tuple(pltpu.with_memory_space_constraint(array, pltpu.HBM) for array in arrays)


def shaped(shape, dtype):
    return jax.ShapeDtypeStruct(shape, dtype)


def from_behind(shard, axis, by):
    peers = lax.axis_size(axis)
    return lax.ppermute(shard, axis, [(i, (i + by) % peers) for i in range(peers)])


def on_device(
    node_feat,
    node_pos,
    node_cot,
    mesh_senders,
    edge_mask,
    halo_up,
    halo_down,
    contact_rows,
    contact_dst,
    contact_mask,
    w_one,
    b_one,
    w_dist,
    w_two,
    w_scal,
    w_vec,
    w_ten,
):
    f32, bf16 = jnp.float32, jnp.bfloat16
    node_count = node_feat.shape[1]
    contact_count = contact_rows.shape[0]
    device_count = lax.axis_size("dom") * lax.axis_size("sub")
    slot = contact_count // device_count
    chunks = contact_count // CHUNK
    grad_scale = 1.0 / math.sqrt(device_count * node_count * DEGREE)
    table, requests = call(
        table_kernel,
        (
            shaped((ROWS, node_count), bf16),
            shaped((device_count, 1, slot), jnp.int32),
        ),
        (
            pltpu.VMEM((3, node_count), bf16),
            pltpu.VMEM((1, node_count), jnp.int32),
            pltpu.VMEM((1, node_count), jnp.int32),
            pltpu.VMEM((contact_count // LANES, LANES), jnp.int32),
            pltpu.SemaphoreType.DMA((5,)),
        ),
        in_specs=[IN_HBM] * 5,
        out_specs=(IN_VMEM, IN_VMEM),
    )(
        *in_hbm(
            node_feat,
            node_pos,
            halo_up[None],
            halo_down[None],
            contact_rows.reshape(contact_count // LANES, LANES),
        )
    )
    wanted = exchange(requests)
    wanted, table_late = lax.optimization_barrier((wanted, table))
    low = from_behind(table_late, "sub", 1)
    high = from_behind(table_late, "sub", -1)
    half = slot // 2
    height = -(-ROWS // (LANES // half * 16)) * 16
    near, far = (
        call(
            functools.partial(contact_gather_kernel, first, half),
            shaped((device_count, height, LANES), bf16),
            in_specs=[IN_VMEM, IN_VMEM],
            out_specs=IN_VMEM,
        )(table, wanted)
        for first in (0, half)
    )
    near, mesh_senders, edge_mask, contact_dst, contact_mask, b_one, w_dist = (
        lax.optimization_barrier(
            (near, mesh_senders, edge_mask, contact_dst, contact_mask, b_one, w_dist)
        )
    )
    near = exchange(near)
    far = exchange(far)
    mesh_code = (
        jnp.where(edge_mask != 0, mesh_senders, -1)
        .reshape(node_count, DEGREE)
        .T.reshape(DEGREE, 1, node_count)
    )
    contact_code = (
        jnp.where(contact_mask != 0, contact_dst, -1)
        .reshape(device_count, 2, half)
        .transpose(1, 0, 2)
        .reshape(chunks, 1, CHUNK)
    )
    b_column = b_one[:, None]
    dist_column = w_dist[:, None]
    mesh_rows = HID + GATES + 16
    recv_rows = FEAT + 16 + CS
    mesh_agg, mesh_grads, recv = call(
        mesh_kernel,
        (
            pltpu.HBM((FEAT, node_count), f32),
            pltpu.HBM((mesh_rows, LANES), f32),
            pltpu.HBM((chunks, recv_rows, CHUNK), bf16),
        ),
        (
            pltpu.VMEM((FEAT, node_count), f32),
            pltpu.VMEM((mesh_rows, LANES), f32),
            pltpu.VMEM((chunks, recv_rows, CHUNK), bf16),
            pltpu.VMEM((recv_rows, node_count), bf16),
            pltpu.VMEM((ROWS, 3 * node_count), bf16),
            pltpu.VMEM((FEAT, FEAT), bf16),
            pltpu.SemaphoreType.DMA((3,)),
        ),
        in_specs=[IN_VMEM] * 13,
        out_specs=(IN_HBM, IN_HBM, IN_HBM),
        cost_estimate=pl.CostEstimate(
            flops=40_000_000_000, bytes_accessed=8_000_000, transcendentals=400_000
        ),
    )(
        table,
        low,
        high,
        mesh_code,
        node_cot,
        w_one,
        b_column,
        dist_column,
        w_two,
        w_scal,
        w_vec,
        w_ten,
        contact_code,
    )
    packed_rows = mesh_rows + CS
    contact_scratch = (
        pltpu.VMEM((chunks, 1, CHUNK), jnp.int32),
        pltpu.VMEM((chunks // 2, recv_rows, CHUNK), bf16),
        pltpu.VMEM((FEAT, node_count), f32),
        pltpu.VMEM((mesh_rows, LANES), f32),
        pltpu.VMEM((HID, 2 * CS), bf16),
        pltpu.VMEM((GATES, HID), bf16),
        pltpu.SemaphoreType.DMA((chunks // 2 + 5,)),
    )
    near_agg, near_grads = call(
        near_contact_kernel,
        (pltpu.HBM((FEAT, node_count), f32), pltpu.HBM((mesh_rows, LANES), f32)),
        contact_scratch,
        in_specs=[IN_VMEM] * 3 + [IN_HBM] * 6,
        out_specs=(IN_HBM, IN_HBM),
    )(
        near,
        b_column,
        dist_column,
        *in_hbm(contact_code, recv, mesh_agg, mesh_grads, w_one, w_two),
    )
    agg_rows, packed = call(
        functools.partial(far_contact_kernel, grad_scale, chunks // 2),
        (shaped((FEAT, node_count), bf16), shaped((device_count, 16, LANES), bf16)),
        contact_scratch + (pltpu.VMEM((packed_rows, LANES), f32),),
        in_specs=[IN_VMEM] * 4 + [IN_HBM] * 6,
        out_specs=(IN_VMEM, IN_VMEM),
    )(
        node_cot,
        far,
        b_column,
        dist_column,
        *in_hbm(contact_code, recv, near_agg, near_grads, w_one, w_two),
    )
    node_out = call(
        update_kernel,
        shaped((FEAT, node_count), bf16),
        (pltpu.VMEM((FEAT, FEAT), bf16),),
    )(table, agg_rows, w_scal, w_vec, w_ten)
    shares = call(sum_kernel, shaped((device_count, 16, LANES), bf16))(exchange(packed))
    one, bias, dist, two, scal, vec, ten = call(
        unpack_kernel,
        (
            shaped((HID, 2 * CS), f32),
            shaped((1, HID), f32),
            shaped((1, HID), f32),
            shaped((GATES, HID), f32),
            shaped((CS, CS), f32),
            shaped((CV, CV), f32),
            shaped((CT, CT), f32),
        ),
    )(exchange(shares))
    return node_out, one, bias[0], dist[0], two, scal, vec, ten


def solution(mesh):
    along = P(("dom", "sub"))
    columns = P(None, ("dom", "sub"))
    in_specs = (columns,) * 3 + (along,) * 7 + (P(),) * 7
    out_specs = (columns,) + (P(),) * 7
    return jax.shard_map(
        on_device, mesh=mesh, in_specs=in_specs, out_specs=out_specs, check_vma=False
    )
```

```python
import functools
import math

import jax
import jax.numpy as jnp
from jax import lax
from jax.experimental import pallas as pl
from jax.experimental.pallas import tpu as pltpu
from jax.sharding import PartitionSpec as P

CS = 64
CV = 32
CT = 16
HID = 128
DEGREE = 6
GATES = 144
FEAT = CS + 3 * CV + 9 * CT
ROWS = 320
LANES = 128
CHUNK = 512
VMEM_BYTES = 48 * 1024 * 1024


def dot(lhs, rhs, lhs_dim=1, rhs_dim=0):
    return lax.dot_general(
        lhs, rhs, (((lhs_dim,), (rhs_dim,)), ((), ())), preferred_element_type=jnp.float32
    )


def one_hot(code, width):
    rows = lax.broadcasted_iota(jnp.int32, (width, code.shape[1]), 0)
    return jnp.where(rows == code, 1.0, 0.0).astype(jnp.bfloat16)


def join_index(table, row):
    pair = table[row : row + 2].astype(jnp.float32)
    return (pair[0:1] * 128.0 + pair[1:2]).astype(jnp.int32)


def table_kernel(
    feat_ref,
    pos_ref,
    up_ref,
    down_ref,
    rows_ref,
    table_ref,
    request_ref,
    pos_scr,
    up_scr,
    down_scr,
    rows_scr,
    sems,
):
    node_count = table_ref.shape[1]
    copies = [
        pltpu.make_async_copy(rows_ref, rows_scr, sems.at[0]),
        pltpu.make_async_copy(feat_ref, table_ref.at[:FEAT], sems.at[1]),
        pltpu.make_async_copy(pos_ref, pos_scr, sems.at[2]),
        pltpu.make_async_copy(up_ref, up_scr, sems.at[3]),
        pltpu.make_async_copy(down_ref, down_scr, sems.at[4]),
    ]
    for copy in copies:
        copy.start()
    copies[0].wait()
    slot = request_ref.shape[2]
    parts = LANES // slot
    for row in range(rows_scr.shape[0]):
        line = rows_scr[row : row + 1]
        for part in range(parts):
            request_ref[row * parts + part] = line[:, part * slot : (part + 1) * slot]
    for copy in copies[2:]:
        copy.wait()
    rows = lax.broadcasted_iota(jnp.int32, (ROWS - FEAT, node_count), 0)
    pos = pos_scr[...].astype(jnp.float32)
    tail = jnp.zeros((ROWS - FEAT, node_count), jnp.float32)
    for k in range(3):
        tail = jnp.where(rows == k, pos[k : k + 1], tail)
    for k, index_ref in ((3, up_scr), (5, down_scr)):
        index = index_ref[...]
        high = index >> 7
        tail = jnp.where(rows == k, high.astype(jnp.float32), tail)
        tail = jnp.where(rows == k + 1, (index - (high << 7)).astype(jnp.float32), tail)
    table_ref[FEAT:] = tail.astype(jnp.bfloat16)
    copies[1].wait()


def contact_gather_kernel(slot, table_ref, wanted_ref, out_ref):
    node_count = table_ref.shape[1]
    parts = LANES // slot
    height = out_ref.shape[1]
    per_chunk = CHUNK // slot
    for chunk in range(wanted_ref.shape[0] // per_chunk):
        wanted = [wanted_ref[chunk * per_chunk + peer] for peer in range(per_chunk)]
        hot = one_hot(jnp.concatenate(wanted, 1), node_count)
        rows = dot(table_ref[...], hot).astype(jnp.bfloat16)
        if parts * height > ROWS:
            rows = jnp.concatenate(
                [rows, jnp.zeros((parts * height - ROWS, CHUNK), jnp.bfloat16)], 0
            )
        for peer in range(per_chunk):
            out_ref[chunk * per_chunk + peer] = jnp.concatenate(
                [
                    rows[part * height : (part + 1) * height, peer * slot : (peer + 1) * slot]
                    for part in range(parts)
                ],
                1,
            )


def edge_math(src, base, first, inputs, pos_recv, back, live, weights):
    w_dist, w_two, w_two_t = weights
    edges = src.shape[1]
    offset = src[FEAT : FEAT + 3] - pos_recv
    if live is not None:
        offset = offset * live
    distance = jnp.sum(offset * offset, 0, keepdims=True)
    linear = base + first + w_dist * distance
    squashed = 0.5 * jnp.tanh(0.5 * linear) + 0.5
    hidden = (linear * squashed).astype(jnp.bfloat16)
    gates = dot(w_two, hidden)
    gate_vec = gates[CS : CS + CV]
    gate_dir = gates[CS + CV : CS + 2 * CV]
    gate_ten = gates[CS + 2 * CV :]
    message = [gates[:CS] * src[:CS]]
    vec_part = jnp.zeros((CV, edges), jnp.float32)
    dir_part = jnp.zeros((CV, edges), jnp.float32)
    for k in range(3):
        rows = slice(CS + k * CV, CS + (k + 1) * CV)
        message.append(gate_vec * src[rows] + gate_dir * offset[k : k + 1])
        vec_part = vec_part + back[rows] * src[rows]
        dir_part = dir_part + back[rows] * offset[k : k + 1]
    ten_part = jnp.zeros((CT, edges), jnp.float32)
    for m in range(9):
        rows = slice(CS + 3 * CV + m * CT, CS + 3 * CV + (m + 1) * CT)
        message.append(gate_ten * src[rows])
        ten_part = ten_part + back[rows] * src[rows]
    message = jnp.concatenate(message, 0)
    dgates = jnp.concatenate([back[:CS] * src[:CS], vec_part, dir_part, ten_part], 0).astype(
        jnp.bfloat16
    )
    hidden_grad = dot(w_two_t, dgates)
    linear_grad = (hidden_grad * squashed * (1.0 + linear * (1.0 - squashed))).astype(jnp.bfloat16)
    rows = lax.broadcasted_iota(jnp.int32, (16, edges), 0)
    coarse = distance.astype(jnp.bfloat16).astype(jnp.float32)
    extra = jnp.where(
        rows == 0, 1.0, jnp.where(rows == 1, coarse, jnp.where(rows == 2, distance - coarse, 0.0))
    ).astype(jnp.bfloat16)
    grads = (
        dot(linear_grad, inputs, 1, 1),
        dot(dgates, hidden, 1, 1),
        dot(extra, linear_grad, 1, 1),
    )
    return message, grads


def as_columns(first_row, second_row):
    rows = lax.broadcasted_iota(jnp.int32, (LANES, LANES), 0)
    columns = jnp.where(rows == 0, first_row, jnp.where(rows == 1, second_row, 0.0)).T
    return columns[:, 0:1], columns[:, 1:2]


def add_grads(grads_ref, grads):
    grads_ref[:HID] += grads[0]
    grads_ref[HID : HID + GATES] += grads[1]
    grads_ref[HID + GATES : HID + GATES + 16] += grads[2]


def block_diagonal(block_ref, w_scal, w_vec, w_ten):
    block_ref[...] = jnp.zeros_like(block_ref)
    block_ref[:CS, :CS] = w_scal[...]
    for k in range(3):
        rows = slice(CS + k * CV, CS + (k + 1) * CV)
        block_ref[rows, rows] = w_vec[...]
    for m in range(9):
        rows = slice(CS + 3 * CV + m * CT, CS + 3 * CV + (m + 1) * CT)
        block_ref[rows, rows] = w_ten[...]


def mesh_kernel(
    table_ref,
    low_ref,
    high_ref,
    code_ref,
    cot_ref,
    w_one_ref,
    b_one_ref,
    w_dist_ref,
    w_two_ref,
    w_scal_ref,
    w_vec_ref,
    w_ten_ref,
    dst_ref,
    mask_ref,
    agg_out_ref,
    grads_out_ref,
    recv_out_ref,
    code_out_ref,
    agg_ref,
    grads_ref,
    recv_ref,
    receive_ref,
    source_ref,
    block_ref,
    contact_ref,
    sems,
):
    node_count = table_ref.shape[1]
    source_ref[:, :node_count] = table_ref[...]
    low = low_ref[...]
    high = high_ref[...]
    source_ref[:, node_count : 2 * node_count] = dot(
        low, one_hot(join_index(low, FEAT + 3), node_count)
    ).astype(jnp.bfloat16)
    source_ref[:, 2 * node_count :] = dot(
        high, one_hot(join_index(high, FEAT + 5), node_count)
    ).astype(jnp.bfloat16)
    block_diagonal(block_ref, w_scal_ref, w_vec_ref, w_ten_ref)
    receive_ref[:FEAT] = dot(block_ref[...], cot_ref[...], 0, 0).astype(jnp.bfloat16)
    receive_ref[FEAT : FEAT + 16] = table_ref[FEAT:]
    receive_ref[FEAT + 16 :] = table_ref[:CS]
    w_one = w_one_ref[...]
    w_two = w_two_ref[...]
    b_column, dist_column = as_columns(b_one_ref[...], w_dist_ref[...])
    scal_recv = table_ref[:CS]
    recv_linear = dot(w_one[:, :CS], scal_recv) + b_column
    weights = (dist_column, w_two, w_two.T)
    pos_recv = table_ref[FEAT:].astype(jnp.float32)[:3]
    grads_ref[...] = jnp.zeros_like(grads_ref)
    agg_ref[...] = jnp.zeros_like(agg_ref)
    for step in range(DEGREE):
        code = code_ref[step]
        src = dot(source_ref[...], one_hot(code, 3 * node_count))
        live = jnp.where(code >= 0, 1.0, 0.0)
        back = receive_ref[:FEAT].astype(jnp.float32)
        scal_send = src[:CS].astype(jnp.bfloat16)
        inputs = jnp.concatenate([scal_recv, scal_send], 0)
        message, grads = edge_math(
            src, recv_linear, dot(w_one[:, CS:], scal_send), inputs, pos_recv, back, live, weights
        )
        agg_ref[...] += message
        add_grads(grads_ref, grads)
    contact_ref[...] = jnp.where(mask_ref[...] != 0, dst_ref[...], -1)
    for chunk in range(contact_ref.shape[0]):
        recv_ref[chunk] = dot(
            receive_ref[...], one_hot(contact_ref[chunk], node_count)
        ).astype(jnp.bfloat16)
    copies = [
        pltpu.make_async_copy(agg_ref, agg_out_ref, sems.at[0]),
        pltpu.make_async_copy(grads_ref, grads_out_ref, sems.at[1]),
        pltpu.make_async_copy(recv_ref, recv_out_ref, sems.at[2]),
        pltpu.make_async_copy(contact_ref, code_out_ref, sems.at[3]),
    ]
    for copy in copies:
        copy.start()
    for copy in copies:
        copy.wait()


def contact_kernel(
    slot,
    grad_scale,
    reply_ref,
    cot_ref,
    code_hbm,
    recv_hbm,
    mesh_agg_hbm,
    mesh_grads_hbm,
    w_one_hbm,
    w_two_hbm,
    b_one_hbm,
    w_dist_hbm,
    agg_out_ref,
    packed_ref,
    code_ref,
    recv_ref,
    agg_ref,
    grads_ref,
    w_one_ref,
    w_two_ref,
    b_one_ref,
    w_dist_ref,
    packed_scr,
    sems,
):
    chunks = code_ref.shape[0]
    sources = [
        (b_one_hbm, b_one_ref),
        (w_dist_hbm, w_dist_ref),
        (w_one_hbm, w_one_ref),
        (w_two_hbm, w_two_ref),
        (code_hbm, code_ref),
    ]
    sources += [(recv_hbm.at[chunk], recv_ref.at[chunk]) for chunk in range(chunks)]
    sources += [(mesh_agg_hbm, agg_ref), (mesh_grads_hbm, grads_ref)]
    copies = [
        pltpu.make_async_copy(source, target, sems.at[at])
        for at, (source, target) in enumerate(sources)
    ]
    for copy in copies:
        copy.start()
    node_count = cot_ref.shape[1]
    parts = LANES // slot
    per_chunk = CHUNK // slot
    for copy in copies[:6]:
        copy.wait()
    w_one = w_one_ref[...]
    w_two = w_two_ref[...]
    b_column, dist_column = as_columns(b_one_ref[...], w_dist_ref[...])
    weights = (dist_column, w_two, w_two.T)
    for chunk in range(chunks):
        blocks = [reply_ref[chunk * per_chunk + peer] for peer in range(per_chunk)]
        src_rows = jnp.concatenate(
            [
                jnp.concatenate(
                    [block[:, part * slot : (part + 1) * slot] for block in blocks], 1
                )
                for part in range(parts)
            ],
            0,
        )[:ROWS]
        if chunk == 1:
            for copy in copies[6:]:
                copy.wait()
        recv = recv_ref[chunk]
        inputs = jnp.concatenate([recv[FEAT + 16 :], src_rows[:CS]], 0)
        message, grads = edge_math(
            src_rows.astype(jnp.float32),
            b_column,
            dot(w_one, inputs),
            inputs,
            recv[FEAT : FEAT + 16].astype(jnp.float32)[:3],
            recv[:FEAT].astype(jnp.float32),
            None,
            weights,
        )
        scattered = dot(message.astype(jnp.bfloat16), one_hot(code_ref[chunk], node_count), 1, 1)
        if chunk == 0:
            held = (scattered, grads)
            continue
        agg_ref[...] += scattered
        add_grads(grads_ref, grads)
        if chunk == 1:
            agg_ref[...] += held[0]
            add_grads(grads_ref, held[1])
    agg_rows = agg_ref[...].astype(jnp.bfloat16)
    agg_out_ref[...] = agg_rows
    cot = cot_ref[...]
    low = HID + GATES
    packed_scr[:low] = grads_ref[:low] * grad_scale
    packed_scr[low : low + CS] = jnp.concatenate(
        [
            dot(cot[:CS], agg_rows[:CS], 1, 1) * grad_scale,
            jnp.zeros((CS, LANES - CS), jnp.float32),
        ],
        1,
    )
    grad_vec = jnp.zeros((CV, CV), jnp.float32)
    for k in range(3):
        rows = slice(CS + k * CV, CS + (k + 1) * CV)
        grad_vec = grad_vec + dot(cot[rows], agg_rows[rows], 1, 1)
    packed_scr[low : low + CV, CS : CS + CV] = grad_vec * grad_scale
    grad_ten = jnp.zeros((CT, CT), jnp.float32)
    for m in range(9):
        rows = slice(CS + 3 * CV + m * CT, CS + 3 * CV + (m + 1) * CT)
        grad_ten = grad_ten + dot(cot[rows], agg_rows[rows], 1, 1)
    packed_scr[low : low + CT, CS + CV : CS + CV + CT] = grad_ten * grad_scale
    extra = grads_ref[low:] * grad_scale
    rows = lax.broadcasted_iota(jnp.int32, (16, LANES), 0)
    packed_scr[low + CS :] = jnp.where(rows == 1, extra[1:2] + extra[2:3], extra)
    packed = packed_scr[...].astype(jnp.bfloat16)
    height = packed_ref.shape[1]
    for peer in range(packed_ref.shape[0]):
        for row in range(0, height, 16):
            at = peer * height + row
            if at < packed.shape[0]:
                packed_ref[peer, row : row + 16] = packed[at : at + 16]
            else:
                packed_ref[peer, row : row + 16] = jnp.zeros((16, LANES), jnp.bfloat16)


def sum_kernel(parts_ref, out_ref):
    total = parts_ref[0].astype(jnp.float32)
    for peer in range(1, parts_ref.shape[0]):
        total = total + parts_ref[peer].astype(jnp.float32)
    total = total.astype(jnp.bfloat16)
    for peer in range(out_ref.shape[0]):
        out_ref[peer] = total


def finish_kernel(
    blocks_ref,
    table_ref,
    agg_ref,
    w_scal_ref,
    w_vec_ref,
    w_ten_ref,
    out_ref,
    one_ref,
    bias_ref,
    dist_ref,
    two_ref,
    scal_ref,
    vec_ref,
    ten_ref,
    block_ref,
):
    height = blocks_ref.shape[1]
    block_diagonal(block_ref, w_scal_ref, w_vec_ref, w_ten_ref)
    out_ref[...] = (
        table_ref[:FEAT].astype(jnp.float32) + dot(block_ref[...], agg_ref[...])
    ).astype(jnp.bfloat16)

    def rows_of(block):
        peer, row = divmod(block * 16, height)
        return blocks_ref[peer, row : row + 16].astype(jnp.float32)

    for block in range(HID // 16):
        one_ref[block * 16 : (block + 1) * 16] = rows_of(block)
    for block in range(GATES // 16):
        two_ref[block * 16 : (block + 1) * 16] = rows_of(HID // 16 + block)
    low = (HID + GATES) // 16
    for block in range(CS // 16):
        rows = rows_of(low + block)
        scal_ref[block * 16 : (block + 1) * 16] = rows[:, :CS]
        if block < CV // 16:
            vec_ref[block * 16 : (block + 1) * 16] = rows[:, CS : CS + CV]
        if block == 0:
            ten_ref[...] = rows[:, CS + CV : CS + CV + CT]
    extra = rows_of(low + CS // 16)
    bias_ref[...] = extra[0:1]
    dist_ref[...] = extra[1:2]


def call(kernel, out_shape, scratch=(), in_specs=None, out_specs=None, cost_estimate=None):
    specs = {}
    if cost_estimate is not None:
        specs["cost_estimate"] = cost_estimate
    if in_specs is not None:
        specs["in_specs"] = in_specs
    if out_specs is not None:
        specs["out_specs"] = out_specs
    return pl.pallas_call(
        kernel,
        out_shape=out_shape,
        scratch_shapes=list(scratch),
        compiler_params=pltpu.CompilerParams(vmem_limit_bytes=VMEM_BYTES),
        **specs,
    )


IN_VMEM = pl.BlockSpec(memory_space=pltpu.VMEM)
IN_HBM = pl.BlockSpec(memory_space=pltpu.HBM)
ANYWHERE = pl.BlockSpec(memory_space=pl.ANY)


def exchange(blocks, axes=("dom", "sub")):
    return lax.all_to_all(blocks, axes, split_axis=0, concat_axis=0, tiled=True)


def in_hbm(*arrays):
    return tuple(pltpu.with_memory_space_constraint(array, pltpu.HBM) for array in arrays)


def shaped(shape, dtype):
    return jax.ShapeDtypeStruct(shape, dtype)


def from_behind(shard, axis, by):
    peers = lax.axis_size(axis)
    return lax.ppermute(shard, axis, [(i, (i + by) % peers) for i in range(peers)])


def on_device(
    node_feat,
    node_pos,
    node_cot,
    mesh_senders,
    edge_mask,
    halo_up,
    halo_down,
    contact_rows,
    contact_dst,
    contact_mask,
    w_one,
    b_one,
    w_dist,
    w_two,
    w_scal,
    w_vec,
    w_ten,
):
    f32, bf16 = jnp.float32, jnp.bfloat16
    node_count = node_feat.shape[1]
    contact_count = contact_rows.shape[0]
    device_count = lax.axis_size("dom") * lax.axis_size("sub")
    slot = contact_count // device_count
    chunks = contact_count // CHUNK
    parts = LANES // slot
    height = -(-ROWS // (parts * 16)) * 16
    grad_scale = 1.0 / math.sqrt(device_count * node_count * DEGREE)
    table, requests = call(
        table_kernel,
        (
            shaped((ROWS, node_count), bf16),
            shaped((device_count, 1, slot), jnp.int32),
        ),
        (
            pltpu.VMEM((3, node_count), bf16),
            pltpu.VMEM((1, node_count), jnp.int32),
            pltpu.VMEM((1, node_count), jnp.int32),
            pltpu.VMEM((contact_count // LANES, LANES), jnp.int32),
            pltpu.SemaphoreType.DMA((5,)),
        ),
        in_specs=[IN_HBM] * 5,
        out_specs=(IN_VMEM, IN_VMEM),
    )(
        *in_hbm(
            node_feat,
            node_pos,
            halo_up[None],
            halo_down[None],
            contact_rows.reshape(contact_count // LANES, LANES),
        )
    )
    wanted = exchange(requests)
    wanted, table_late = lax.optimization_barrier((wanted, table))
    low = from_behind(table_late, "sub", 1)
    high = from_behind(table_late, "sub", -1)
    found = call(
        functools.partial(contact_gather_kernel, slot),
        shaped((device_count, height, LANES), bf16),
        in_specs=[IN_VMEM, IN_VMEM],
        out_specs=IN_VMEM,
    )(table, wanted)
    found, mesh_senders, edge_mask = lax.optimization_barrier((found, mesh_senders, edge_mask))
    replies = exchange(found)
    mesh_code = (
        jnp.where(edge_mask != 0, mesh_senders, -1)
        .reshape(node_count, DEGREE)
        .T.reshape(DEGREE, 1, node_count)
    )
    contact_dst = contact_dst.reshape(chunks, 1, CHUNK)
    contact_mask = contact_mask.reshape(chunks, 1, CHUNK)
    mesh_rows = HID + GATES + 16
    recv_rows = FEAT + 16 + CS
    mesh_agg, mesh_grads, recv, contact_code = call(
        mesh_kernel,
        (
            pltpu.HBM((FEAT, node_count), f32),
            pltpu.HBM((mesh_rows, LANES), f32),
            pltpu.HBM((chunks, recv_rows, CHUNK), bf16),
            pltpu.HBM((chunks, 1, CHUNK), jnp.int32),
        ),
        (
            pltpu.VMEM((FEAT, node_count), f32),
            pltpu.VMEM((mesh_rows, LANES), f32),
            pltpu.VMEM((chunks, recv_rows, CHUNK), bf16),
            pltpu.VMEM((recv_rows, node_count), bf16),
            pltpu.VMEM((ROWS, 3 * node_count), bf16),
            pltpu.VMEM((FEAT, FEAT), bf16),
            pltpu.VMEM((chunks, 1, CHUNK), jnp.int32),
            pltpu.SemaphoreType.DMA((4,)),
        ),
        in_specs=[IN_VMEM] * 14,
        out_specs=(IN_HBM,) * 4,
        cost_estimate=pl.CostEstimate(
            flops=40_000_000_000, bytes_accessed=8_000_000, transcendentals=400_000
        ),
    )(
        table,
        low,
        high,
        mesh_code,
        node_cot,
        w_one,
        b_one[None],
        w_dist[None],
        w_two,
        w_scal,
        w_vec,
        w_ten,
        contact_dst,
        contact_mask,
    )
    packed_rows = mesh_rows + CS
    agg_rows, packed = call(
        functools.partial(contact_kernel, slot, grad_scale),
        (shaped((FEAT, node_count), bf16), shaped((device_count, 16, LANES), bf16)),
        (
            pltpu.VMEM((chunks, 1, CHUNK), jnp.int32),
            pltpu.VMEM((chunks, recv_rows, CHUNK), bf16),
            pltpu.VMEM((FEAT, node_count), f32),
            pltpu.VMEM((mesh_rows, LANES), f32),
            pltpu.VMEM((HID, 2 * CS), bf16),
            pltpu.VMEM((GATES, HID), bf16),
            pltpu.VMEM((1, HID), f32),
            pltpu.VMEM((1, HID), f32),
            pltpu.VMEM((packed_rows, LANES), f32),
            pltpu.SemaphoreType.DMA((chunks + 7,)),
        ),
        in_specs=[IN_VMEM] * 2 + [IN_HBM] * 8,
        out_specs=(IN_VMEM, IN_VMEM),
    )(
        replies,
        node_cot,
        *in_hbm(
            contact_code, recv, mesh_agg, mesh_grads, w_one, w_two, b_one[None], w_dist[None]
        ),
    )
    shares = call(sum_kernel, shaped((device_count, 16, LANES), bf16))(exchange(packed))
    node_out, one, bias, dist, two, scal, vec, ten = call(
        finish_kernel,
        (
            shaped((FEAT, node_count), bf16),
            shaped((HID, 2 * CS), f32),
            shaped((1, HID), f32),
            shaped((1, HID), f32),
            shaped((GATES, HID), f32),
            shaped((CS, CS), f32),
            shaped((CV, CV), f32),
            shaped((CT, CT), f32),
        ),
        (pltpu.VMEM((FEAT, FEAT), bf16),),
    )(exchange(shares), table, agg_rows, w_scal, w_vec, w_ten)
    return node_out, one, bias[0], dist[0], two, scal, vec, ten


def solution(mesh):
    along = P(("dom", "sub"))
    columns = P(None, ("dom", "sub"))
    in_specs = (columns,) * 3 + (along,) * 7 + (P(),) * 7
    out_specs = (columns,) + (P(),) * 7
    return jax.shard_map(
        on_device, mesh=mesh, in_specs=in_specs, out_specs=out_specs, check_vma=False
    )
```

```python
import functools
import math

import jax
import jax.numpy as jnp
from jax import lax
from jax.experimental import pallas as pl
from jax.experimental.pallas import tpu as pltpu
from jax.sharding import PartitionSpec as P

CS = 64
CV = 32
CT = 16
HID = 128
DEGREE = 6
GATES = 144
FEAT = CS + 3 * CV + 9 * CT
ROWS = 320
LANES = 128
CHUNK = 512
VMEM_BYTES = 48 * 1024 * 1024


def dot(lhs, rhs, lhs_dim=1, rhs_dim=0):
    return lax.dot_general(
        lhs, rhs, (((lhs_dim,), (rhs_dim,)), ((), ())), preferred_element_type=jnp.float32
    )


def one_hot(code, width):
    rows = lax.broadcasted_iota(jnp.int16, (width, code.shape[1]), 0)
    return jnp.where(rows == code.astype(jnp.int16), jnp.bfloat16(1), jnp.bfloat16(0))


def join_index(table, row):
    pair = table[row : row + 2].astype(jnp.float32)
    return (pair[0:1] * 128.0 + pair[1:2]).astype(jnp.int32)


def table_kernel(
    feat_ref,
    pos_ref,
    up_ref,
    down_ref,
    rows_ref,
    table_ref,
    request_ref,
    pos_scr,
    up_scr,
    down_scr,
    rows_scr,
    sems,
):
    node_count = table_ref.shape[1]
    copies = [
        pltpu.make_async_copy(rows_ref, rows_scr, sems.at[0]),
        pltpu.make_async_copy(feat_ref, table_ref.at[:FEAT], sems.at[1]),
        pltpu.make_async_copy(pos_ref, pos_scr, sems.at[2]),
        pltpu.make_async_copy(up_ref, up_scr, sems.at[3]),
        pltpu.make_async_copy(down_ref, down_scr, sems.at[4]),
    ]
    for copy in copies:
        copy.start()
    copies[0].wait()
    slot = request_ref.shape[2]
    parts = LANES // slot
    for row in range(rows_scr.shape[0]):
        line = rows_scr[row : row + 1]
        for part in range(parts):
            request_ref[row * parts + part] = line[:, part * slot : (part + 1) * slot]
    for copy in copies[2:]:
        copy.wait()
    rows = lax.broadcasted_iota(jnp.int32, (ROWS - FEAT, node_count), 0)
    pos = pos_scr[...].astype(jnp.float32)
    tail = jnp.zeros((ROWS - FEAT, node_count), jnp.float32)
    for k in range(3):
        tail = jnp.where(rows == k, pos[k : k + 1], tail)
    for k, index_ref in ((3, up_scr), (5, down_scr)):
        index = index_ref[...]
        high = index >> 7
        tail = jnp.where(rows == k, high.astype(jnp.float32), tail)
        tail = jnp.where(rows == k + 1, (index - (high << 7)).astype(jnp.float32), tail)
    table_ref[FEAT:] = tail.astype(jnp.bfloat16)
    copies[1].wait()


def contact_gather_kernel(slot, table_ref, wanted_ref, out_hbm, out_ref, sems):
    node_count = table_ref.shape[1]
    parts = LANES // slot
    height = out_ref.shape[1]
    per_chunk = CHUNK // slot
    copies = []
    for chunk in range(wanted_ref.shape[0] // per_chunk):
        wanted = [wanted_ref[chunk * per_chunk + peer] for peer in range(per_chunk)]
        hot = one_hot(jnp.concatenate(wanted, 1), node_count)
        rows = dot(table_ref[...], hot).astype(jnp.bfloat16)
        if parts * height > ROWS:
            rows = jnp.concatenate(
                [rows, jnp.zeros((parts * height - ROWS, CHUNK), jnp.bfloat16)], 0
            )
        for peer in range(per_chunk):
            out_ref[chunk * per_chunk + peer] = jnp.concatenate(
                [
                    rows[part * height : (part + 1) * height, peer * slot : (peer + 1) * slot]
                    for part in range(parts)
                ],
                1,
            )
        done = pl.ds(chunk * per_chunk, per_chunk)
        copies.append(
            pltpu.make_async_copy(out_ref.at[done], out_hbm.at[done], sems.at[chunk])
        )
        copies[-1].start()
    for copy in copies:
        copy.wait()


def edge_math(src, base, first, inputs, pos_recv, back, live, weights):
    w_dist, w_two, w_two_t = weights
    edges = src.shape[1]
    offset = src[FEAT : FEAT + 3] - pos_recv
    if live is not None:
        offset = offset * live
    distance = jnp.sum(offset * offset, 0, keepdims=True)
    linear = base + first + w_dist * distance
    squashed = 0.5 * jnp.tanh(0.5 * linear) + 0.5
    hidden = (linear * squashed).astype(jnp.bfloat16)
    gates = dot(w_two, hidden)
    gate_vec = gates[CS : CS + CV]
    gate_dir = gates[CS + CV : CS + 2 * CV]
    gate_ten = gates[CS + 2 * CV :]
    message = [gates[:CS] * src[:CS]]
    vec_part = jnp.zeros((CV, edges), jnp.float32)
    dir_part = jnp.zeros((CV, edges), jnp.float32)
    for k in range(3):
        rows = slice(CS + k * CV, CS + (k + 1) * CV)
        message.append(gate_vec * src[rows] + gate_dir * offset[k : k + 1])
        vec_part = vec_part + back[rows] * src[rows]
        dir_part = dir_part + back[rows] * offset[k : k + 1]
    ten_part = jnp.zeros((CT, edges), jnp.float32)
    for m in range(9):
        rows = slice(CS + 3 * CV + m * CT, CS + 3 * CV + (m + 1) * CT)
        message.append(gate_ten * src[rows])
        ten_part = ten_part + back[rows] * src[rows]
    message = jnp.concatenate(message, 0)
    dgates = jnp.concatenate([back[:CS] * src[:CS], vec_part, dir_part, ten_part], 0).astype(
        jnp.bfloat16
    )
    hidden_grad = dot(w_two_t, dgates)
    linear_grad = (hidden_grad * squashed * (1.0 + linear * (1.0 - squashed))).astype(jnp.bfloat16)
    rows = lax.broadcasted_iota(jnp.int32, (16, edges), 0)
    coarse = distance.astype(jnp.bfloat16).astype(jnp.float32)
    extra = jnp.where(
        rows == 0, 1.0, jnp.where(rows == 1, coarse, jnp.where(rows == 2, distance - coarse, 0.0))
    ).astype(jnp.bfloat16)
    grads = (
        dot(linear_grad, inputs, 1, 1),
        dot(dgates, hidden, 1, 1),
        dot(extra, linear_grad, 1, 1),
    )
    return message, grads


def as_columns(first_row, second_row):
    rows = lax.broadcasted_iota(jnp.int32, (LANES, LANES), 0)
    columns = jnp.where(rows == 0, first_row, jnp.where(rows == 1, second_row, 0.0)).T
    return columns[:, 0:1], columns[:, 1:2]


def add_grads(grads_ref, grads):
    grads_ref[:HID] += grads[0]
    grads_ref[HID : HID + GATES] += grads[1]
    grads_ref[HID + GATES : HID + GATES + 16] += grads[2]


def block_diagonal(block_ref, w_scal, w_vec, w_ten):
    block_ref[...] = jnp.zeros_like(block_ref)
    block_ref[:CS, :CS] = w_scal[...]
    for k in range(3):
        rows = slice(CS + k * CV, CS + (k + 1) * CV)
        block_ref[rows, rows] = w_vec[...]
    for m in range(9):
        rows = slice(CS + 3 * CV + m * CT, CS + 3 * CV + (m + 1) * CT)
        block_ref[rows, rows] = w_ten[...]


def mesh_kernel(
    table_ref,
    low_ref,
    high_ref,
    code_ref,
    cot_ref,
    w_one_ref,
    b_one_ref,
    w_dist_ref,
    w_two_ref,
    w_scal_ref,
    w_vec_ref,
    w_ten_ref,
    dst_ref,
    mask_ref,
    agg_out_ref,
    grads_out_ref,
    recv_out_ref,
    code_out_ref,
    agg_ref,
    grads_ref,
    recv_ref,
    receive_ref,
    source_ref,
    block_ref,
    contact_ref,
    sems,
):
    node_count = table_ref.shape[1]
    source_ref[:, :node_count] = table_ref[...]
    low = low_ref[...]
    high = high_ref[...]
    source_ref[:, node_count : 2 * node_count] = dot(
        low, one_hot(join_index(low, FEAT + 3), node_count)
    ).astype(jnp.bfloat16)
    source_ref[:, 2 * node_count :] = dot(
        high, one_hot(join_index(high, FEAT + 5), node_count)
    ).astype(jnp.bfloat16)
    block_diagonal(block_ref, w_scal_ref, w_vec_ref, w_ten_ref)
    receive_ref[:FEAT] = dot(block_ref[...], cot_ref[...], 0, 0).astype(jnp.bfloat16)
    receive_ref[FEAT : FEAT + 16] = table_ref[FEAT:]
    receive_ref[FEAT + 16 :] = table_ref[:CS]
    w_one = w_one_ref[...]
    w_two = w_two_ref[...]
    b_column, dist_column = as_columns(b_one_ref[...], w_dist_ref[...])
    scal_recv = table_ref[:CS]
    recv_linear = dot(w_one[:, :CS], scal_recv) + b_column
    weights = (dist_column, w_two, w_two.T)
    pos_recv = table_ref[FEAT:].astype(jnp.float32)[:3]
    grads_ref[...] = jnp.zeros_like(grads_ref)
    agg_ref[...] = jnp.zeros_like(agg_ref)
    for step in range(DEGREE):
        code = code_ref[step]
        src = dot(source_ref[...], one_hot(code, 3 * node_count))
        live = jnp.where(code >= 0, 1.0, 0.0)
        back = receive_ref[:FEAT].astype(jnp.float32)
        scal_send = src[:CS].astype(jnp.bfloat16)
        inputs = jnp.concatenate([scal_recv, scal_send], 0)
        message, grads = edge_math(
            src, recv_linear, dot(w_one[:, CS:], scal_send), inputs, pos_recv, back, live, weights
        )
        agg_ref[...] += message
        add_grads(grads_ref, grads)
    contact_ref[...] = jnp.where(mask_ref[...] != 0, dst_ref[...], -1)
    for chunk in range(contact_ref.shape[0]):
        recv_ref[chunk] = dot(
            receive_ref[...], one_hot(contact_ref[chunk], node_count)
        ).astype(jnp.bfloat16)
    copies = [
        pltpu.make_async_copy(agg_ref, agg_out_ref, sems.at[0]),
        pltpu.make_async_copy(grads_ref, grads_out_ref, sems.at[1]),
        pltpu.make_async_copy(recv_ref, recv_out_ref, sems.at[2]),
        pltpu.make_async_copy(contact_ref, code_out_ref, sems.at[3]),
    ]
    for copy in copies:
        copy.start()
    for copy in copies:
        copy.wait()


def contact_kernel(
    slot,
    grad_scale,
    reply_ref,
    cot_ref,
    code_hbm,
    recv_hbm,
    mesh_agg_hbm,
    mesh_grads_hbm,
    w_one_hbm,
    w_two_hbm,
    b_one_hbm,
    w_dist_hbm,
    agg_out_ref,
    packed_ref,
    code_ref,
    recv_ref,
    agg_ref,
    grads_ref,
    w_one_ref,
    w_two_ref,
    b_one_ref,
    w_dist_ref,
    packed_scr,
    sems,
):
    chunks = code_ref.shape[0]
    sources = [
        (b_one_hbm, b_one_ref),
        (w_dist_hbm, w_dist_ref),
        (w_one_hbm, w_one_ref),
        (w_two_hbm, w_two_ref),
        (code_hbm, code_ref),
    ]
    sources += [(recv_hbm.at[chunk], recv_ref.at[chunk]) for chunk in range(chunks)]
    sources += [(mesh_agg_hbm, agg_ref), (mesh_grads_hbm, grads_ref)]
    copies = [
        pltpu.make_async_copy(source, target, sems.at[at])
        for at, (source, target) in enumerate(sources)
    ]
    for copy in copies:
        copy.start()
    node_count = cot_ref.shape[1]
    parts = LANES // slot
    per_chunk = CHUNK // slot
    for copy in copies[:6]:
        copy.wait()
    w_one = w_one_ref[...]
    w_two = w_two_ref[...]
    b_column, dist_column = as_columns(b_one_ref[...], w_dist_ref[...])
    weights = (dist_column, w_two, w_two.T)
    for chunk in range(chunks):
        blocks = [reply_ref[chunk * per_chunk + peer] for peer in range(per_chunk)]
        src_rows = jnp.concatenate(
            [
                jnp.concatenate(
                    [block[:, part * slot : (part + 1) * slot] for block in blocks], 1
                )
                for part in range(parts)
            ],
            0,
        )[:ROWS]
        if chunk == 1:
            for copy in copies[6:]:
                copy.wait()
        recv = recv_ref[chunk]
        inputs = jnp.concatenate([recv[FEAT + 16 :], src_rows[:CS]], 0)
        message, grads = edge_math(
            src_rows.astype(jnp.float32),
            b_column,
            dot(w_one, inputs),
            inputs,
            recv[FEAT : FEAT + 16].astype(jnp.float32)[:3],
            recv[:FEAT].astype(jnp.float32),
            None,
            weights,
        )
        scattered = dot(message.astype(jnp.bfloat16), one_hot(code_ref[chunk], node_count), 1, 1)
        if chunk == 0:
            held = (scattered, grads)
            continue
        agg_ref[...] += scattered
        add_grads(grads_ref, grads)
        if chunk == 1:
            agg_ref[...] += held[0]
            add_grads(grads_ref, held[1])
    agg_rows = agg_ref[...].astype(jnp.bfloat16)
    agg_out_ref[...] = agg_rows
    cot = cot_ref[...]
    low = HID + GATES
    packed_scr[:low] = grads_ref[:low] * grad_scale
    packed_scr[low : low + CS] = jnp.concatenate(
        [
            dot(cot[:CS], agg_rows[:CS], 1, 1) * grad_scale,
            jnp.zeros((CS, LANES - CS), jnp.float32),
        ],
        1,
    )
    grad_vec = jnp.zeros((CV, CV), jnp.float32)
    for k in range(3):
        rows = slice(CS + k * CV, CS + (k + 1) * CV)
        grad_vec = grad_vec + dot(cot[rows], agg_rows[rows], 1, 1)
    packed_scr[low : low + CV, CS : CS + CV] = grad_vec * grad_scale
    grad_ten = jnp.zeros((CT, CT), jnp.float32)
    for m in range(9):
        rows = slice(CS + 3 * CV + m * CT, CS + 3 * CV + (m + 1) * CT)
        grad_ten = grad_ten + dot(cot[rows], agg_rows[rows], 1, 1)
    packed_scr[low : low + CT, CS + CV : CS + CV + CT] = grad_ten * grad_scale
    extra = grads_ref[low:] * grad_scale
    rows = lax.broadcasted_iota(jnp.int32, (16, LANES), 0)
    packed_scr[low + CS :] = jnp.where(rows == 1, extra[1:2] + extra[2:3], extra)
    packed = packed_scr[...].astype(jnp.bfloat16)
    height = packed_ref.shape[1]
    for peer in range(packed_ref.shape[0]):
        for row in range(0, height, 16):
            at = peer * height + row
            if at < packed.shape[0]:
                packed_ref[peer, row : row + 16] = packed[at : at + 16]
            else:
                packed_ref[peer, row : row + 16] = jnp.zeros((16, LANES), jnp.bfloat16)


def sum_kernel(parts_ref, out_ref):
    total = parts_ref[0].astype(jnp.float32)
    for peer in range(1, parts_ref.shape[0]):
        total = total + parts_ref[peer].astype(jnp.float32)
    total = total.astype(jnp.bfloat16)
    for peer in range(out_ref.shape[0]):
        out_ref[peer] = total


def finish_kernel(
    blocks_ref,
    table_ref,
    agg_ref,
    w_scal_ref,
    w_vec_ref,
    w_ten_ref,
    out_ref,
    one_ref,
    bias_ref,
    dist_ref,
    two_ref,
    scal_ref,
    vec_ref,
    ten_ref,
    block_ref,
):
    height = blocks_ref.shape[1]
    block_diagonal(block_ref, w_scal_ref, w_vec_ref, w_ten_ref)
    out_ref[...] = (
        table_ref[:FEAT].astype(jnp.float32) + dot(block_ref[...], agg_ref[...])
    ).astype(jnp.bfloat16)

    def rows_of(block):
        peer, row = divmod(block * 16, height)
        return blocks_ref[peer, row : row + 16].astype(jnp.float32)

    for block in range(HID // 16):
        one_ref[block * 16 : (block + 1) * 16] = rows_of(block)
    for block in range(GATES // 16):
        two_ref[block * 16 : (block + 1) * 16] = rows_of(HID // 16 + block)
    low = (HID + GATES) // 16
    for block in range(CS // 16):
        rows = rows_of(low + block)
        scal_ref[block * 16 : (block + 1) * 16] = rows[:, :CS]
        if block < CV // 16:
            vec_ref[block * 16 : (block + 1) * 16] = rows[:, CS : CS + CV]
        if block == 0:
            ten_ref[...] = rows[:, CS + CV : CS + CV + CT]
    extra = rows_of(low + CS // 16)
    bias_ref[...] = extra[0:1]
    dist_ref[...] = extra[1:2]


def call(kernel, out_shape, scratch=(), in_specs=None, out_specs=None, cost_estimate=None):
    specs = {}
    if cost_estimate is not None:
        specs["cost_estimate"] = cost_estimate
    if in_specs is not None:
        specs["in_specs"] = in_specs
    if out_specs is not None:
        specs["out_specs"] = out_specs
    return pl.pallas_call(
        kernel,
        out_shape=out_shape,
        scratch_shapes=list(scratch),
        compiler_params=pltpu.CompilerParams(vmem_limit_bytes=VMEM_BYTES),
        **specs,
    )


IN_VMEM = pl.BlockSpec(memory_space=pltpu.VMEM)
IN_HBM = pl.BlockSpec(memory_space=pltpu.HBM)
ANYWHERE = pl.BlockSpec(memory_space=pl.ANY)


def exchange(blocks, axes=("dom", "sub")):
    return lax.all_to_all(blocks, axes, split_axis=0, concat_axis=0, tiled=True)


def in_hbm(*arrays):
    return tuple(pltpu.with_memory_space_constraint(array, pltpu.HBM) for array in arrays)


def shaped(shape, dtype):
    return jax.ShapeDtypeStruct(shape, dtype)


def from_behind(shard, axis, by):
    peers = lax.axis_size(axis)
    return lax.ppermute(shard, axis, [(i, (i + by) % peers) for i in range(peers)])


def on_device(
    node_feat,
    node_pos,
    node_cot,
    mesh_senders,
    edge_mask,
    halo_up,
    halo_down,
    contact_rows,
    contact_dst,
    contact_mask,
    w_one,
    b_one,
    w_dist,
    w_two,
    w_scal,
    w_vec,
    w_ten,
):
    f32, bf16 = jnp.float32, jnp.bfloat16
    node_count = node_feat.shape[1]
    contact_count = contact_rows.shape[0]
    device_count = lax.axis_size("dom") * lax.axis_size("sub")
    slot = contact_count // device_count
    chunks = contact_count // CHUNK
    parts = LANES // slot
    height = -(-ROWS // (parts * 16)) * 16
    grad_scale = 1.0 / math.sqrt(device_count * node_count * DEGREE)
    table, requests = call(
        table_kernel,
        (
            shaped((ROWS, node_count), bf16),
            shaped((device_count, 1, slot), jnp.int32),
        ),
        (
            pltpu.VMEM((3, node_count), bf16),
            pltpu.VMEM((1, node_count), jnp.int32),
            pltpu.VMEM((1, node_count), jnp.int32),
            pltpu.VMEM((contact_count // LANES, LANES), jnp.int32),
            pltpu.SemaphoreType.DMA((5,)),
        ),
        in_specs=[IN_HBM] * 5,
        out_specs=(IN_VMEM, IN_VMEM),
    )(
        *in_hbm(
            node_feat,
            node_pos,
            halo_up[None],
            halo_down[None],
            contact_rows.reshape(contact_count // LANES, LANES),
        )
    )
    wanted = exchange(requests)
    low = from_behind(table, "sub", 1)
    high = from_behind(table, "sub", -1)
    found = call(
        functools.partial(contact_gather_kernel, slot),
        pltpu.HBM((device_count, height, LANES), bf16),
        (
            pltpu.VMEM((device_count, height, LANES), bf16),
            pltpu.SemaphoreType.DMA((chunks,)),
        ),
        in_specs=[IN_VMEM, IN_VMEM],
        out_specs=IN_HBM,
    )(table, wanted)
    found, mesh_senders, edge_mask = lax.optimization_barrier((found, mesh_senders, edge_mask))
    replies = exchange(found)
    mesh_code = (
        jnp.where(edge_mask != 0, mesh_senders, -1)
        .reshape(node_count, DEGREE)
        .T.reshape(DEGREE, 1, node_count)
    )
    contact_dst = contact_dst.reshape(chunks, 1, CHUNK)
    contact_mask = contact_mask.reshape(chunks, 1, CHUNK)
    mesh_rows = HID + GATES + 16
    recv_rows = FEAT + 16 + CS
    mesh_agg, mesh_grads, recv, contact_code = call(
        mesh_kernel,
        (
            pltpu.HBM((FEAT, node_count), f32),
            pltpu.HBM((mesh_rows, LANES), f32),
            pltpu.HBM((chunks, recv_rows, CHUNK), bf16),
            pltpu.HBM((chunks, 1, CHUNK), jnp.int32),
        ),
        (
            pltpu.VMEM((FEAT, node_count), f32),
            pltpu.VMEM((mesh_rows, LANES), f32),
            pltpu.VMEM((chunks, recv_rows, CHUNK), bf16),
            pltpu.VMEM((recv_rows, node_count), bf16),
            pltpu.VMEM((ROWS, 3 * node_count), bf16),
            pltpu.VMEM((FEAT, FEAT), bf16),
            pltpu.VMEM((chunks, 1, CHUNK), jnp.int32),
            pltpu.SemaphoreType.DMA((4,)),
        ),
        in_specs=[IN_VMEM] * 14,
        out_specs=(IN_HBM,) * 4,
        cost_estimate=pl.CostEstimate(
            flops=40_000_000_000, bytes_accessed=8_000_000, transcendentals=400_000
        ),
    )(
        table,
        low,
        high,
        mesh_code,
        node_cot,
        w_one,
        b_one[None],
        w_dist[None],
        w_two,
        w_scal,
        w_vec,
        w_ten,
        contact_dst,
        contact_mask,
    )
    packed_rows = mesh_rows + CS
    agg_rows, packed = call(
        functools.partial(contact_kernel, slot, grad_scale),
        (shaped((FEAT, node_count), bf16), shaped((device_count, 16, LANES), bf16)),
        (
            pltpu.VMEM((chunks, 1, CHUNK), jnp.int32),
            pltpu.VMEM((chunks, recv_rows, CHUNK), bf16),
            pltpu.VMEM((FEAT, node_count), f32),
            pltpu.VMEM((mesh_rows, LANES), f32),
            pltpu.VMEM((HID, 2 * CS), bf16),
            pltpu.VMEM((GATES, HID), bf16),
            pltpu.VMEM((1, HID), f32),
            pltpu.VMEM((1, HID), f32),
            pltpu.VMEM((packed_rows, LANES), f32),
            pltpu.SemaphoreType.DMA((chunks + 7,)),
        ),
        in_specs=[IN_VMEM] * 2 + [IN_HBM] * 8,
        out_specs=(IN_VMEM, IN_VMEM),
    )(
        replies,
        node_cot,
        *in_hbm(
            contact_code, recv, mesh_agg, mesh_grads, w_one, w_two, b_one[None], w_dist[None]
        ),
    )
    shares = call(sum_kernel, shaped((device_count, 16, LANES), bf16))(exchange(packed))
    node_out, one, bias, dist, two, scal, vec, ten = call(
        finish_kernel,
        (
            shaped((FEAT, node_count), bf16),
            shaped((HID, 2 * CS), f32),
            shaped((1, HID), f32),
            shaped((1, HID), f32),
            shaped((GATES, HID), f32),
            shaped((CS, CS), f32),
            shaped((CV, CV), f32),
            shaped((CT, CT), f32),
        ),
        (pltpu.VMEM((FEAT, FEAT), bf16),),
    )(exchange(shares), table, agg_rows, w_scal, w_vec, w_ten)
    return node_out, one, bias[0], dist[0], two, scal, vec, ten


def solution(mesh):
    along = P(("dom", "sub"))
    columns = P(None, ("dom", "sub"))
    in_specs = (columns,) * 3 + (along,) * 7 + (P(),) * 7
    out_specs = (columns,) + (P(),) * 7
    return jax.shard_map(
        on_device, mesh=mesh, in_specs=in_specs, out_specs=out_specs, check_vma=False
    )
```

```python
import functools
import math

import jax
import jax.numpy as jnp
from jax import lax
from jax.experimental import pallas as pl
from jax.experimental.pallas import tpu as pltpu
from jax.sharding import PartitionSpec as P

CS = 64
CV = 32
CT = 16
HID = 128
DEGREE = 6
GATES = 144
FEAT = CS + 3 * CV + 9 * CT
ROWS = 320
LANES = 128
CHUNK = 512
WIDE = 1024
VMEM_BYTES = 48 * 1024 * 1024


def dot(lhs, rhs, lhs_dim=1, rhs_dim=0):
    return lax.dot_general(
        lhs, rhs, (((lhs_dim,), (rhs_dim,)), ((), ())), preferred_element_type=jnp.float32
    )


def one_hot(code, width):
    rows = lax.broadcasted_iota(jnp.int16, (width, code.shape[1]), 0)
    return jnp.where(rows == code.astype(jnp.int16), jnp.bfloat16(1), jnp.bfloat16(0))


def join_index(table, row):
    pair = table[row : row + 2].astype(jnp.float32)
    return (pair[0:1] * 128.0 + pair[1:2]).astype(jnp.int32)


def table_kernel(
    feat_ref,
    pos_ref,
    up_ref,
    down_ref,
    rows_ref,
    table_ref,
    request_ref,
    pos_scr,
    up_scr,
    down_scr,
    rows_scr,
    sems,
):
    node_count = table_ref.shape[1]
    copies = [
        pltpu.make_async_copy(rows_ref, rows_scr, sems.at[0]),
        pltpu.make_async_copy(feat_ref, table_ref.at[:FEAT], sems.at[1]),
        pltpu.make_async_copy(pos_ref, pos_scr, sems.at[2]),
        pltpu.make_async_copy(up_ref, up_scr, sems.at[3]),
        pltpu.make_async_copy(down_ref, down_scr, sems.at[4]),
    ]
    for copy in copies:
        copy.start()
    copies[0].wait()
    slot = request_ref.shape[2]
    parts = LANES // slot
    for row in range(rows_scr.shape[0]):
        line = rows_scr[row : row + 1]
        for part in range(parts):
            request_ref[row * parts + part] = line[:, part * slot : (part + 1) * slot]
    for copy in copies[2:]:
        copy.wait()
    rows = lax.broadcasted_iota(jnp.int32, (ROWS - FEAT, node_count), 0)
    pos = pos_scr[...].astype(jnp.float32)
    tail = jnp.zeros((ROWS - FEAT, node_count), jnp.float32)
    for k in range(3):
        tail = jnp.where(rows == k, pos[k : k + 1], tail)
    for k, index_ref in ((3, up_scr), (5, down_scr)):
        index = index_ref[...]
        high = index >> 7
        tail = jnp.where(rows == k, high.astype(jnp.float32), tail)
        tail = jnp.where(rows == k + 1, (index - (high << 7)).astype(jnp.float32), tail)
    table_ref[FEAT:] = tail.astype(jnp.bfloat16)
    copies[1].wait()


def contact_gather_kernel(slot, table_ref, wanted_ref, out_hbm, out_ref, sems):
    node_count = table_ref.shape[1]
    parts = LANES // slot
    height = out_ref.shape[1]
    per_chunk = CHUNK // slot
    copies = []
    for chunk in range(wanted_ref.shape[0] // per_chunk):
        wanted = [wanted_ref[chunk * per_chunk + peer] for peer in range(per_chunk)]
        hot = one_hot(jnp.concatenate(wanted, 1), node_count)
        rows = dot(table_ref[...], hot).astype(jnp.bfloat16)
        if parts * height > ROWS:
            rows = jnp.concatenate(
                [rows, jnp.zeros((parts * height - ROWS, CHUNK), jnp.bfloat16)], 0
            )
        for peer in range(per_chunk):
            out_ref[chunk * per_chunk + peer] = jnp.concatenate(
                [
                    rows[part * height : (part + 1) * height, peer * slot : (peer + 1) * slot]
                    for part in range(parts)
                ],
                1,
            )
        done = pl.ds(chunk * per_chunk, per_chunk)
        copies.append(
            pltpu.make_async_copy(out_ref.at[done], out_hbm.at[done], sems.at[chunk])
        )
        copies[-1].start()
    for copy in copies:
        copy.wait()


def edge_math(src, base, first, inputs, pos_recv, back, live, weights):
    w_dist, w_two, w_two_t = weights
    edges = src.shape[1]
    offset = src[FEAT : FEAT + 3] - pos_recv
    if live is not None:
        offset = offset * live
    distance = jnp.sum(offset * offset, 0, keepdims=True)
    linear = base + first + w_dist * distance
    squashed = 0.5 * jnp.tanh(0.5 * linear) + 0.5
    hidden = (linear * squashed).astype(jnp.bfloat16)
    gates = dot(w_two, hidden)
    gate_vec = gates[CS : CS + CV]
    gate_dir = gates[CS + CV : CS + 2 * CV]
    gate_ten = gates[CS + 2 * CV :]
    message = [gates[:CS] * src[:CS]]
    vec_part = jnp.zeros((CV, edges), jnp.float32)
    dir_part = jnp.zeros((CV, edges), jnp.float32)
    for k in range(3):
        rows = slice(CS + k * CV, CS + (k + 1) * CV)
        message.append(gate_vec * src[rows] + gate_dir * offset[k : k + 1])
        vec_part = vec_part + back[rows] * src[rows]
        dir_part = dir_part + back[rows] * offset[k : k + 1]
    ten_part = jnp.zeros((CT, edges), jnp.float32)
    for m in range(9):
        rows = slice(CS + 3 * CV + m * CT, CS + 3 * CV + (m + 1) * CT)
        message.append(gate_ten * src[rows])
        ten_part = ten_part + back[rows] * src[rows]
    message = jnp.concatenate(message, 0)
    dgates = jnp.concatenate([back[:CS] * src[:CS], vec_part, dir_part, ten_part], 0).astype(
        jnp.bfloat16
    )
    hidden_grad = dot(w_two_t, dgates)
    linear_grad = (hidden_grad * squashed * (1.0 + linear * (1.0 - squashed))).astype(jnp.bfloat16)
    rows = lax.broadcasted_iota(jnp.int32, (16, edges), 0)
    coarse = distance.astype(jnp.bfloat16).astype(jnp.float32)
    extra = jnp.where(
        rows == 0, 1.0, jnp.where(rows == 1, coarse, jnp.where(rows == 2, distance - coarse, 0.0))
    ).astype(jnp.bfloat16)
    grads = (
        dot(linear_grad, inputs, 1, 1),
        dot(dgates, hidden, 1, 1),
        dot(extra, linear_grad, 1, 1),
    )
    return message, grads


def as_columns(first_row, second_row):
    rows = lax.broadcasted_iota(jnp.int32, (LANES, LANES), 0)
    columns = jnp.where(rows == 0, first_row, jnp.where(rows == 1, second_row, 0.0)).T
    return columns[:, 0:1], columns[:, 1:2]


def add_grads(grads_ref, grads):
    grads_ref[:HID] += grads[0]
    grads_ref[HID : HID + GATES] += grads[1]
    grads_ref[HID + GATES : HID + GATES + 16] += grads[2]


def block_diagonal(block_ref, w_scal, w_vec, w_ten):
    block_ref[...] = jnp.zeros_like(block_ref)
    block_ref[:CS, :CS] = w_scal[...]
    for k in range(3):
        rows = slice(CS + k * CV, CS + (k + 1) * CV)
        block_ref[rows, rows] = w_vec[...]
    for m in range(9):
        rows = slice(CS + 3 * CV + m * CT, CS + 3 * CV + (m + 1) * CT)
        block_ref[rows, rows] = w_ten[...]


def mesh_kernel(
    table_ref,
    low_ref,
    high_ref,
    code_ref,
    cot_ref,
    w_one_ref,
    b_one_ref,
    w_dist_ref,
    w_two_ref,
    w_scal_ref,
    w_vec_ref,
    w_ten_ref,
    dst_ref,
    mask_ref,
    agg_out_ref,
    grads_out_ref,
    recv_out_ref,
    code_out_ref,
    agg_ref,
    grads_ref,
    recv_ref,
    receive_ref,
    source_ref,
    block_ref,
    contact_ref,
    sems,
):
    node_count = table_ref.shape[1]
    source_ref[:, :node_count] = table_ref[...]
    low = low_ref[...]
    high = high_ref[...]
    source_ref[:, node_count : 2 * node_count] = dot(
        low, one_hot(join_index(low, FEAT + 3), node_count)
    ).astype(jnp.bfloat16)
    source_ref[:, 2 * node_count :] = dot(
        high, one_hot(join_index(high, FEAT + 5), node_count)
    ).astype(jnp.bfloat16)
    block_diagonal(block_ref, w_scal_ref, w_vec_ref, w_ten_ref)
    receive_ref[:FEAT] = dot(block_ref[...], cot_ref[...], 0, 0).astype(jnp.bfloat16)
    receive_ref[FEAT : FEAT + 16] = table_ref[FEAT:]
    receive_ref[FEAT + 16 :] = table_ref[:CS]
    w_one = w_one_ref[...]
    w_two = w_two_ref[...]
    b_column, dist_column = as_columns(b_one_ref[...], w_dist_ref[...])
    scal_recv = table_ref[:CS]
    recv_linear = dot(w_one[:, :CS], scal_recv) + b_column
    weights = (dist_column, w_two, w_two.T)
    pos_recv = table_ref[FEAT:].astype(jnp.float32)[:3]
    grads_ref[...] = jnp.zeros_like(grads_ref)
    agg_ref[...] = jnp.zeros_like(agg_ref)
    for step in range(DEGREE):
        code = code_ref[step]
        src = dot(source_ref[...], one_hot(code, 3 * node_count))
        live = jnp.where(code >= 0, 1.0, 0.0)
        back = receive_ref[:FEAT].astype(jnp.float32)
        scal_send = src[:CS].astype(jnp.bfloat16)
        inputs = jnp.concatenate([scal_recv, scal_send], 0)
        message, grads = edge_math(
            src, recv_linear, dot(w_one[:, CS:], scal_send), inputs, pos_recv, back, live, weights
        )
        agg_ref[...] += message
        add_grads(grads_ref, grads)
    contact_ref[...] = jnp.where(mask_ref[...] != 0, dst_ref[...], -1)
    for chunk in range(contact_ref.shape[0]):
        recv_ref[chunk] = dot(
            receive_ref[...], one_hot(contact_ref[chunk], node_count)
        ).astype(jnp.bfloat16)
    copies = [
        pltpu.make_async_copy(agg_ref, agg_out_ref, sems.at[0]),
        pltpu.make_async_copy(grads_ref, grads_out_ref, sems.at[1]),
        pltpu.make_async_copy(recv_ref, recv_out_ref, sems.at[2]),
        pltpu.make_async_copy(contact_ref, code_out_ref, sems.at[3]),
    ]
    for copy in copies:
        copy.start()
    for copy in copies:
        copy.wait()


def contact_kernel(
    slot,
    grad_scale,
    reply_ref,
    cot_ref,
    code_hbm,
    recv_hbm,
    mesh_agg_hbm,
    mesh_grads_hbm,
    w_one_hbm,
    w_two_hbm,
    b_one_hbm,
    w_dist_hbm,
    agg_out_ref,
    packed_ref,
    code_ref,
    recv_ref,
    agg_ref,
    grads_ref,
    w_one_ref,
    w_two_ref,
    b_one_ref,
    w_dist_ref,
    src_scr,
    packed_scr,
    sems,
):
    chunks = code_ref.shape[0]
    sources = [
        (b_one_hbm, b_one_ref),
        (w_dist_hbm, w_dist_ref),
        (w_one_hbm, w_one_ref),
        (w_two_hbm, w_two_ref),
        (code_hbm, code_ref),
    ]
    sources += [(recv_hbm.at[chunk], recv_ref.at[chunk]) for chunk in range(chunks)]
    sources += [(mesh_agg_hbm, agg_ref), (mesh_grads_hbm, grads_ref)]
    copies = [
        pltpu.make_async_copy(source, target, sems.at[at])
        for at, (source, target) in enumerate(sources)
    ]
    for copy in copies:
        copy.start()
    node_count = cot_ref.shape[1]
    parts = LANES // slot
    per_chunk = WIDE // slot
    for chunk in range(chunks):
        blocks = [reply_ref[chunk * per_chunk + peer] for peer in range(per_chunk)]
        src_scr[chunk] = jnp.concatenate(
            [
                jnp.concatenate(
                    [block[:, part * slot : (part + 1) * slot] for block in blocks], 1
                )
                for part in range(parts)
            ],
            0,
        )[:ROWS]
    for copy in copies[:6]:
        copy.wait()
    w_one = w_one_ref[...]
    w_two = w_two_ref[...]
    b_column, dist_column = as_columns(b_one_ref[...], w_dist_ref[...])
    weights = (dist_column, w_two, w_two.T)
    for chunk in range(chunks):
        src_rows = src_scr[chunk]
        if chunk == 1:
            for copy in copies[6:]:
                copy.wait()
        recv = recv_ref[chunk]
        inputs = jnp.concatenate([recv[FEAT + 16 :], src_rows[:CS]], 0)
        message, grads = edge_math(
            src_rows.astype(jnp.float32),
            b_column,
            dot(w_one, inputs),
            inputs,
            recv[FEAT : FEAT + 16].astype(jnp.float32)[:3],
            recv[:FEAT].astype(jnp.float32),
            None,
            weights,
        )
        scattered = dot(message.astype(jnp.bfloat16), one_hot(code_ref[chunk], node_count), 1, 1)
        if chunk == 0:
            held = (scattered, grads)
            continue
        agg_ref[...] += scattered
        add_grads(grads_ref, grads)
        if chunk == 1:
            agg_ref[...] += held[0]
            add_grads(grads_ref, held[1])
    agg_rows = agg_ref[...].astype(jnp.bfloat16)
    agg_out_ref[...] = agg_rows
    cot = cot_ref[...]
    low = HID + GATES
    packed_scr[:low] = grads_ref[:low] * grad_scale
    packed_scr[low : low + CS] = jnp.concatenate(
        [
            dot(cot[:CS], agg_rows[:CS], 1, 1) * grad_scale,
            jnp.zeros((CS, LANES - CS), jnp.float32),
        ],
        1,
    )
    grad_vec = jnp.zeros((CV, CV), jnp.float32)
    for k in range(3):
        rows = slice(CS + k * CV, CS + (k + 1) * CV)
        grad_vec = grad_vec + dot(cot[rows], agg_rows[rows], 1, 1)
    packed_scr[low : low + CV, CS : CS + CV] = grad_vec * grad_scale
    grad_ten = jnp.zeros((CT, CT), jnp.float32)
    for m in range(9):
        rows = slice(CS + 3 * CV + m * CT, CS + 3 * CV + (m + 1) * CT)
        grad_ten = grad_ten + dot(cot[rows], agg_rows[rows], 1, 1)
    packed_scr[low : low + CT, CS + CV : CS + CV + CT] = grad_ten * grad_scale
    extra = grads_ref[low:] * grad_scale
    rows = lax.broadcasted_iota(jnp.int32, (16, LANES), 0)
    packed_scr[low + CS :] = jnp.where(rows == 1, extra[1:2] + extra[2:3], extra)
    packed = packed_scr[...].astype(jnp.bfloat16)
    height = packed_ref.shape[1]
    for peer in range(packed_ref.shape[0]):
        for row in range(0, height, 16):
            at = peer * height + row
            if at < packed.shape[0]:
                packed_ref[peer, row : row + 16] = packed[at : at + 16]
            else:
                packed_ref[peer, row : row + 16] = jnp.zeros((16, LANES), jnp.bfloat16)


def sum_kernel(parts_ref, out_ref):
    total = parts_ref[0].astype(jnp.float32)
    for peer in range(1, parts_ref.shape[0]):
        total = total + parts_ref[peer].astype(jnp.float32)
    total = total.astype(jnp.bfloat16)
    for peer in range(out_ref.shape[0]):
        out_ref[peer] = total


def finish_kernel(
    blocks_ref,
    table_ref,
    agg_ref,
    w_scal_ref,
    w_vec_ref,
    w_ten_ref,
    out_ref,
    one_ref,
    bias_ref,
    dist_ref,
    two_ref,
    scal_ref,
    vec_ref,
    ten_ref,
    block_ref,
):
    height = blocks_ref.shape[1]
    block_diagonal(block_ref, w_scal_ref, w_vec_ref, w_ten_ref)
    out_ref[...] = (
        table_ref[:FEAT].astype(jnp.float32) + dot(block_ref[...], agg_ref[...])
    ).astype(jnp.bfloat16)

    def rows_of(block):
        peer, row = divmod(block * 16, height)
        return blocks_ref[peer, row : row + 16].astype(jnp.float32)

    for block in range(HID // 16):
        one_ref[block * 16 : (block + 1) * 16] = rows_of(block)
    for block in range(GATES // 16):
        two_ref[block * 16 : (block + 1) * 16] = rows_of(HID // 16 + block)
    low = (HID + GATES) // 16
    for block in range(CS // 16):
        rows = rows_of(low + block)
        scal_ref[block * 16 : (block + 1) * 16] = rows[:, :CS]
        if block < CV // 16:
            vec_ref[block * 16 : (block + 1) * 16] = rows[:, CS : CS + CV]
        if block == 0:
            ten_ref[...] = rows[:, CS + CV : CS + CV + CT]
    extra = rows_of(low + CS // 16)
    bias_ref[...] = extra[0:1]
    dist_ref[...] = extra[1:2]


def call(kernel, out_shape, scratch=(), in_specs=None, out_specs=None, cost_estimate=None):
    specs = {}
    if cost_estimate is not None:
        specs["cost_estimate"] = cost_estimate
    if in_specs is not None:
        specs["in_specs"] = in_specs
    if out_specs is not None:
        specs["out_specs"] = out_specs
    return pl.pallas_call(
        kernel,
        out_shape=out_shape,
        scratch_shapes=list(scratch),
        compiler_params=pltpu.CompilerParams(vmem_limit_bytes=VMEM_BYTES),
        **specs,
    )


IN_VMEM = pl.BlockSpec(memory_space=pltpu.VMEM)
IN_HBM = pl.BlockSpec(memory_space=pltpu.HBM)
ANYWHERE = pl.BlockSpec(memory_space=pl.ANY)


def exchange(blocks, axes=("dom", "sub")):
    return lax.all_to_all(blocks, axes, split_axis=0, concat_axis=0, tiled=True)


def in_hbm(*arrays):
    return tuple(pltpu.with_memory_space_constraint(array, pltpu.HBM) for array in arrays)


def shaped(shape, dtype):
    return jax.ShapeDtypeStruct(shape, dtype)


def from_behind(shard, axis, by):
    peers = lax.axis_size(axis)
    return lax.ppermute(shard, axis, [(i, (i + by) % peers) for i in range(peers)])


def on_device(
    node_feat,
    node_pos,
    node_cot,
    mesh_senders,
    edge_mask,
    halo_up,
    halo_down,
    contact_rows,
    contact_dst,
    contact_mask,
    w_one,
    b_one,
    w_dist,
    w_two,
    w_scal,
    w_vec,
    w_ten,
):
    f32, bf16 = jnp.float32, jnp.bfloat16
    node_count = node_feat.shape[1]
    contact_count = contact_rows.shape[0]
    device_count = lax.axis_size("dom") * lax.axis_size("sub")
    slot = contact_count // device_count
    chunks = contact_count // CHUNK
    wides = contact_count // WIDE
    parts = LANES // slot
    height = -(-ROWS // (parts * 16)) * 16
    grad_scale = 1.0 / math.sqrt(device_count * node_count * DEGREE)
    table, requests = call(
        table_kernel,
        (
            shaped((ROWS, node_count), bf16),
            shaped((device_count, 1, slot), jnp.int32),
        ),
        (
            pltpu.VMEM((3, node_count), bf16),
            pltpu.VMEM((1, node_count), jnp.int32),
            pltpu.VMEM((1, node_count), jnp.int32),
            pltpu.VMEM((contact_count // LANES, LANES), jnp.int32),
            pltpu.SemaphoreType.DMA((5,)),
        ),
        in_specs=[IN_HBM] * 5,
        out_specs=(IN_VMEM, IN_VMEM),
    )(
        *in_hbm(
            node_feat,
            node_pos,
            halo_up[None],
            halo_down[None],
            contact_rows.reshape(contact_count // LANES, LANES),
        )
    )
    wanted = exchange(requests)
    wanted, table_late = lax.optimization_barrier((wanted, table))
    low = from_behind(table_late, "sub", 1)
    high = from_behind(table_late, "sub", -1)
    found = call(
        functools.partial(contact_gather_kernel, slot),
        pltpu.HBM((device_count, height, LANES), bf16),
        (
            pltpu.VMEM((device_count, height, LANES), bf16),
            pltpu.SemaphoreType.DMA((chunks,)),
        ),
        in_specs=[IN_VMEM, IN_VMEM],
        out_specs=IN_HBM,
    )(table, wanted)
    found, mesh_senders, edge_mask = lax.optimization_barrier((found, mesh_senders, edge_mask))
    replies = exchange(found)
    mesh_code = (
        jnp.where(edge_mask != 0, mesh_senders, -1)
        .reshape(node_count, DEGREE)
        .T.reshape(DEGREE, 1, node_count)
    )
    contact_dst = contact_dst.reshape(wides, 1, WIDE)
    contact_mask = contact_mask.reshape(wides, 1, WIDE)
    mesh_rows = HID + GATES + 16
    recv_rows = FEAT + 16 + CS
    mesh_agg, mesh_grads, recv, contact_code = call(
        mesh_kernel,
        (
            pltpu.HBM((FEAT, node_count), f32),
            pltpu.HBM((mesh_rows, LANES), f32),
            pltpu.HBM((wides, recv_rows, WIDE), bf16),
            pltpu.HBM((wides, 1, WIDE), jnp.int32),
        ),
        (
            pltpu.VMEM((FEAT, node_count), f32),
            pltpu.VMEM((mesh_rows, LANES), f32),
            pltpu.VMEM((wides, recv_rows, WIDE), bf16),
            pltpu.VMEM((recv_rows, node_count), bf16),
            pltpu.VMEM((ROWS, 3 * node_count), bf16),
            pltpu.VMEM((FEAT, FEAT), bf16),
            pltpu.VMEM((wides, 1, WIDE), jnp.int32),
            pltpu.SemaphoreType.DMA((4,)),
        ),
        in_specs=[IN_VMEM] * 14,
        out_specs=(IN_HBM,) * 4,
        cost_estimate=pl.CostEstimate(
            flops=40_000_000_000, bytes_accessed=8_000_000, transcendentals=400_000
        ),
    )(
        table,
        low,
        high,
        mesh_code,
        node_cot,
        w_one,
        b_one[None],
        w_dist[None],
        w_two,
        w_scal,
        w_vec,
        w_ten,
        contact_dst,
        contact_mask,
    )
    packed_rows = mesh_rows + CS
    agg_rows, packed = call(
        functools.partial(contact_kernel, slot, grad_scale),
        (shaped((FEAT, node_count), bf16), shaped((device_count, 16, LANES), bf16)),
        (
            pltpu.VMEM((wides, 1, WIDE), jnp.int32),
            pltpu.VMEM((wides, recv_rows, WIDE), bf16),
            pltpu.VMEM((FEAT, node_count), f32),
            pltpu.VMEM((mesh_rows, LANES), f32),
            pltpu.VMEM((HID, 2 * CS), bf16),
            pltpu.VMEM((GATES, HID), bf16),
            pltpu.VMEM((1, HID), f32),
            pltpu.VMEM((1, HID), f32),
            pltpu.VMEM((wides, ROWS, WIDE), bf16),
            pltpu.VMEM((packed_rows, LANES), f32),
            pltpu.SemaphoreType.DMA((wides + 7,)),
        ),
        in_specs=[IN_VMEM] * 2 + [IN_HBM] * 8,
        out_specs=(IN_VMEM, IN_VMEM),
    )(
        replies,
        node_cot,
        *in_hbm(
            contact_code, recv, mesh_agg, mesh_grads, w_one, w_two, b_one[None], w_dist[None]
        ),
    )
    shares = call(sum_kernel, shaped((device_count, 16, LANES), bf16))(exchange(packed))
    node_out, one, bias, dist, two, scal, vec, ten = call(
        finish_kernel,
        (
            shaped((FEAT, node_count), bf16),
            shaped((HID, 2 * CS), f32),
            shaped((1, HID), f32),
            shaped((1, HID), f32),
            shaped((GATES, HID), f32),
            shaped((CS, CS), f32),
            shaped((CV, CV), f32),
            shaped((CT, CT), f32),
        ),
        (pltpu.VMEM((FEAT, FEAT), bf16),),
    )(exchange(shares), table, agg_rows, w_scal, w_vec, w_ten)
    return node_out, one, bias[0], dist[0], two, scal, vec, ten


def solution(mesh):
    along = P(("dom", "sub"))
    columns = P(None, ("dom", "sub"))
    in_specs = (columns,) * 3 + (along,) * 7 + (P(),) * 7
    out_specs = (columns,) + (P(),) * 7
    return jax.shard_map(
        on_device, mesh=mesh, in_specs=in_specs, out_specs=out_specs, check_vma=False
    )
```

```python
import functools
import math

import jax
import jax.numpy as jnp
from jax import lax
from jax.experimental import pallas as pl
from jax.experimental.pallas import tpu as pltpu
from jax.sharding import PartitionSpec as P

CS = 64
CV = 32
CT = 16
HID = 128
DEGREE = 6
GATES = 144
FEAT = CS + 3 * CV + 9 * CT
ROWS = 320
LANES = 128
CHUNK = 512
WIDE = 1024
VMEM_BYTES = 48 * 1024 * 1024


def dot(lhs, rhs, lhs_dim=1, rhs_dim=0):
    return lax.dot_general(
        lhs, rhs, (((lhs_dim,), (rhs_dim,)), ((), ())), preferred_element_type=jnp.float32
    )


def one_hot(code, width):
    rows = lax.broadcasted_iota(jnp.int16, (width, code.shape[1]), 0)
    return jnp.where(rows == code.astype(jnp.int16), jnp.bfloat16(1), jnp.bfloat16(0))


def join_index(table, row):
    pair = table[row : row + 2].astype(jnp.float32)
    return (pair[0:1] * 128.0 + pair[1:2]).astype(jnp.int32)


def table_kernel(
    feat_ref,
    pos_ref,
    up_ref,
    down_ref,
    rows_ref,
    table_ref,
    request_ref,
    pos_scr,
    up_scr,
    down_scr,
    rows_scr,
    sems,
):
    node_count = table_ref.shape[1]
    copies = [
        pltpu.make_async_copy(rows_ref, rows_scr, sems.at[0]),
        pltpu.make_async_copy(feat_ref, table_ref.at[:FEAT], sems.at[1]),
        pltpu.make_async_copy(pos_ref, pos_scr, sems.at[2]),
        pltpu.make_async_copy(up_ref, up_scr, sems.at[3]),
        pltpu.make_async_copy(down_ref, down_scr, sems.at[4]),
    ]
    for copy in copies:
        copy.start()
    copies[0].wait()
    slot = request_ref.shape[2]
    parts = LANES // slot
    for row in range(rows_scr.shape[0]):
        line = rows_scr[row : row + 1]
        for part in range(parts):
            request_ref[row * parts + part] = line[:, part * slot : (part + 1) * slot]
    for copy in copies[2:]:
        copy.wait()
    rows = lax.broadcasted_iota(jnp.int32, (ROWS - FEAT, node_count), 0)
    pos = pos_scr[...].astype(jnp.float32)
    tail = jnp.zeros((ROWS - FEAT, node_count), jnp.float32)
    for k in range(3):
        tail = jnp.where(rows == k, pos[k : k + 1], tail)
    for k, index_ref in ((3, up_scr), (5, down_scr)):
        index = index_ref[...]
        high = index >> 7
        tail = jnp.where(rows == k, high.astype(jnp.float32), tail)
        tail = jnp.where(rows == k + 1, (index - (high << 7)).astype(jnp.float32), tail)
    table_ref[FEAT:] = tail.astype(jnp.bfloat16)
    copies[1].wait()


def contact_gather_kernel(slot, table_ref, wanted_ref, out_hbm, out_ref, sems):
    node_count = table_ref.shape[1]
    parts = LANES // slot
    height = out_ref.shape[1]
    per_chunk = CHUNK // slot
    copies = []
    for chunk in range(wanted_ref.shape[0] // per_chunk):
        wanted = [wanted_ref[chunk * per_chunk + peer] for peer in range(per_chunk)]
        hot = one_hot(jnp.concatenate(wanted, 1), node_count)
        rows = dot(table_ref[...], hot).astype(jnp.bfloat16)
        if parts * height > ROWS:
            rows = jnp.concatenate(
                [rows, jnp.zeros((parts * height - ROWS, CHUNK), jnp.bfloat16)], 0
            )
        for peer in range(per_chunk):
            out_ref[chunk * per_chunk + peer] = jnp.concatenate(
                [
                    rows[part * height : (part + 1) * height, peer * slot : (peer + 1) * slot]
                    for part in range(parts)
                ],
                1,
            )
        done = pl.ds(chunk * per_chunk, per_chunk)
        copies.append(
            pltpu.make_async_copy(out_ref.at[done], out_hbm.at[done], sems.at[chunk])
        )
        copies[-1].start()
    for copy in copies:
        copy.wait()


def edge_math(src, base, first, inputs, pos_recv, back, live, weights):
    w_dist, w_two, w_two_t = weights
    edges = src.shape[1]
    offset = src[FEAT : FEAT + 3] - pos_recv
    if live is not None:
        offset = offset * live
    distance = jnp.sum(offset * offset, 0, keepdims=True)
    linear = base + first + w_dist * distance
    squashed = 0.5 * jnp.tanh(0.5 * linear) + 0.5
    hidden = (linear * squashed).astype(jnp.bfloat16)
    gates = dot(w_two, hidden)
    gate_vec = gates[CS : CS + CV]
    gate_dir = gates[CS + CV : CS + 2 * CV]
    gate_ten = gates[CS + 2 * CV :]
    message = [gates[:CS] * src[:CS]]
    vec_part = jnp.zeros((CV, edges), jnp.float32)
    dir_part = jnp.zeros((CV, edges), jnp.float32)
    for k in range(3):
        rows = slice(CS + k * CV, CS + (k + 1) * CV)
        message.append(gate_vec * src[rows] + gate_dir * offset[k : k + 1])
        vec_part = vec_part + back[rows] * src[rows]
        dir_part = dir_part + back[rows] * offset[k : k + 1]
    ten_part = jnp.zeros((CT, edges), jnp.float32)
    for m in range(9):
        rows = slice(CS + 3 * CV + m * CT, CS + 3 * CV + (m + 1) * CT)
        message.append(gate_ten * src[rows])
        ten_part = ten_part + back[rows] * src[rows]
    message = jnp.concatenate(message, 0)
    dgates = jnp.concatenate([back[:CS] * src[:CS], vec_part, dir_part, ten_part], 0).astype(
        jnp.bfloat16
    )
    hidden_grad = dot(w_two_t, dgates)
    linear_grad = (hidden_grad * squashed * (1.0 + linear * (1.0 - squashed))).astype(jnp.bfloat16)
    rows = lax.broadcasted_iota(jnp.int32, (16, edges), 0)
    coarse = distance.astype(jnp.bfloat16).astype(jnp.float32)
    extra = jnp.where(
        rows == 0, 1.0, jnp.where(rows == 1, coarse, jnp.where(rows == 2, distance - coarse, 0.0))
    ).astype(jnp.bfloat16)
    grads = (
        dot(linear_grad, jnp.concatenate([inputs, extra], 0), 1, 1),
        dot(dgates, hidden, 1, 1),
    )
    return message, grads


def as_columns(first_row, second_row):
    rows = lax.broadcasted_iota(jnp.int32, (LANES, LANES), 0)
    columns = jnp.where(rows == 0, first_row, jnp.where(rows == 1, second_row, 0.0)).T
    return columns[:, 0:1], columns[:, 1:2]


def add_grads(grads_ref, grads):
    grads_ref[:HID, : 2 * CS + 16] += grads[0]
    grads_ref[HID:, :HID] += grads[1]


def block_diagonal(block_ref, w_scal, w_vec, w_ten):
    block_ref[...] = jnp.zeros_like(block_ref)
    block_ref[:CS, :CS] = w_scal[...]
    for k in range(3):
        rows = slice(CS + k * CV, CS + (k + 1) * CV)
        block_ref[rows, rows] = w_vec[...]
    for m in range(9):
        rows = slice(CS + 3 * CV + m * CT, CS + 3 * CV + (m + 1) * CT)
        block_ref[rows, rows] = w_ten[...]


def mesh_kernel(
    table_ref,
    low_ref,
    high_ref,
    code_ref,
    cot_ref,
    w_one_ref,
    b_one_ref,
    w_dist_ref,
    w_two_ref,
    w_scal_ref,
    w_vec_ref,
    w_ten_ref,
    dst_ref,
    mask_ref,
    agg_out_ref,
    grads_out_ref,
    recv_out_ref,
    code_out_ref,
    agg_ref,
    grads_ref,
    recv_ref,
    receive_ref,
    source_ref,
    block_ref,
    contact_ref,
    sems,
):
    node_count = table_ref.shape[1]
    source_ref[:, :node_count] = table_ref[...]
    low = low_ref[...]
    high = high_ref[...]
    source_ref[:, node_count : 2 * node_count] = dot(
        low, one_hot(join_index(low, FEAT + 3), node_count)
    ).astype(jnp.bfloat16)
    source_ref[:, 2 * node_count :] = dot(
        high, one_hot(join_index(high, FEAT + 5), node_count)
    ).astype(jnp.bfloat16)
    block_diagonal(block_ref, w_scal_ref, w_vec_ref, w_ten_ref)
    receive_ref[:FEAT] = dot(block_ref[...], cot_ref[...], 0, 0).astype(jnp.bfloat16)
    receive_ref[FEAT : FEAT + 16] = table_ref[FEAT:]
    receive_ref[FEAT + 16 :] = table_ref[:CS]
    w_one = w_one_ref[...]
    w_two = w_two_ref[...]
    b_column, dist_column = as_columns(b_one_ref[...], w_dist_ref[...])
    scal_recv = table_ref[:CS]
    recv_linear = dot(w_one[:, :CS], scal_recv) + b_column
    weights = (dist_column, w_two, w_two.T)
    pos_recv = table_ref[FEAT:].astype(jnp.float32)[:3]
    grads_ref[...] = jnp.zeros_like(grads_ref)
    agg_ref[...] = jnp.zeros_like(agg_ref)
    for step in range(DEGREE):
        code = code_ref[step]
        src = dot(source_ref[...], one_hot(code, 3 * node_count))
        live = jnp.where(code >= 0, 1.0, 0.0)
        back = receive_ref[:FEAT].astype(jnp.float32)
        scal_send = src[:CS].astype(jnp.bfloat16)
        inputs = jnp.concatenate([scal_recv, scal_send], 0)
        message, grads = edge_math(
            src, recv_linear, dot(w_one[:, CS:], scal_send), inputs, pos_recv, back, live, weights
        )
        agg_ref[...] += message
        add_grads(grads_ref, grads)
    contact_ref[...] = jnp.where(mask_ref[...] != 0, dst_ref[...], -1)
    for chunk in range(contact_ref.shape[0]):
        recv_ref[chunk] = dot(
            receive_ref[...], one_hot(contact_ref[chunk], node_count)
        ).astype(jnp.bfloat16)
    copies = [
        pltpu.make_async_copy(agg_ref, agg_out_ref, sems.at[0]),
        pltpu.make_async_copy(grads_ref, grads_out_ref, sems.at[1]),
        pltpu.make_async_copy(recv_ref, recv_out_ref, sems.at[2]),
        pltpu.make_async_copy(contact_ref, code_out_ref, sems.at[3]),
    ]
    for copy in copies:
        copy.start()
    for copy in copies:
        copy.wait()


def contact_kernel(
    slot,
    grad_scale,
    reply_ref,
    cot_ref,
    code_hbm,
    recv_hbm,
    mesh_agg_hbm,
    mesh_grads_hbm,
    w_one_hbm,
    w_two_hbm,
    b_one_hbm,
    w_dist_hbm,
    agg_out_ref,
    packed_ref,
    code_ref,
    recv_ref,
    agg_ref,
    grads_ref,
    w_one_ref,
    w_two_ref,
    b_one_ref,
    w_dist_ref,
    src_scr,
    packed_scr,
    sems,
):
    chunks = code_ref.shape[0]
    sources = [
        (b_one_hbm, b_one_ref),
        (w_dist_hbm, w_dist_ref),
        (w_one_hbm, w_one_ref),
        (w_two_hbm, w_two_ref),
        (code_hbm, code_ref),
    ]
    sources += [(recv_hbm.at[chunk], recv_ref.at[chunk]) for chunk in range(chunks)]
    sources += [(mesh_agg_hbm, agg_ref), (mesh_grads_hbm, grads_ref)]
    copies = [
        pltpu.make_async_copy(source, target, sems.at[at])
        for at, (source, target) in enumerate(sources)
    ]
    for copy in copies:
        copy.start()
    node_count = cot_ref.shape[1]
    parts = LANES // slot
    per_chunk = WIDE // slot
    for chunk in range(chunks):
        blocks = [reply_ref[chunk * per_chunk + peer] for peer in range(per_chunk)]
        src_scr[chunk] = jnp.concatenate(
            [
                jnp.concatenate(
                    [block[:, part * slot : (part + 1) * slot] for block in blocks], 1
                )
                for part in range(parts)
            ],
            0,
        )[:ROWS]
    for copy in copies[:6]:
        copy.wait()
    w_one = w_one_ref[...]
    w_two = w_two_ref[...]
    b_column, dist_column = as_columns(b_one_ref[...], w_dist_ref[...])
    weights = (dist_column, w_two, w_two.T)
    for chunk in range(chunks):
        src_rows = src_scr[chunk]
        if chunk == 1:
            for copy in copies[6:]:
                copy.wait()
        recv = recv_ref[chunk]
        inputs = jnp.concatenate([recv[FEAT + 16 :], src_rows[:CS]], 0)
        message, grads = edge_math(
            src_rows.astype(jnp.float32),
            b_column,
            dot(w_one, inputs),
            inputs,
            recv[FEAT : FEAT + 16].astype(jnp.float32)[:3],
            recv[:FEAT].astype(jnp.float32),
            None,
            weights,
        )
        scattered = dot(message.astype(jnp.bfloat16), one_hot(code_ref[chunk], node_count), 1, 1)
        if chunk == 0:
            held = (scattered, grads)
            continue
        agg_ref[...] += scattered
        add_grads(grads_ref, grads)
        if chunk == 1:
            agg_ref[...] += held[0]
            add_grads(grads_ref, held[1])
    agg_rows = agg_ref[...].astype(jnp.bfloat16)
    agg_out_ref[...] = agg_rows
    cot = cot_ref[...]
    low = HID + GATES
    packed_scr[:low] = grads_ref[:, :LANES] * grad_scale
    packed_scr[low : low + CS] = jnp.concatenate(
        [
            dot(cot[:CS], agg_rows[:CS], 1, 1) * grad_scale,
            jnp.zeros((CS, LANES - CS), jnp.float32),
        ],
        1,
    )
    mixed = dot(cot[CS:], agg_rows[CS:], 1, 1)
    grad_vec = jnp.zeros((CV, CV), jnp.float32)
    for k in range(3):
        rows = slice(k * CV, (k + 1) * CV)
        grad_vec = grad_vec + mixed[rows, rows]
    packed_scr[low : low + CV, CS : CS + CV] = grad_vec * grad_scale
    grad_ten = jnp.zeros((CT, CT), jnp.float32)
    for m in range(9):
        rows = slice(3 * CV + m * CT, 3 * CV + (m + 1) * CT)
        grad_ten = grad_ten + mixed[rows, rows]
    packed_scr[low : low + CT, CS + CV : CS + CV + CT] = grad_ten * grad_scale
    extra = (grads_ref[:HID, LANES:] * grad_scale).T[:16]
    rows = lax.broadcasted_iota(jnp.int32, (16, LANES), 0)
    packed_scr[low + CS :] = jnp.where(rows == 1, extra[1:2] + extra[2:3], extra)
    packed = packed_scr[...].astype(jnp.bfloat16)
    height = packed_ref.shape[1]
    for peer in range(packed_ref.shape[0]):
        for row in range(0, height, 16):
            at = peer * height + row
            if at < packed.shape[0]:
                packed_ref[peer, row : row + 16] = packed[at : at + 16]
            else:
                packed_ref[peer, row : row + 16] = jnp.zeros((16, LANES), jnp.bfloat16)


def sum_kernel(parts_ref, out_ref):
    total = parts_ref[0].astype(jnp.float32)
    for peer in range(1, parts_ref.shape[0]):
        total = total + parts_ref[peer].astype(jnp.float32)
    total = total.astype(jnp.bfloat16)
    for peer in range(out_ref.shape[0]):
        out_ref[peer] = total


def finish_kernel(
    blocks_ref,
    table_ref,
    agg_ref,
    w_scal_ref,
    w_vec_ref,
    w_ten_ref,
    out_ref,
    one_ref,
    bias_ref,
    dist_ref,
    two_ref,
    scal_ref,
    vec_ref,
    ten_ref,
    block_ref,
):
    height = blocks_ref.shape[1]
    block_diagonal(block_ref, w_scal_ref, w_vec_ref, w_ten_ref)
    out_ref[...] = (
        table_ref[:FEAT].astype(jnp.float32) + dot(block_ref[...], agg_ref[...])
    ).astype(jnp.bfloat16)

    def rows_of(block):
        peer, row = divmod(block * 16, height)
        return blocks_ref[peer, row : row + 16].astype(jnp.float32)

    for block in range(HID // 16):
        one_ref[block * 16 : (block + 1) * 16] = rows_of(block)
    for block in range(GATES // 16):
        two_ref[block * 16 : (block + 1) * 16] = rows_of(HID // 16 + block)
    low = (HID + GATES) // 16
    for block in range(CS // 16):
        rows = rows_of(low + block)
        scal_ref[block * 16 : (block + 1) * 16] = rows[:, :CS]
        if block < CV // 16:
            vec_ref[block * 16 : (block + 1) * 16] = rows[:, CS : CS + CV]
        if block == 0:
            ten_ref[...] = rows[:, CS + CV : CS + CV + CT]
    extra = rows_of(low + CS // 16)
    bias_ref[...] = extra[0:1]
    dist_ref[...] = extra[1:2]


def call(kernel, out_shape, scratch=(), in_specs=None, out_specs=None, cost_estimate=None):
    specs = {}
    if cost_estimate is not None:
        specs["cost_estimate"] = cost_estimate
    if in_specs is not None:
        specs["in_specs"] = in_specs
    if out_specs is not None:
        specs["out_specs"] = out_specs
    return pl.pallas_call(
        kernel,
        out_shape=out_shape,
        scratch_shapes=list(scratch),
        compiler_params=pltpu.CompilerParams(vmem_limit_bytes=VMEM_BYTES),
        **specs,
    )


IN_VMEM = pl.BlockSpec(memory_space=pltpu.VMEM)
IN_HBM = pl.BlockSpec(memory_space=pltpu.HBM)
ANYWHERE = pl.BlockSpec(memory_space=pl.ANY)


def exchange(blocks, axes=("dom", "sub")):
    return lax.all_to_all(blocks, axes, split_axis=0, concat_axis=0, tiled=True)


def in_hbm(*arrays):
    return tuple(pltpu.with_memory_space_constraint(array, pltpu.HBM) for array in arrays)


def shaped(shape, dtype):
    return jax.ShapeDtypeStruct(shape, dtype)


def from_behind(shard, axis, by):
    peers = lax.axis_size(axis)
    return lax.ppermute(shard, axis, [(i, (i + by) % peers) for i in range(peers)])


def on_device(
    node_feat,
    node_pos,
    node_cot,
    mesh_senders,
    edge_mask,
    halo_up,
    halo_down,
    contact_rows,
    contact_dst,
    contact_mask,
    w_one,
    b_one,
    w_dist,
    w_two,
    w_scal,
    w_vec,
    w_ten,
):
    f32, bf16 = jnp.float32, jnp.bfloat16
    node_count = node_feat.shape[1]
    contact_count = contact_rows.shape[0]
    device_count = lax.axis_size("dom") * lax.axis_size("sub")
    slot = contact_count // device_count
    chunks = contact_count // CHUNK
    wides = contact_count // WIDE
    parts = LANES // slot
    height = -(-ROWS // (parts * 16)) * 16
    grad_scale = 1.0 / math.sqrt(device_count * node_count * DEGREE)
    table, requests = call(
        table_kernel,
        (
            shaped((ROWS, node_count), bf16),
            shaped((device_count, 1, slot), jnp.int32),
        ),
        (
            pltpu.VMEM((3, node_count), bf16),
            pltpu.VMEM((1, node_count), jnp.int32),
            pltpu.VMEM((1, node_count), jnp.int32),
            pltpu.VMEM((contact_count // LANES, LANES), jnp.int32),
            pltpu.SemaphoreType.DMA((5,)),
        ),
        in_specs=[IN_HBM] * 5,
        out_specs=(IN_VMEM, IN_VMEM),
    )(
        *in_hbm(
            node_feat,
            node_pos,
            halo_up[None],
            halo_down[None],
            contact_rows.reshape(contact_count // LANES, LANES),
        )
    )
    wanted = exchange(requests)
    wanted, table_late = lax.optimization_barrier((wanted, table))
    low = from_behind(table_late, "sub", 1)
    high = from_behind(table_late, "sub", -1)
    found = call(
        functools.partial(contact_gather_kernel, slot),
        pltpu.HBM((device_count, height, LANES), bf16),
        (
            pltpu.VMEM((device_count, height, LANES), bf16),
            pltpu.SemaphoreType.DMA((chunks,)),
        ),
        in_specs=[IN_VMEM, IN_VMEM],
        out_specs=IN_HBM,
    )(table, wanted)
    found, mesh_senders, edge_mask = lax.optimization_barrier((found, mesh_senders, edge_mask))
    replies = exchange(found)
    mesh_code = (
        jnp.where(edge_mask != 0, mesh_senders, -1)
        .reshape(node_count, DEGREE)
        .T.reshape(DEGREE, 1, node_count)
    )
    contact_dst = contact_dst.reshape(wides, 1, WIDE)
    contact_mask = contact_mask.reshape(wides, 1, WIDE)
    mesh_rows = HID + GATES
    recv_rows = FEAT + 16 + CS
    mesh_agg, mesh_grads, recv, contact_code = call(
        mesh_kernel,
        (
            pltpu.HBM((FEAT, node_count), f32),
            pltpu.HBM((mesh_rows, 2 * LANES), f32),
            pltpu.HBM((wides, recv_rows, WIDE), bf16),
            pltpu.HBM((wides, 1, WIDE), jnp.int32),
        ),
        (
            pltpu.VMEM((FEAT, node_count), f32),
            pltpu.VMEM((mesh_rows, 2 * LANES), f32),
            pltpu.VMEM((wides, recv_rows, WIDE), bf16),
            pltpu.VMEM((recv_rows, node_count), bf16),
            pltpu.VMEM((ROWS, 3 * node_count), bf16),
            pltpu.VMEM((FEAT, FEAT), bf16),
            pltpu.VMEM((wides, 1, WIDE), jnp.int32),
            pltpu.SemaphoreType.DMA((4,)),
        ),
        in_specs=[IN_VMEM] * 14,
        out_specs=(IN_HBM,) * 4,
        cost_estimate=pl.CostEstimate(
            flops=40_000_000_000, bytes_accessed=8_000_000, transcendentals=400_000
        ),
    )(
        table,
        low,
        high,
        mesh_code,
        node_cot,
        w_one,
        b_one[None],
        w_dist[None],
        w_two,
        w_scal,
        w_vec,
        w_ten,
        contact_dst,
        contact_mask,
    )
    packed_rows = mesh_rows + CS + 16
    agg_rows, packed = call(
        functools.partial(contact_kernel, slot, grad_scale),
        (shaped((FEAT, node_count), bf16), shaped((device_count, 16, LANES), bf16)),
        (
            pltpu.VMEM((wides, 1, WIDE), jnp.int32),
            pltpu.VMEM((wides, recv_rows, WIDE), bf16),
            pltpu.VMEM((FEAT, node_count), f32),
            pltpu.VMEM((mesh_rows, 2 * LANES), f32),
            pltpu.VMEM((HID, 2 * CS), bf16),
            pltpu.VMEM((GATES, HID), bf16),
            pltpu.VMEM((1, HID), f32),
            pltpu.VMEM((1, HID), f32),
            pltpu.VMEM((wides, ROWS, WIDE), bf16),
            pltpu.VMEM((packed_rows, LANES), f32),
            pltpu.SemaphoreType.DMA((wides + 7,)),
        ),
        in_specs=[IN_VMEM] * 2 + [IN_HBM] * 8,
        out_specs=(IN_VMEM, IN_VMEM),
    )(
        replies,
        node_cot,
        *in_hbm(
            contact_code, recv, mesh_agg, mesh_grads, w_one, w_two, b_one[None], w_dist[None]
        ),
    )
    shares = call(sum_kernel, shaped((device_count, 16, LANES), bf16))(exchange(packed))
    node_out, one, bias, dist, two, scal, vec, ten = call(
        finish_kernel,
        (
            shaped((FEAT, node_count), bf16),
            shaped((HID, 2 * CS), f32),
            shaped((1, HID), f32),
            shaped((1, HID), f32),
            shaped((GATES, HID), f32),
            shaped((CS, CS), f32),
            shaped((CV, CV), f32),
            shaped((CT, CT), f32),
        ),
        (pltpu.VMEM((FEAT, FEAT), bf16),),
    )(exchange(shares), table, agg_rows, w_scal, w_vec, w_ten)
    return node_out, one, bias[0], dist[0], two, scal, vec, ten


def solution(mesh):
    along = P(("dom", "sub"))
    columns = P(None, ("dom", "sub"))
    in_specs = (columns,) * 3 + (along,) * 7 + (P(),) * 7
    out_specs = (columns,) + (P(),) * 7
    return jax.shard_map(
        on_device, mesh=mesh, in_specs=in_specs, out_specs=out_specs, check_vma=False
    )
```

```python
import functools
import math

import jax
import jax.numpy as jnp
from jax import lax
from jax.experimental import pallas as pl
from jax.experimental.pallas import tpu as pltpu
from jax.sharding import PartitionSpec as P

CS = 64
CV = 32
CT = 16
HID = 128
DEGREE = 6
GATES = 144
FEAT = CS + 3 * CV + 9 * CT
ROWS = 320
LANES = 128
CHUNK = 512
WIDE = 1024
VMEM_BYTES = 48 * 1024 * 1024


def dot(lhs, rhs, lhs_dim=1, rhs_dim=0):
    return lax.dot_general(
        lhs, rhs, (((lhs_dim,), (rhs_dim,)), ((), ())), preferred_element_type=jnp.float32
    )


def one_hot(code, width):
    rows = lax.broadcasted_iota(jnp.int16, (width, code.shape[1]), 0)
    return jnp.where(rows == code.astype(jnp.int16), jnp.bfloat16(1), jnp.bfloat16(0))


def join_index(table, row):
    pair = table[row : row + 2].astype(jnp.float32)
    return (pair[0:1] * 128.0 + pair[1:2]).astype(jnp.int32)


def table_kernel(
    feat_ref,
    pos_ref,
    up_ref,
    down_ref,
    rows_ref,
    table_ref,
    request_ref,
    pos_scr,
    up_scr,
    down_scr,
    rows_scr,
    sems,
):
    node_count = table_ref.shape[1]
    copies = [
        pltpu.make_async_copy(rows_ref, rows_scr, sems.at[0]),
        pltpu.make_async_copy(feat_ref, table_ref.at[:FEAT], sems.at[1]),
        pltpu.make_async_copy(pos_ref, pos_scr, sems.at[2]),
        pltpu.make_async_copy(up_ref, up_scr, sems.at[3]),
        pltpu.make_async_copy(down_ref, down_scr, sems.at[4]),
    ]
    for copy in copies:
        copy.start()
    copies[0].wait()
    slot = request_ref.shape[2]
    parts = LANES // slot
    for row in range(rows_scr.shape[0]):
        line = rows_scr[row : row + 1]
        for part in range(parts):
            request_ref[row * parts + part] = line[:, part * slot : (part + 1) * slot]
    for copy in copies[2:]:
        copy.wait()
    rows = lax.broadcasted_iota(jnp.int32, (ROWS - FEAT, node_count), 0)
    pos = pos_scr[...].astype(jnp.float32)
    tail = jnp.zeros((ROWS - FEAT, node_count), jnp.float32)
    for k in range(3):
        tail = jnp.where(rows == k, pos[k : k + 1], tail)
    for k, index_ref in ((3, up_scr), (5, down_scr)):
        index = index_ref[...]
        high = index >> 7
        tail = jnp.where(rows == k, high.astype(jnp.float32), tail)
        tail = jnp.where(rows == k + 1, (index - (high << 7)).astype(jnp.float32), tail)
    table_ref[FEAT:] = tail.astype(jnp.bfloat16)
    copies[1].wait()


def contact_gather_kernel(slot, doms, table_ref, wanted_ref, out_hbm, out_ref, sems):
    node_count = table_ref.shape[1]
    parts = LANES // slot
    height = out_ref.shape[1]
    per_chunk = CHUNK // slot
    for chunk in range(wanted_ref.shape[0] // per_chunk):
        wanted = [wanted_ref[chunk * per_chunk + peer] for peer in range(per_chunk)]
        hot = one_hot(jnp.concatenate(wanted, 1), node_count)
        rows = dot(table_ref[...], hot).astype(jnp.bfloat16)
        if parts * height > ROWS:
            rows = jnp.concatenate(
                [rows, jnp.zeros((parts * height - ROWS, CHUNK), jnp.bfloat16)], 0
            )
        for peer in range(per_chunk):
            out_ref[place_of(doms, chunk * per_chunk + peer, out_ref.shape[0])] = jnp.concatenate(
                [
                    rows[part * height : (part + 1) * height, peer * slot : (peer + 1) * slot]
                    for part in range(parts)
                ],
                1,
            )
    copy = pltpu.make_async_copy(out_ref, out_hbm, sems.at[0])
    copy.start()
    copy.wait()


def edge_math(src, base, first, inputs, pos_recv, back, live, weights):
    w_dist, w_two, w_two_t = weights
    edges = src.shape[1]
    offset = src[FEAT : FEAT + 3] - pos_recv
    if live is not None:
        offset = offset * live
    distance = jnp.sum(offset * offset, 0, keepdims=True)
    linear = base + first + w_dist * distance
    squashed = 0.5 * jnp.tanh(0.5 * linear) + 0.5
    hidden = (linear * squashed).astype(jnp.bfloat16)
    gates = dot(w_two, hidden)
    gate_vec = gates[CS : CS + CV]
    gate_dir = gates[CS + CV : CS + 2 * CV]
    gate_ten = gates[CS + 2 * CV :]
    message = [gates[:CS] * src[:CS]]
    vec_part = jnp.zeros((CV, edges), jnp.float32)
    dir_part = jnp.zeros((CV, edges), jnp.float32)
    for k in range(3):
        rows = slice(CS + k * CV, CS + (k + 1) * CV)
        message.append(gate_vec * src[rows] + gate_dir * offset[k : k + 1])
        vec_part = vec_part + back[rows] * src[rows]
        dir_part = dir_part + back[rows] * offset[k : k + 1]
    ten_part = jnp.zeros((CT, edges), jnp.float32)
    for m in range(9):
        rows = slice(CS + 3 * CV + m * CT, CS + 3 * CV + (m + 1) * CT)
        message.append(gate_ten * src[rows])
        ten_part = ten_part + back[rows] * src[rows]
    message = jnp.concatenate(message, 0)
    dgates = jnp.concatenate([back[:CS] * src[:CS], vec_part, dir_part, ten_part], 0).astype(
        jnp.bfloat16
    )
    hidden_grad = dot(w_two_t, dgates)
    linear_grad = (hidden_grad * squashed * (1.0 + linear * (1.0 - squashed))).astype(jnp.bfloat16)
    rows = lax.broadcasted_iota(jnp.int32, (16, edges), 0)
    coarse = distance.astype(jnp.bfloat16).astype(jnp.float32)
    extra = jnp.where(
        rows == 0, 1.0, jnp.where(rows == 1, coarse, jnp.where(rows == 2, distance - coarse, 0.0))
    ).astype(jnp.bfloat16)
    grads = (
        dot(linear_grad, jnp.concatenate([inputs, extra], 0), 1, 1),
        dot(dgates, hidden, 1, 1),
    )
    return message, grads


def as_columns(first_row, second_row):
    rows = lax.broadcasted_iota(jnp.int32, (LANES, LANES), 0)
    columns = jnp.where(rows == 0, first_row, jnp.where(rows == 1, second_row, 0.0)).T
    return columns[:, 0:1], columns[:, 1:2]


def add_grads(grads_ref, grads):
    grads_ref[:HID, : 2 * CS + 16] += grads[0]
    grads_ref[HID:, :HID] += grads[1]


def block_diagonal(block_ref, w_scal, w_vec, w_ten):
    block_ref[...] = jnp.zeros_like(block_ref)
    block_ref[:CS, :CS] = w_scal[...]
    for k in range(3):
        rows = slice(CS + k * CV, CS + (k + 1) * CV)
        block_ref[rows, rows] = w_vec[...]
    for m in range(9):
        rows = slice(CS + 3 * CV + m * CT, CS + 3 * CV + (m + 1) * CT)
        block_ref[rows, rows] = w_ten[...]


def mesh_kernel(
    table_ref,
    low_ref,
    high_ref,
    code_ref,
    cot_ref,
    w_one_ref,
    b_one_ref,
    w_dist_ref,
    w_two_ref,
    w_scal_ref,
    w_vec_ref,
    w_ten_ref,
    dst_ref,
    mask_ref,
    agg_out_ref,
    grads_out_ref,
    recv_out_ref,
    code_out_ref,
    agg_ref,
    grads_ref,
    recv_ref,
    receive_ref,
    source_ref,
    block_ref,
    contact_ref,
    sems,
):
    node_count = table_ref.shape[1]
    source_ref[:, :node_count] = table_ref[...]
    low = low_ref[...]
    high = high_ref[...]
    source_ref[:, node_count : 2 * node_count] = dot(
        low, one_hot(join_index(low, FEAT + 3), node_count)
    ).astype(jnp.bfloat16)
    source_ref[:, 2 * node_count :] = dot(
        high, one_hot(join_index(high, FEAT + 5), node_count)
    ).astype(jnp.bfloat16)
    block_diagonal(block_ref, w_scal_ref, w_vec_ref, w_ten_ref)
    receive_ref[:FEAT] = dot(block_ref[...], cot_ref[...], 0, 0).astype(jnp.bfloat16)
    receive_ref[FEAT : FEAT + 16] = table_ref[FEAT:]
    receive_ref[FEAT + 16 :] = table_ref[:CS]
    w_one = w_one_ref[...]
    w_two = w_two_ref[...]
    b_column, dist_column = as_columns(b_one_ref[...], w_dist_ref[...])
    scal_recv = table_ref[:CS]
    recv_linear = dot(w_one[:, :CS], scal_recv) + b_column
    weights = (dist_column, w_two, w_two.T)
    pos_recv = table_ref[FEAT:].astype(jnp.float32)[:3]
    grads_ref[...] = jnp.zeros_like(grads_ref)
    agg_ref[...] = jnp.zeros_like(agg_ref)
    for step in range(DEGREE):
        code = code_ref[step]
        src = dot(source_ref[...], one_hot(code, 3 * node_count))
        live = jnp.where(code >= 0, 1.0, 0.0)
        back = receive_ref[:FEAT].astype(jnp.float32)
        scal_send = src[:CS].astype(jnp.bfloat16)
        inputs = jnp.concatenate([scal_recv, scal_send], 0)
        message, grads = edge_math(
            src, recv_linear, dot(w_one[:, CS:], scal_send), inputs, pos_recv, back, live, weights
        )
        agg_ref[...] += message
        add_grads(grads_ref, grads)
    contact_ref[...] = jnp.where(mask_ref[...] != 0, dst_ref[...], -1)
    for chunk in range(contact_ref.shape[0]):
        recv_ref[chunk] = dot(
            receive_ref[...], one_hot(contact_ref[chunk], node_count)
        ).astype(jnp.bfloat16)
    copies = [
        pltpu.make_async_copy(agg_ref, agg_out_ref, sems.at[0]),
        pltpu.make_async_copy(grads_ref, grads_out_ref, sems.at[1]),
        pltpu.make_async_copy(recv_ref, recv_out_ref, sems.at[2]),
        pltpu.make_async_copy(contact_ref, code_out_ref, sems.at[3]),
    ]
    for copy in copies:
        copy.start()
    for copy in copies:
        copy.wait()


def edge_blocks(src, recv, weights, scratch):
    w_one, w_two, w_two_t, b_wide, dist_wide = weights
    inputs, product, slope, hidden, gates, message, dgates, linear_grad = scratch
    edges = src.shape[1]
    blocks = [slice(at, at + LANES) for at in range(0, edges, LANES)]
    inputs[:CS] = recv[FEAT + 16 :]
    inputs[CS : 2 * CS] = src[:CS]
    offset = (src[FEAT:].astype(jnp.float32) - recv[FEAT : FEAT + 16].astype(jnp.float32))[:3]
    distance = jnp.sum(offset * offset, 0, keepdims=True)
    rows = lax.broadcasted_iota(jnp.int32, (16, edges), 0)
    coarse = distance.astype(jnp.bfloat16).astype(jnp.float32)
    inputs[2 * CS :] = jnp.where(
        rows == 0, 1.0, jnp.where(rows == 1, coarse, jnp.where(rows == 2, distance - coarse, 0.0))
    ).astype(jnp.bfloat16)
    product[...] = dot(w_one, inputs[: 2 * CS])
    for lanes in blocks:
        linear = product[:, lanes] + b_wide[...] + dist_wide[...] * distance[:, lanes]
        squashed = 0.5 * jnp.tanh(0.5 * linear) + 0.5
        hidden[:, lanes] = (linear * squashed).astype(jnp.bfloat16)
        slope[:, lanes] = squashed * (1.0 + linear * (1.0 - squashed))
    gates[...] = dot(w_two, hidden[...])

    def sent(rows, lanes):
        return src[rows, lanes].astype(jnp.float32)

    def back(rows, lanes):
        return recv[rows, lanes].astype(jnp.float32)

    for lanes in blocks:
        scal = slice(0, CS)
        value = sent(scal, lanes)
        message[scal, lanes] = (gates[scal, lanes] * value).astype(jnp.bfloat16)
        dgates[scal, lanes] = (back(scal, lanes) * value).astype(jnp.bfloat16)
        gate_vec = gates[CS : CS + CV, lanes]
        gate_dir = gates[CS + CV : CS + 2 * CV, lanes]
        vec_part = jnp.zeros((CV, LANES), jnp.float32)
        dir_part = jnp.zeros((CV, LANES), jnp.float32)
        for k in range(3):
            rows = slice(CS + k * CV, CS + (k + 1) * CV)
            value, pull, along = sent(rows, lanes), back(rows, lanes), offset[k : k + 1, lanes]
            message[rows, lanes] = (gate_vec * value + gate_dir * along).astype(jnp.bfloat16)
            vec_part = vec_part + pull * value
            dir_part = dir_part + pull * along
        dgates[CS : CS + CV, lanes] = vec_part.astype(jnp.bfloat16)
        dgates[CS + CV : CS + 2 * CV, lanes] = dir_part.astype(jnp.bfloat16)
        gate_ten = gates[CS + 2 * CV :, lanes]
        ten_part = jnp.zeros((CT, LANES), jnp.float32)
        for m in range(9):
            rows = slice(CS + 3 * CV + m * CT, CS + 3 * CV + (m + 1) * CT)
            value = sent(rows, lanes)
            message[rows, lanes] = (gate_ten * value).astype(jnp.bfloat16)
            ten_part = ten_part + back(rows, lanes) * value
        dgates[CS + 2 * CV :, lanes] = ten_part.astype(jnp.bfloat16)
    product[...] = dot(w_two_t, dgates[...])
    for lanes in blocks:
        linear_grad[:, lanes] = (product[:, lanes] * slope[:, lanes]).astype(jnp.bfloat16)
    return (
        dot(linear_grad[...], inputs[...], 1, 1),
        dot(dgates[...], hidden[...], 1, 1),
    )


def contact_kernel(
    slot,
    doms,
    grad_scale,
    reply_ref,
    cot_ref,
    code_hbm,
    recv_hbm,
    mesh_agg_hbm,
    mesh_grads_hbm,
    w_one_hbm,
    w_two_hbm,
    b_one_hbm,
    w_dist_hbm,
    agg_out_ref,
    packed_ref,
    code_ref,
    recv_ref,
    agg_ref,
    grads_ref,
    w_one_ref,
    w_two_ref,
    b_one_ref,
    w_dist_ref,
    src_scr,
    packed_scr,
    b_wide,
    dist_wide,
    *rest,
):
    scratch, sems = rest[:-1], rest[-1]

    chunks = code_ref.shape[0]
    sources = [
        (b_one_hbm, b_one_ref),
        (w_dist_hbm, w_dist_ref),
        (w_one_hbm, w_one_ref),
        (w_two_hbm, w_two_ref),
        (code_hbm, code_ref),
    ]
    sources += [(recv_hbm.at[chunk], recv_ref.at[chunk]) for chunk in range(chunks)]
    sources += [(mesh_agg_hbm, agg_ref), (mesh_grads_hbm, grads_ref)]
    copies = [
        pltpu.make_async_copy(source, target, sems.at[at])
        for at, (source, target) in enumerate(sources)
    ]
    for copy in copies:
        copy.start()
    node_count = cot_ref.shape[1]
    parts = LANES // slot
    per_chunk = WIDE // slot
    for chunk in range(chunks):
        at = range(chunk * per_chunk, (chunk + 1) * per_chunk)
        blocks = [reply_ref[place_of(doms, peer, reply_ref.shape[0])] for peer in at]
        src_scr[chunk] = jnp.concatenate(
            [
                jnp.concatenate(
                    [block[:, part * slot : (part + 1) * slot] for block in blocks], 1
                )
                for part in range(parts)
            ],
            0,
        )[:ROWS]
    for copy in copies[:6]:
        copy.wait()
    w_one = w_one_ref[...]
    w_two = w_two_ref[...]
    b_column, dist_column = as_columns(b_one_ref[...], w_dist_ref[...])
    b_wide[...] = jnp.broadcast_to(b_column, (HID, LANES))
    dist_wide[...] = jnp.broadcast_to(dist_column, (HID, LANES))
    weights = (w_one, w_two, w_two.T, b_wide, dist_wide)
    for chunk in range(chunks):
        if chunk == 1:
            for copy in copies[6:]:
                copy.wait()
        grads = edge_blocks(src_scr.at[chunk], recv_ref.at[chunk], weights, scratch)
        hot = one_hot(code_ref[chunk], node_count)
        scattered = dot(scratch[5][...], hot, 1, 1)
        if chunk == 0:
            held = (scattered, grads)
            continue
        agg_ref[...] += scattered
        add_grads(grads_ref, grads)
        if chunk == 1:
            agg_ref[...] += held[0]
            add_grads(grads_ref, held[1])
    agg_rows = agg_ref[...].astype(jnp.bfloat16)
    agg_out_ref[...] = agg_rows
    cot = cot_ref[...]
    low = HID + GATES
    packed_scr[:low] = grads_ref[:, :LANES] * grad_scale
    packed_scr[low : low + CS] = jnp.concatenate(
        [
            dot(cot[:CS], agg_rows[:CS], 1, 1) * grad_scale,
            jnp.zeros((CS, LANES - CS), jnp.float32),
        ],
        1,
    )
    mixed = dot(cot[CS:], agg_rows[CS:], 1, 1)
    grad_vec = jnp.zeros((CV, CV), jnp.float32)
    for k in range(3):
        rows = slice(k * CV, (k + 1) * CV)
        grad_vec = grad_vec + mixed[rows, rows]
    packed_scr[low : low + CV, CS : CS + CV] = grad_vec * grad_scale
    grad_ten = jnp.zeros((CT, CT), jnp.float32)
    for m in range(9):
        rows = slice(3 * CV + m * CT, 3 * CV + (m + 1) * CT)
        grad_ten = grad_ten + mixed[rows, rows]
    packed_scr[low : low + CT, CS + CV : CS + CV + CT] = grad_ten * grad_scale
    extra = (grads_ref[:HID, LANES:] * grad_scale).T[:16]
    rows = lax.broadcasted_iota(jnp.int32, (16, LANES), 0)
    packed_scr[low + CS :] = jnp.where(rows == 1, extra[1:2] + extra[2:3], extra)
    packed = packed_scr[...].astype(jnp.bfloat16)
    height = packed_ref.shape[1]
    for peer in range(packed_ref.shape[0]):
        for row in range(0, height, 16):
            at = peer * height + row
            if at < packed.shape[0]:
                packed_ref[peer, row : row + 16] = packed[at : at + 16]
            else:
                packed_ref[peer, row : row + 16] = jnp.zeros((16, LANES), jnp.bfloat16)


def sum_kernel(parts_ref, out_ref):
    total = parts_ref[0].astype(jnp.float32)
    for peer in range(1, parts_ref.shape[0]):
        total = total + parts_ref[peer].astype(jnp.float32)
    total = total.astype(jnp.bfloat16)
    for peer in range(out_ref.shape[0]):
        out_ref[peer] = total


def finish_kernel(
    blocks_ref,
    table_ref,
    agg_ref,
    w_scal_ref,
    w_vec_ref,
    w_ten_ref,
    out_ref,
    one_ref,
    bias_ref,
    dist_ref,
    two_ref,
    scal_ref,
    vec_ref,
    ten_ref,
    block_ref,
):
    height = blocks_ref.shape[1]
    block_diagonal(block_ref, w_scal_ref, w_vec_ref, w_ten_ref)
    out_ref[...] = (
        table_ref[:FEAT].astype(jnp.float32) + dot(block_ref[...], agg_ref[...])
    ).astype(jnp.bfloat16)

    def rows_of(block):
        peer, row = divmod(block * 16, height)
        return blocks_ref[peer, row : row + 16].astype(jnp.float32)

    for block in range(HID // 16):
        one_ref[block * 16 : (block + 1) * 16] = rows_of(block)
    for block in range(GATES // 16):
        two_ref[block * 16 : (block + 1) * 16] = rows_of(HID // 16 + block)
    low = (HID + GATES) // 16
    for block in range(CS // 16):
        rows = rows_of(low + block)
        scal_ref[block * 16 : (block + 1) * 16] = rows[:, :CS]
        if block < CV // 16:
            vec_ref[block * 16 : (block + 1) * 16] = rows[:, CS : CS + CV]
        if block == 0:
            ten_ref[...] = rows[:, CS + CV : CS + CV + CT]
    extra = rows_of(low + CS // 16)
    bias_ref[...] = extra[0:1]
    dist_ref[...] = extra[1:2]


def call(kernel, out_shape, scratch=(), in_specs=None, out_specs=None, cost_estimate=None):
    specs = {}
    if cost_estimate is not None:
        specs["cost_estimate"] = cost_estimate
    if in_specs is not None:
        specs["in_specs"] = in_specs
    if out_specs is not None:
        specs["out_specs"] = out_specs
    return pl.pallas_call(
        kernel,
        out_shape=out_shape,
        scratch_shapes=list(scratch),
        compiler_params=pltpu.CompilerParams(vmem_limit_bytes=VMEM_BYTES),
        **specs,
    )


IN_VMEM = pl.BlockSpec(memory_space=pltpu.VMEM)
IN_HBM = pl.BlockSpec(memory_space=pltpu.HBM)
ANYWHERE = pl.BlockSpec(memory_space=pl.ANY)


def place_of(doms, peer, peers):
    subs = peers // doms
    return peer % subs * doms + peer // subs


def exchange(blocks, axes=("dom", "sub")):
    return lax.all_to_all(blocks, axes, split_axis=0, concat_axis=0, tiled=True)


def in_hbm(*arrays):
    return tuple(pltpu.with_memory_space_constraint(array, pltpu.HBM) for array in arrays)


def shaped(shape, dtype):
    return jax.ShapeDtypeStruct(shape, dtype)


def from_behind(shard, axis, by):
    peers = lax.axis_size(axis)
    return lax.ppermute(shard, axis, [(i, (i + by) % peers) for i in range(peers)])


def on_device(
    node_feat,
    node_pos,
    node_cot,
    mesh_senders,
    edge_mask,
    halo_up,
    halo_down,
    contact_rows,
    contact_dst,
    contact_mask,
    w_one,
    b_one,
    w_dist,
    w_two,
    w_scal,
    w_vec,
    w_ten,
):
    f32, bf16 = jnp.float32, jnp.bfloat16
    node_count = node_feat.shape[1]
    contact_count = contact_rows.shape[0]
    device_count = lax.axis_size("dom") * lax.axis_size("sub")
    slot = contact_count // device_count
    chunks = contact_count // CHUNK
    wides = contact_count // WIDE
    parts = LANES // slot
    height = -(-ROWS // (parts * 16)) * 16
    grad_scale = 1.0 / math.sqrt(device_count * node_count * DEGREE)
    table, requests = call(
        table_kernel,
        (
            shaped((ROWS, node_count), bf16),
            shaped((device_count, 1, slot), jnp.int32),
        ),
        (
            pltpu.VMEM((3, node_count), bf16),
            pltpu.VMEM((1, node_count), jnp.int32),
            pltpu.VMEM((1, node_count), jnp.int32),
            pltpu.VMEM((contact_count // LANES, LANES), jnp.int32),
            pltpu.SemaphoreType.DMA((5,)),
        ),
        in_specs=[IN_HBM] * 5,
        out_specs=(IN_VMEM, IN_VMEM),
    )(
        *in_hbm(
            node_feat,
            node_pos,
            halo_up[None],
            halo_down[None],
            contact_rows.reshape(contact_count // LANES, LANES),
        )
    )
    wanted = exchange(requests)
    wanted, table_late = lax.optimization_barrier((wanted, table))
    low = from_behind(table_late, "sub", 1)
    high = from_behind(table_late, "sub", -1)
    found = call(
        functools.partial(contact_gather_kernel, slot, lax.axis_size("dom")),
        pltpu.HBM((device_count, height, LANES), bf16),
        (
            pltpu.VMEM((device_count, height, LANES), bf16),
            pltpu.SemaphoreType.DMA((chunks,)),
        ),
        in_specs=[IN_VMEM, IN_VMEM],
        out_specs=IN_HBM,
    )(table, wanted)
    found, mesh_senders, edge_mask = lax.optimization_barrier((found, mesh_senders, edge_mask))
    replies = exchange(found, ("sub", "dom"))
    mesh_code = (
        jnp.where(edge_mask != 0, mesh_senders, -1)
        .reshape(node_count, DEGREE)
        .T.reshape(DEGREE, 1, node_count)
    )
    contact_dst = contact_dst.reshape(wides, 1, WIDE)
    contact_mask = contact_mask.reshape(wides, 1, WIDE)
    mesh_rows = HID + GATES
    recv_rows = FEAT + 16 + CS
    mesh_agg, mesh_grads, recv, contact_code = call(
        mesh_kernel,
        (
            pltpu.HBM((FEAT, node_count), f32),
            pltpu.HBM((mesh_rows, 2 * LANES), f32),
            pltpu.HBM((wides, recv_rows, WIDE), bf16),
            pltpu.HBM((wides, 1, WIDE), jnp.int32),
        ),
        (
            pltpu.VMEM((FEAT, node_count), f32),
            pltpu.VMEM((mesh_rows, 2 * LANES), f32),
            pltpu.VMEM((wides, recv_rows, WIDE), bf16),
            pltpu.VMEM((recv_rows, node_count), bf16),
            pltpu.VMEM((ROWS, 3 * node_count), bf16),
            pltpu.VMEM((FEAT, FEAT), bf16),
            pltpu.VMEM((wides, 1, WIDE), jnp.int32),
            pltpu.SemaphoreType.DMA((4,)),
        ),
        in_specs=[IN_VMEM] * 14,
        out_specs=(IN_HBM,) * 4,
        cost_estimate=pl.CostEstimate(
            flops=40_000_000_000, bytes_accessed=8_000_000, transcendentals=400_000
        ),
    )(
        table,
        low,
        high,
        mesh_code,
        node_cot,
        w_one,
        b_one[None],
        w_dist[None],
        w_two,
        w_scal,
        w_vec,
        w_ten,
        contact_dst,
        contact_mask,
    )
    packed_rows = mesh_rows + CS + 16
    agg_rows, packed = call(
        functools.partial(contact_kernel, slot, lax.axis_size("dom"), grad_scale),
        (shaped((FEAT, node_count), bf16), shaped((device_count, 16, LANES), bf16)),
        (
            pltpu.VMEM((wides, 1, WIDE), jnp.int32),
            pltpu.VMEM((wides, recv_rows, WIDE), bf16),
            pltpu.VMEM((FEAT, node_count), f32),
            pltpu.VMEM((mesh_rows, 2 * LANES), f32),
            pltpu.VMEM((HID, 2 * CS), bf16),
            pltpu.VMEM((GATES, HID), bf16),
            pltpu.VMEM((1, HID), f32),
            pltpu.VMEM((1, HID), f32),
            pltpu.VMEM((wides, ROWS, WIDE), bf16),
            pltpu.VMEM((packed_rows, LANES), f32),
            pltpu.VMEM((HID, LANES), f32),
            pltpu.VMEM((HID, LANES), f32),
            pltpu.VMEM((2 * CS + 16, WIDE), bf16),
            pltpu.VMEM((HID, WIDE), f32),
            pltpu.VMEM((HID, WIDE), f32),
            pltpu.VMEM((HID, WIDE), bf16),
            pltpu.VMEM((GATES, WIDE), f32),
            pltpu.VMEM((FEAT, WIDE), bf16),
            pltpu.VMEM((GATES, WIDE), bf16),
            pltpu.VMEM((HID, WIDE), bf16),
            pltpu.SemaphoreType.DMA((wides + 7,)),
        ),
        in_specs=[IN_VMEM] * 2 + [IN_HBM] * 8,
        out_specs=(IN_VMEM, IN_VMEM),
    )(
        replies,
        node_cot,
        *in_hbm(
            contact_code, recv, mesh_agg, mesh_grads, w_one, w_two, b_one[None], w_dist[None]
        ),
    )
    shares = call(sum_kernel, shaped((device_count, 16, LANES), bf16))(exchange(packed))
    node_out, one, bias, dist, two, scal, vec, ten = call(
        finish_kernel,
        (
            shaped((FEAT, node_count), bf16),
            shaped((HID, 2 * CS), f32),
            shaped((1, HID), f32),
            shaped((1, HID), f32),
            shaped((GATES, HID), f32),
            shaped((CS, CS), f32),
            shaped((CV, CV), f32),
            shaped((CT, CT), f32),
        ),
        (pltpu.VMEM((FEAT, FEAT), bf16),),
    )(exchange(shares), table, agg_rows, w_scal, w_vec, w_ten)
    return node_out, one, bias[0], dist[0], two, scal, vec, ten


def solution(mesh):
    along = P(("dom", "sub"))
    columns = P(None, ("dom", "sub"))
    in_specs = (columns,) * 3 + (along,) * 7 + (P(),) * 7
    out_specs = (columns,) + (P(),) * 7
    return jax.shard_map(
        on_device, mesh=mesh, in_specs=in_specs, out_specs=out_specs, check_vma=False
    )
```

```python
import functools
import math

import jax
import jax.numpy as jnp
from jax import lax
from jax.experimental import pallas as pl
from jax.experimental.pallas import tpu as pltpu
from jax.sharding import PartitionSpec as P

CS = 64
CV = 32
CT = 16
HID = 128
DEGREE = 6
GATES = 144
FEAT = CS + 3 * CV + 9 * CT
ROWS = 320
LANES = 128
FINE = 4
CHUNK = 512
WIDE = 1024
VMEM_BYTES = 48 * 1024 * 1024


def dot(lhs, rhs, lhs_dim=1, rhs_dim=0):
    return lax.dot_general(
        lhs, rhs, (((lhs_dim,), (rhs_dim,)), ((), ())), preferred_element_type=jnp.float32
    )


def one_hot(code, width):
    rows = lax.broadcasted_iota(jnp.int16, (width, code.shape[1]), 0)
    return jnp.where(rows == code.astype(jnp.int16), jnp.bfloat16(1), jnp.bfloat16(0))


def join_index(table, row):
    pair = table[row : row + 2].astype(jnp.float32)
    return (pair[0:1] * 128.0 + pair[1:2]).astype(jnp.int32)


def table_kernel(
    feat_ref,
    pos_ref,
    up_ref,
    down_ref,
    rows_ref,
    table_ref,
    request_ref,
    pos_scr,
    up_scr,
    down_scr,
    rows_scr,
    sems,
):
    node_count = table_ref.shape[1]
    copies = [
        pltpu.make_async_copy(rows_ref, rows_scr, sems.at[0]),
        pltpu.make_async_copy(feat_ref, table_ref.at[:FEAT], sems.at[1]),
        pltpu.make_async_copy(pos_ref, pos_scr, sems.at[2]),
        pltpu.make_async_copy(up_ref, up_scr, sems.at[3]),
        pltpu.make_async_copy(down_ref, down_scr, sems.at[4]),
    ]
    for copy in copies:
        copy.start()
    copies[0].wait()
    slot = request_ref.shape[2]
    parts = LANES // slot
    for row in range(rows_scr.shape[0]):
        line = rows_scr[row : row + 1]
        for part in range(parts):
            request_ref[row * parts + part] = line[:, part * slot : (part + 1) * slot]
    for copy in copies[2:]:
        copy.wait()
    rows = lax.broadcasted_iota(jnp.int32, (ROWS - FEAT, node_count), 0)
    pos = pos_scr[...].astype(jnp.float32)
    tail = jnp.zeros((ROWS - FEAT, node_count), jnp.float32)
    for k in range(3):
        tail = jnp.where(rows == k, pos[k : k + 1], tail)
    for k, index_ref in ((3, up_scr), (5, down_scr)):
        index = index_ref[...]
        high = index >> 7
        tail = jnp.where(rows == k, high.astype(jnp.float32), tail)
        tail = jnp.where(rows == k + 1, (index - (high << 7)).astype(jnp.float32), tail)
    table_ref[FEAT:] = tail.astype(jnp.bfloat16)
    copies[1].wait()


def contact_gather_kernel(slot, table_ref, wanted_ref, out_hbm, out_ref, sems):
    node_count = table_ref.shape[1]
    parts = LANES // slot
    height = out_ref.shape[1]
    per_chunk = CHUNK // slot
    copies = []
    for chunk in range(wanted_ref.shape[0] // per_chunk):
        wanted = [wanted_ref[chunk * per_chunk + peer] for peer in range(per_chunk)]
        hot = one_hot(jnp.concatenate(wanted, 1), node_count)
        rows = dot(table_ref[...], hot).astype(jnp.bfloat16)
        if parts * height > ROWS:
            rows = jnp.concatenate(
                [rows, jnp.zeros((parts * height - ROWS, CHUNK), jnp.bfloat16)], 0
            )
        for peer in range(per_chunk):
            out_ref[chunk * per_chunk + peer] = jnp.concatenate(
                [
                    rows[part * height : (part + 1) * height, peer * slot : (peer + 1) * slot]
                    for part in range(parts)
                ],
                1,
            )
        done = pl.ds(chunk * per_chunk, per_chunk)
        copies.append(
            pltpu.make_async_copy(out_ref.at[done], out_hbm.at[done], sems.at[chunk])
        )
        copies[-1].start()
    for copy in copies:
        copy.wait()


def edge_math(src, base, first, inputs, pos_recv, back, live, weights):
    w_dist, w_two, w_two_t = weights
    edges = src.shape[1]
    offset = src[FEAT : FEAT + 3] - pos_recv
    if live is not None:
        offset = offset * live
    distance = jnp.sum(offset * offset, 0, keepdims=True)
    linear = base + first + w_dist * distance
    squashed = 0.5 * jnp.tanh(0.5 * linear) + 0.5
    hidden = (linear * squashed).astype(jnp.bfloat16)
    gates = dot(w_two, hidden)
    gate_vec = gates[CS : CS + CV]
    gate_dir = gates[CS + CV : CS + 2 * CV]
    gate_ten = gates[CS + 2 * CV :]
    message = [gates[:CS] * src[:CS]]
    vec_part = jnp.zeros((CV, edges), jnp.float32)
    dir_part = jnp.zeros((CV, edges), jnp.float32)
    for k in range(3):
        rows = slice(CS + k * CV, CS + (k + 1) * CV)
        message.append(gate_vec * src[rows] + gate_dir * offset[k : k + 1])
        vec_part = vec_part + back[rows] * src[rows]
        dir_part = dir_part + back[rows] * offset[k : k + 1]
    ten_part = jnp.zeros((CT, edges), jnp.float32)
    for m in range(9):
        rows = slice(CS + 3 * CV + m * CT, CS + 3 * CV + (m + 1) * CT)
        message.append(gate_ten * src[rows])
        ten_part = ten_part + back[rows] * src[rows]
    message = jnp.concatenate(message, 0)
    dgates = jnp.concatenate([back[:CS] * src[:CS], vec_part, dir_part, ten_part], 0).astype(
        jnp.bfloat16
    )
    hidden_grad = dot(w_two_t, dgates)
    linear_grad = (hidden_grad * squashed * (1.0 + linear * (1.0 - squashed))).astype(jnp.bfloat16)
    rows = lax.broadcasted_iota(jnp.int32, (16, edges), 0)
    coarse = distance.astype(jnp.bfloat16).astype(jnp.float32)
    extra = jnp.where(
        rows == 0, 1.0, jnp.where(rows == 1, coarse, jnp.where(rows == 2, distance - coarse, 0.0))
    ).astype(jnp.bfloat16)
    grads = (
        dot(linear_grad, jnp.concatenate([inputs, extra], 0), 1, 1),
        dot(dgates, hidden, 1, 1),
    )
    return message, grads


def as_columns(first_row, second_row):
    rows = lax.broadcasted_iota(jnp.int32, (LANES, LANES), 0)
    columns = jnp.where(rows == 0, first_row, jnp.where(rows == 1, second_row, 0.0)).T
    return columns[:, 0:1], columns[:, 1:2]


def add_grads(grads_ref, grads):
    grads_ref[:HID, : 2 * CS + 16] += grads[0]
    grads_ref[HID:, :HID] += grads[1]


def block_diagonal(block_ref, w_scal, w_vec, w_ten):
    block_ref[...] = jnp.zeros_like(block_ref)
    block_ref[:CS, :CS] = w_scal[...]
    for k in range(3):
        rows = slice(CS + k * CV, CS + (k + 1) * CV)
        block_ref[rows, rows] = w_vec[...]
    for m in range(9):
        rows = slice(CS + 3 * CV + m * CT, CS + 3 * CV + (m + 1) * CT)
        block_ref[rows, rows] = w_ten[...]


def mesh_kernel(
    table_ref,
    low_ref,
    high_ref,
    code_ref,
    cot_ref,
    w_one_ref,
    b_one_ref,
    w_dist_ref,
    w_two_ref,
    w_scal_ref,
    w_vec_ref,
    w_ten_ref,
    dst_ref,
    mask_ref,
    agg_out_ref,
    grads_out_ref,
    recv_out_ref,
    code_out_ref,
    agg_ref,
    grads_ref,
    recv_ref,
    receive_ref,
    source_ref,
    block_ref,
    contact_ref,
    sems,
):
    node_count = table_ref.shape[1]
    source_ref[:, :node_count] = table_ref[...]
    low = low_ref[...]
    high = high_ref[...]
    source_ref[:, node_count : 2 * node_count] = dot(
        low, one_hot(join_index(low, FEAT + 3), node_count)
    ).astype(jnp.bfloat16)
    source_ref[:, 2 * node_count :] = dot(
        high, one_hot(join_index(high, FEAT + 5), node_count)
    ).astype(jnp.bfloat16)
    block_diagonal(block_ref, w_scal_ref, w_vec_ref, w_ten_ref)
    receive_ref[:FEAT] = dot(block_ref[...], cot_ref[...], 0, 0).astype(jnp.bfloat16)
    receive_ref[FEAT : FEAT + 16] = table_ref[FEAT:]
    receive_ref[FEAT + 16 :] = table_ref[:CS]
    w_one = w_one_ref[...]
    w_two = w_two_ref[...]
    b_column, dist_column = as_columns(b_one_ref[...], w_dist_ref[...])
    scal_recv = table_ref[:CS]
    recv_linear = dot(w_one[:, :CS], scal_recv) + b_column
    weights = (dist_column, w_two, w_two.T)
    pos_recv = table_ref[FEAT:].astype(jnp.float32)[:3]
    grads_ref[...] = jnp.zeros_like(grads_ref)
    agg_ref[...] = jnp.zeros_like(agg_ref)
    for step in range(DEGREE):
        code = code_ref[step]
        src = dot(source_ref[...], one_hot(code, 3 * node_count))
        live = jnp.where(code >= 0, 1.0, 0.0)
        back = receive_ref[:FEAT].astype(jnp.float32)
        scal_send = src[:CS].astype(jnp.bfloat16)
        inputs = jnp.concatenate([scal_recv, scal_send], 0)
        message, grads = edge_math(
            src, recv_linear, dot(w_one[:, CS:], scal_send), inputs, pos_recv, back, live, weights
        )
        agg_ref[...] += message
        add_grads(grads_ref, grads)
    contact_ref[...] = jnp.where(mask_ref[...] != 0, dst_ref[...], -1)
    for chunk in range(contact_ref.shape[0]):
        recv_ref[chunk] = dot(
            receive_ref[...], one_hot(contact_ref[chunk], node_count)
        ).astype(jnp.bfloat16)
    copies = [
        pltpu.make_async_copy(agg_ref, agg_out_ref, sems.at[0]),
        pltpu.make_async_copy(grads_ref, grads_out_ref, sems.at[1]),
        pltpu.make_async_copy(recv_ref, recv_out_ref, sems.at[2]),
        pltpu.make_async_copy(contact_ref, code_out_ref, sems.at[3]),
    ]
    for copy in copies:
        copy.start()
    for copy in copies:
        copy.wait()


def contact_kernel(
    slot,
    grad_scale,
    reply_ref,
    cot_ref,
    code_hbm,
    recv_hbm,
    mesh_agg_hbm,
    mesh_grads_hbm,
    w_one_hbm,
    w_two_hbm,
    b_one_hbm,
    w_dist_hbm,
    agg_out_ref,
    packed_ref,
    code_ref,
    recv_ref,
    agg_ref,
    grads_ref,
    w_one_ref,
    w_two_ref,
    b_one_ref,
    w_dist_ref,
    src_scr,
    packed_scr,
    sems,
):
    chunks = code_ref.shape[0]
    sources = [
        (b_one_hbm, b_one_ref),
        (w_dist_hbm, w_dist_ref),
        (w_one_hbm, w_one_ref),
        (w_two_hbm, w_two_ref),
        (code_hbm, code_ref),
    ]
    sources += [(recv_hbm.at[chunk], recv_ref.at[chunk]) for chunk in range(chunks)]
    sources += [(mesh_agg_hbm, agg_ref), (mesh_grads_hbm, grads_ref)]
    copies = [
        pltpu.make_async_copy(source, target, sems.at[at])
        for at, (source, target) in enumerate(sources)
    ]
    for copy in copies:
        copy.start()
    node_count = cot_ref.shape[1]
    parts = LANES // slot
    per_chunk = WIDE // slot
    for chunk in range(chunks):
        blocks = [reply_ref[chunk * per_chunk + peer] for peer in range(per_chunk)]
        src_scr[chunk] = jnp.concatenate(
            [
                jnp.concatenate(
                    [block[:, part * slot : (part + 1) * slot] for block in blocks], 1
                )
                for part in range(parts)
            ],
            0,
        )[:ROWS]
    for copy in copies[:6]:
        copy.wait()
    w_one = w_one_ref[...]
    w_two = w_two_ref[...]
    b_column, dist_column = as_columns(b_one_ref[...], w_dist_ref[...])
    weights = (dist_column, w_two, w_two.T)
    for chunk in range(chunks):
        src_rows = src_scr[chunk]
        if chunk == 1:
            for copy in copies[6:]:
                copy.wait()
        recv = recv_ref[chunk]
        inputs = jnp.concatenate([recv[FEAT + 16 :], src_rows[:CS]], 0)
        message, grads = edge_math(
            src_rows.astype(jnp.float32),
            b_column,
            dot(w_one, inputs),
            inputs,
            recv[FEAT : FEAT + 16].astype(jnp.float32)[:3],
            recv[:FEAT].astype(jnp.float32),
            None,
            weights,
        )
        scattered = dot(message.astype(jnp.bfloat16), one_hot(code_ref[chunk], node_count), 1, 1)
        if chunk == 0:
            held = (scattered, grads)
            continue
        agg_ref[...] += scattered
        add_grads(grads_ref, grads)
        if chunk == 1:
            agg_ref[...] += held[0]
            add_grads(grads_ref, held[1])
    agg_rows = agg_ref[...].astype(jnp.bfloat16)
    agg_out_ref[...] = agg_rows
    cot = cot_ref[...]
    low = HID + GATES
    packed_scr[:low] = grads_ref[:, :LANES] * grad_scale
    packed_scr[low : low + CS] = jnp.concatenate(
        [
            dot(cot[:CS], agg_rows[:CS], 1, 1) * grad_scale,
            jnp.zeros((CS, LANES - CS), jnp.float32),
        ],
        1,
    )
    mixed = dot(cot[CS:], agg_rows[CS:], 1, 1)
    grad_vec = jnp.zeros((CV, CV), jnp.float32)
    for k in range(3):
        rows = slice(k * CV, (k + 1) * CV)
        grad_vec = grad_vec + mixed[rows, rows]
    packed_scr[low : low + CV, CS : CS + CV] = grad_vec * grad_scale
    grad_ten = jnp.zeros((CT, CT), jnp.float32)
    for m in range(9):
        rows = slice(3 * CV + m * CT, 3 * CV + (m + 1) * CT)
        grad_ten = grad_ten + mixed[rows, rows]
    packed_scr[low : low + CT, CS + CV : CS + CV + CT] = grad_ten * grad_scale
    extra = (grads_ref[:HID, LANES:] * grad_scale).T[:16]
    rows = lax.broadcasted_iota(jnp.int32, (16, LANES), 0)
    packed_scr[low + CS :] = jnp.where(rows == 1, extra[1:2] + extra[2:3], extra)
    packed = packed_scr[...].astype(jnp.bfloat16)
    tiles = packed_ref.shape[1]
    for peer in range(packed_ref.shape[0]):
        for tile in range(tiles):
            at = (peer * tiles + tile) * FINE
            if at < packed.shape[0]:
                packed_ref[peer, tile] = packed[at : at + FINE]
            else:
                packed_ref[peer, tile] = jnp.zeros((FINE, LANES), jnp.bfloat16)


def sum_kernel(parts_ref, out_ref):
    total = parts_ref[0].astype(jnp.float32)
    for peer in range(1, parts_ref.shape[0]):
        total = total + parts_ref[peer].astype(jnp.float32)
    total = total.astype(jnp.bfloat16)
    for peer in range(out_ref.shape[0]):
        out_ref[peer] = total


def finish_kernel(
    blocks_ref,
    table_ref,
    agg_ref,
    w_scal_ref,
    w_vec_ref,
    w_ten_ref,
    out_ref,
    one_ref,
    bias_ref,
    dist_ref,
    two_ref,
    scal_ref,
    vec_ref,
    ten_ref,
    block_ref,
):
    block_diagonal(block_ref, w_scal_ref, w_vec_ref, w_ten_ref)
    out_ref[...] = (
        table_ref[:FEAT].astype(jnp.float32) + dot(block_ref[...], agg_ref[...])
    ).astype(jnp.bfloat16)

    tiles = blocks_ref.shape[1]

    def rows_of(at):
        peer, tile = divmod(at // FINE, tiles)
        return blocks_ref[peer, tile].astype(jnp.float32)

    for at in range(0, HID, FINE):
        one_ref[at : at + FINE] = rows_of(at)
    for at in range(0, GATES, FINE):
        two_ref[at : at + FINE] = rows_of(HID + at)
    low = HID + GATES
    for at in range(0, CS, FINE):
        rows = rows_of(low + at)
        scal_ref[at : at + FINE] = rows[:, :CS]
        if at < CV:
            vec_ref[at : at + FINE] = rows[:, CS : CS + CV]
        if at < CT:
            ten_ref[at : at + FINE] = rows[:, CS + CV : CS + CV + CT]
    extra = rows_of(low + CS)
    bias_ref[...] = extra[0:1]
    dist_ref[...] = extra[1:2]


def call(kernel, out_shape, scratch=(), in_specs=None, out_specs=None, cost_estimate=None):
    specs = {}
    if cost_estimate is not None:
        specs["cost_estimate"] = cost_estimate
    if in_specs is not None:
        specs["in_specs"] = in_specs
    if out_specs is not None:
        specs["out_specs"] = out_specs
    return pl.pallas_call(
        kernel,
        out_shape=out_shape,
        scratch_shapes=list(scratch),
        compiler_params=pltpu.CompilerParams(vmem_limit_bytes=VMEM_BYTES),
        **specs,
    )


IN_VMEM = pl.BlockSpec(memory_space=pltpu.VMEM)
IN_HBM = pl.BlockSpec(memory_space=pltpu.HBM)
ANYWHERE = pl.BlockSpec(memory_space=pl.ANY)


def exchange(blocks, axes=("dom", "sub")):
    return lax.all_to_all(blocks, axes, split_axis=0, concat_axis=0, tiled=True)


def in_hbm(*arrays):
    return tuple(pltpu.with_memory_space_constraint(array, pltpu.HBM) for array in arrays)


def shaped(shape, dtype):
    return jax.ShapeDtypeStruct(shape, dtype)


def from_behind(shard, axis, by):
    peers = lax.axis_size(axis)
    return lax.ppermute(shard, axis, [(i, (i + by) % peers) for i in range(peers)])


def on_device(
    node_feat,
    node_pos,
    node_cot,
    mesh_senders,
    edge_mask,
    halo_up,
    halo_down,
    contact_rows,
    contact_dst,
    contact_mask,
    w_one,
    b_one,
    w_dist,
    w_two,
    w_scal,
    w_vec,
    w_ten,
):
    f32, bf16 = jnp.float32, jnp.bfloat16
    node_count = node_feat.shape[1]
    contact_count = contact_rows.shape[0]
    device_count = lax.axis_size("dom") * lax.axis_size("sub")
    slot = contact_count // device_count
    chunks = contact_count // CHUNK
    wides = contact_count // WIDE
    parts = LANES // slot
    height = -(-ROWS // (parts * 16)) * 16
    grad_scale = 1.0 / math.sqrt(device_count * node_count * DEGREE)
    table, requests = call(
        table_kernel,
        (
            shaped((ROWS, node_count), bf16),
            shaped((device_count, 1, slot), jnp.int32),
        ),
        (
            pltpu.VMEM((3, node_count), bf16),
            pltpu.VMEM((1, node_count), jnp.int32),
            pltpu.VMEM((1, node_count), jnp.int32),
            pltpu.VMEM((contact_count // LANES, LANES), jnp.int32),
            pltpu.SemaphoreType.DMA((5,)),
        ),
        in_specs=[IN_HBM] * 5,
        out_specs=(IN_VMEM, IN_VMEM),
    )(
        *in_hbm(
            node_feat,
            node_pos,
            halo_up[None],
            halo_down[None],
            contact_rows.reshape(contact_count // LANES, LANES),
        )
    )
    wanted = exchange(requests)
    wanted, table_late = lax.optimization_barrier((wanted, table))
    low = from_behind(table_late, "sub", 1)
    high = from_behind(table_late, "sub", -1)
    found = call(
        functools.partial(contact_gather_kernel, slot),
        pltpu.HBM((device_count, height, LANES), bf16),
        (
            pltpu.VMEM((device_count, height, LANES), bf16),
            pltpu.SemaphoreType.DMA((chunks,)),
        ),
        in_specs=[IN_VMEM, IN_VMEM],
        out_specs=IN_HBM,
    )(table, wanted)
    found, mesh_senders, edge_mask = lax.optimization_barrier((found, mesh_senders, edge_mask))
    replies = exchange(found)
    mesh_code = (
        jnp.where(edge_mask != 0, mesh_senders, -1)
        .reshape(node_count, DEGREE)
        .T.reshape(DEGREE, 1, node_count)
    )
    contact_dst = contact_dst.reshape(wides, 1, WIDE)
    contact_mask = contact_mask.reshape(wides, 1, WIDE)
    mesh_rows = HID + GATES
    recv_rows = FEAT + 16 + CS
    mesh_agg, mesh_grads, recv, contact_code = call(
        mesh_kernel,
        (
            pltpu.HBM((FEAT, node_count), f32),
            pltpu.HBM((mesh_rows, 2 * LANES), f32),
            pltpu.HBM((wides, recv_rows, WIDE), bf16),
            pltpu.HBM((wides, 1, WIDE), jnp.int32),
        ),
        (
            pltpu.VMEM((FEAT, node_count), f32),
            pltpu.VMEM((mesh_rows, 2 * LANES), f32),
            pltpu.VMEM((wides, recv_rows, WIDE), bf16),
            pltpu.VMEM((recv_rows, node_count), bf16),
            pltpu.VMEM((ROWS, 3 * node_count), bf16),
            pltpu.VMEM((FEAT, FEAT), bf16),
            pltpu.VMEM((wides, 1, WIDE), jnp.int32),
            pltpu.SemaphoreType.DMA((4,)),
        ),
        in_specs=[IN_VMEM] * 14,
        out_specs=(IN_HBM,) * 4,
        cost_estimate=pl.CostEstimate(
            flops=40_000_000_000, bytes_accessed=8_000_000, transcendentals=400_000
        ),
    )(
        table,
        low,
        high,
        mesh_code,
        node_cot,
        w_one,
        b_one[None],
        w_dist[None],
        w_two,
        w_scal,
        w_vec,
        w_ten,
        contact_dst,
        contact_mask,
    )
    packed_rows = mesh_rows + CS + 16
    tiles = -(-packed_rows // (FINE * device_count))
    share = (device_count, tiles, FINE, LANES)
    agg_rows, packed = call(
        functools.partial(contact_kernel, slot, grad_scale),
        (shaped((FEAT, node_count), bf16), shaped(share, bf16)),
        (
            pltpu.VMEM((wides, 1, WIDE), jnp.int32),
            pltpu.VMEM((wides, recv_rows, WIDE), bf16),
            pltpu.VMEM((FEAT, node_count), f32),
            pltpu.VMEM((mesh_rows, 2 * LANES), f32),
            pltpu.VMEM((HID, 2 * CS), bf16),
            pltpu.VMEM((GATES, HID), bf16),
            pltpu.VMEM((1, HID), f32),
            pltpu.VMEM((1, HID), f32),
            pltpu.VMEM((wides, ROWS, WIDE), bf16),
            pltpu.VMEM((packed_rows, LANES), f32),
            pltpu.SemaphoreType.DMA((wides + 7,)),
        ),
        in_specs=[IN_VMEM] * 2 + [IN_HBM] * 8,
        out_specs=(IN_VMEM, IN_VMEM),
    )(
        replies,
        node_cot,
        *in_hbm(
            contact_code, recv, mesh_agg, mesh_grads, w_one, w_two, b_one[None], w_dist[None]
        ),
    )
    shares = call(sum_kernel, shaped(share, bf16))(exchange(packed))
    node_out, one, bias, dist, two, scal, vec, ten = call(
        finish_kernel,
        (
            shaped((FEAT, node_count), bf16),
            shaped((HID, 2 * CS), f32),
            shaped((1, HID), f32),
            shaped((1, HID), f32),
            shaped((GATES, HID), f32),
            shaped((CS, CS), f32),
            shaped((CV, CV), f32),
            shaped((CT, CT), f32),
        ),
        (pltpu.VMEM((FEAT, FEAT), bf16),),
    )(exchange(shares), table, agg_rows, w_scal, w_vec, w_ten)
    return node_out, one, bias[0], dist[0], two, scal, vec, ten


def solution(mesh):
    along = P(("dom", "sub"))
    columns = P(None, ("dom", "sub"))
    in_specs = (columns,) * 3 + (along,) * 7 + (P(),) * 7
    out_specs = (columns,) + (P(),) * 7
    return jax.shard_map(
        on_device, mesh=mesh, in_specs=in_specs, out_specs=out_specs, check_vma=False
    )
```

```python
import functools
import math

import jax
import jax.numpy as jnp
from jax import lax
from jax.experimental import pallas as pl
from jax.experimental.pallas import tpu as pltpu
from jax.sharding import PartitionSpec as P

CS = 64
CV = 32
CT = 16
HID = 128
DEGREE = 6
GATES = 144
FEAT = CS + 3 * CV + 9 * CT
ROWS = 320
LANES = 128
FINE = 2
CHUNK = 512
WIDE = 1024
VMEM_BYTES = 48 * 1024 * 1024


def dot(lhs, rhs, lhs_dim=1, rhs_dim=0):
    return lax.dot_general(
        lhs, rhs, (((lhs_dim,), (rhs_dim,)), ((), ())), preferred_element_type=jnp.float32
    )


def one_hot(code, width):
    rows = lax.broadcasted_iota(jnp.int16, (width, code.shape[1]), 0)
    return jnp.where(rows == code.astype(jnp.int16), jnp.bfloat16(1), jnp.bfloat16(0))


def join_index(table, row):
    pair = table[row : row + 2].astype(jnp.float32)
    return (pair[0:1] * 128.0 + pair[1:2]).astype(jnp.int32)


def table_kernel(
    feat_ref,
    pos_ref,
    up_ref,
    down_ref,
    rows_ref,
    table_ref,
    request_ref,
    pos_scr,
    up_scr,
    down_scr,
    rows_scr,
    sems,
):
    node_count = table_ref.shape[1]
    copies = [
        pltpu.make_async_copy(rows_ref, rows_scr, sems.at[0]),
        pltpu.make_async_copy(feat_ref, table_ref.at[:FEAT], sems.at[1]),
        pltpu.make_async_copy(pos_ref, pos_scr, sems.at[2]),
        pltpu.make_async_copy(up_ref, up_scr, sems.at[3]),
        pltpu.make_async_copy(down_ref, down_scr, sems.at[4]),
    ]
    for copy in copies:
        copy.start()
    copies[0].wait()
    slot = request_ref.shape[2]
    parts = LANES // slot
    for row in range(rows_scr.shape[0]):
        line = rows_scr[row : row + 1]
        for part in range(parts):
            request_ref[row * parts + part] = line[:, part * slot : (part + 1) * slot]
    for copy in copies[2:]:
        copy.wait()
    rows = lax.broadcasted_iota(jnp.int32, (ROWS - FEAT, node_count), 0)
    pos = pos_scr[...].astype(jnp.float32)
    tail = jnp.zeros((ROWS - FEAT, node_count), jnp.float32)
    for k in range(3):
        tail = jnp.where(rows == k, pos[k : k + 1], tail)
    for k, index_ref in ((3, up_scr), (5, down_scr)):
        index = index_ref[...]
        high = index >> 7
        tail = jnp.where(rows == k, high.astype(jnp.float32), tail)
        tail = jnp.where(rows == k + 1, (index - (high << 7)).astype(jnp.float32), tail)
    table_ref[FEAT:] = tail.astype(jnp.bfloat16)
    copies[1].wait()


def contact_gather_kernel(slot, table_ref, wanted_ref, out_hbm, out_ref, sems):
    node_count = table_ref.shape[1]
    parts = LANES // slot
    height = out_ref.shape[1]
    per_chunk = CHUNK // slot
    copies = []
    for chunk in range(wanted_ref.shape[0] // per_chunk):
        wanted = [wanted_ref[chunk * per_chunk + peer] for peer in range(per_chunk)]
        hot = one_hot(jnp.concatenate(wanted, 1), node_count)
        rows = dot(table_ref[...], hot).astype(jnp.bfloat16)
        if parts * height > ROWS:
            rows = jnp.concatenate(
                [rows, jnp.zeros((parts * height - ROWS, CHUNK), jnp.bfloat16)], 0
            )
        for peer in range(per_chunk):
            out_ref[chunk * per_chunk + peer] = jnp.concatenate(
                [
                    rows[part * height : (part + 1) * height, peer * slot : (peer + 1) * slot]
                    for part in range(parts)
                ],
                1,
            )
        done = pl.ds(chunk * per_chunk, per_chunk)
        copies.append(
            pltpu.make_async_copy(out_ref.at[done], out_hbm.at[done], sems.at[chunk])
        )
        copies[-1].start()
    for copy in copies:
        copy.wait()


def edge_math(src, base, first, inputs, pos_recv, back, live, weights):
    w_dist, w_two, w_two_t = weights
    edges = src.shape[1]
    offset = src[FEAT : FEAT + 3] - pos_recv
    if live is not None:
        offset = offset * live
    distance = jnp.sum(offset * offset, 0, keepdims=True)
    linear = base + first + w_dist * distance
    squashed = 0.5 * jnp.tanh(0.5 * linear) + 0.5
    hidden = (linear * squashed).astype(jnp.bfloat16)
    gates = dot(w_two, hidden)
    gate_vec = gates[CS : CS + CV]
    gate_dir = gates[CS + CV : CS + 2 * CV]
    gate_ten = gates[CS + 2 * CV :]
    message = [gates[:CS] * src[:CS]]
    vec_part = jnp.zeros((CV, edges), jnp.float32)
    dir_part = jnp.zeros((CV, edges), jnp.float32)
    for k in range(3):
        rows = slice(CS + k * CV, CS + (k + 1) * CV)
        message.append(gate_vec * src[rows] + gate_dir * offset[k : k + 1])
        vec_part = vec_part + back[rows] * src[rows]
        dir_part = dir_part + back[rows] * offset[k : k + 1]
    ten_part = jnp.zeros((CT, edges), jnp.float32)
    for m in range(9):
        rows = slice(CS + 3 * CV + m * CT, CS + 3 * CV + (m + 1) * CT)
        message.append(gate_ten * src[rows])
        ten_part = ten_part + back[rows] * src[rows]
    message = jnp.concatenate(message, 0)
    dgates = jnp.concatenate([back[:CS] * src[:CS], vec_part, dir_part, ten_part], 0).astype(
        jnp.bfloat16
    )
    hidden_grad = dot(w_two_t, dgates)
    linear_grad = (hidden_grad * squashed * (1.0 + linear * (1.0 - squashed))).astype(jnp.bfloat16)
    rows = lax.broadcasted_iota(jnp.int32, (16, edges), 0)
    coarse = distance.astype(jnp.bfloat16).astype(jnp.float32)
    extra = jnp.where(
        rows == 0, 1.0, jnp.where(rows == 1, coarse, jnp.where(rows == 2, distance - coarse, 0.0))
    ).astype(jnp.bfloat16)
    grads = (
        dot(linear_grad, jnp.concatenate([inputs, extra], 0), 1, 1),
        dot(dgates, hidden, 1, 1),
    )
    return message, grads


def as_columns(first_row, second_row):
    rows = lax.broadcasted_iota(jnp.int32, (LANES, LANES), 0)
    columns = jnp.where(rows == 0, first_row, jnp.where(rows == 1, second_row, 0.0)).T
    return columns[:, 0:1], columns[:, 1:2]


def add_grads(grads_ref, grads):
    grads_ref[:HID, : 2 * CS + 16] += grads[0]
    grads_ref[HID:, :HID] += grads[1]


def block_diagonal(block_ref, w_scal, w_vec, w_ten):
    block_ref[...] = jnp.zeros_like(block_ref)
    block_ref[:CS, :CS] = w_scal[...]
    for k in range(3):
        rows = slice(CS + k * CV, CS + (k + 1) * CV)
        block_ref[rows, rows] = w_vec[...]
    for m in range(9):
        rows = slice(CS + 3 * CV + m * CT, CS + 3 * CV + (m + 1) * CT)
        block_ref[rows, rows] = w_ten[...]


def mesh_kernel(
    table_ref,
    low_ref,
    high_ref,
    code_ref,
    cot_ref,
    w_one_ref,
    b_one_ref,
    w_dist_ref,
    w_two_ref,
    w_scal_ref,
    w_vec_ref,
    w_ten_ref,
    dst_ref,
    mask_ref,
    agg_out_ref,
    grads_out_ref,
    recv_out_ref,
    first_out_ref,
    code_out_ref,
    layers_out_ref,
    rows_out_ref,
    agg_ref,
    grads_ref,
    recv_ref,
    receive_ref,
    source_ref,
    block_ref,
    sems,
):
    node_count = table_ref.shape[1]
    source_ref[:, :node_count] = table_ref[...]
    low = low_ref[...]
    high = high_ref[...]
    source_ref[:, node_count : 2 * node_count] = dot(
        low, one_hot(join_index(low, FEAT + 3), node_count)
    ).astype(jnp.bfloat16)
    source_ref[:, 2 * node_count :] = dot(
        high, one_hot(join_index(high, FEAT + 5), node_count)
    ).astype(jnp.bfloat16)
    block_diagonal(block_ref, w_scal_ref, w_vec_ref, w_ten_ref)
    receive_ref[:FEAT] = dot(block_ref[...], cot_ref[...], 0, 0).astype(jnp.bfloat16)
    receive_ref[FEAT : FEAT + 16] = table_ref[FEAT:]
    receive_ref[FEAT + 16 :] = table_ref[:CS]
    w_one = w_one_ref[...]
    w_two = w_two_ref[...]
    b_column, dist_column = as_columns(b_one_ref[...], w_dist_ref[...])
    scal_recv = table_ref[:CS]
    recv_linear = dot(w_one[:, :CS], scal_recv) + b_column
    weights = (dist_column, w_two, w_two.T)
    pos_recv = table_ref[FEAT:].astype(jnp.float32)[:3]
    grads_ref[...] = jnp.zeros_like(grads_ref)
    agg_ref[...] = jnp.zeros_like(agg_ref)
    for step in range(DEGREE):
        code = code_ref[step]
        src = dot(source_ref[...], one_hot(code, 3 * node_count))
        live = jnp.where(code >= 0, 1.0, 0.0)
        back = receive_ref[:FEAT].astype(jnp.float32)
        scal_send = src[:CS].astype(jnp.bfloat16)
        inputs = jnp.concatenate([scal_recv, scal_send], 0)
        message, grads = edge_math(
            src, recv_linear, dot(w_one[:, CS:], scal_send), inputs, pos_recv, back, live, weights
        )
        agg_ref[...] += message
        add_grads(grads_ref, grads)
    code_out_ref[...] = jnp.where(mask_ref[...] != 0, dst_ref[...], -1)
    for chunk in range(code_out_ref.shape[0]):
        target = first_out_ref if chunk == 0 else recv_ref.at[chunk - 1]
        target[...] = dot(
            receive_ref[...], one_hot(code_out_ref[chunk], node_count)
        ).astype(jnp.bfloat16)
    layers_out_ref[:HID] = w_one
    layers_out_ref[HID:] = w_two
    rows = lax.broadcasted_iota(jnp.int32, (8, HID), 0)
    rows_out_ref[...] = jnp.where(rows == 0, b_one_ref[...], w_dist_ref[...])
    copies = [
        pltpu.make_async_copy(agg_ref, agg_out_ref, sems.at[0]),
        pltpu.make_async_copy(grads_ref, grads_out_ref, sems.at[1]),
        pltpu.make_async_copy(recv_ref, recv_out_ref, sems.at[2]),
    ]
    for copy in copies:
        copy.start()
    for copy in copies:
        copy.wait()


def contact_kernel(
    slot,
    grad_scale,
    reply_ref,
    first_ref,
    code_ref,
    layers_ref,
    rows_ref,
    recv_hbm,
    mesh_agg_hbm,
    mesh_grads_hbm,
    cot_hbm,
    agg_out_ref,
    packed_ref,
    recv_ref,
    agg_ref,
    grads_ref,
    cot_ref,
    src_scr,
    packed_scr,
    sems,
):
    chunks = code_ref.shape[0]
    sources = [
        (recv_hbm, recv_ref),
        (mesh_agg_hbm, agg_ref),
        (mesh_grads_hbm, grads_ref),
        (cot_hbm, cot_ref),
    ]
    copies = [
        pltpu.make_async_copy(source, target, sems.at[at])
        for at, (source, target) in enumerate(sources)
    ]
    for copy in copies:
        copy.start()
    node_count = cot_ref.shape[1]
    parts = LANES // slot
    per_chunk = WIDE // slot
    for chunk in range(chunks):
        blocks = [reply_ref[chunk * per_chunk + peer] for peer in range(per_chunk)]
        src_scr[chunk] = jnp.concatenate(
            [
                jnp.concatenate(
                    [block[:, part * slot : (part + 1) * slot] for block in blocks], 1
                )
                for part in range(parts)
            ],
            0,
        )[:ROWS]
    w_one = layers_ref[:HID]
    w_two = layers_ref[HID:]
    b_column, dist_column = as_columns(rows_ref[0:1], rows_ref[1:2])
    weights = (dist_column, w_two, w_two.T)
    for chunk in range(chunks):
        src_rows = src_scr[chunk]
        if chunk == 1:
            for copy in copies:
                copy.wait()
        recv = first_ref[...] if chunk == 0 else recv_ref[chunk - 1]
        inputs = jnp.concatenate([recv[FEAT + 16 :], src_rows[:CS]], 0)
        message, grads = edge_math(
            src_rows.astype(jnp.float32),
            b_column,
            dot(w_one, inputs),
            inputs,
            recv[FEAT : FEAT + 16].astype(jnp.float32)[:3],
            recv[:FEAT].astype(jnp.float32),
            None,
            weights,
        )
        scattered = dot(message.astype(jnp.bfloat16), one_hot(code_ref[chunk], node_count), 1, 1)
        if chunk == 0:
            held = (scattered, grads)
            continue
        agg_ref[...] += scattered
        add_grads(grads_ref, grads)
        if chunk == 1:
            agg_ref[...] += held[0]
            add_grads(grads_ref, held[1])
    agg_rows = agg_ref[...].astype(jnp.bfloat16)
    agg_out_ref[...] = agg_rows
    cot = cot_ref[...]
    low = HID + GATES
    packed_scr[:low] = grads_ref[:, :LANES] * grad_scale
    scal = dot(cot[:CS], agg_rows[:CS], 1, 1) * grad_scale
    packed_scr[low : low + CS // 2] = jnp.concatenate([scal[: CS // 2], scal[CS // 2 :]], 1)
    low = low + CS // 2
    mixed = dot(cot[CS:], agg_rows[CS:], 1, 1)
    grad_vec = jnp.zeros((CV, CV), jnp.float32)
    for k in range(3):
        rows = slice(k * CV, (k + 1) * CV)
        grad_vec = grad_vec + mixed[rows, rows]
    each = CV * CV // LANES
    packed_scr[low : low + each] = grad_scale * jnp.concatenate(
        [grad_vec[at : at + each] for at in range(0, CV, each)], 1
    )
    low = low + each
    grad_ten = jnp.zeros((CT, CT), jnp.float32)
    for m in range(9):
        rows = slice(3 * CV + m * CT, 3 * CV + (m + 1) * CT)
        grad_ten = grad_ten + mixed[rows, rows]
    each = CT * CT // LANES
    packed_scr[low : low + each] = grad_scale * jnp.concatenate(
        [grad_ten[at : at + each] for at in range(0, CT, each)], 1
    )
    low = low + each
    extra = (grads_ref[:HID, LANES:] * grad_scale).T
    packed_scr[low : low + 1] = extra[0:1]
    packed_scr[low + 1 : low + 2] = extra[1:2] + extra[2:3]
    packed = packed_scr[...].astype(jnp.bfloat16)
    tiles = packed_ref.shape[1]
    for peer in range(packed_ref.shape[0]):
        for tile in range(tiles):
            at = (peer * tiles + tile) * FINE
            if at < packed.shape[0]:
                packed_ref[peer, tile] = packed[at : at + FINE]
            else:
                packed_ref[peer, tile] = jnp.zeros((FINE, LANES), jnp.bfloat16)


def sum_kernel(parts_ref, out_ref):
    total = parts_ref[0].astype(jnp.float32)
    for peer in range(1, parts_ref.shape[0]):
        total = total + parts_ref[peer].astype(jnp.float32)
    total = total.astype(jnp.bfloat16)
    for peer in range(out_ref.shape[0]):
        out_ref[peer] = total


def finish_kernel(
    blocks_ref,
    table_ref,
    agg_ref,
    w_scal_ref,
    w_vec_ref,
    w_ten_ref,
    out_ref,
    one_ref,
    bias_ref,
    dist_ref,
    two_ref,
    scal_ref,
    vec_ref,
    ten_ref,
    block_ref,
):
    block_diagonal(block_ref, w_scal_ref, w_vec_ref, w_ten_ref)
    out_ref[...] = (
        table_ref[:FEAT].astype(jnp.float32) + dot(block_ref[...], agg_ref[...])
    ).astype(jnp.bfloat16)

    tiles = blocks_ref.shape[1]

    def rows_of(at):
        peer, tile = divmod(at // FINE, tiles)
        return blocks_ref[peer, tile].astype(jnp.float32)

    for at in range(0, HID, FINE):
        one_ref[at : at + FINE] = rows_of(at)
    for at in range(0, GATES, FINE):
        two_ref[at : at + FINE] = rows_of(HID + at)
    low = HID + GATES
    for at in range(0, CS // 2, FINE):
        rows = rows_of(low + at)
        scal_ref[at : at + FINE] = rows[:, :CS]
        scal_ref[CS // 2 + at : CS // 2 + at + FINE] = rows[:, CS:]
    low = low + CS // 2
    for ref, width in ((vec_ref, CV), (ten_ref, CT)):
        each = width * width // LANES
        for at in range(0, each, FINE):
            rows = rows_of(low + at)
            for piece in range(width // each):
                to = piece * each + at
                ref[to : to + FINE] = rows[:, piece * width : (piece + 1) * width]
        low = low + each
    extra = rows_of(low)
    bias_ref[...] = extra[0:1]
    dist_ref[...] = extra[1:2]


def call(kernel, out_shape, scratch=(), in_specs=None, out_specs=None, cost_estimate=None):
    specs = {}
    if cost_estimate is not None:
        specs["cost_estimate"] = cost_estimate
    if in_specs is not None:
        specs["in_specs"] = in_specs
    if out_specs is not None:
        specs["out_specs"] = out_specs
    return pl.pallas_call(
        kernel,
        out_shape=out_shape,
        scratch_shapes=list(scratch),
        compiler_params=pltpu.CompilerParams(vmem_limit_bytes=VMEM_BYTES),
        **specs,
    )


IN_VMEM = pl.BlockSpec(memory_space=pltpu.VMEM)
IN_HBM = pl.BlockSpec(memory_space=pltpu.HBM)
ANYWHERE = pl.BlockSpec(memory_space=pl.ANY)


def exchange(blocks, axes=("dom", "sub")):
    return lax.all_to_all(blocks, axes, split_axis=0, concat_axis=0, tiled=True)


def in_hbm(*arrays):
    return tuple(pltpu.with_memory_space_constraint(array, pltpu.HBM) for array in arrays)


def shaped(shape, dtype):
    return jax.ShapeDtypeStruct(shape, dtype)


def from_behind(shard, axis, by):
    peers = lax.axis_size(axis)
    return lax.ppermute(shard, axis, [(i, (i + by) % peers) for i in range(peers)])


def on_device(
    node_feat,
    node_pos,
    node_cot,
    mesh_senders,
    edge_mask,
    halo_up,
    halo_down,
    contact_rows,
    contact_dst,
    contact_mask,
    w_one,
    b_one,
    w_dist,
    w_two,
    w_scal,
    w_vec,
    w_ten,
):
    f32, bf16 = jnp.float32, jnp.bfloat16
    node_count = node_feat.shape[1]
    contact_count = contact_rows.shape[0]
    device_count = lax.axis_size("dom") * lax.axis_size("sub")
    slot = contact_count // device_count
    chunks = contact_count // CHUNK
    wides = contact_count // WIDE
    parts = LANES // slot
    height = -(-ROWS // (parts * 16)) * 16
    grad_scale = 1.0 / math.sqrt(device_count * node_count * DEGREE)
    table, requests = call(
        table_kernel,
        (
            shaped((ROWS, node_count), bf16),
            shaped((device_count, 1, slot), jnp.int32),
        ),
        (
            pltpu.VMEM((3, node_count), bf16),
            pltpu.VMEM((1, node_count), jnp.int32),
            pltpu.VMEM((1, node_count), jnp.int32),
            pltpu.VMEM((contact_count // LANES, LANES), jnp.int32),
            pltpu.SemaphoreType.DMA((5,)),
        ),
        in_specs=[IN_HBM] * 5,
        out_specs=(IN_VMEM, IN_VMEM),
    )(
        *in_hbm(
            node_feat,
            node_pos,
            halo_up[None],
            halo_down[None],
            contact_rows.reshape(contact_count // LANES, LANES),
        )
    )
    wanted = exchange(requests)
    wanted, table_late = lax.optimization_barrier((wanted, table))
    low = from_behind(table_late, "sub", 1)
    high = from_behind(table_late, "sub", -1)
    found = call(
        functools.partial(contact_gather_kernel, slot),
        pltpu.HBM((device_count, height, LANES), bf16),
        (
            pltpu.VMEM((device_count, height, LANES), bf16),
            pltpu.SemaphoreType.DMA((chunks,)),
        ),
        in_specs=[IN_VMEM, IN_VMEM],
        out_specs=IN_HBM,
    )(table, wanted)
    found, mesh_senders, edge_mask = lax.optimization_barrier((found, mesh_senders, edge_mask))
    replies = exchange(found)
    mesh_code = (
        jnp.where(edge_mask != 0, mesh_senders, -1)
        .reshape(node_count, DEGREE)
        .T.reshape(DEGREE, 1, node_count)
    )
    contact_dst = contact_dst.reshape(wides, 1, WIDE)
    contact_mask = contact_mask.reshape(wides, 1, WIDE)
    mesh_rows = HID + GATES
    recv_rows = FEAT + 16 + CS
    mesh_agg, mesh_grads, recv, first, contact_code, layers, rows = call(
        mesh_kernel,
        (
            pltpu.HBM((FEAT, node_count), f32),
            pltpu.HBM((mesh_rows, 2 * LANES), f32),
            pltpu.HBM((wides - 1, recv_rows, WIDE), bf16),
            shaped((recv_rows, WIDE), bf16),
            shaped((wides, 1, WIDE), jnp.int32),
            shaped((mesh_rows, HID), bf16),
            shaped((8, HID), f32),
        ),
        (
            pltpu.VMEM((FEAT, node_count), f32),
            pltpu.VMEM((mesh_rows, 2 * LANES), f32),
            pltpu.VMEM((wides - 1, recv_rows, WIDE), bf16),
            pltpu.VMEM((recv_rows, node_count), bf16),
            pltpu.VMEM((ROWS, 3 * node_count), bf16),
            pltpu.VMEM((FEAT, FEAT), bf16),
            pltpu.SemaphoreType.DMA((3,)),
        ),
        in_specs=[IN_VMEM] * 14,
        out_specs=(IN_HBM,) * 3 + (IN_VMEM,) * 4,
        cost_estimate=pl.CostEstimate(
            flops=40_000_000_000, bytes_accessed=8_000_000, transcendentals=400_000
        ),
    )(
        table,
        low,
        high,
        mesh_code,
        node_cot,
        w_one,
        b_one[None],
        w_dist[None],
        w_two,
        w_scal,
        w_vec,
        w_ten,
        contact_dst,
        contact_mask,
    )
    packed_rows = mesh_rows + (CS * CS + CV * CV + CT * CT) // LANES + 2
    tiles = -(-packed_rows // (FINE * device_count))
    share = (device_count, tiles, FINE, LANES)
    agg_rows, packed = call(
        functools.partial(contact_kernel, slot, grad_scale),
        (shaped((FEAT, node_count), bf16), shaped(share, bf16)),
        (
            pltpu.VMEM((wides - 1, recv_rows, WIDE), bf16),
            pltpu.VMEM((FEAT, node_count), f32),
            pltpu.VMEM((mesh_rows, 2 * LANES), f32),
            pltpu.VMEM((FEAT, node_count), bf16),
            pltpu.VMEM((wides, ROWS, WIDE), bf16),
            pltpu.VMEM((packed_rows, LANES), f32),
            pltpu.SemaphoreType.DMA((4,)),
        ),
        in_specs=[IN_VMEM] * 5 + [IN_HBM] * 4,
        out_specs=(IN_VMEM, IN_VMEM),
    )(
        replies,
        first,
        contact_code,
        layers,
        rows,
        *in_hbm(recv, mesh_agg, mesh_grads, node_cot),
    )
    shares = call(sum_kernel, shaped(share, bf16))(exchange(packed))
    node_out, one, bias, dist, two, scal, vec, ten = call(
        finish_kernel,
        (
            shaped((FEAT, node_count), bf16),
            shaped((HID, 2 * CS), f32),
            shaped((1, HID), f32),
            shaped((1, HID), f32),
            shaped((GATES, HID), f32),
            shaped((CS, CS), f32),
            shaped((CV, CV), f32),
            shaped((CT, CT), f32),
        ),
        (pltpu.VMEM((FEAT, FEAT), bf16),),
    )(exchange(shares), table, agg_rows, w_scal, w_vec, w_ten)
    return node_out, one, bias[0], dist[0], two, scal, vec, ten


def solution(mesh):
    along = P(("dom", "sub"))
    columns = P(None, ("dom", "sub"))
    in_specs = (columns,) * 3 + (along,) * 7 + (P(),) * 7
    out_specs = (columns,) + (P(),) * 7
    return jax.shard_map(
        on_device, mesh=mesh, in_specs=in_specs, out_specs=out_specs, check_vma=False
    )
```

```python
import functools
import math

import jax
import jax.numpy as jnp
from jax import lax
from jax.experimental import pallas as pl
from jax.experimental.pallas import tpu as pltpu
from jax.sharding import PartitionSpec as P

CS = 64
CV = 32
CT = 16
HID = 128
DEGREE = 6
GATES = 144
FEAT = CS + 3 * CV + 9 * CT
ROWS = 320
LANES = 128
FINE = 2
CHUNK = 512
WIDE = 1024
VMEM_BYTES = 48 * 1024 * 1024


def dot(lhs, rhs, lhs_dim=1, rhs_dim=0):
    return lax.dot_general(
        lhs, rhs, (((lhs_dim,), (rhs_dim,)), ((), ())), preferred_element_type=jnp.float32
    )


def one_hot(code, width):
    rows = lax.broadcasted_iota(jnp.int16, (width, code.shape[1]), 0)
    return jnp.where(rows == code.astype(jnp.int16), jnp.bfloat16(1), jnp.bfloat16(0))


def join_index(table, row):
    pair = table[row : row + 2].astype(jnp.float32)
    return (pair[0:1] * 128.0 + pair[1:2]).astype(jnp.int32)


def table_kernel(
    feat_ref,
    pos_ref,
    up_ref,
    down_ref,
    rows_ref,
    table_ref,
    request_ref,
    pos_scr,
    up_scr,
    down_scr,
    rows_scr,
    sems,
):
    node_count = table_ref.shape[1]
    copies = [
        pltpu.make_async_copy(rows_ref, rows_scr, sems.at[0]),
        pltpu.make_async_copy(feat_ref, table_ref.at[:FEAT], sems.at[1]),
        pltpu.make_async_copy(pos_ref, pos_scr, sems.at[2]),
        pltpu.make_async_copy(up_ref, up_scr, sems.at[3]),
        pltpu.make_async_copy(down_ref, down_scr, sems.at[4]),
    ]
    for copy in copies:
        copy.start()
    copies[0].wait()
    slot = request_ref.shape[2]
    parts = LANES // slot
    for row in range(rows_scr.shape[0]):
        line = rows_scr[row : row + 1]
        for part in range(parts):
            request_ref[row * parts + part] = line[:, part * slot : (part + 1) * slot]
    for copy in copies[2:]:
        copy.wait()
    rows = lax.broadcasted_iota(jnp.int32, (ROWS - FEAT, node_count), 0)
    pos = pos_scr[...].astype(jnp.float32)
    tail = jnp.zeros((ROWS - FEAT, node_count), jnp.float32)
    for k in range(3):
        tail = jnp.where(rows == k, pos[k : k + 1], tail)
    for k, index_ref in ((3, up_scr), (5, down_scr)):
        index = index_ref[...]
        high = index >> 7
        tail = jnp.where(rows == k, high.astype(jnp.float32), tail)
        tail = jnp.where(rows == k + 1, (index - (high << 7)).astype(jnp.float32), tail)
    table_ref[FEAT:] = tail.astype(jnp.bfloat16)
    copies[1].wait()


def contact_gather_kernel(slot, table_ref, wanted_ref, out_hbm, out_ref, sems):
    node_count = table_ref.shape[1]
    parts = LANES // slot
    height = out_ref.shape[1]
    per_chunk = CHUNK // slot
    copies = []
    for chunk in range(wanted_ref.shape[0] // per_chunk):
        wanted = [wanted_ref[chunk * per_chunk + peer] for peer in range(per_chunk)]
        hot = one_hot(jnp.concatenate(wanted, 1), node_count)
        rows = dot(table_ref[...], hot).astype(jnp.bfloat16)
        if parts * height > ROWS:
            rows = jnp.concatenate(
                [rows, jnp.zeros((parts * height - ROWS, CHUNK), jnp.bfloat16)], 0
            )
        for peer in range(per_chunk):
            out_ref[chunk * per_chunk + peer] = jnp.concatenate(
                [
                    rows[part * height : (part + 1) * height, peer * slot : (peer + 1) * slot]
                    for part in range(parts)
                ],
                1,
            )
        done = pl.ds(chunk * per_chunk, per_chunk)
        copies.append(
            pltpu.make_async_copy(out_ref.at[done], out_hbm.at[done], sems.at[chunk])
        )
        copies[-1].start()
    for copy in copies:
        copy.wait()


def edge_math(src, base, first, inputs, pos_recv, back, live, weights):
    w_dist, w_two, w_two_t = weights
    edges = src.shape[1]
    offset = src[FEAT : FEAT + 3] - pos_recv
    if live is not None:
        offset = offset * live
    distance = jnp.sum(offset * offset, 0, keepdims=True)
    linear = base + first + w_dist * distance
    squashed = 0.5 * jnp.tanh(0.5 * linear) + 0.5
    hidden = (linear * squashed).astype(jnp.bfloat16)
    gates = dot(w_two, hidden)
    gate_vec = gates[CS : CS + CV]
    gate_dir = gates[CS + CV : CS + 2 * CV]
    gate_ten = gates[CS + 2 * CV :]
    message = [gates[:CS] * src[:CS]]
    vec_part = jnp.zeros((CV, edges), jnp.float32)
    dir_part = jnp.zeros((CV, edges), jnp.float32)
    for k in range(3):
        rows = slice(CS + k * CV, CS + (k + 1) * CV)
        message.append(gate_vec * src[rows] + gate_dir * offset[k : k + 1])
        vec_part = vec_part + back[rows] * src[rows]
        dir_part = dir_part + back[rows] * offset[k : k + 1]
    ten_part = jnp.zeros((CT, edges), jnp.float32)
    for m in range(9):
        rows = slice(CS + 3 * CV + m * CT, CS + 3 * CV + (m + 1) * CT)
        message.append(gate_ten * src[rows])
        ten_part = ten_part + back[rows] * src[rows]
    message = jnp.concatenate(message, 0)
    dgates = jnp.concatenate([back[:CS] * src[:CS], vec_part, dir_part, ten_part], 0).astype(
        jnp.bfloat16
    )
    hidden_grad = dot(w_two_t, dgates)
    linear_grad = (hidden_grad * squashed * (1.0 + linear * (1.0 - squashed))).astype(jnp.bfloat16)
    rows = lax.broadcasted_iota(jnp.int32, (16, edges), 0)
    coarse = distance.astype(jnp.bfloat16).astype(jnp.float32)
    extra = jnp.where(
        rows == 0, 1.0, jnp.where(rows == 1, coarse, jnp.where(rows == 2, distance - coarse, 0.0))
    ).astype(jnp.bfloat16)
    grads = (
        dot(linear_grad, jnp.concatenate([inputs, extra], 0), 1, 1),
        dot(dgates, hidden, 1, 1),
    )
    return message, grads


def as_columns(first_row, second_row):
    rows = lax.broadcasted_iota(jnp.int32, (LANES, LANES), 0)
    columns = jnp.where(rows == 0, first_row, jnp.where(rows == 1, second_row, 0.0)).T
    return columns[:, 0:1], columns[:, 1:2]


def add_grads(grads_ref, grads):
    grads_ref[:HID, : 2 * CS + 16] += grads[0]
    grads_ref[HID:, :HID] += grads[1]


def block_diagonal(block_ref, w_scal, w_vec, w_ten):
    block_ref[...] = jnp.zeros_like(block_ref)
    block_ref[:CS, :CS] = w_scal[...]
    for k in range(3):
        rows = slice(CS + k * CV, CS + (k + 1) * CV)
        block_ref[rows, rows] = w_vec[...]
    for m in range(9):
        rows = slice(CS + 3 * CV + m * CT, CS + 3 * CV + (m + 1) * CT)
        block_ref[rows, rows] = w_ten[...]


def mesh_kernel(
    table_ref,
    low_ref,
    high_ref,
    code_ref,
    cot_ref,
    w_one_ref,
    b_one_ref,
    w_dist_ref,
    w_two_ref,
    w_scal_ref,
    w_vec_ref,
    w_ten_ref,
    dst_ref,
    mask_ref,
    agg_out_ref,
    grads_out_ref,
    recv_out_ref,
    first_out_ref,
    code_out_ref,
    layers_out_ref,
    rows_out_ref,
    agg_ref,
    grads_ref,
    recv_ref,
    receive_ref,
    source_ref,
    block_ref,
    sems,
):
    node_count = table_ref.shape[1]
    source_ref[:, :node_count] = table_ref[...]
    low = low_ref[...]
    high = high_ref[...]
    source_ref[:, node_count : 2 * node_count] = dot(
        low, one_hot(join_index(low, FEAT + 3), node_count)
    ).astype(jnp.bfloat16)
    source_ref[:, 2 * node_count :] = dot(
        high, one_hot(join_index(high, FEAT + 5), node_count)
    ).astype(jnp.bfloat16)
    block_diagonal(block_ref, w_scal_ref, w_vec_ref, w_ten_ref)
    receive_ref[:FEAT] = dot(block_ref[...], cot_ref[...], 0, 0).astype(jnp.bfloat16)
    receive_ref[FEAT : FEAT + 16] = table_ref[FEAT:]
    receive_ref[FEAT + 16 :] = table_ref[:CS]
    w_one = w_one_ref[...]
    w_two = w_two_ref[...]
    b_column, dist_column = as_columns(b_one_ref[...], w_dist_ref[...])
    scal_recv = table_ref[:CS]
    recv_linear = dot(w_one[:, :CS], scal_recv) + b_column
    weights = (dist_column, w_two, w_two.T)
    pos_recv = table_ref[FEAT:].astype(jnp.float32)[:3]
    grads_ref[...] = jnp.zeros_like(grads_ref)
    agg_ref[...] = jnp.zeros_like(agg_ref)
    for step in range(DEGREE):
        code = code_ref[step]
        src = dot(source_ref[...], one_hot(code, 3 * node_count))
        live = jnp.where(code >= 0, 1.0, 0.0)
        back = receive_ref[:FEAT].astype(jnp.float32)
        scal_send = src[:CS].astype(jnp.bfloat16)
        inputs = jnp.concatenate([scal_recv, scal_send], 0)
        message, grads = edge_math(
            src, recv_linear, dot(w_one[:, CS:], scal_send), inputs, pos_recv, back, live, weights
        )
        agg_ref[...] += message
        add_grads(grads_ref, grads)
    code_out_ref[...] = jnp.where(mask_ref[...] != 0, dst_ref[...], -1)
    for chunk in range(code_out_ref.shape[0]):
        target = first_out_ref if chunk == 0 else recv_ref.at[chunk - 1]
        target[...] = dot(
            receive_ref[...], one_hot(code_out_ref[chunk], node_count)
        ).astype(jnp.bfloat16)
    layers_out_ref[:HID] = w_one
    layers_out_ref[HID:] = w_two
    rows = lax.broadcasted_iota(jnp.int32, (8, HID), 0)
    rows_out_ref[...] = jnp.where(rows == 0, b_one_ref[...], w_dist_ref[...])
    copies = [
        pltpu.make_async_copy(agg_ref, agg_out_ref, sems.at[0]),
        pltpu.make_async_copy(grads_ref, grads_out_ref, sems.at[1]),
        pltpu.make_async_copy(recv_ref, recv_out_ref, sems.at[2]),
    ]
    for copy in copies:
        copy.start()
    for copy in copies:
        copy.wait()


def contact_kernel(
    slot,
    grad_scale,
    reply_ref,
    first_ref,
    code_ref,
    layers_ref,
    rows_ref,
    recv_hbm,
    mesh_agg_hbm,
    mesh_grads_hbm,
    cot_hbm,
    agg_out_ref,
    packed_ref,
    recv_ref,
    agg_ref,
    grads_ref,
    cot_ref,
    src_scr,
    packed_scr,
    sems,
):
    chunks = code_ref.shape[0]
    sources = [
        (recv_hbm, recv_ref),
        (mesh_agg_hbm, agg_ref),
        (mesh_grads_hbm, grads_ref),
        (cot_hbm, cot_ref),
    ]
    copies = [
        pltpu.make_async_copy(source, target, sems.at[at])
        for at, (source, target) in enumerate(sources)
    ]
    for copy in copies:
        copy.start()
    node_count = cot_ref.shape[1]
    parts = LANES // slot
    per_chunk = WIDE // slot
    for chunk in range(chunks):
        blocks = [reply_ref[chunk * per_chunk + peer] for peer in range(per_chunk)]
        src_scr[chunk] = jnp.concatenate(
            [
                jnp.concatenate(
                    [block[:, part * slot : (part + 1) * slot] for block in blocks], 1
                )
                for part in range(parts)
            ],
            0,
        )[:ROWS]
    w_one = layers_ref[:HID]
    w_two = layers_ref[HID:]
    b_column, dist_column = as_columns(rows_ref[0:1], rows_ref[1:2])
    weights = (dist_column, w_two, w_two.T)
    for chunk in range(chunks):
        src_rows = src_scr[chunk]
        if chunk == 1:
            for copy in copies:
                copy.wait()
        recv = first_ref[...] if chunk == 0 else recv_ref[chunk - 1]
        inputs = jnp.concatenate([recv[FEAT + 16 :], src_rows[:CS]], 0)
        message, grads = edge_math(
            src_rows.astype(jnp.float32),
            b_column,
            dot(w_one, inputs),
            inputs,
            recv[FEAT : FEAT + 16].astype(jnp.float32)[:3],
            recv[:FEAT].astype(jnp.float32),
            None,
            weights,
        )
        scattered = dot(message.astype(jnp.bfloat16), one_hot(code_ref[chunk], node_count), 1, 1)
        if chunk == 0:
            held = (scattered, grads)
            continue
        agg_ref[...] += scattered
        add_grads(grads_ref, grads)
        if chunk == 1:
            agg_ref[...] += held[0]
            add_grads(grads_ref, held[1])
    agg_rows = agg_ref[...].astype(jnp.bfloat16)
    agg_out_ref[...] = agg_rows
    cot = cot_ref[...]
    low = HID + GATES
    packed_scr[:low] = grads_ref[:, :LANES] * grad_scale
    scal = dot(cot[:CS], agg_rows[:CS], 1, 1) * grad_scale
    packed_scr[low : low + CS // 2] = jnp.concatenate([scal[: CS // 2], scal[CS // 2 :]], 1)
    low = low + CS // 2
    mixed = dot(cot[CS:], agg_rows[CS:], 1, 1)
    grad_vec = jnp.zeros((CV, CV), jnp.float32)
    for k in range(3):
        rows = slice(k * CV, (k + 1) * CV)
        grad_vec = grad_vec + mixed[rows, rows]
    each = CV * CV // LANES
    packed_scr[low : low + each] = grad_scale * jnp.concatenate(
        [grad_vec[at : at + each] for at in range(0, CV, each)], 1
    )
    low = low + each
    grad_ten = jnp.zeros((CT, CT), jnp.float32)
    for m in range(9):
        rows = slice(3 * CV + m * CT, 3 * CV + (m + 1) * CT)
        grad_ten = grad_ten + mixed[rows, rows]
    each = CT * CT // LANES
    packed_scr[low : low + each] = grad_scale * jnp.concatenate(
        [grad_ten[at : at + each] for at in range(0, CT, each)], 1
    )
    low = low + each
    extra = (grads_ref[:HID, LANES:] * grad_scale).T
    packed_scr[low : low + 1] = extra[0:1]
    packed_scr[low + 1 : low + 2] = extra[1:2] + extra[2:3]
    packed = packed_scr[...].astype(jnp.bfloat16)
    tiles = packed_ref.shape[1]
    for peer in range(packed_ref.shape[0]):
        for tile in range(tiles):
            at = (peer * tiles + tile) * FINE
            if at < packed.shape[0]:
                packed_ref[peer, tile] = packed[at : at + FINE]
            else:
                packed_ref[peer, tile] = jnp.zeros((FINE, LANES), jnp.bfloat16)


def sum_kernel(parts_ref, out_ref):
    total = parts_ref[0].astype(jnp.float32)
    for peer in range(1, parts_ref.shape[0]):
        total = total + parts_ref[peer].astype(jnp.float32)
    total = total.astype(jnp.bfloat16)
    for peer in range(out_ref.shape[0]):
        out_ref[peer] = total


def finish_kernel(
    blocks_ref,
    table_ref,
    agg_ref,
    w_scal_ref,
    w_vec_ref,
    w_ten_ref,
    out_hbm,
    one_ref,
    bias_ref,
    dist_ref,
    two_ref,
    scal_ref,
    vec_ref,
    ten_ref,
    out_ref,
    block_ref,
    sem,
):
    block_diagonal(block_ref, w_scal_ref, w_vec_ref, w_ten_ref)
    out_ref[...] = (
        table_ref[:FEAT].astype(jnp.float32) + dot(block_ref[...], agg_ref[...])
    ).astype(jnp.bfloat16)
    copy = pltpu.make_async_copy(out_ref, out_hbm, sem)
    copy.start()

    tiles = blocks_ref.shape[1]

    def rows_of(at):
        peer, tile = divmod(at // FINE, tiles)
        return blocks_ref[peer, tile].astype(jnp.float32)

    for at in range(0, HID, FINE):
        one_ref[at : at + FINE] = rows_of(at)
    for at in range(0, GATES, FINE):
        two_ref[at : at + FINE] = rows_of(HID + at)
    low = HID + GATES
    for at in range(0, CS // 2, FINE):
        rows = rows_of(low + at)
        scal_ref[at : at + FINE] = rows[:, :CS]
        scal_ref[CS // 2 + at : CS // 2 + at + FINE] = rows[:, CS:]
    low = low + CS // 2
    for ref, width in ((vec_ref, CV), (ten_ref, CT)):
        each = width * width // LANES
        for at in range(0, each, FINE):
            rows = rows_of(low + at)
            for piece in range(width // each):
                to = piece * each + at
                ref[to : to + FINE] = rows[:, piece * width : (piece + 1) * width]
        low = low + each
    extra = rows_of(low)
    bias_ref[...] = extra[0:1]
    dist_ref[...] = extra[1:2]
    copy.wait()


def call(kernel, out_shape, scratch=(), in_specs=None, out_specs=None, cost_estimate=None):
    specs = {}
    if cost_estimate is not None:
        specs["cost_estimate"] = cost_estimate
    if in_specs is not None:
        specs["in_specs"] = in_specs
    if out_specs is not None:
        specs["out_specs"] = out_specs
    return pl.pallas_call(
        kernel,
        out_shape=out_shape,
        scratch_shapes=list(scratch),
        compiler_params=pltpu.CompilerParams(vmem_limit_bytes=VMEM_BYTES),
        **specs,
    )


IN_VMEM = pl.BlockSpec(memory_space=pltpu.VMEM)
IN_HBM = pl.BlockSpec(memory_space=pltpu.HBM)
ANYWHERE = pl.BlockSpec(memory_space=pl.ANY)


def exchange(blocks, axes=("dom", "sub")):
    return lax.all_to_all(blocks, axes, split_axis=0, concat_axis=0, tiled=True)


def in_hbm(*arrays):
    return tuple(pltpu.with_memory_space_constraint(array, pltpu.HBM) for array in arrays)


def shaped(shape, dtype):
    return jax.ShapeDtypeStruct(shape, dtype)


def from_behind(shard, axis, by):
    peers = lax.axis_size(axis)
    return lax.ppermute(shard, axis, [(i, (i + by) % peers) for i in range(peers)])


def on_device(
    node_feat,
    node_pos,
    node_cot,
    mesh_senders,
    edge_mask,
    halo_up,
    halo_down,
    contact_rows,
    contact_dst,
    contact_mask,
    w_one,
    b_one,
    w_dist,
    w_two,
    w_scal,
    w_vec,
    w_ten,
):
    f32, bf16 = jnp.float32, jnp.bfloat16
    node_count = node_feat.shape[1]
    contact_count = contact_rows.shape[0]
    device_count = lax.axis_size("dom") * lax.axis_size("sub")
    slot = contact_count // device_count
    chunks = contact_count // CHUNK
    wides = contact_count // WIDE
    parts = LANES // slot
    height = -(-ROWS // (parts * 16)) * 16
    grad_scale = 1.0 / math.sqrt(device_count * node_count * DEGREE)
    table, requests = call(
        table_kernel,
        (
            shaped((ROWS, node_count), bf16),
            shaped((device_count, 1, slot), jnp.int32),
        ),
        (
            pltpu.VMEM((3, node_count), bf16),
            pltpu.VMEM((1, node_count), jnp.int32),
            pltpu.VMEM((1, node_count), jnp.int32),
            pltpu.VMEM((contact_count // LANES, LANES), jnp.int32),
            pltpu.SemaphoreType.DMA((5,)),
        ),
        in_specs=[IN_HBM] * 5,
        out_specs=(IN_VMEM, IN_VMEM),
    )(
        *in_hbm(
            node_feat,
            node_pos,
            halo_up[None],
            halo_down[None],
            contact_rows.reshape(contact_count // LANES, LANES),
        )
    )
    wanted = exchange(requests)
    found = call(
        functools.partial(contact_gather_kernel, slot),
        pltpu.HBM((device_count, height, LANES), bf16),
        (
            pltpu.VMEM((device_count, height, LANES), bf16),
            pltpu.SemaphoreType.DMA((chunks,)),
        ),
        in_specs=[IN_VMEM, IN_VMEM],
        out_specs=IN_HBM,
    )(table, wanted)
    found, table_late, mesh_senders, edge_mask = lax.optimization_barrier(
        (found, table, mesh_senders, edge_mask)
    )
    low = from_behind(table_late, "sub", 1)
    high = from_behind(table_late, "sub", -1)
    replies = exchange(found)
    mesh_code = (
        jnp.where(edge_mask != 0, mesh_senders, -1)
        .reshape(node_count, DEGREE)
        .T.reshape(DEGREE, 1, node_count)
    )
    contact_dst = contact_dst.reshape(wides, 1, WIDE)
    contact_mask = contact_mask.reshape(wides, 1, WIDE)
    mesh_rows = HID + GATES
    recv_rows = FEAT + 16 + CS
    mesh_agg, mesh_grads, recv, first, contact_code, layers, rows = call(
        mesh_kernel,
        (
            pltpu.HBM((FEAT, node_count), f32),
            pltpu.HBM((mesh_rows, 2 * LANES), f32),
            pltpu.HBM((wides - 1, recv_rows, WIDE), bf16),
            shaped((recv_rows, WIDE), bf16),
            shaped((wides, 1, WIDE), jnp.int32),
            shaped((mesh_rows, HID), bf16),
            shaped((8, HID), f32),
        ),
        (
            pltpu.VMEM((FEAT, node_count), f32),
            pltpu.VMEM((mesh_rows, 2 * LANES), f32),
            pltpu.VMEM((wides - 1, recv_rows, WIDE), bf16),
            pltpu.VMEM((recv_rows, node_count), bf16),
            pltpu.VMEM((ROWS, 3 * node_count), bf16),
            pltpu.VMEM((FEAT, FEAT), bf16),
            pltpu.SemaphoreType.DMA((3,)),
        ),
        in_specs=[IN_VMEM] * 14,
        out_specs=(IN_HBM,) * 3 + (IN_VMEM,) * 4,
        cost_estimate=pl.CostEstimate(
            flops=40_000_000_000, bytes_accessed=8_000_000, transcendentals=400_000
        ),
    )(
        table,
        low,
        high,
        mesh_code,
        node_cot,
        w_one,
        b_one[None],
        w_dist[None],
        w_two,
        w_scal,
        w_vec,
        w_ten,
        contact_dst,
        contact_mask,
    )
    packed_rows = mesh_rows + (CS * CS + CV * CV + CT * CT) // LANES + 2
    tiles = -(-packed_rows // (FINE * device_count))
    share = (device_count, tiles, FINE, LANES)
    agg_rows, packed = call(
        functools.partial(contact_kernel, slot, grad_scale),
        (shaped((FEAT, node_count), bf16), shaped(share, bf16)),
        (
            pltpu.VMEM((wides - 1, recv_rows, WIDE), bf16),
            pltpu.VMEM((FEAT, node_count), f32),
            pltpu.VMEM((mesh_rows, 2 * LANES), f32),
            pltpu.VMEM((FEAT, node_count), bf16),
            pltpu.VMEM((wides, ROWS, WIDE), bf16),
            pltpu.VMEM((packed_rows, LANES), f32),
            pltpu.SemaphoreType.DMA((4,)),
        ),
        in_specs=[IN_VMEM] * 5 + [IN_HBM] * 4,
        out_specs=(IN_VMEM, IN_VMEM),
    )(
        replies,
        first,
        contact_code,
        layers,
        rows,
        *in_hbm(recv, mesh_agg, mesh_grads, node_cot),
    )
    shares = call(sum_kernel, shaped(share, bf16))(exchange(packed))
    node_out, one, bias, dist, two, scal, vec, ten = call(
        finish_kernel,
        (
            pltpu.HBM((FEAT, node_count), bf16),
            shaped((HID, 2 * CS), f32),
            shaped((1, HID), f32),
            shaped((1, HID), f32),
            shaped((GATES, HID), f32),
            shaped((CS, CS), f32),
            shaped((CV, CV), f32),
            shaped((CT, CT), f32),
        ),
        (
            pltpu.VMEM((FEAT, node_count), bf16),
            pltpu.VMEM((FEAT, FEAT), bf16),
            pltpu.SemaphoreType.DMA(()),
        ),
        in_specs=[IN_VMEM] * 6,
        out_specs=(IN_HBM,) + (IN_VMEM,) * 7,
    )(exchange(shares), table, agg_rows, w_scal, w_vec, w_ten)
    return node_out, one, bias[0], dist[0], two, scal, vec, ten


def solution(mesh):
    along = P(("dom", "sub"))
    columns = P(None, ("dom", "sub"))
    in_specs = (columns,) * 3 + (along,) * 7 + (P(),) * 7
    out_specs = (columns,) + (P(),) * 7
    return jax.shard_map(
        on_device, mesh=mesh, in_specs=in_specs, out_specs=out_specs, check_vma=False
    )
```

```python
import functools
import math

import jax
import jax.numpy as jnp
from jax import lax
from jax.experimental import pallas as pl
from jax.experimental.pallas import tpu as pltpu
from jax.sharding import PartitionSpec as P

CS = 64
CV = 32
CT = 16
HID = 128
DEGREE = 6
GATES = 144
FEAT = CS + 3 * CV + 9 * CT
ROWS = 320
LANES = 128
FINE = 2
CHUNK = 512
WIDE = 1024
VMEM_BYTES = 48 * 1024 * 1024


def dot(lhs, rhs, lhs_dim=1, rhs_dim=0):
    return lax.dot_general(
        lhs, rhs, (((lhs_dim,), (rhs_dim,)), ((), ())), preferred_element_type=jnp.float32
    )


def one_hot(code, width):
    rows = lax.broadcasted_iota(jnp.int16, (width, code.shape[1]), 0)
    return jnp.where(rows == code.astype(jnp.int16), jnp.bfloat16(1), jnp.bfloat16(0))


def join_index(table, row):
    pair = table[row : row + 2].astype(jnp.float32)
    return (pair[0:1] * 128.0 + pair[1:2]).astype(jnp.int32)


def table_kernel(
    feat_ref,
    pos_ref,
    up_ref,
    down_ref,
    rows_ref,
    table_ref,
    request_ref,
    pos_scr,
    up_scr,
    down_scr,
    rows_scr,
    sems,
):
    node_count = table_ref.shape[1]
    copies = [
        pltpu.make_async_copy(rows_ref, rows_scr, sems.at[0]),
        pltpu.make_async_copy(feat_ref, table_ref.at[:FEAT], sems.at[1]),
        pltpu.make_async_copy(pos_ref, pos_scr, sems.at[2]),
        pltpu.make_async_copy(up_ref, up_scr, sems.at[3]),
        pltpu.make_async_copy(down_ref, down_scr, sems.at[4]),
    ]
    for copy in copies:
        copy.start()
    copies[0].wait()
    slot = request_ref.shape[2]
    parts = LANES // slot
    for row in range(rows_scr.shape[0]):
        line = rows_scr[row : row + 1]
        for part in range(parts):
            request_ref[row * parts + part] = line[:, part * slot : (part + 1) * slot]
    for copy in copies[2:]:
        copy.wait()
    rows = lax.broadcasted_iota(jnp.int32, (ROWS - FEAT, node_count), 0)
    pos = pos_scr[...].astype(jnp.float32)
    tail = jnp.zeros((ROWS - FEAT, node_count), jnp.float32)
    for k in range(3):
        tail = jnp.where(rows == k, pos[k : k + 1], tail)
    for k, index_ref in ((3, up_scr), (5, down_scr)):
        index = index_ref[...]
        high = index >> 7
        tail = jnp.where(rows == k, high.astype(jnp.float32), tail)
        tail = jnp.where(rows == k + 1, (index - (high << 7)).astype(jnp.float32), tail)
    table_ref[FEAT:] = tail.astype(jnp.bfloat16)
    copies[1].wait()


def contact_gather_kernel(slot, table_ref, wanted_ref, out_hbm, out_ref, sems):
    node_count = table_ref.shape[1]
    parts = LANES // slot
    height = out_ref.shape[1]
    per_chunk = CHUNK // slot
    copies = []
    for chunk in range(wanted_ref.shape[0] // per_chunk):
        wanted = [wanted_ref[chunk * per_chunk + peer] for peer in range(per_chunk)]
        hot = one_hot(jnp.concatenate(wanted, 1), node_count)
        rows = dot(table_ref[...], hot).astype(jnp.bfloat16)
        if parts * height > ROWS:
            rows = jnp.concatenate(
                [rows, jnp.zeros((parts * height - ROWS, CHUNK), jnp.bfloat16)], 0
            )
        for peer in range(per_chunk):
            out_ref[chunk * per_chunk + peer] = jnp.concatenate(
                [
                    rows[part * height : (part + 1) * height, peer * slot : (peer + 1) * slot]
                    for part in range(parts)
                ],
                1,
            )
        done = pl.ds(chunk * per_chunk, per_chunk)
        copies.append(
            pltpu.make_async_copy(out_ref.at[done], out_hbm.at[done], sems.at[chunk])
        )
        copies[-1].start()
    for copy in copies:
        copy.wait()


def edge_math(src, base, first, inputs, pos_recv, back, live, weights):
    w_dist, w_two, w_two_t = weights
    edges = src.shape[1]
    offset = src[FEAT : FEAT + 3] - pos_recv
    if live is not None:
        offset = offset * live
    distance = jnp.sum(offset * offset, 0, keepdims=True)
    linear = base + first + w_dist * distance
    squashed = 0.5 * jnp.tanh(0.5 * linear) + 0.5
    hidden = (linear * squashed).astype(jnp.bfloat16)
    gates = dot(w_two, hidden)
    gate_vec = gates[CS : CS + CV]
    gate_dir = gates[CS + CV : CS + 2 * CV]
    gate_ten = gates[CS + 2 * CV :]
    message = [gates[:CS] * src[:CS]]
    vec_part = jnp.zeros((CV, edges), jnp.float32)
    dir_part = jnp.zeros((CV, edges), jnp.float32)
    for k in range(3):
        rows = slice(CS + k * CV, CS + (k + 1) * CV)
        message.append(gate_vec * src[rows] + gate_dir * offset[k : k + 1])
        vec_part = vec_part + back[rows] * src[rows]
        dir_part = dir_part + back[rows] * offset[k : k + 1]
    ten_part = jnp.zeros((CT, edges), jnp.float32)
    for m in range(9):
        rows = slice(CS + 3 * CV + m * CT, CS + 3 * CV + (m + 1) * CT)
        message.append(gate_ten * src[rows])
        ten_part = ten_part + back[rows] * src[rows]
    message = jnp.concatenate(message, 0)
    dgates = jnp.concatenate([back[:CS] * src[:CS], vec_part, dir_part, ten_part], 0).astype(
        jnp.bfloat16
    )
    hidden_grad = dot(w_two_t, dgates)
    linear_grad = (hidden_grad * squashed * (1.0 + linear * (1.0 - squashed))).astype(jnp.bfloat16)
    rows = lax.broadcasted_iota(jnp.int32, (16, edges), 0)
    coarse = distance.astype(jnp.bfloat16).astype(jnp.float32)
    extra = jnp.where(
        rows == 0, 1.0, jnp.where(rows == 1, coarse, jnp.where(rows == 2, distance - coarse, 0.0))
    ).astype(jnp.bfloat16)
    grads = (
        dot(linear_grad, jnp.concatenate([inputs, extra], 0), 1, 1),
        dot(dgates, hidden, 1, 1),
    )
    return message, grads


def as_columns(first_row, second_row):
    rows = lax.broadcasted_iota(jnp.int32, (LANES, LANES), 0)
    columns = jnp.where(rows == 0, first_row, jnp.where(rows == 1, second_row, 0.0)).T
    return columns[:, 0:1], columns[:, 1:2]


def add_grads(grads_ref, grads):
    grads_ref[:HID, : 2 * CS + 16] += grads[0]
    grads_ref[HID:, :HID] += grads[1]


def block_diagonal(block_ref, w_scal, w_vec, w_ten):
    block_ref[...] = jnp.zeros_like(block_ref)
    block_ref[:CS, :CS] = w_scal[...]
    for k in range(3):
        rows = slice(CS + k * CV, CS + (k + 1) * CV)
        block_ref[rows, rows] = w_vec[...]
    for m in range(9):
        rows = slice(CS + 3 * CV + m * CT, CS + 3 * CV + (m + 1) * CT)
        block_ref[rows, rows] = w_ten[...]


def mesh_kernel(
    table_ref,
    inner_ref,
    outer_ref,
    code_ref,
    cot_ref,
    w_one_ref,
    b_one_ref,
    w_dist_ref,
    w_two_ref,
    w_scal_ref,
    w_vec_ref,
    w_ten_ref,
    dst_ref,
    mask_ref,
    agg_out_ref,
    grads_out_ref,
    recv_out_ref,
    first_out_ref,
    code_out_ref,
    layers_out_ref,
    rows_out_ref,
    agg_ref,
    grads_ref,
    recv_ref,
    receive_ref,
    source_ref,
    block_ref,
    sems,
):
    node_count = table_ref.shape[1]
    source_ref[:, :node_count] = table_ref[...]
    even = lax.rem(lax.axis_index("sub"), 2) == 0
    low = lax.cond(even, lambda: outer_ref[...], lambda: inner_ref[...])
    high = lax.cond(even, lambda: inner_ref[...], lambda: outer_ref[...])
    source_ref[:, node_count : 2 * node_count] = dot(
        low, one_hot(join_index(low, FEAT + 3), node_count)
    ).astype(jnp.bfloat16)
    source_ref[:, 2 * node_count :] = dot(
        high, one_hot(join_index(high, FEAT + 5), node_count)
    ).astype(jnp.bfloat16)
    block_diagonal(block_ref, w_scal_ref, w_vec_ref, w_ten_ref)
    receive_ref[:FEAT] = dot(block_ref[...], cot_ref[...], 0, 0).astype(jnp.bfloat16)
    receive_ref[FEAT : FEAT + 16] = table_ref[FEAT:]
    receive_ref[FEAT + 16 :] = table_ref[:CS]
    w_one = w_one_ref[...]
    w_two = w_two_ref[...]
    b_column, dist_column = as_columns(b_one_ref[...], w_dist_ref[...])
    scal_recv = table_ref[:CS]
    recv_linear = dot(w_one[:, :CS], scal_recv) + b_column
    weights = (dist_column, w_two, w_two.T)
    pos_recv = table_ref[FEAT:].astype(jnp.float32)[:3]
    grads_ref[...] = jnp.zeros_like(grads_ref)
    agg_ref[...] = jnp.zeros_like(agg_ref)
    for step in range(DEGREE):
        code = code_ref[step]
        src = dot(source_ref[...], one_hot(code, 3 * node_count))
        live = jnp.where(code >= 0, 1.0, 0.0)
        back = receive_ref[:FEAT].astype(jnp.float32)
        scal_send = src[:CS].astype(jnp.bfloat16)
        inputs = jnp.concatenate([scal_recv, scal_send], 0)
        message, grads = edge_math(
            src, recv_linear, dot(w_one[:, CS:], scal_send), inputs, pos_recv, back, live, weights
        )
        agg_ref[...] += message
        add_grads(grads_ref, grads)
    code_out_ref[...] = jnp.where(mask_ref[...] != 0, dst_ref[...], -1)
    for chunk in range(code_out_ref.shape[0]):
        target = first_out_ref if chunk == 0 else recv_ref.at[chunk - 1]
        target[...] = dot(
            receive_ref[...], one_hot(code_out_ref[chunk], node_count)
        ).astype(jnp.bfloat16)
    layers_out_ref[:HID] = w_one
    layers_out_ref[HID:] = w_two
    rows = lax.broadcasted_iota(jnp.int32, (8, HID), 0)
    rows_out_ref[...] = jnp.where(rows == 0, b_one_ref[...], w_dist_ref[...])
    copies = [
        pltpu.make_async_copy(agg_ref, agg_out_ref, sems.at[0]),
        pltpu.make_async_copy(grads_ref, grads_out_ref, sems.at[1]),
        pltpu.make_async_copy(recv_ref, recv_out_ref, sems.at[2]),
    ]
    for copy in copies:
        copy.start()
    for copy in copies:
        copy.wait()


def contact_kernel(
    slot,
    grad_scale,
    reply_ref,
    first_ref,
    code_ref,
    layers_ref,
    rows_ref,
    recv_hbm,
    mesh_agg_hbm,
    mesh_grads_hbm,
    cot_hbm,
    agg_out_ref,
    packed_ref,
    recv_ref,
    agg_ref,
    grads_ref,
    cot_ref,
    src_scr,
    packed_scr,
    sems,
):
    chunks = code_ref.shape[0]
    sources = [
        (recv_hbm, recv_ref),
        (mesh_agg_hbm, agg_ref),
        (mesh_grads_hbm, grads_ref),
        (cot_hbm, cot_ref),
    ]
    copies = [
        pltpu.make_async_copy(source, target, sems.at[at])
        for at, (source, target) in enumerate(sources)
    ]
    for copy in copies:
        copy.start()
    node_count = cot_ref.shape[1]
    parts = LANES // slot
    per_chunk = WIDE // slot
    for chunk in range(chunks):
        blocks = [reply_ref[chunk * per_chunk + peer] for peer in range(per_chunk)]
        src_scr[chunk] = jnp.concatenate(
            [
                jnp.concatenate(
                    [block[:, part * slot : (part + 1) * slot] for block in blocks], 1
                )
                for part in range(parts)
            ],
            0,
        )[:ROWS]
    w_one = layers_ref[:HID]
    w_two = layers_ref[HID:]
    b_column, dist_column = as_columns(rows_ref[0:1], rows_ref[1:2])
    weights = (dist_column, w_two, w_two.T)
    for chunk in range(chunks):
        src_rows = src_scr[chunk]
        if chunk == 1:
            for copy in copies:
                copy.wait()
        recv = first_ref[...] if chunk == 0 else recv_ref[chunk - 1]
        inputs = jnp.concatenate([recv[FEAT + 16 :], src_rows[:CS]], 0)
        message, grads = edge_math(
            src_rows.astype(jnp.float32),
            b_column,
            dot(w_one, inputs),
            inputs,
            recv[FEAT : FEAT + 16].astype(jnp.float32)[:3],
            recv[:FEAT].astype(jnp.float32),
            None,
            weights,
        )
        scattered = dot(message.astype(jnp.bfloat16), one_hot(code_ref[chunk], node_count), 1, 1)
        if chunk == 0:
            held = (scattered, grads)
            continue
        agg_ref[...] += scattered
        add_grads(grads_ref, grads)
        if chunk == 1:
            agg_ref[...] += held[0]
            add_grads(grads_ref, held[1])
    agg_rows = agg_ref[...].astype(jnp.bfloat16)
    agg_out_ref[...] = agg_rows
    cot = cot_ref[...]
    low = HID + GATES
    packed_scr[:low] = grads_ref[:, :LANES] * grad_scale
    scal = dot(cot[:CS], agg_rows[:CS], 1, 1) * grad_scale
    packed_scr[low : low + CS // 2] = jnp.concatenate([scal[: CS // 2], scal[CS // 2 :]], 1)
    low = low + CS // 2
    mixed = dot(cot[CS:], agg_rows[CS:], 1, 1)
    grad_vec = jnp.zeros((CV, CV), jnp.float32)
    for k in range(3):
        rows = slice(k * CV, (k + 1) * CV)
        grad_vec = grad_vec + mixed[rows, rows]
    each = CV * CV // LANES
    packed_scr[low : low + each] = grad_scale * jnp.concatenate(
        [grad_vec[at : at + each] for at in range(0, CV, each)], 1
    )
    low = low + each
    grad_ten = jnp.zeros((CT, CT), jnp.float32)
    for m in range(9):
        rows = slice(3 * CV + m * CT, 3 * CV + (m + 1) * CT)
        grad_ten = grad_ten + mixed[rows, rows]
    each = CT * CT // LANES
    packed_scr[low : low + each] = grad_scale * jnp.concatenate(
        [grad_ten[at : at + each] for at in range(0, CT, each)], 1
    )
    low = low + each
    extra = (grads_ref[:HID, LANES:] * grad_scale).T
    packed_scr[low : low + 1] = extra[0:1]
    packed_scr[low + 1 : low + 2] = extra[1:2] + extra[2:3]
    packed = packed_scr[...].astype(jnp.bfloat16)
    tiles = packed_ref.shape[1]
    for peer in range(packed_ref.shape[0]):
        for tile in range(tiles):
            at = (peer * tiles + tile) * FINE
            if at < packed.shape[0]:
                packed_ref[peer, tile] = packed[at : at + FINE]
            else:
                packed_ref[peer, tile] = jnp.zeros((FINE, LANES), jnp.bfloat16)


def sum_kernel(parts_ref, out_ref):
    total = parts_ref[0].astype(jnp.float32)
    for peer in range(1, parts_ref.shape[0]):
        total = total + parts_ref[peer].astype(jnp.float32)
    total = total.astype(jnp.bfloat16)
    for peer in range(out_ref.shape[0]):
        out_ref[peer] = total


def finish_kernel(
    blocks_ref,
    table_ref,
    agg_ref,
    w_scal_ref,
    w_vec_ref,
    w_ten_ref,
    out_ref,
    one_ref,
    bias_ref,
    dist_ref,
    two_ref,
    scal_ref,
    vec_ref,
    ten_ref,
    block_ref,
):
    block_diagonal(block_ref, w_scal_ref, w_vec_ref, w_ten_ref)
    out_ref[...] = (
        table_ref[:FEAT].astype(jnp.float32) + dot(block_ref[...], agg_ref[...])
    ).astype(jnp.bfloat16)

    tiles = blocks_ref.shape[1]

    def rows_of(at):
        peer, tile = divmod(at // FINE, tiles)
        return blocks_ref[peer, tile].astype(jnp.float32)

    for at in range(0, HID, FINE):
        one_ref[at : at + FINE] = rows_of(at)
    for at in range(0, GATES, FINE):
        two_ref[at : at + FINE] = rows_of(HID + at)
    low = HID + GATES
    for at in range(0, CS // 2, FINE):
        rows = rows_of(low + at)
        scal_ref[at : at + FINE] = rows[:, :CS]
        scal_ref[CS // 2 + at : CS // 2 + at + FINE] = rows[:, CS:]
    low = low + CS // 2
    for ref, width in ((vec_ref, CV), (ten_ref, CT)):
        each = width * width // LANES
        for at in range(0, each, FINE):
            rows = rows_of(low + at)
            for piece in range(width // each):
                to = piece * each + at
                ref[to : to + FINE] = rows[:, piece * width : (piece + 1) * width]
        low = low + each
    extra = rows_of(low)
    bias_ref[...] = extra[0:1]
    dist_ref[...] = extra[1:2]


def call(kernel, out_shape, scratch=(), in_specs=None, out_specs=None, cost_estimate=None):
    specs = {}
    if cost_estimate is not None:
        specs["cost_estimate"] = cost_estimate
    if in_specs is not None:
        specs["in_specs"] = in_specs
    if out_specs is not None:
        specs["out_specs"] = out_specs
    return pl.pallas_call(
        kernel,
        out_shape=out_shape,
        scratch_shapes=list(scratch),
        compiler_params=pltpu.CompilerParams(vmem_limit_bytes=VMEM_BYTES),
        **specs,
    )


IN_VMEM = pl.BlockSpec(memory_space=pltpu.VMEM)
IN_HBM = pl.BlockSpec(memory_space=pltpu.HBM)
ANYWHERE = pl.BlockSpec(memory_space=pl.ANY)


def exchange(blocks, axes=("dom", "sub")):
    return lax.all_to_all(blocks, axes, split_axis=0, concat_axis=0, tiled=True)


def in_hbm(*arrays):
    return tuple(pltpu.with_memory_space_constraint(array, pltpu.HBM) for array in arrays)


def shaped(shape, dtype):
    return jax.ShapeDtypeStruct(shape, dtype)


def swapped(shard, axis, first):
    peers = lax.axis_size(axis)
    pairs = [(at, (at + 1) % peers) for at in range(first, peers, 2)]
    return lax.ppermute(shard, axis, pairs + [(there, here) for here, there in pairs])


def on_device(
    node_feat,
    node_pos,
    node_cot,
    mesh_senders,
    edge_mask,
    halo_up,
    halo_down,
    contact_rows,
    contact_dst,
    contact_mask,
    w_one,
    b_one,
    w_dist,
    w_two,
    w_scal,
    w_vec,
    w_ten,
):
    f32, bf16 = jnp.float32, jnp.bfloat16
    node_count = node_feat.shape[1]
    contact_count = contact_rows.shape[0]
    device_count = lax.axis_size("dom") * lax.axis_size("sub")
    slot = contact_count // device_count
    chunks = contact_count // CHUNK
    wides = contact_count // WIDE
    parts = LANES // slot
    height = -(-ROWS // (parts * 16)) * 16
    grad_scale = 1.0 / math.sqrt(device_count * node_count * DEGREE)
    table, requests = call(
        table_kernel,
        (
            shaped((ROWS, node_count), bf16),
            shaped((device_count, 1, slot), jnp.int32),
        ),
        (
            pltpu.VMEM((3, node_count), bf16),
            pltpu.VMEM((1, node_count), jnp.int32),
            pltpu.VMEM((1, node_count), jnp.int32),
            pltpu.VMEM((contact_count // LANES, LANES), jnp.int32),
            pltpu.SemaphoreType.DMA((5,)),
        ),
        in_specs=[IN_HBM] * 5,
        out_specs=(IN_VMEM, IN_VMEM),
    )(
        *in_hbm(
            node_feat,
            node_pos,
            halo_up[None],
            halo_down[None],
            contact_rows.reshape(contact_count // LANES, LANES),
        )
    )
    wanted = exchange(requests)
    wanted, table_late = lax.optimization_barrier((wanted, table))
    inner = swapped(table_late, "sub", 0)
    outer = swapped(table_late, "sub", 1)
    found = call(
        functools.partial(contact_gather_kernel, slot),
        pltpu.HBM((device_count, height, LANES), bf16),
        (
            pltpu.VMEM((device_count, height, LANES), bf16),
            pltpu.SemaphoreType.DMA((chunks,)),
        ),
        in_specs=[IN_VMEM, IN_VMEM],
        out_specs=IN_HBM,
    )(table, wanted)
    found, mesh_senders, edge_mask = lax.optimization_barrier((found, mesh_senders, edge_mask))
    replies = exchange(found)
    mesh_code = (
        jnp.where(edge_mask != 0, mesh_senders, -1)
        .reshape(node_count, DEGREE)
        .T.reshape(DEGREE, 1, node_count)
    )
    contact_dst = contact_dst.reshape(wides, 1, WIDE)
    contact_mask = contact_mask.reshape(wides, 1, WIDE)
    mesh_rows = HID + GATES
    recv_rows = FEAT + 16 + CS
    mesh_agg, mesh_grads, recv, first, contact_code, layers, rows = call(
        mesh_kernel,
        (
            pltpu.HBM((FEAT, node_count), f32),
            pltpu.HBM((mesh_rows, 2 * LANES), f32),
            pltpu.HBM((wides - 1, recv_rows, WIDE), bf16),
            shaped((recv_rows, WIDE), bf16),
            shaped((wides, 1, WIDE), jnp.int32),
            shaped((mesh_rows, HID), bf16),
            shaped((8, HID), f32),
        ),
        (
            pltpu.VMEM((FEAT, node_count), f32),
            pltpu.VMEM((mesh_rows, 2 * LANES), f32),
            pltpu.VMEM((wides - 1, recv_rows, WIDE), bf16),
            pltpu.VMEM((recv_rows, node_count), bf16),
            pltpu.VMEM((ROWS, 3 * node_count), bf16),
            pltpu.VMEM((FEAT, FEAT), bf16),
            pltpu.SemaphoreType.DMA((3,)),
        ),
        in_specs=[IN_VMEM] * 14,
        out_specs=(IN_HBM,) * 3 + (IN_VMEM,) * 4,
        cost_estimate=pl.CostEstimate(
            flops=40_000_000_000, bytes_accessed=8_000_000, transcendentals=400_000
        ),
    )(
        table,
        inner,
        outer,
        mesh_code,
        node_cot,
        w_one,
        b_one[None],
        w_dist[None],
        w_two,
        w_scal,
        w_vec,
        w_ten,
        contact_dst,
        contact_mask,
    )
    packed_rows = mesh_rows + (CS * CS + CV * CV + CT * CT) // LANES + 2
    tiles = -(-packed_rows // (FINE * device_count))
    share = (device_count, tiles, FINE, LANES)
    agg_rows, packed = call(
        functools.partial(contact_kernel, slot, grad_scale),
        (shaped((FEAT, node_count), bf16), shaped(share, bf16)),
        (
            pltpu.VMEM((wides - 1, recv_rows, WIDE), bf16),
            pltpu.VMEM((FEAT, node_count), f32),
            pltpu.VMEM((mesh_rows, 2 * LANES), f32),
            pltpu.VMEM((FEAT, node_count), bf16),
            pltpu.VMEM((wides, ROWS, WIDE), bf16),
            pltpu.VMEM((packed_rows, LANES), f32),
            pltpu.SemaphoreType.DMA((4,)),
        ),
        in_specs=[IN_VMEM] * 5 + [IN_HBM] * 4,
        out_specs=(IN_VMEM, IN_VMEM),
    )(
        replies,
        first,
        contact_code,
        layers,
        rows,
        *in_hbm(recv, mesh_agg, mesh_grads, node_cot),
    )
    shares = call(sum_kernel, shaped(share, bf16))(exchange(packed))
    node_out, one, bias, dist, two, scal, vec, ten = call(
        finish_kernel,
        (
            shaped((FEAT, node_count), bf16),
            shaped((HID, 2 * CS), f32),
            shaped((1, HID), f32),
            shaped((1, HID), f32),
            shaped((GATES, HID), f32),
            shaped((CS, CS), f32),
            shaped((CV, CV), f32),
            shaped((CT, CT), f32),
        ),
        (pltpu.VMEM((FEAT, FEAT), bf16),),
    )(exchange(shares), table, agg_rows, w_scal, w_vec, w_ten)
    return node_out, one, bias[0], dist[0], two, scal, vec, ten


def solution(mesh):
    along = P(("dom", "sub"))
    columns = P(None, ("dom", "sub"))
    in_specs = (columns,) * 3 + (along,) * 7 + (P(),) * 7
    out_specs = (columns,) + (P(),) * 7
    return jax.shard_map(
        on_device, mesh=mesh, in_specs=in_specs, out_specs=out_specs, check_vma=False
    )
```

```python
import functools
import math

import jax
import jax.numpy as jnp
from jax import lax
from jax.experimental import pallas as pl
from jax.experimental.pallas import tpu as pltpu
from jax.sharding import PartitionSpec as P

CS = 64
CV = 32
CT = 16
HID = 128
DEGREE = 6
GATES = 144
FEAT = CS + 3 * CV + 9 * CT
ROWS = 320
LANES = 128
FINE = 2
CHUNK = 512
WIDE = 1024
VMEM_BYTES = 48 * 1024 * 1024


def dot(lhs, rhs, lhs_dim=1, rhs_dim=0):
    return lax.dot_general(
        lhs, rhs, (((lhs_dim,), (rhs_dim,)), ((), ())), preferred_element_type=jnp.float32
    )


def one_hot(code, width):
    rows = lax.broadcasted_iota(jnp.int16, (width, code.shape[1]), 0)
    return jnp.where(rows == code.astype(jnp.int16), jnp.bfloat16(1), jnp.bfloat16(0))


def join_index(table, row):
    pair = table[row : row + 2].astype(jnp.float32)
    return (pair[0:1] * 128.0 + pair[1:2]).astype(jnp.int32)


def table_kernel(
    feat_ref,
    pos_ref,
    up_ref,
    down_ref,
    rows_ref,
    table_ref,
    request_ref,
    pos_scr,
    up_scr,
    down_scr,
    rows_scr,
    sems,
):
    node_count = table_ref.shape[1]
    copies = [
        pltpu.make_async_copy(rows_ref, rows_scr, sems.at[0]),
        pltpu.make_async_copy(feat_ref, table_ref.at[:FEAT], sems.at[1]),
        pltpu.make_async_copy(pos_ref, pos_scr, sems.at[2]),
        pltpu.make_async_copy(up_ref, up_scr, sems.at[3]),
        pltpu.make_async_copy(down_ref, down_scr, sems.at[4]),
    ]
    for copy in copies:
        copy.start()
    copies[0].wait()
    slot = request_ref.shape[2]
    parts = LANES // slot
    for row in range(rows_scr.shape[0]):
        line = rows_scr[row : row + 1]
        for part in range(parts):
            request_ref[row * parts + part] = line[:, part * slot : (part + 1) * slot]
    for copy in copies[2:]:
        copy.wait()
    rows = lax.broadcasted_iota(jnp.int32, (ROWS - FEAT, node_count), 0)
    pos = pos_scr[...].astype(jnp.float32)
    tail = jnp.zeros((ROWS - FEAT, node_count), jnp.float32)
    for k in range(3):
        tail = jnp.where(rows == k, pos[k : k + 1], tail)
    for k, index_ref in ((3, up_scr), (5, down_scr)):
        index = index_ref[...]
        high = index >> 7
        tail = jnp.where(rows == k, high.astype(jnp.float32), tail)
        tail = jnp.where(rows == k + 1, (index - (high << 7)).astype(jnp.float32), tail)
    table_ref[FEAT:] = tail.astype(jnp.bfloat16)
    copies[1].wait()


def contact_gather_kernel(slot, table_ref, wanted_ref, out_hbm, out_ref, sems):
    node_count = table_ref.shape[1]
    parts = LANES // slot
    height = out_ref.shape[1]
    per_chunk = CHUNK // slot
    copies = []
    for chunk in range(wanted_ref.shape[0] // per_chunk):
        wanted = [wanted_ref[chunk * per_chunk + peer] for peer in range(per_chunk)]
        hot = one_hot(jnp.concatenate(wanted, 1), node_count)
        rows = dot(table_ref[...], hot).astype(jnp.bfloat16)
        if parts * height > ROWS:
            rows = jnp.concatenate(
                [rows, jnp.zeros((parts * height - ROWS, CHUNK), jnp.bfloat16)], 0
            )
        for peer in range(per_chunk):
            out_ref[chunk * per_chunk + peer] = jnp.concatenate(
                [
                    rows[part * height : (part + 1) * height, peer * slot : (peer + 1) * slot]
                    for part in range(parts)
                ],
                1,
            )
        done = pl.ds(chunk * per_chunk, per_chunk)
        copies.append(
            pltpu.make_async_copy(out_ref.at[done], out_hbm.at[done], sems.at[chunk])
        )
        copies[-1].start()
    for copy in copies:
        copy.wait()


def edge_math(*operands):
    steps = edge_steps(*operands)
    while True:
        try:
            next(steps)
        except StopIteration as end:
            return end.value


def edge_steps(src, base, w_first, first, inputs, pos_recv, back, live, weights):
    w_dist, w_two, w_two_t = weights
    edges = src.shape[1]
    offset = src[FEAT : FEAT + 3] - pos_recv
    if live is not None:
        offset = offset * live
    distance = jnp.sum(offset * offset, 0, keepdims=True)
    product = dot(w_first, first)
    yield
    linear = base + product + w_dist * distance
    squashed = 0.5 * jnp.tanh(0.5 * linear) + 0.5
    hidden = (linear * squashed).astype(jnp.bfloat16)
    yield
    gates = dot(w_two, hidden)
    yield
    gate_vec = gates[CS : CS + CV]
    gate_dir = gates[CS + CV : CS + 2 * CV]
    gate_ten = gates[CS + 2 * CV :]
    message = [gates[:CS] * src[:CS]]
    vec_part = jnp.zeros((CV, edges), jnp.float32)
    dir_part = jnp.zeros((CV, edges), jnp.float32)
    for k in range(3):
        rows = slice(CS + k * CV, CS + (k + 1) * CV)
        message.append(gate_vec * src[rows] + gate_dir * offset[k : k + 1])
        vec_part = vec_part + back[rows] * src[rows]
        dir_part = dir_part + back[rows] * offset[k : k + 1]
    ten_part = jnp.zeros((CT, edges), jnp.float32)
    for m in range(9):
        rows = slice(CS + 3 * CV + m * CT, CS + 3 * CV + (m + 1) * CT)
        message.append(gate_ten * src[rows])
        ten_part = ten_part + back[rows] * src[rows]
    message = jnp.concatenate(message, 0)
    dgates = jnp.concatenate([back[:CS] * src[:CS], vec_part, dir_part, ten_part], 0).astype(
        jnp.bfloat16
    )
    message = message.astype(jnp.bfloat16) if live is None else message
    yield
    hidden_grad = dot(w_two_t, dgates)
    yield
    linear_grad = (hidden_grad * squashed * (1.0 + linear * (1.0 - squashed))).astype(jnp.bfloat16)
    rows = lax.broadcasted_iota(jnp.int32, (16, edges), 0)
    coarse = distance.astype(jnp.bfloat16).astype(jnp.float32)
    extra = jnp.where(
        rows == 0, 1.0, jnp.where(rows == 1, coarse, jnp.where(rows == 2, distance - coarse, 0.0))
    ).astype(jnp.bfloat16)
    grads = (
        dot(linear_grad, jnp.concatenate([inputs, extra], 0), 1, 1),
        dot(dgates, hidden, 1, 1),
    )
    return message, grads


def as_columns(first_row, second_row):
    rows = lax.broadcasted_iota(jnp.int32, (LANES, LANES), 0)
    columns = jnp.where(rows == 0, first_row, jnp.where(rows == 1, second_row, 0.0)).T
    return columns[:, 0:1], columns[:, 1:2]


def add_grads(grads_ref, grads):
    grads_ref[:HID, : 2 * CS + 16] += grads[0]
    grads_ref[HID:, :HID] += grads[1]


def block_diagonal(block_ref, w_scal, w_vec, w_ten):
    block_ref[...] = jnp.zeros_like(block_ref)
    block_ref[:CS, :CS] = w_scal[...]
    for k in range(3):
        rows = slice(CS + k * CV, CS + (k + 1) * CV)
        block_ref[rows, rows] = w_vec[...]
    for m in range(9):
        rows = slice(CS + 3 * CV + m * CT, CS + 3 * CV + (m + 1) * CT)
        block_ref[rows, rows] = w_ten[...]


def mesh_kernel(
    table_ref,
    inner_ref,
    outer_ref,
    code_ref,
    cot_ref,
    w_one_ref,
    b_one_ref,
    w_dist_ref,
    w_two_ref,
    w_scal_ref,
    w_vec_ref,
    w_ten_ref,
    dst_ref,
    mask_ref,
    agg_out_ref,
    grads_out_ref,
    recv_out_ref,
    first_out_ref,
    code_out_ref,
    layers_out_ref,
    rows_out_ref,
    agg_ref,
    grads_ref,
    recv_ref,
    receive_ref,
    source_ref,
    block_ref,
    sems,
):
    node_count = table_ref.shape[1]
    source_ref[:, :node_count] = table_ref[...]
    even = lax.rem(lax.axis_index("sub"), 2) == 0
    low = lax.cond(even, lambda: outer_ref[...], lambda: inner_ref[...])
    high = lax.cond(even, lambda: inner_ref[...], lambda: outer_ref[...])
    source_ref[:, node_count : 2 * node_count] = dot(
        low, one_hot(join_index(low, FEAT + 3), node_count)
    ).astype(jnp.bfloat16)
    source_ref[:, 2 * node_count :] = dot(
        high, one_hot(join_index(high, FEAT + 5), node_count)
    ).astype(jnp.bfloat16)
    block_diagonal(block_ref, w_scal_ref, w_vec_ref, w_ten_ref)
    receive_ref[:FEAT] = dot(block_ref[...], cot_ref[...], 0, 0).astype(jnp.bfloat16)
    receive_ref[FEAT : FEAT + 16] = table_ref[FEAT:]
    receive_ref[FEAT + 16 :] = table_ref[:CS]
    w_one = w_one_ref[...]
    w_two = w_two_ref[...]
    b_column, dist_column = as_columns(b_one_ref[...], w_dist_ref[...])
    scal_recv = table_ref[:CS]
    recv_linear = dot(w_one[:, :CS], scal_recv) + b_column
    weights = (dist_column, w_two, w_two.T)
    pos_recv = table_ref[FEAT:].astype(jnp.float32)[:3]
    grads_ref[...] = jnp.zeros_like(grads_ref)
    agg_ref[...] = jnp.zeros_like(agg_ref)
    for step in range(DEGREE):
        code = code_ref[step]
        src = dot(source_ref[...], one_hot(code, 3 * node_count))
        live = jnp.where(code >= 0, 1.0, 0.0)
        back = receive_ref[:FEAT].astype(jnp.float32)
        scal_send = src[:CS].astype(jnp.bfloat16)
        inputs = jnp.concatenate([scal_recv, scal_send], 0)
        message, grads = edge_math(
            src, recv_linear, w_one[:, CS:], scal_send, inputs, pos_recv, back, live, weights
        )
        agg_ref[...] += message
        add_grads(grads_ref, grads)
    code_out_ref[...] = jnp.where(mask_ref[...] != 0, dst_ref[...], -1)
    for chunk in range(code_out_ref.shape[0]):
        target = first_out_ref if chunk == 0 else recv_ref.at[chunk - 1]
        target[...] = dot(
            receive_ref[...], one_hot(code_out_ref[chunk], node_count)
        ).astype(jnp.bfloat16)
    layers_out_ref[:HID] = w_one
    layers_out_ref[HID:] = w_two
    rows = lax.broadcasted_iota(jnp.int32, (8, HID), 0)
    rows_out_ref[...] = jnp.where(rows == 0, b_one_ref[...], w_dist_ref[...])
    copies = [
        pltpu.make_async_copy(agg_ref, agg_out_ref, sems.at[0]),
        pltpu.make_async_copy(grads_ref, grads_out_ref, sems.at[1]),
        pltpu.make_async_copy(recv_ref, recv_out_ref, sems.at[2]),
    ]
    for copy in copies:
        copy.start()
    for copy in copies:
        copy.wait()


def contact_kernel(
    slot,
    grad_scale,
    reply_ref,
    first_ref,
    code_ref,
    layers_ref,
    rows_ref,
    recv_hbm,
    mesh_agg_hbm,
    mesh_grads_hbm,
    cot_hbm,
    agg_out_ref,
    packed_ref,
    recv_ref,
    agg_ref,
    grads_ref,
    cot_ref,
    src_scr,
    packed_scr,
    sems,
):
    chunks = code_ref.shape[0]
    sources = [
        (recv_hbm, recv_ref),
        (mesh_agg_hbm, agg_ref),
        (mesh_grads_hbm, grads_ref),
        (cot_hbm, cot_ref),
    ]
    copies = [
        pltpu.make_async_copy(source, target, sems.at[at])
        for at, (source, target) in enumerate(sources)
    ]
    for copy in copies:
        copy.start()
    node_count = cot_ref.shape[1]
    parts = LANES // slot
    per_chunk = WIDE // slot
    for chunk in range(chunks):
        blocks = [reply_ref[chunk * per_chunk + peer] for peer in range(per_chunk)]
        src_scr[chunk] = jnp.concatenate(
            [
                jnp.concatenate(
                    [block[:, part * slot : (part + 1) * slot] for block in blocks], 1
                )
                for part in range(parts)
            ],
            0,
        )[:ROWS]
    w_one = layers_ref[:HID]
    w_two = layers_ref[HID:]
    b_column, dist_column = as_columns(rows_ref[0:1], rows_ref[1:2])
    weights = (dist_column, w_two, w_two.T)
    def steps_of(chunk):
        src_rows = src_scr[chunk]
        recv = first_ref[...] if chunk == 0 else recv_ref[chunk - 1]
        inputs = jnp.concatenate([recv[FEAT + 16 :], src_rows[:CS]], 0)
        message, grads = yield from edge_steps(
            src_rows.astype(jnp.float32),
            b_column,
            w_one,
            inputs,
            inputs,
            recv[FEAT : FEAT + 16].astype(jnp.float32)[:3],
            recv[:FEAT].astype(jnp.float32),
            None,
            weights,
        )
        yield
        return dot(message, one_hot(code_ref[chunk], node_count), 1, 1), grads

    running = [steps_of(0)]
    next(running[0])
    for copy in copies:
        copy.wait()
    running += [steps_of(chunk) for chunk in range(1, chunks)]
    while running:
        for steps in list(running):
            try:
                next(steps)
            except StopIteration as end:
                agg_ref[...] += end.value[0]
                add_grads(grads_ref, end.value[1])
                running.remove(steps)
    agg_rows = agg_ref[...].astype(jnp.bfloat16)
    agg_out_ref[...] = agg_rows
    cot = cot_ref[...]
    low = HID + GATES
    packed_scr[:low] = grads_ref[:, :LANES] * grad_scale
    scal = dot(cot[:CS], agg_rows[:CS], 1, 1) * grad_scale
    packed_scr[low : low + CS // 2] = jnp.concatenate([scal[: CS // 2], scal[CS // 2 :]], 1)
    low = low + CS // 2
    mixed = dot(cot[CS:], agg_rows[CS:], 1, 1)
    grad_vec = jnp.zeros((CV, CV), jnp.float32)
    for k in range(3):
        rows = slice(k * CV, (k + 1) * CV)
        grad_vec = grad_vec + mixed[rows, rows]
    each = CV * CV // LANES
    packed_scr[low : low + each] = grad_scale * jnp.concatenate(
        [grad_vec[at : at + each] for at in range(0, CV, each)], 1
    )
    low = low + each
    grad_ten = jnp.zeros((CT, CT), jnp.float32)
    for m in range(9):
        rows = slice(3 * CV + m * CT, 3 * CV + (m + 1) * CT)
        grad_ten = grad_ten + mixed[rows, rows]
    each = CT * CT // LANES
    packed_scr[low : low + each] = grad_scale * jnp.concatenate(
        [grad_ten[at : at + each] for at in range(0, CT, each)], 1
    )
    low = low + each
    extra = (grads_ref[:HID, LANES:] * grad_scale).T
    packed_scr[low : low + 1] = extra[0:1]
    packed_scr[low + 1 : low + 2] = extra[1:2] + extra[2:3]
    packed = packed_scr[...].astype(jnp.bfloat16)
    tiles = packed_ref.shape[1]
    for peer in range(packed_ref.shape[0]):
        for tile in range(tiles):
            at = (peer * tiles + tile) * FINE
            if at < packed.shape[0]:
                packed_ref[peer, tile] = packed[at : at + FINE]
            else:
                packed_ref[peer, tile] = jnp.zeros((FINE, LANES), jnp.bfloat16)


def sum_kernel(parts_ref, out_ref):
    total = parts_ref[0].astype(jnp.float32)
    for peer in range(1, parts_ref.shape[0]):
        total = total + parts_ref[peer].astype(jnp.float32)
    total = total.astype(jnp.bfloat16)
    for peer in range(out_ref.shape[0]):
        out_ref[peer] = total


def finish_kernel(
    blocks_ref,
    table_ref,
    agg_ref,
    w_scal_ref,
    w_vec_ref,
    w_ten_ref,
    out_ref,
    one_ref,
    bias_ref,
    dist_ref,
    two_ref,
    scal_ref,
    vec_ref,
    ten_ref,
    block_ref,
):
    block_diagonal(block_ref, w_scal_ref, w_vec_ref, w_ten_ref)
    out_ref[...] = (
        table_ref[:FEAT].astype(jnp.float32) + dot(block_ref[...], agg_ref[...])
    ).astype(jnp.bfloat16)

    tiles = blocks_ref.shape[1]

    def rows_of(at):
        peer, tile = divmod(at // FINE, tiles)
        return blocks_ref[peer, tile].astype(jnp.float32)

    for at in range(0, HID, FINE):
        one_ref[at : at + FINE] = rows_of(at)
    for at in range(0, GATES, FINE):
        two_ref[at : at + FINE] = rows_of(HID + at)
    low = HID + GATES
    for at in range(0, CS // 2, FINE):
        rows = rows_of(low + at)
        scal_ref[at : at + FINE] = rows[:, :CS]
        scal_ref[CS // 2 + at : CS // 2 + at + FINE] = rows[:, CS:]
    low = low + CS // 2
    for ref, width in ((vec_ref, CV), (ten_ref, CT)):
        each = width * width // LANES
        for at in range(0, each, FINE):
            rows = rows_of(low + at)
            for piece in range(width // each):
                to = piece * each + at
                ref[to : to + FINE] = rows[:, piece * width : (piece + 1) * width]
        low = low + each
    extra = rows_of(low)
    bias_ref[...] = extra[0:1]
    dist_ref[...] = extra[1:2]


def call(kernel, out_shape, scratch=(), in_specs=None, out_specs=None, cost_estimate=None):
    specs = {}
    if cost_estimate is not None:
        specs["cost_estimate"] = cost_estimate
    if in_specs is not None:
        specs["in_specs"] = in_specs
    if out_specs is not None:
        specs["out_specs"] = out_specs
    return pl.pallas_call(
        kernel,
        out_shape=out_shape,
        scratch_shapes=list(scratch),
        compiler_params=pltpu.CompilerParams(vmem_limit_bytes=VMEM_BYTES),
        **specs,
    )


IN_VMEM = pl.BlockSpec(memory_space=pltpu.VMEM)
IN_HBM = pl.BlockSpec(memory_space=pltpu.HBM)
ANYWHERE = pl.BlockSpec(memory_space=pl.ANY)


def exchange(blocks, axes=("dom", "sub")):
    return lax.all_to_all(blocks, axes, split_axis=0, concat_axis=0, tiled=True)


def in_hbm(*arrays):
    return tuple(pltpu.with_memory_space_constraint(array, pltpu.HBM) for array in arrays)


def shaped(shape, dtype):
    return jax.ShapeDtypeStruct(shape, dtype)


def swapped(shard, axis, first):
    peers = lax.axis_size(axis)
    pairs = [(at, (at + 1) % peers) for at in range(first, peers, 2)]
    return lax.ppermute(shard, axis, pairs + [(there, here) for here, there in pairs])


def on_device(
    node_feat,
    node_pos,
    node_cot,
    mesh_senders,
    edge_mask,
    halo_up,
    halo_down,
    contact_rows,
    contact_dst,
    contact_mask,
    w_one,
    b_one,
    w_dist,
    w_two,
    w_scal,
    w_vec,
    w_ten,
):
    f32, bf16 = jnp.float32, jnp.bfloat16
    node_count = node_feat.shape[1]
    contact_count = contact_rows.shape[0]
    device_count = lax.axis_size("dom") * lax.axis_size("sub")
    slot = contact_count // device_count
    chunks = contact_count // CHUNK
    wides = contact_count // WIDE
    parts = LANES // slot
    height = -(-ROWS // (parts * 16)) * 16
    grad_scale = 1.0 / math.sqrt(device_count * node_count * DEGREE)
    table, requests = call(
        table_kernel,
        (
            shaped((ROWS, node_count), bf16),
            shaped((device_count, 1, slot), jnp.int32),
        ),
        (
            pltpu.VMEM((3, node_count), bf16),
            pltpu.VMEM((1, node_count), jnp.int32),
            pltpu.VMEM((1, node_count), jnp.int32),
            pltpu.VMEM((contact_count // LANES, LANES), jnp.int32),
            pltpu.SemaphoreType.DMA((5,)),
        ),
        in_specs=[IN_HBM] * 5,
        out_specs=(IN_VMEM, IN_VMEM),
    )(
        *in_hbm(
            node_feat,
            node_pos,
            halo_up[None],
            halo_down[None],
            contact_rows.reshape(contact_count // LANES, LANES),
        )
    )
    wanted = exchange(requests)
    wanted, table_late = lax.optimization_barrier((wanted, table))
    inner = swapped(table_late, "sub", 0)
    outer = swapped(table_late, "sub", 1)
    found = call(
        functools.partial(contact_gather_kernel, slot),
        pltpu.HBM((device_count, height, LANES), bf16),
        (
            pltpu.VMEM((device_count, height, LANES), bf16),
            pltpu.SemaphoreType.DMA((chunks,)),
        ),
        in_specs=[IN_VMEM, IN_VMEM],
        out_specs=IN_HBM,
    )(table, wanted)
    found, mesh_senders, edge_mask = lax.optimization_barrier((found, mesh_senders, edge_mask))
    replies = exchange(found)
    mesh_code = (
        jnp.where(edge_mask != 0, mesh_senders, -1)
        .reshape(node_count, DEGREE)
        .T.reshape(DEGREE, 1, node_count)
    )
    contact_dst = contact_dst.reshape(wides, 1, WIDE)
    contact_mask = contact_mask.reshape(wides, 1, WIDE)
    mesh_rows = HID + GATES
    recv_rows = FEAT + 16 + CS
    mesh_agg, mesh_grads, recv, first, contact_code, layers, rows = call(
        mesh_kernel,
        (
            pltpu.HBM((FEAT, node_count), f32),
            pltpu.HBM((mesh_rows, 2 * LANES), f32),
            pltpu.HBM((wides - 1, recv_rows, WIDE), bf16),
            shaped((recv_rows, WIDE), bf16),
            shaped((wides, 1, WIDE), jnp.int32),
            shaped((mesh_rows, HID), bf16),
            shaped((8, HID), f32),
        ),
        (
            pltpu.VMEM((FEAT, node_count), f32),
            pltpu.VMEM((mesh_rows, 2 * LANES), f32),
            pltpu.VMEM((wides - 1, recv_rows, WIDE), bf16),
            pltpu.VMEM((recv_rows, node_count), bf16),
            pltpu.VMEM((ROWS, 3 * node_count), bf16),
            pltpu.VMEM((FEAT, FEAT), bf16),
            pltpu.SemaphoreType.DMA((3,)),
        ),
        in_specs=[IN_VMEM] * 14,
        out_specs=(IN_HBM,) * 3 + (IN_VMEM,) * 4,
        cost_estimate=pl.CostEstimate(
            flops=40_000_000_000, bytes_accessed=8_000_000, transcendentals=400_000
        ),
    )(
        table,
        inner,
        outer,
        mesh_code,
        node_cot,
        w_one,
        b_one[None],
        w_dist[None],
        w_two,
        w_scal,
        w_vec,
        w_ten,
        contact_dst,
        contact_mask,
    )
    packed_rows = mesh_rows + (CS * CS + CV * CV + CT * CT) // LANES + 2
    tiles = -(-packed_rows // (FINE * device_count))
    share = (device_count, tiles, FINE, LANES)
    agg_rows, packed = call(
        functools.partial(contact_kernel, slot, grad_scale),
        (shaped((FEAT, node_count), bf16), shaped(share, bf16)),
        (
            pltpu.VMEM((wides - 1, recv_rows, WIDE), bf16),
            pltpu.VMEM((FEAT, node_count), f32),
            pltpu.VMEM((mesh_rows, 2 * LANES), f32),
            pltpu.VMEM((FEAT, node_count), bf16),
            pltpu.VMEM((wides, ROWS, WIDE), bf16),
            pltpu.VMEM((packed_rows, LANES), f32),
            pltpu.SemaphoreType.DMA((4,)),
        ),
        in_specs=[IN_VMEM] * 5 + [IN_HBM] * 4,
        out_specs=(IN_VMEM, IN_VMEM),
    )(
        replies,
        first,
        contact_code,
        layers,
        rows,
        *in_hbm(recv, mesh_agg, mesh_grads, node_cot),
    )
    shares = call(sum_kernel, shaped(share, bf16))(exchange(packed))
    node_out, one, bias, dist, two, scal, vec, ten = call(
        finish_kernel,
        (
            shaped((FEAT, node_count), bf16),
            shaped((HID, 2 * CS), f32),
            shaped((1, HID), f32),
            shaped((1, HID), f32),
            shaped((GATES, HID), f32),
            shaped((CS, CS), f32),
            shaped((CV, CV), f32),
            shaped((CT, CT), f32),
        ),
        (pltpu.VMEM((FEAT, FEAT), bf16),),
    )(exchange(shares), table, agg_rows, w_scal, w_vec, w_ten)
    return node_out, one, bias[0], dist[0], two, scal, vec, ten


def solution(mesh):
    along = P(("dom", "sub"))
    columns = P(None, ("dom", "sub"))
    in_specs = (columns,) * 3 + (along,) * 7 + (P(),) * 7
    out_specs = (columns,) + (P(),) * 7
    return jax.shard_map(
        on_device, mesh=mesh, in_specs=in_specs, out_specs=out_specs, check_vma=False
    )
```

```python
import functools
import math

import jax
import jax.numpy as jnp
from jax import lax
from jax.experimental import pallas as pl
from jax.experimental.pallas import tpu as pltpu
from jax.sharding import PartitionSpec as P

CS = 64
CV = 32
CT = 16
HID = 128
DEGREE = 6
GATES = 144
FEAT = CS + 3 * CV + 9 * CT
ROWS = 320
LANES = 128
FINE = 2
CHUNK = 512
WIDE = 1024
VMEM_BYTES = 48 * 1024 * 1024


def dot(lhs, rhs, lhs_dim=1, rhs_dim=0):
    return lax.dot_general(
        lhs, rhs, (((lhs_dim,), (rhs_dim,)), ((), ())), preferred_element_type=jnp.float32
    )


def one_hot(code, width):
    rows = lax.broadcasted_iota(jnp.int16, (width, code.shape[1]), 0)
    return jnp.where(rows == code.astype(jnp.int16), jnp.bfloat16(1), jnp.bfloat16(0))


def join_index(table, row):
    pair = table[row : row + 2].astype(jnp.float32)
    return (pair[0:1] * 128.0 + pair[1:2]).astype(jnp.int32)


def table_kernel(
    feat_ref,
    pos_ref,
    up_ref,
    down_ref,
    rows_ref,
    table_ref,
    request_ref,
    pos_scr,
    up_scr,
    down_scr,
    rows_scr,
    sems,
):
    node_count = table_ref.shape[1]
    copies = [
        pltpu.make_async_copy(rows_ref, rows_scr, sems.at[0]),
        pltpu.make_async_copy(feat_ref, table_ref.at[:FEAT], sems.at[1]),
        pltpu.make_async_copy(pos_ref, pos_scr, sems.at[2]),
        pltpu.make_async_copy(up_ref, up_scr, sems.at[3]),
        pltpu.make_async_copy(down_ref, down_scr, sems.at[4]),
    ]
    for copy in copies:
        copy.start()
    copies[0].wait()
    slot = request_ref.shape[2]
    parts = LANES // slot
    for row in range(rows_scr.shape[0]):
        line = rows_scr[row : row + 1]
        for part in range(parts):
            request_ref[row * parts + part] = line[:, part * slot : (part + 1) * slot]
    for copy in copies[2:]:
        copy.wait()
    rows = lax.broadcasted_iota(jnp.int32, (ROWS - FEAT, node_count), 0)
    pos = pos_scr[...].astype(jnp.float32)
    tail = jnp.zeros((ROWS - FEAT, node_count), jnp.float32)
    for k in range(3):
        tail = jnp.where(rows == k, pos[k : k + 1], tail)
    for k, index_ref in ((3, up_scr), (5, down_scr)):
        index = index_ref[...]
        high = index >> 7
        tail = jnp.where(rows == k, high.astype(jnp.float32), tail)
        tail = jnp.where(rows == k + 1, (index - (high << 7)).astype(jnp.float32), tail)
    table_ref[FEAT:] = tail.astype(jnp.bfloat16)
    copies[1].wait()


def contact_gather_kernel(slot, table_ref, wanted_ref, out_hbm, out_ref, sems):
    node_count = table_ref.shape[1]
    parts = LANES // slot
    height = out_ref.shape[1]
    per_chunk = CHUNK // slot
    copies = []
    for chunk in range(wanted_ref.shape[0] // per_chunk):
        wanted = [wanted_ref[chunk * per_chunk + peer] for peer in range(per_chunk)]
        hot = one_hot(jnp.concatenate(wanted, 1), node_count)
        rows = dot(table_ref[...], hot).astype(jnp.bfloat16)
        if parts * height > ROWS:
            rows = jnp.concatenate(
                [rows, jnp.zeros((parts * height - ROWS, CHUNK), jnp.bfloat16)], 0
            )
        for peer in range(per_chunk):
            out_ref[chunk * per_chunk + peer] = jnp.concatenate(
                [
                    rows[part * height : (part + 1) * height, peer * slot : (peer + 1) * slot]
                    for part in range(parts)
                ],
                1,
            )
        done = pl.ds(chunk * per_chunk, per_chunk)
        copies.append(
            pltpu.make_async_copy(out_ref.at[done], out_hbm.at[done], sems.at[chunk])
        )
        copies[-1].start()
    for copy in copies:
        copy.wait()


def edge_math(src, base, first, inputs, pos_recv, back, live, weights):
    w_dist, w_two, w_two_t = weights
    edges = inputs.shape[1]
    bf16 = jnp.bfloat16
    kept = jnp.float32 if live is not None else bf16
    offset = src(slice(FEAT, ROWS))[:3] - pos_recv
    if live is not None:
        offset = offset * live
    distance = jnp.sum(offset * offset, 0, keepdims=True)
    linear = base + first + w_dist * distance
    squashed = 0.5 * jnp.tanh(0.5 * linear) + 0.5
    hidden = (linear * squashed).astype(jnp.bfloat16)
    gates = dot(w_two, hidden)
    gate_vec = gates[CS : CS + CV]
    gate_dir = gates[CS + CV : CS + 2 * CV]
    gate_ten = gates[CS + 2 * CV :]
    scal = src(slice(0, CS))
    message = [(gates[:CS] * scal).astype(kept)]
    dgates = [(back(slice(0, CS)) * scal).astype(bf16)]
    vec_part = jnp.zeros((CV, edges), jnp.float32)
    dir_part = jnp.zeros((CV, edges), jnp.float32)
    for k in range(3):
        rows = slice(CS + k * CV, CS + (k + 1) * CV)
        sent, pull = src(rows), back(rows)
        message.append((gate_vec * sent + gate_dir * offset[k : k + 1]).astype(kept))
        vec_part = vec_part + pull * sent
        dir_part = dir_part + pull * offset[k : k + 1]
    ten_part = jnp.zeros((CT, edges), jnp.float32)
    for m in range(9):
        rows = slice(CS + 3 * CV + m * CT, CS + 3 * CV + (m + 1) * CT)
        sent = src(rows)
        message.append((gate_ten * sent).astype(kept))
        ten_part = ten_part + back(rows) * sent
    message = jnp.concatenate(message, 0)
    dgates += [part.astype(bf16) for part in (vec_part, dir_part, ten_part)]
    dgates = jnp.concatenate(dgates, 0)
    hidden_grad = dot(w_two_t, dgates)
    linear_grad = (hidden_grad * squashed * (1.0 + linear * (1.0 - squashed))).astype(jnp.bfloat16)
    rows = lax.broadcasted_iota(jnp.int32, (16, edges), 0)
    coarse = distance.astype(jnp.bfloat16).astype(jnp.float32)
    extra = jnp.where(
        rows == 0, 1.0, jnp.where(rows == 1, coarse, jnp.where(rows == 2, distance - coarse, 0.0))
    ).astype(jnp.bfloat16)
    grads = (
        dot(linear_grad, jnp.concatenate([inputs, extra], 0), 1, 1),
        dot(dgates, hidden, 1, 1),
    )
    return message, grads


def as_columns(first_row, second_row):
    rows = lax.broadcasted_iota(jnp.int32, (LANES, LANES), 0)
    columns = jnp.where(rows == 0, first_row, jnp.where(rows == 1, second_row, 0.0)).T
    return columns[:, 0:1], columns[:, 1:2]


def add_grads(grads_ref, grads):
    grads_ref[:HID, : 2 * CS + 16] += grads[0]
    grads_ref[HID:, :HID] += grads[1]


def block_diagonal(block_ref, w_scal, w_vec, w_ten):
    block_ref[...] = jnp.zeros_like(block_ref)
    block_ref[:CS, :CS] = w_scal[...]
    for k in range(3):
        rows = slice(CS + k * CV, CS + (k + 1) * CV)
        block_ref[rows, rows] = w_vec[...]
    for m in range(9):
        rows = slice(CS + 3 * CV + m * CT, CS + 3 * CV + (m + 1) * CT)
        block_ref[rows, rows] = w_ten[...]


def mesh_kernel(
    table_ref,
    inner_ref,
    outer_ref,
    code_ref,
    cot_ref,
    w_one_ref,
    b_one_ref,
    w_dist_ref,
    w_two_ref,
    w_scal_ref,
    w_vec_ref,
    w_ten_ref,
    dst_ref,
    mask_ref,
    agg_out_ref,
    grads_out_ref,
    recv_out_ref,
    first_out_ref,
    code_out_ref,
    layers_out_ref,
    rows_out_ref,
    agg_ref,
    grads_ref,
    recv_ref,
    receive_ref,
    source_ref,
    block_ref,
    sems,
):
    node_count = table_ref.shape[1]
    source_ref[:, :node_count] = table_ref[...]
    even = lax.rem(lax.axis_index("sub"), 2) == 0
    low = lax.cond(even, lambda: outer_ref[...], lambda: inner_ref[...])
    high = lax.cond(even, lambda: inner_ref[...], lambda: outer_ref[...])
    source_ref[:, node_count : 2 * node_count] = dot(
        low, one_hot(join_index(low, FEAT + 3), node_count)
    ).astype(jnp.bfloat16)
    source_ref[:, 2 * node_count :] = dot(
        high, one_hot(join_index(high, FEAT + 5), node_count)
    ).astype(jnp.bfloat16)
    block_diagonal(block_ref, w_scal_ref, w_vec_ref, w_ten_ref)
    receive_ref[:FEAT] = dot(block_ref[...], cot_ref[...], 0, 0).astype(jnp.bfloat16)
    receive_ref[FEAT : FEAT + 16] = table_ref[FEAT:]
    receive_ref[FEAT + 16 :] = table_ref[:CS]
    w_one = w_one_ref[...]
    w_two = w_two_ref[...]
    b_column, dist_column = as_columns(b_one_ref[...], w_dist_ref[...])
    scal_recv = table_ref[:CS]
    recv_linear = dot(w_one[:, :CS], scal_recv) + b_column
    weights = (dist_column, w_two, w_two.T)
    pos_recv = table_ref[FEAT:].astype(jnp.float32)[:3]
    grads_ref[...] = jnp.zeros_like(grads_ref)
    agg_ref[...] = jnp.zeros_like(agg_ref)
    for step in range(DEGREE):
        code = code_ref[step]
        src = dot(source_ref[...], one_hot(code, 3 * node_count))
        live = jnp.where(code >= 0, 1.0, 0.0)
        scal_send = src[:CS].astype(jnp.bfloat16)
        inputs = jnp.concatenate([scal_recv, scal_send], 0)
        message, grads = edge_math(
            lambda rows: src[rows],
            recv_linear,
            dot(w_one[:, CS:], scal_send),
            inputs,
            pos_recv,
            lambda rows: receive_ref[rows].astype(jnp.float32),
            live,
            weights,
        )
        agg_ref[...] += message
        add_grads(grads_ref, grads)
    code_out_ref[...] = jnp.where(mask_ref[...] != 0, dst_ref[...], -1)
    for chunk in range(code_out_ref.shape[0]):
        target = first_out_ref if chunk == 0 else recv_ref.at[chunk - 1]
        target[...] = dot(
            receive_ref[...], one_hot(code_out_ref[chunk], node_count)
        ).astype(jnp.bfloat16)
    layers_out_ref[:HID] = w_one
    layers_out_ref[HID:] = w_two
    rows = lax.broadcasted_iota(jnp.int32, (8, HID), 0)
    rows_out_ref[...] = jnp.where(rows == 0, b_one_ref[...], w_dist_ref[...])
    copies = [
        pltpu.make_async_copy(agg_ref, agg_out_ref, sems.at[0]),
        pltpu.make_async_copy(grads_ref, grads_out_ref, sems.at[1]),
        pltpu.make_async_copy(recv_ref, recv_out_ref, sems.at[2]),
    ]
    for copy in copies:
        copy.start()
    for copy in copies:
        copy.wait()


def contact_kernel(
    slot,
    grad_scale,
    reply_ref,
    first_ref,
    code_ref,
    layers_ref,
    rows_ref,
    recv_hbm,
    mesh_agg_hbm,
    mesh_grads_hbm,
    cot_hbm,
    agg_out_ref,
    packed_ref,
    recv_ref,
    agg_ref,
    grads_ref,
    cot_ref,
    src_scr,
    packed_scr,
    sems,
):
    chunks = code_ref.shape[0]
    sources = [
        (recv_hbm, recv_ref),
        (mesh_agg_hbm, agg_ref),
        (mesh_grads_hbm, grads_ref),
        (cot_hbm, cot_ref),
    ]
    copies = [
        pltpu.make_async_copy(source, target, sems.at[at])
        for at, (source, target) in enumerate(sources)
    ]
    for copy in copies:
        copy.start()
    node_count = cot_ref.shape[1]
    parts = LANES // slot
    per_chunk = WIDE // slot
    for chunk in range(chunks):
        blocks = [reply_ref[chunk * per_chunk + peer] for peer in range(per_chunk)]
        src_scr[chunk] = jnp.concatenate(
            [
                jnp.concatenate(
                    [block[:, part * slot : (part + 1) * slot] for block in blocks], 1
                )
                for part in range(parts)
            ],
            0,
        )[:ROWS]
    w_one = layers_ref[:HID]
    w_two = layers_ref[HID:]
    b_column, dist_column = as_columns(rows_ref[0:1], rows_ref[1:2])
    weights = (dist_column, w_two, w_two.T)
    for chunk in range(chunks):
        if chunk == 1:
            for copy in copies:
                copy.wait()
        recv = first_ref if chunk == 0 else recv_ref.at[chunk - 1]
        inputs = jnp.concatenate([recv[FEAT + 16 :], src_scr[chunk, :CS]], 0)
        message, grads = edge_math(
            lambda rows: src_scr[chunk, rows].astype(jnp.float32),
            b_column,
            dot(w_one, inputs),
            inputs,
            recv[FEAT : FEAT + 16].astype(jnp.float32)[:3],
            lambda rows: recv[rows].astype(jnp.float32),
            None,
            weights,
        )
        scattered = dot(message, one_hot(code_ref[chunk], node_count), 1, 1)
        if chunk == 0:
            held = (scattered, grads)
            continue
        agg_ref[...] += scattered
        add_grads(grads_ref, grads)
        if chunk == 1:
            agg_ref[...] += held[0]
            add_grads(grads_ref, held[1])
    agg_rows = agg_ref[...].astype(jnp.bfloat16)
    agg_out_ref[...] = agg_rows
    cot = cot_ref[...]
    low = HID + GATES
    packed_scr[:low] = grads_ref[:, :LANES] * grad_scale
    scal = dot(cot[:CS], agg_rows[:CS], 1, 1) * grad_scale
    packed_scr[low : low + CS // 2] = jnp.concatenate([scal[: CS // 2], scal[CS // 2 :]], 1)
    low = low + CS // 2
    mixed = dot(cot[CS:], agg_rows[CS:], 1, 1)
    grad_vec = jnp.zeros((CV, CV), jnp.float32)
    for k in range(3):
        rows = slice(k * CV, (k + 1) * CV)
        grad_vec = grad_vec + mixed[rows, rows]
    each = CV * CV // LANES
    packed_scr[low : low + each] = grad_scale * jnp.concatenate(
        [grad_vec[at : at + each] for at in range(0, CV, each)], 1
    )
    low = low + each
    grad_ten = jnp.zeros((CT, CT), jnp.float32)
    for m in range(9):
        rows = slice(3 * CV + m * CT, 3 * CV + (m + 1) * CT)
        grad_ten = grad_ten + mixed[rows, rows]
    each = CT * CT // LANES
    packed_scr[low : low + each] = grad_scale * jnp.concatenate(
        [grad_ten[at : at + each] for at in range(0, CT, each)], 1
    )
    low = low + each
    extra = (grads_ref[:HID, LANES:] * grad_scale).T
    packed_scr[low : low + 1] = extra[0:1]
    packed_scr[low + 1 : low + 2] = extra[1:2] + extra[2:3]
    packed = packed_scr[...].astype(jnp.bfloat16)
    tiles = packed_ref.shape[1]
    for peer in range(packed_ref.shape[0]):
        for tile in range(tiles):
            at = (peer * tiles + tile) * FINE
            if at < packed.shape[0]:
                packed_ref[peer, tile] = packed[at : at + FINE]
            else:
                packed_ref[peer, tile] = jnp.zeros((FINE, LANES), jnp.bfloat16)


def sum_kernel(parts_ref, out_ref):
    total = parts_ref[0].astype(jnp.float32)
    for peer in range(1, parts_ref.shape[0]):
        total = total + parts_ref[peer].astype(jnp.float32)
    total = total.astype(jnp.bfloat16)
    for peer in range(out_ref.shape[0]):
        out_ref[peer] = total


def finish_kernel(
    blocks_ref,
    table_ref,
    agg_ref,
    w_scal_ref,
    w_vec_ref,
    w_ten_ref,
    out_ref,
    one_ref,
    bias_ref,
    dist_ref,
    two_ref,
    scal_ref,
    vec_ref,
    ten_ref,
    block_ref,
):
    block_diagonal(block_ref, w_scal_ref, w_vec_ref, w_ten_ref)
    out_ref[...] = (
        table_ref[:FEAT].astype(jnp.float32) + dot(block_ref[...], agg_ref[...])
    ).astype(jnp.bfloat16)

    tiles = blocks_ref.shape[1]

    def rows_of(at):
        peer, tile = divmod(at // FINE, tiles)
        return blocks_ref[peer, tile].astype(jnp.float32)

    for at in range(0, HID, FINE):
        one_ref[at : at + FINE] = rows_of(at)
    for at in range(0, GATES, FINE):
        two_ref[at : at + FINE] = rows_of(HID + at)
    low = HID + GATES
    for at in range(0, CS // 2, FINE):
        rows = rows_of(low + at)
        scal_ref[at : at + FINE] = rows[:, :CS]
        scal_ref[CS // 2 + at : CS // 2 + at + FINE] = rows[:, CS:]
    low = low + CS // 2
    for ref, width in ((vec_ref, CV), (ten_ref, CT)):
        each = width * width // LANES
        for at in range(0, each, FINE):
            rows = rows_of(low + at)
            for piece in range(width // each):
                to = piece * each + at
                ref[to : to + FINE] = rows[:, piece * width : (piece + 1) * width]
        low = low + each
    extra = rows_of(low)
    bias_ref[...] = extra[0:1]
    dist_ref[...] = extra[1:2]


def call(kernel, out_shape, scratch=(), in_specs=None, out_specs=None, cost_estimate=None):
    specs = {}
    if cost_estimate is not None:
        specs["cost_estimate"] = cost_estimate
    if in_specs is not None:
        specs["in_specs"] = in_specs
    if out_specs is not None:
        specs["out_specs"] = out_specs
    return pl.pallas_call(
        kernel,
        out_shape=out_shape,
        scratch_shapes=list(scratch),
        compiler_params=pltpu.CompilerParams(vmem_limit_bytes=VMEM_BYTES),
        **specs,
    )


IN_VMEM = pl.BlockSpec(memory_space=pltpu.VMEM)
IN_HBM = pl.BlockSpec(memory_space=pltpu.HBM)
ANYWHERE = pl.BlockSpec(memory_space=pl.ANY)


def exchange(blocks, axes=("dom", "sub")):
    return lax.all_to_all(blocks, axes, split_axis=0, concat_axis=0, tiled=True)


def in_hbm(*arrays):
    return tuple(pltpu.with_memory_space_constraint(array, pltpu.HBM) for array in arrays)


def shaped(shape, dtype):
    return jax.ShapeDtypeStruct(shape, dtype)


def swapped(shard, axis, first):
    peers = lax.axis_size(axis)
    pairs = [(at, (at + 1) % peers) for at in range(first, peers, 2)]
    return lax.ppermute(shard, axis, pairs + [(there, here) for here, there in pairs])


def on_device(
    node_feat,
    node_pos,
    node_cot,
    mesh_senders,
    edge_mask,
    halo_up,
    halo_down,
    contact_rows,
    contact_dst,
    contact_mask,
    w_one,
    b_one,
    w_dist,
    w_two,
    w_scal,
    w_vec,
    w_ten,
):
    f32, bf16 = jnp.float32, jnp.bfloat16
    node_count = node_feat.shape[1]
    contact_count = contact_rows.shape[0]
    device_count = lax.axis_size("dom") * lax.axis_size("sub")
    slot = contact_count // device_count
    chunks = contact_count // CHUNK
    wides = contact_count // WIDE
    parts = LANES // slot
    height = -(-ROWS // (parts * 16)) * 16
    grad_scale = 1.0 / math.sqrt(device_count * node_count * DEGREE)
    table, requests = call(
        table_kernel,
        (
            shaped((ROWS, node_count), bf16),
            shaped((device_count, 1, slot), jnp.int32),
        ),
        (
            pltpu.VMEM((3, node_count), bf16),
            pltpu.VMEM((1, node_count), jnp.int32),
            pltpu.VMEM((1, node_count), jnp.int32),
            pltpu.VMEM((contact_count // LANES, LANES), jnp.int32),
            pltpu.SemaphoreType.DMA((5,)),
        ),
        in_specs=[IN_HBM] * 5,
        out_specs=(IN_VMEM, IN_VMEM),
    )(
        *in_hbm(
            node_feat,
            node_pos,
            halo_up[None],
            halo_down[None],
            contact_rows.reshape(contact_count // LANES, LANES),
        )
    )
    wanted = exchange(requests)
    wanted, table_late = lax.optimization_barrier((wanted, table))
    inner = swapped(table_late, "sub", 0)
    outer = swapped(table_late, "sub", 1)
    found = call(
        functools.partial(contact_gather_kernel, slot),
        pltpu.HBM((device_count, height, LANES), bf16),
        (
            pltpu.VMEM((device_count, height, LANES), bf16),
            pltpu.SemaphoreType.DMA((chunks,)),
        ),
        in_specs=[IN_VMEM, IN_VMEM],
        out_specs=IN_HBM,
    )(table, wanted)
    found, mesh_senders, edge_mask = lax.optimization_barrier((found, mesh_senders, edge_mask))
    replies = exchange(found)
    mesh_code = (
        jnp.where(edge_mask != 0, mesh_senders, -1)
        .reshape(node_count, DEGREE)
        .T.reshape(DEGREE, 1, node_count)
    )
    contact_dst = contact_dst.reshape(wides, 1, WIDE)
    contact_mask = contact_mask.reshape(wides, 1, WIDE)
    mesh_rows = HID + GATES
    recv_rows = FEAT + 16 + CS
    mesh_agg, mesh_grads, recv, first, contact_code, layers, rows = call(
        mesh_kernel,
        (
            pltpu.HBM((FEAT, node_count), f32),
            pltpu.HBM((mesh_rows, 2 * LANES), f32),
            pltpu.HBM((wides - 1, recv_rows, WIDE), bf16),
            shaped((recv_rows, WIDE), bf16),
            shaped((wides, 1, WIDE), jnp.int32),
            shaped((mesh_rows, HID), bf16),
            shaped((8, HID), f32),
        ),
        (
            pltpu.VMEM((FEAT, node_count), f32),
            pltpu.VMEM((mesh_rows, 2 * LANES), f32),
            pltpu.VMEM((wides - 1, recv_rows, WIDE), bf16),
            pltpu.VMEM((recv_rows, node_count), bf16),
            pltpu.VMEM((ROWS, 3 * node_count), bf16),
            pltpu.VMEM((FEAT, FEAT), bf16),
            pltpu.SemaphoreType.DMA((3,)),
        ),
        in_specs=[IN_VMEM] * 14,
        out_specs=(IN_HBM,) * 3 + (IN_VMEM,) * 4,
        cost_estimate=pl.CostEstimate(
            flops=40_000_000_000, bytes_accessed=8_000_000, transcendentals=400_000
        ),
    )(
        table,
        inner,
        outer,
        mesh_code,
        node_cot,
        w_one,
        b_one[None],
        w_dist[None],
        w_two,
        w_scal,
        w_vec,
        w_ten,
        contact_dst,
        contact_mask,
    )
    packed_rows = mesh_rows + (CS * CS + CV * CV + CT * CT) // LANES + 2
    tiles = -(-packed_rows // (FINE * device_count))
    share = (device_count, tiles, FINE, LANES)
    agg_rows, packed = call(
        functools.partial(contact_kernel, slot, grad_scale),
        (shaped((FEAT, node_count), bf16), shaped(share, bf16)),
        (
            pltpu.VMEM((wides - 1, recv_rows, WIDE), bf16),
            pltpu.VMEM((FEAT, node_count), f32),
            pltpu.VMEM((mesh_rows, 2 * LANES), f32),
            pltpu.VMEM((FEAT, node_count), bf16),
            pltpu.VMEM((wides, ROWS, WIDE), bf16),
            pltpu.VMEM((packed_rows, LANES), f32),
            pltpu.SemaphoreType.DMA((4,)),
        ),
        in_specs=[IN_VMEM] * 5 + [IN_HBM] * 4,
        out_specs=(IN_VMEM, IN_VMEM),
    )(
        replies,
        first,
        contact_code,
        layers,
        rows,
        *in_hbm(recv, mesh_agg, mesh_grads, node_cot),
    )
    shares = call(sum_kernel, shaped(share, bf16))(exchange(packed))
    node_out, one, bias, dist, two, scal, vec, ten = call(
        finish_kernel,
        (
            shaped((FEAT, node_count), bf16),
            shaped((HID, 2 * CS), f32),
            shaped((1, HID), f32),
            shaped((1, HID), f32),
            shaped((GATES, HID), f32),
            shaped((CS, CS), f32),
            shaped((CV, CV), f32),
            shaped((CT, CT), f32),
        ),
        (pltpu.VMEM((FEAT, FEAT), bf16),),
    )(exchange(shares), table, agg_rows, w_scal, w_vec, w_ten)
    return node_out, one, bias[0], dist[0], two, scal, vec, ten


def solution(mesh):
    along = P(("dom", "sub"))
    columns = P(None, ("dom", "sub"))
    in_specs = (columns,) * 3 + (along,) * 7 + (P(),) * 7
    out_specs = (columns,) + (P(),) * 7
    return jax.shard_map(
        on_device, mesh=mesh, in_specs=in_specs, out_specs=out_specs, check_vma=False
    )
```

```python
import functools
import math

import jax
import jax.numpy as jnp
from jax import lax
from jax.experimental import pallas as pl
from jax.experimental.pallas import tpu as pltpu
from jax.sharding import PartitionSpec as P

CS = 64
CV = 32
CT = 16
HID = 128
DEGREE = 6
GATES = 144
FEAT = CS + 3 * CV + 9 * CT
ROWS = 320
LANES = 128
FINE = 2
CHUNK = 512
WIDE = 512
VMEM_BYTES = 48 * 1024 * 1024


def dot(lhs, rhs, lhs_dim=1, rhs_dim=0):
    return lax.dot_general(
        lhs, rhs, (((lhs_dim,), (rhs_dim,)), ((), ())), preferred_element_type=jnp.float32
    )


def one_hot(code, width):
    rows = lax.broadcasted_iota(jnp.int16, (width, code.shape[1]), 0)
    return jnp.where(rows == code.astype(jnp.int16), jnp.bfloat16(1), jnp.bfloat16(0))


def join_index(table, row):
    pair = table[row : row + 2].astype(jnp.float32)
    return (pair[0:1] * 128.0 + pair[1:2]).astype(jnp.int32)


def table_kernel(
    feat_ref,
    pos_ref,
    up_ref,
    down_ref,
    rows_ref,
    table_ref,
    request_ref,
    pos_scr,
    up_scr,
    down_scr,
    rows_scr,
    sems,
):
    node_count = table_ref.shape[1]
    copies = [
        pltpu.make_async_copy(rows_ref, rows_scr, sems.at[0]),
        pltpu.make_async_copy(feat_ref, table_ref.at[:FEAT], sems.at[1]),
        pltpu.make_async_copy(pos_ref, pos_scr, sems.at[2]),
        pltpu.make_async_copy(up_ref, up_scr, sems.at[3]),
        pltpu.make_async_copy(down_ref, down_scr, sems.at[4]),
    ]
    for copy in copies:
        copy.start()
    copies[0].wait()
    slot = request_ref.shape[2]
    parts = LANES // slot
    for row in range(rows_scr.shape[0]):
        line = rows_scr[row : row + 1]
        for part in range(parts):
            request_ref[row * parts + part] = line[:, part * slot : (part + 1) * slot]
    for copy in copies[2:]:
        copy.wait()
    rows = lax.broadcasted_iota(jnp.int32, (ROWS - FEAT, node_count), 0)
    pos = pos_scr[...].astype(jnp.float32)
    tail = jnp.zeros((ROWS - FEAT, node_count), jnp.float32)
    for k in range(3):
        tail = jnp.where(rows == k, pos[k : k + 1], tail)
    for k, index_ref in ((3, up_scr), (5, down_scr)):
        index = index_ref[...]
        high = index >> 7
        tail = jnp.where(rows == k, high.astype(jnp.float32), tail)
        tail = jnp.where(rows == k + 1, (index - (high << 7)).astype(jnp.float32), tail)
    table_ref[FEAT:] = tail.astype(jnp.bfloat16)
    copies[1].wait()


def contact_gather_kernel(slot, table_ref, wanted_ref, out_hbm, out_ref, sems):
    node_count = table_ref.shape[1]
    parts = LANES // slot
    height = out_ref.shape[1]
    per_chunk = CHUNK // slot
    copies = []
    for chunk in range(wanted_ref.shape[0] // per_chunk):
        wanted = [wanted_ref[chunk * per_chunk + peer] for peer in range(per_chunk)]
        hot = one_hot(jnp.concatenate(wanted, 1), node_count)
        rows = dot(table_ref[...], hot).astype(jnp.bfloat16)
        if parts * height > ROWS:
            rows = jnp.concatenate(
                [rows, jnp.zeros((parts * height - ROWS, CHUNK), jnp.bfloat16)], 0
            )
        for peer in range(per_chunk):
            out_ref[chunk * per_chunk + peer] = jnp.concatenate(
                [
                    rows[part * height : (part + 1) * height, peer * slot : (peer + 1) * slot]
                    for part in range(parts)
                ],
                1,
            )
        done = pl.ds(chunk * per_chunk, per_chunk)
        copies.append(
            pltpu.make_async_copy(out_ref.at[done], out_hbm.at[done], sems.at[chunk])
        )
        copies[-1].start()
    for copy in copies:
        copy.wait()


def edge_math(src, base, first, inputs, pos_recv, back, live, weights):
    w_dist, w_two, w_two_t = weights
    edges = inputs.shape[1]
    bf16 = jnp.bfloat16
    kept = jnp.float32 if live is not None else bf16
    offset = src(slice(FEAT, ROWS))[:3] - pos_recv
    if live is not None:
        offset = offset * live
    distance = jnp.sum(offset * offset, 0, keepdims=True)
    linear = base + first + w_dist * distance
    squashed = 0.5 * jnp.tanh(0.5 * linear) + 0.5
    hidden = (linear * squashed).astype(jnp.bfloat16)
    gates = dot(w_two, hidden)
    gate_vec = gates[CS : CS + CV]
    gate_dir = gates[CS + CV : CS + 2 * CV]
    gate_ten = gates[CS + 2 * CV :]
    scal = src(slice(0, CS))
    message = [(gates[:CS] * scal).astype(kept)]
    dgates = [(back(slice(0, CS)) * scal).astype(bf16)]
    vec_part = jnp.zeros((CV, edges), jnp.float32)
    dir_part = jnp.zeros((CV, edges), jnp.float32)
    for k in range(3):
        rows = slice(CS + k * CV, CS + (k + 1) * CV)
        sent, pull = src(rows), back(rows)
        message.append((gate_vec * sent + gate_dir * offset[k : k + 1]).astype(kept))
        vec_part = vec_part + pull * sent
        dir_part = dir_part + pull * offset[k : k + 1]
    ten_part = jnp.zeros((CT, edges), jnp.float32)
    for m in range(9):
        rows = slice(CS + 3 * CV + m * CT, CS + 3 * CV + (m + 1) * CT)
        sent = src(rows)
        message.append((gate_ten * sent).astype(kept))
        ten_part = ten_part + back(rows) * sent
    message = jnp.concatenate(message, 0)
    dgates += [part.astype(bf16) for part in (vec_part, dir_part, ten_part)]
    dgates = jnp.concatenate(dgates, 0)
    hidden_grad = dot(w_two_t, dgates)
    linear_grad = (hidden_grad * squashed * (1.0 + linear * (1.0 - squashed))).astype(jnp.bfloat16)
    rows = lax.broadcasted_iota(jnp.int32, (16, edges), 0)
    coarse = distance.astype(jnp.bfloat16).astype(jnp.float32)
    extra = jnp.where(
        rows == 0, 1.0, jnp.where(rows == 1, coarse, jnp.where(rows == 2, distance - coarse, 0.0))
    ).astype(jnp.bfloat16)
    grads = (
        dot(linear_grad, jnp.concatenate([inputs, extra], 0), 1, 1),
        dot(dgates, hidden, 1, 1),
    )
    return message, grads


def as_columns(first_row, second_row):
    rows = lax.broadcasted_iota(jnp.int32, (LANES, LANES), 0)
    columns = jnp.where(rows == 0, first_row, jnp.where(rows == 1, second_row, 0.0)).T
    return columns[:, 0:1], columns[:, 1:2]


def add_grads(grads_ref, grads):
    grads_ref[:HID, : 2 * CS + 16] += grads[0]
    grads_ref[HID:, :HID] += grads[1]


def block_diagonal(block_ref, w_scal, w_vec, w_ten):
    block_ref[...] = jnp.zeros_like(block_ref)
    block_ref[:CS, :CS] = w_scal[...]
    for k in range(3):
        rows = slice(CS + k * CV, CS + (k + 1) * CV)
        block_ref[rows, rows] = w_vec[...]
    for m in range(9):
        rows = slice(CS + 3 * CV + m * CT, CS + 3 * CV + (m + 1) * CT)
        block_ref[rows, rows] = w_ten[...]


def mesh_kernel(
    table_ref,
    inner_ref,
    outer_ref,
    code_ref,
    cot_ref,
    w_one_ref,
    b_one_ref,
    w_dist_ref,
    w_two_ref,
    w_scal_ref,
    w_vec_ref,
    w_ten_ref,
    dst_ref,
    mask_ref,
    agg_out_ref,
    grads_out_ref,
    recv_out_ref,
    first_out_ref,
    code_out_ref,
    layers_out_ref,
    rows_out_ref,
    agg_ref,
    grads_ref,
    recv_ref,
    receive_ref,
    source_ref,
    block_ref,
    sems,
):
    node_count = table_ref.shape[1]
    source_ref[:, :node_count] = table_ref[...]
    even = lax.rem(lax.axis_index("sub"), 2) == 0
    low = lax.cond(even, lambda: outer_ref[...], lambda: inner_ref[...])
    high = lax.cond(even, lambda: inner_ref[...], lambda: outer_ref[...])
    source_ref[:, node_count : 2 * node_count] = dot(
        low, one_hot(join_index(low, FEAT + 3), node_count)
    ).astype(jnp.bfloat16)
    source_ref[:, 2 * node_count :] = dot(
        high, one_hot(join_index(high, FEAT + 5), node_count)
    ).astype(jnp.bfloat16)
    block_diagonal(block_ref, w_scal_ref, w_vec_ref, w_ten_ref)
    receive_ref[:FEAT] = dot(block_ref[...], cot_ref[...], 0, 0).astype(jnp.bfloat16)
    receive_ref[FEAT : FEAT + 16] = table_ref[FEAT:]
    receive_ref[FEAT + 16 :] = table_ref[:CS]
    w_one = w_one_ref[...]
    w_two = w_two_ref[...]
    b_column, dist_column = as_columns(b_one_ref[...], w_dist_ref[...])
    scal_recv = table_ref[:CS]
    recv_linear = dot(w_one[:, :CS], scal_recv) + b_column
    weights = (dist_column, w_two, w_two.T)
    pos_recv = table_ref[FEAT:].astype(jnp.float32)[:3]
    grads_ref[...] = jnp.zeros_like(grads_ref)
    agg_ref[...] = jnp.zeros_like(agg_ref)
    for step in range(DEGREE):
        code = code_ref[step]
        src = dot(source_ref[...], one_hot(code, 3 * node_count))
        live = jnp.where(code >= 0, 1.0, 0.0)
        scal_send = src[:CS].astype(jnp.bfloat16)
        inputs = jnp.concatenate([scal_recv, scal_send], 0)
        message, grads = edge_math(
            lambda rows: src[rows],
            recv_linear,
            dot(w_one[:, CS:], scal_send),
            inputs,
            pos_recv,
            lambda rows: receive_ref[rows].astype(jnp.float32),
            live,
            weights,
        )
        agg_ref[...] += message
        add_grads(grads_ref, grads)
    code_out_ref[...] = jnp.where(mask_ref[...] != 0, dst_ref[...], -1)
    for chunk in range(code_out_ref.shape[0]):
        target = first_out_ref if chunk == 0 else recv_ref.at[chunk - 1]
        target[...] = dot(
            receive_ref[...], one_hot(code_out_ref[chunk], node_count)
        ).astype(jnp.bfloat16)
    layers_out_ref[:HID] = w_one
    layers_out_ref[HID:] = w_two
    rows = lax.broadcasted_iota(jnp.int32, (8, HID), 0)
    rows_out_ref[...] = jnp.where(rows == 0, b_one_ref[...], w_dist_ref[...])
    copies = [
        pltpu.make_async_copy(agg_ref, agg_out_ref, sems.at[0]),
        pltpu.make_async_copy(grads_ref, grads_out_ref, sems.at[1]),
        pltpu.make_async_copy(recv_ref, recv_out_ref, sems.at[2]),
    ]
    for copy in copies:
        copy.start()
    for copy in copies:
        copy.wait()


def contact_kernel(
    slot,
    grad_scale,
    reply_ref,
    first_ref,
    code_ref,
    layers_ref,
    rows_ref,
    recv_hbm,
    mesh_agg_hbm,
    mesh_grads_hbm,
    cot_hbm,
    agg_out_ref,
    packed_ref,
    recv_ref,
    agg_ref,
    grads_ref,
    cot_ref,
    src_scr,
    packed_scr,
    sems,
):
    chunks = code_ref.shape[0]
    sources = [
        (recv_hbm, recv_ref),
        (mesh_agg_hbm, agg_ref),
        (mesh_grads_hbm, grads_ref),
        (cot_hbm, cot_ref),
    ]
    copies = [
        pltpu.make_async_copy(source, target, sems.at[at])
        for at, (source, target) in enumerate(sources)
    ]
    for copy in copies:
        copy.start()
    node_count = cot_ref.shape[1]
    parts = LANES // slot
    per_chunk = WIDE // slot
    for chunk in range(chunks):
        blocks = [reply_ref[chunk * per_chunk + peer] for peer in range(per_chunk)]
        src_scr[chunk] = jnp.concatenate(
            [
                jnp.concatenate(
                    [block[:, part * slot : (part + 1) * slot] for block in blocks], 1
                )
                for part in range(parts)
            ],
            0,
        )[:ROWS]
    w_one = layers_ref[:HID]
    w_two = layers_ref[HID:]
    b_column, dist_column = as_columns(rows_ref[0:1], rows_ref[1:2])
    weights = (dist_column, w_two, w_two.T)
    for chunk in range(chunks):
        if chunk == 1:
            for copy in copies:
                copy.wait()
        recv = first_ref if chunk == 0 else recv_ref.at[chunk - 1]
        inputs = jnp.concatenate([recv[FEAT + 16 :], src_scr[chunk, :CS]], 0)
        message, grads = edge_math(
            lambda rows: src_scr[chunk, rows].astype(jnp.float32),
            b_column,
            dot(w_one, inputs),
            inputs,
            recv[FEAT : FEAT + 16].astype(jnp.float32)[:3],
            lambda rows: recv[rows].astype(jnp.float32),
            None,
            weights,
        )
        scattered = dot(message, one_hot(code_ref[chunk], node_count), 1, 1)
        if chunk == 0:
            held = (scattered, grads)
            continue
        agg_ref[...] += scattered
        add_grads(grads_ref, grads)
        if chunk == 1:
            agg_ref[...] += held[0]
            add_grads(grads_ref, held[1])
    agg_rows = agg_ref[...].astype(jnp.bfloat16)
    agg_out_ref[...] = agg_rows
    cot = cot_ref[...]
    low = HID + GATES
    packed_scr[:low] = grads_ref[:, :LANES] * grad_scale
    scal = dot(cot[:CS], agg_rows[:CS], 1, 1) * grad_scale
    packed_scr[low : low + CS // 2] = jnp.concatenate([scal[: CS // 2], scal[CS // 2 :]], 1)
    low = low + CS // 2
    mixed = dot(cot[CS:], agg_rows[CS:], 1, 1)
    grad_vec = jnp.zeros((CV, CV), jnp.float32)
    for k in range(3):
        rows = slice(k * CV, (k + 1) * CV)
        grad_vec = grad_vec + mixed[rows, rows]
    each = CV * CV // LANES
    packed_scr[low : low + each] = grad_scale * jnp.concatenate(
        [grad_vec[at : at + each] for at in range(0, CV, each)], 1
    )
    low = low + each
    grad_ten = jnp.zeros((CT, CT), jnp.float32)
    for m in range(9):
        rows = slice(3 * CV + m * CT, 3 * CV + (m + 1) * CT)
        grad_ten = grad_ten + mixed[rows, rows]
    each = CT * CT // LANES
    packed_scr[low : low + each] = grad_scale * jnp.concatenate(
        [grad_ten[at : at + each] for at in range(0, CT, each)], 1
    )
    low = low + each
    extra = (grads_ref[:HID, LANES:] * grad_scale).T
    packed_scr[low : low + 1] = extra[0:1]
    packed_scr[low + 1 : low + 2] = extra[1:2] + extra[2:3]
    packed = packed_scr[...].astype(jnp.bfloat16)
    tiles = packed_ref.shape[1]
    for peer in range(packed_ref.shape[0]):
        for tile in range(tiles):
            at = (peer * tiles + tile) * FINE
            if at < packed.shape[0]:
                packed_ref[peer, tile] = packed[at : at + FINE]
            else:
                packed_ref[peer, tile] = jnp.zeros((FINE, LANES), jnp.bfloat16)


def sum_kernel(parts_ref, out_ref):
    total = parts_ref[0].astype(jnp.float32)
    for peer in range(1, parts_ref.shape[0]):
        total = total + parts_ref[peer].astype(jnp.float32)
    total = total.astype(jnp.bfloat16)
    for peer in range(out_ref.shape[0]):
        out_ref[peer] = total


def finish_kernel(
    blocks_ref,
    table_ref,
    agg_ref,
    w_scal_ref,
    w_vec_ref,
    w_ten_ref,
    out_ref,
    one_ref,
    bias_ref,
    dist_ref,
    two_ref,
    scal_ref,
    vec_ref,
    ten_ref,
    block_ref,
):
    block_diagonal(block_ref, w_scal_ref, w_vec_ref, w_ten_ref)
    out_ref[...] = (
        table_ref[:FEAT].astype(jnp.float32) + dot(block_ref[...], agg_ref[...])
    ).astype(jnp.bfloat16)

    tiles = blocks_ref.shape[1]

    def rows_of(at):
        peer, tile = divmod(at // FINE, tiles)
        return blocks_ref[peer, tile].astype(jnp.float32)

    for at in range(0, HID, FINE):
        one_ref[at : at + FINE] = rows_of(at)
    for at in range(0, GATES, FINE):
        two_ref[at : at + FINE] = rows_of(HID + at)
    low = HID + GATES
    for at in range(0, CS // 2, FINE):
        rows = rows_of(low + at)
        scal_ref[at : at + FINE] = rows[:, :CS]
        scal_ref[CS // 2 + at : CS // 2 + at + FINE] = rows[:, CS:]
    low = low + CS // 2
    for ref, width in ((vec_ref, CV), (ten_ref, CT)):
        each = width * width // LANES
        for at in range(0, each, FINE):
            rows = rows_of(low + at)
            for piece in range(width // each):
                to = piece * each + at
                ref[to : to + FINE] = rows[:, piece * width : (piece + 1) * width]
        low = low + each
    extra = rows_of(low)
    bias_ref[...] = extra[0:1]
    dist_ref[...] = extra[1:2]


def call(kernel, out_shape, scratch=(), in_specs=None, out_specs=None, cost_estimate=None):
    specs = {}
    if cost_estimate is not None:
        specs["cost_estimate"] = cost_estimate
    if in_specs is not None:
        specs["in_specs"] = in_specs
    if out_specs is not None:
        specs["out_specs"] = out_specs
    return pl.pallas_call(
        kernel,
        out_shape=out_shape,
        scratch_shapes=list(scratch),
        compiler_params=pltpu.CompilerParams(vmem_limit_bytes=VMEM_BYTES),
        **specs,
    )


IN_VMEM = pl.BlockSpec(memory_space=pltpu.VMEM)
IN_HBM = pl.BlockSpec(memory_space=pltpu.HBM)
ANYWHERE = pl.BlockSpec(memory_space=pl.ANY)


def exchange(blocks, axes=("dom", "sub")):
    return lax.all_to_all(blocks, axes, split_axis=0, concat_axis=0, tiled=True)


def in_hbm(*arrays):
    return tuple(pltpu.with_memory_space_constraint(array, pltpu.HBM) for array in arrays)


def shaped(shape, dtype):
    return jax.ShapeDtypeStruct(shape, dtype)


def swapped(shard, axis, first):
    peers = lax.axis_size(axis)
    pairs = [(at, (at + 1) % peers) for at in range(first, peers, 2)]
    return lax.ppermute(shard, axis, pairs + [(there, here) for here, there in pairs])


def on_device(
    node_feat,
    node_pos,
    node_cot,
    mesh_senders,
    edge_mask,
    halo_up,
    halo_down,
    contact_rows,
    contact_dst,
    contact_mask,
    w_one,
    b_one,
    w_dist,
    w_two,
    w_scal,
    w_vec,
    w_ten,
):
    f32, bf16 = jnp.float32, jnp.bfloat16
    node_count = node_feat.shape[1]
    contact_count = contact_rows.shape[0]
    device_count = lax.axis_size("dom") * lax.axis_size("sub")
    slot = contact_count // device_count
    chunks = contact_count // CHUNK
    wides = contact_count // WIDE
    parts = LANES // slot
    height = -(-ROWS // (parts * 16)) * 16
    grad_scale = 1.0 / math.sqrt(device_count * node_count * DEGREE)
    table, requests = call(
        table_kernel,
        (
            shaped((ROWS, node_count), bf16),
            shaped((device_count, 1, slot), jnp.int32),
        ),
        (
            pltpu.VMEM((3, node_count), bf16),
            pltpu.VMEM((1, node_count), jnp.int32),
            pltpu.VMEM((1, node_count), jnp.int32),
            pltpu.VMEM((contact_count // LANES, LANES), jnp.int32),
            pltpu.SemaphoreType.DMA((5,)),
        ),
        in_specs=[IN_HBM] * 5,
        out_specs=(IN_VMEM, IN_VMEM),
    )(
        *in_hbm(
            node_feat,
            node_pos,
            halo_up[None],
            halo_down[None],
            contact_rows.reshape(contact_count // LANES, LANES),
        )
    )
    wanted = exchange(requests)
    wanted, table_late = lax.optimization_barrier((wanted, table))
    inner = swapped(table_late, "sub", 0)
    outer = swapped(table_late, "sub", 1)
    found = call(
        functools.partial(contact_gather_kernel, slot),
        pltpu.HBM((device_count, height, LANES), bf16),
        (
            pltpu.VMEM((device_count, height, LANES), bf16),
            pltpu.SemaphoreType.DMA((chunks,)),
        ),
        in_specs=[IN_VMEM, IN_VMEM],
        out_specs=IN_HBM,
    )(table, wanted)
    found, mesh_senders, edge_mask = lax.optimization_barrier((found, mesh_senders, edge_mask))
    replies = exchange(found)
    mesh_code = (
        jnp.where(edge_mask != 0, mesh_senders, -1)
        .reshape(node_count, DEGREE)
        .T.reshape(DEGREE, 1, node_count)
    )
    contact_dst = contact_dst.reshape(wides, 1, WIDE)
    contact_mask = contact_mask.reshape(wides, 1, WIDE)
    mesh_rows = HID + GATES
    recv_rows = FEAT + 16 + CS
    mesh_agg, mesh_grads, recv, first, contact_code, layers, rows = call(
        mesh_kernel,
        (
            pltpu.HBM((FEAT, node_count), f32),
            pltpu.HBM((mesh_rows, 2 * LANES), f32),
            pltpu.HBM((wides - 1, recv_rows, WIDE), bf16),
            shaped((recv_rows, WIDE), bf16),
            shaped((wides, 1, WIDE), jnp.int32),
            shaped((mesh_rows, HID), bf16),
            shaped((8, HID), f32),
        ),
        (
            pltpu.VMEM((FEAT, node_count), f32),
            pltpu.VMEM((mesh_rows, 2 * LANES), f32),
            pltpu.VMEM((wides - 1, recv_rows, WIDE), bf16),
            pltpu.VMEM((recv_rows, node_count), bf16),
            pltpu.VMEM((ROWS, 3 * node_count), bf16),
            pltpu.VMEM((FEAT, FEAT), bf16),
            pltpu.SemaphoreType.DMA((3,)),
        ),
        in_specs=[IN_VMEM] * 14,
        out_specs=(IN_HBM,) * 3 + (IN_VMEM,) * 4,
        cost_estimate=pl.CostEstimate(
            flops=40_000_000_000, bytes_accessed=8_000_000, transcendentals=400_000
        ),
    )(
        table,
        inner,
        outer,
        mesh_code,
        node_cot,
        w_one,
        b_one[None],
        w_dist[None],
        w_two,
        w_scal,
        w_vec,
        w_ten,
        contact_dst,
        contact_mask,
    )
    packed_rows = mesh_rows + (CS * CS + CV * CV + CT * CT) // LANES + 2
    tiles = -(-packed_rows // (FINE * device_count))
    share = (device_count, tiles, FINE, LANES)
    agg_rows, packed = call(
        functools.partial(contact_kernel, slot, grad_scale),
        (shaped((FEAT, node_count), bf16), shaped(share, bf16)),
        (
            pltpu.VMEM((wides - 1, recv_rows, WIDE), bf16),
            pltpu.VMEM((FEAT, node_count), f32),
            pltpu.VMEM((mesh_rows, 2 * LANES), f32),
            pltpu.VMEM((FEAT, node_count), bf16),
            pltpu.VMEM((wides, ROWS, WIDE), bf16),
            pltpu.VMEM((packed_rows, LANES), f32),
            pltpu.SemaphoreType.DMA((4,)),
        ),
        in_specs=[IN_VMEM] * 5 + [IN_HBM] * 4,
        out_specs=(IN_VMEM, IN_VMEM),
    )(
        replies,
        first,
        contact_code,
        layers,
        rows,
        *in_hbm(recv, mesh_agg, mesh_grads, node_cot),
    )
    shares = call(sum_kernel, shaped(share, bf16))(exchange(packed))
    node_out, one, bias, dist, two, scal, vec, ten = call(
        finish_kernel,
        (
            shaped((FEAT, node_count), bf16),
            shaped((HID, 2 * CS), f32),
            shaped((1, HID), f32),
            shaped((1, HID), f32),
            shaped((GATES, HID), f32),
            shaped((CS, CS), f32),
            shaped((CV, CV), f32),
            shaped((CT, CT), f32),
        ),
        (pltpu.VMEM((FEAT, FEAT), bf16),),
    )(exchange(shares), table, agg_rows, w_scal, w_vec, w_ten)
    return node_out, one, bias[0], dist[0], two, scal, vec, ten


def solution(mesh):
    along = P(("dom", "sub"))
    columns = P(None, ("dom", "sub"))
    in_specs = (columns,) * 3 + (along,) * 7 + (P(),) * 7
    out_specs = (columns,) + (P(),) * 7
    return jax.shard_map(
        on_device, mesh=mesh, in_specs=in_specs, out_specs=out_specs, check_vma=False
    )
```

```python
import functools
import math

import jax
import jax.numpy as jnp
from jax import lax
from jax.experimental import pallas as pl
from jax.experimental.pallas import tpu as pltpu
from jax.sharding import PartitionSpec as P

CS = 64
CV = 32
CT = 16
HID = 128
DEGREE = 6
GATES = 144
FEAT = CS + 3 * CV + 9 * CT
ROWS = 320
LANES = 128
FINE = 2
GATHER = 1024
VMEM_BYTES = 48 * 1024 * 1024


def dot(lhs, rhs, lhs_dim=1, rhs_dim=0):
    return lax.dot_general(
        lhs, rhs, (((lhs_dim,), (rhs_dim,)), ((), ())), preferred_element_type=jnp.float32
    )


def one_hot(code, width):
    rows = lax.broadcasted_iota(jnp.int16, (width, code.shape[1]), 0)
    return jnp.where(rows == code.astype(jnp.int16), jnp.bfloat16(1), jnp.bfloat16(0))


def join_index(table, row):
    pair = table[row : row + 2].astype(jnp.float32)
    return (pair[0:1] * 128.0 + pair[1:2]).astype(jnp.int32)


def table_kernel(
    feat_ref,
    pos_ref,
    up_ref,
    down_ref,
    rows_ref,
    table_ref,
    request_ref,
    pos_scr,
    up_scr,
    down_scr,
    rows_scr,
    sems,
):
    node_count = table_ref.shape[1]
    copies = [
        pltpu.make_async_copy(rows_ref, rows_scr, sems.at[0]),
        pltpu.make_async_copy(feat_ref, table_ref.at[:FEAT], sems.at[1]),
        pltpu.make_async_copy(pos_ref, pos_scr, sems.at[2]),
        pltpu.make_async_copy(up_ref, up_scr, sems.at[3]),
        pltpu.make_async_copy(down_ref, down_scr, sems.at[4]),
    ]
    for copy in copies:
        copy.start()
    copies[0].wait()
    slot = request_ref.shape[2]
    parts = LANES // slot
    for row in range(rows_scr.shape[0]):
        line = rows_scr[row : row + 1]
        for part in range(parts):
            request_ref[row * parts + part] = line[:, part * slot : (part + 1) * slot]
    for copy in copies[2:]:
        copy.wait()
    rows = lax.broadcasted_iota(jnp.int32, (ROWS - FEAT, node_count), 0)
    pos = pos_scr[...].astype(jnp.float32)
    tail = jnp.zeros((ROWS - FEAT, node_count), jnp.float32)
    for k in range(3):
        tail = jnp.where(rows == k, pos[k : k + 1], tail)
    for k, index_ref in ((3, up_scr), (5, down_scr)):
        index = index_ref[...]
        high = index >> 7
        tail = jnp.where(rows == k, high.astype(jnp.float32), tail)
        tail = jnp.where(rows == k + 1, (index - (high << 7)).astype(jnp.float32), tail)
    table_ref[FEAT:] = tail.astype(jnp.bfloat16)
    copies[1].wait()


def contact_gather_kernel(slot, table_ref, wanted_ref, out_hbm, out_ref, sems):
    node_count = table_ref.shape[1]
    parts = LANES // slot
    height = out_ref.shape[1]
    per_chunk = GATHER // slot
    copies = []
    for chunk in range(wanted_ref.shape[0] // per_chunk):
        wanted = [wanted_ref[chunk * per_chunk + peer] for peer in range(per_chunk)]
        hot = one_hot(jnp.concatenate(wanted, 1), node_count)
        rows = dot(table_ref[...], hot).astype(jnp.bfloat16)
        if parts * height > ROWS:
            rows = jnp.concatenate(
                [rows, jnp.zeros((parts * height - ROWS, GATHER), jnp.bfloat16)], 0
            )
        for peer in range(per_chunk):
            out_ref[chunk * per_chunk + peer] = jnp.concatenate(
                [
                    rows[part * height : (part + 1) * height, peer * slot : (peer + 1) * slot]
                    for part in range(parts)
                ],
                1,
            )
        done = pl.ds(chunk * per_chunk, per_chunk)
        copies.append(
            pltpu.make_async_copy(out_ref.at[done], out_hbm.at[done], sems.at[chunk])
        )
        copies[-1].start()
    for copy in copies:
        copy.wait()


def edge_math(src, base, first, inputs, pos_recv, back, live, weights):
    w_dist, w_two, w_two_t = weights
    edges = inputs.shape[1]
    bf16 = jnp.bfloat16
    kept = jnp.float32 if live is not None else bf16
    offset = src(slice(FEAT, ROWS))[:3] - pos_recv
    if live is not None:
        offset = offset * live
    distance = jnp.sum(offset * offset, 0, keepdims=True)
    linear = base + first + w_dist * distance
    squashed = 0.5 * jnp.tanh(0.5 * linear) + 0.5
    hidden = (linear * squashed).astype(jnp.bfloat16)
    gates = dot(w_two, hidden)
    gate_vec = gates[CS : CS + CV]
    gate_dir = gates[CS + CV : CS + 2 * CV]
    gate_ten = gates[CS + 2 * CV :]
    scal = src(slice(0, CS))
    message = [(gates[:CS] * scal).astype(kept)]
    dgates = [(back(slice(0, CS)) * scal).astype(bf16)]
    vec_part = jnp.zeros((CV, edges), jnp.float32)
    dir_part = jnp.zeros((CV, edges), jnp.float32)
    for k in range(3):
        rows = slice(CS + k * CV, CS + (k + 1) * CV)
        sent, pull = src(rows), back(rows)
        message.append((gate_vec * sent + gate_dir * offset[k : k + 1]).astype(kept))
        vec_part = vec_part + pull * sent
        dir_part = dir_part + pull * offset[k : k + 1]
    ten_part = jnp.zeros((CT, edges), jnp.float32)
    for m in range(9):
        rows = slice(CS + 3 * CV + m * CT, CS + 3 * CV + (m + 1) * CT)
        sent = src(rows)
        message.append((gate_ten * sent).astype(kept))
        ten_part = ten_part + back(rows) * sent
    message = jnp.concatenate(message, 0)
    dgates += [part.astype(bf16) for part in (vec_part, dir_part, ten_part)]
    dgates = jnp.concatenate(dgates, 0)
    hidden_grad = dot(w_two_t, dgates)
    linear_grad = (hidden_grad * squashed * (1.0 + linear * (1.0 - squashed))).astype(jnp.bfloat16)
    rows = lax.broadcasted_iota(jnp.int32, (16, edges), 0)
    coarse = distance.astype(jnp.bfloat16).astype(jnp.float32)
    extra = jnp.where(
        rows == 0, 1.0, jnp.where(rows == 1, coarse, jnp.where(rows == 2, distance - coarse, 0.0))
    ).astype(jnp.bfloat16)
    grads = (
        dot(linear_grad, jnp.concatenate([inputs, extra], 0), 1, 1),
        dot(dgates, hidden, 1, 1),
    )
    return message, grads


def as_columns(first_row, second_row):
    rows = lax.broadcasted_iota(jnp.int32, (LANES, LANES), 0)
    columns = jnp.where(rows == 0, first_row, jnp.where(rows == 1, second_row, 0.0)).T
    return columns[:, 0:1], columns[:, 1:2]


def add_grads(grads_ref, grads):
    grads_ref[:HID, : 2 * CS + 16] += grads[0]
    grads_ref[HID:, :HID] += grads[1]


def block_diagonal(block_ref, w_scal, w_vec, w_ten):
    block_ref[...] = jnp.zeros_like(block_ref)
    block_ref[:CS, :CS] = w_scal[...]
    for k in range(3):
        rows = slice(CS + k * CV, CS + (k + 1) * CV)
        block_ref[rows, rows] = w_vec[...]
    for m in range(9):
        rows = slice(CS + 3 * CV + m * CT, CS + 3 * CV + (m + 1) * CT)
        block_ref[rows, rows] = w_ten[...]


def mesh_kernel(
    table_ref,
    inner_ref,
    outer_ref,
    code_ref,
    cot_ref,
    w_one_ref,
    b_one_ref,
    w_dist_ref,
    w_two_ref,
    w_scal_ref,
    w_vec_ref,
    w_ten_ref,
    dst_ref,
    mask_ref,
    agg_out_ref,
    grads_out_ref,
    recv_out_ref,
    code_out_ref,
    layers_out_ref,
    rows_out_ref,
    agg_ref,
    grads_ref,
    receive_ref,
    source_ref,
    block_ref,
    sems,
):
    node_count = table_ref.shape[1]
    source_ref[:, :node_count] = table_ref[...]
    even = lax.rem(lax.axis_index("sub"), 2) == 0
    low = lax.cond(even, lambda: outer_ref[...], lambda: inner_ref[...])
    high = lax.cond(even, lambda: inner_ref[...], lambda: outer_ref[...])
    source_ref[:, node_count : 2 * node_count] = dot(
        low, one_hot(join_index(low, FEAT + 3), node_count)
    ).astype(jnp.bfloat16)
    source_ref[:, 2 * node_count :] = dot(
        high, one_hot(join_index(high, FEAT + 5), node_count)
    ).astype(jnp.bfloat16)
    block_diagonal(block_ref, w_scal_ref, w_vec_ref, w_ten_ref)
    receive_ref[:FEAT] = dot(block_ref[...], cot_ref[...], 0, 0).astype(jnp.bfloat16)
    receive_ref[FEAT : FEAT + 16] = table_ref[FEAT:]
    receive_ref[FEAT + 16 :] = table_ref[:CS]
    w_one = w_one_ref[...]
    w_two = w_two_ref[...]
    b_column, dist_column = as_columns(b_one_ref[...], w_dist_ref[...])
    scal_recv = table_ref[:CS]
    recv_linear = dot(w_one[:, :CS], scal_recv) + b_column
    weights = (dist_column, w_two, w_two.T)
    pos_recv = table_ref[FEAT:].astype(jnp.float32)[:3]
    grads_ref[...] = jnp.zeros_like(grads_ref)
    agg_ref[...] = jnp.zeros_like(agg_ref)
    for step in range(DEGREE):
        code = code_ref[step]
        src = dot(source_ref[...], one_hot(code, 3 * node_count))
        live = jnp.where(code >= 0, 1.0, 0.0)
        scal_send = src[:CS].astype(jnp.bfloat16)
        inputs = jnp.concatenate([scal_recv, scal_send], 0)
        message, grads = edge_math(
            lambda rows: src[rows],
            recv_linear,
            dot(w_one[:, CS:], scal_send),
            inputs,
            pos_recv,
            lambda rows: receive_ref[rows].astype(jnp.float32),
            live,
            weights,
        )
        agg_ref[...] += message
        add_grads(grads_ref, grads)
    code_out_ref[...] = jnp.where(mask_ref[...] != 0, dst_ref[...], -1)
    recv_out_ref[...] = dot(
        receive_ref[...], one_hot(code_out_ref[...], node_count)
    ).astype(jnp.bfloat16)
    layers_out_ref[:HID] = w_one
    layers_out_ref[HID:] = w_two
    rows = lax.broadcasted_iota(jnp.int32, (8, HID), 0)
    rows_out_ref[...] = jnp.where(rows == 0, b_one_ref[...], w_dist_ref[...])
    copies = [
        pltpu.make_async_copy(agg_ref, agg_out_ref, sems.at[0]),
        pltpu.make_async_copy(grads_ref, grads_out_ref, sems.at[1]),
    ]
    for copy in copies:
        copy.start()
    for copy in copies:
        copy.wait()


def contact_kernel(
    slot,
    grad_scale,
    reply_ref,
    recv_ref,
    code_ref,
    layers_ref,
    rows_ref,
    mesh_agg_hbm,
    mesh_grads_hbm,
    cot_hbm,
    agg_out_ref,
    packed_ref,
    agg_ref,
    grads_ref,
    cot_ref,
    src_scr,
    packed_scr,
    sems,
):
    sources = [
        (mesh_agg_hbm, agg_ref),
        (mesh_grads_hbm, grads_ref),
        (cot_hbm, cot_ref),
    ]
    copies = [
        pltpu.make_async_copy(source, target, sems.at[at])
        for at, (source, target) in enumerate(sources)
    ]
    for copy in copies:
        copy.start()
    node_count = cot_ref.shape[1]
    parts = LANES // slot
    blocks = [reply_ref[peer] for peer in range(reply_ref.shape[0])]
    src_scr[...] = jnp.concatenate(
        [
            jnp.concatenate([block[:, part * slot : (part + 1) * slot] for block in blocks], 1)
            for part in range(parts)
        ],
        0,
    )[:ROWS]
    w_one = layers_ref[:HID]
    w_two = layers_ref[HID:]
    b_column, dist_column = as_columns(rows_ref[0:1], rows_ref[1:2])
    weights = (dist_column, w_two, w_two.T)
    inputs = jnp.concatenate([recv_ref[FEAT + 16 :], src_scr[:CS]], 0)
    message, grads = edge_math(
        lambda rows: src_scr[rows].astype(jnp.float32),
        b_column,
        dot(w_one, inputs),
        inputs,
        recv_ref[FEAT : FEAT + 16].astype(jnp.float32)[:3],
        lambda rows: recv_ref[rows].astype(jnp.float32),
        None,
        weights,
    )
    scattered = dot(message, one_hot(code_ref[...], node_count), 1, 1)
    for copy in copies:
        copy.wait()
    agg_ref[...] += scattered
    add_grads(grads_ref, grads)
    agg_rows = agg_ref[...].astype(jnp.bfloat16)
    agg_out_ref[...] = agg_rows
    cot = cot_ref[...]
    low = HID + GATES
    packed_scr[:low] = grads_ref[:, :LANES] * grad_scale
    scal = dot(cot[:CS], agg_rows[:CS], 1, 1) * grad_scale
    packed_scr[low : low + CS // 2] = jnp.concatenate([scal[: CS // 2], scal[CS // 2 :]], 1)
    low = low + CS // 2
    mixed = dot(cot[CS:], agg_rows[CS:], 1, 1)
    grad_vec = jnp.zeros((CV, CV), jnp.float32)
    for k in range(3):
        rows = slice(k * CV, (k + 1) * CV)
        grad_vec = grad_vec + mixed[rows, rows]
    each = CV * CV // LANES
    packed_scr[low : low + each] = grad_scale * jnp.concatenate(
        [grad_vec[at : at + each] for at in range(0, CV, each)], 1
    )
    low = low + each
    grad_ten = jnp.zeros((CT, CT), jnp.float32)
    for m in range(9):
        rows = slice(3 * CV + m * CT, 3 * CV + (m + 1) * CT)
        grad_ten = grad_ten + mixed[rows, rows]
    each = CT * CT // LANES
    packed_scr[low : low + each] = grad_scale * jnp.concatenate(
        [grad_ten[at : at + each] for at in range(0, CT, each)], 1
    )
    low = low + each
    extra = (grads_ref[:HID, LANES:] * grad_scale).T
    packed_scr[low : low + 1] = extra[0:1]
    packed_scr[low + 1 : low + 2] = extra[1:2] + extra[2:3]
    packed = packed_scr[...].astype(jnp.bfloat16)
    tiles = packed_ref.shape[1]
    for peer in range(packed_ref.shape[0]):
        for tile in range(tiles):
            at = (peer * tiles + tile) * FINE
            if at < packed.shape[0]:
                packed_ref[peer, tile] = packed[at : at + FINE]
            else:
                packed_ref[peer, tile] = jnp.zeros((FINE, LANES), jnp.bfloat16)


def sum_kernel(parts_ref, out_ref):
    total = parts_ref[0].astype(jnp.float32)
    for peer in range(1, parts_ref.shape[0]):
        total = total + parts_ref[peer].astype(jnp.float32)
    total = total.astype(jnp.bfloat16)
    for peer in range(out_ref.shape[0]):
        out_ref[peer] = total


def finish_kernel(
    blocks_ref,
    table_ref,
    agg_ref,
    w_scal_ref,
    w_vec_ref,
    w_ten_ref,
    out_ref,
    one_ref,
    bias_ref,
    dist_ref,
    two_ref,
    scal_ref,
    vec_ref,
    ten_ref,
    block_ref,
):
    block_diagonal(block_ref, w_scal_ref, w_vec_ref, w_ten_ref)
    out_ref[...] = (
        table_ref[:FEAT].astype(jnp.float32) + dot(block_ref[...], agg_ref[...])
    ).astype(jnp.bfloat16)

    tiles = blocks_ref.shape[1]

    def rows_of(at):
        peer, tile = divmod(at // FINE, tiles)
        return blocks_ref[peer, tile].astype(jnp.float32)

    for at in range(0, HID, FINE):
        one_ref[at : at + FINE] = rows_of(at)
    for at in range(0, GATES, FINE):
        two_ref[at : at + FINE] = rows_of(HID + at)
    low = HID + GATES
    for at in range(0, CS // 2, FINE):
        rows = rows_of(low + at)
        scal_ref[at : at + FINE] = rows[:, :CS]
        scal_ref[CS // 2 + at : CS // 2 + at + FINE] = rows[:, CS:]
    low = low + CS // 2
    for ref, width in ((vec_ref, CV), (ten_ref, CT)):
        each = width * width // LANES
        for at in range(0, each, FINE):
            rows = rows_of(low + at)
            for piece in range(width // each):
                to = piece * each + at
                ref[to : to + FINE] = rows[:, piece * width : (piece + 1) * width]
        low = low + each
    extra = rows_of(low)
    bias_ref[...] = extra[0:1]
    dist_ref[...] = extra[1:2]


def call(kernel, out_shape, scratch=(), in_specs=None, out_specs=None, cost_estimate=None):
    specs = {}
    if cost_estimate is not None:
        specs["cost_estimate"] = cost_estimate
    if in_specs is not None:
        specs["in_specs"] = in_specs
    if out_specs is not None:
        specs["out_specs"] = out_specs
    return pl.pallas_call(
        kernel,
        out_shape=out_shape,
        scratch_shapes=list(scratch),
        compiler_params=pltpu.CompilerParams(vmem_limit_bytes=VMEM_BYTES),
        **specs,
    )


IN_VMEM = pl.BlockSpec(memory_space=pltpu.VMEM)
IN_HBM = pl.BlockSpec(memory_space=pltpu.HBM)
ANYWHERE = pl.BlockSpec(memory_space=pl.ANY)


def exchange(blocks, axes=("dom", "sub")):
    return lax.all_to_all(blocks, axes, split_axis=0, concat_axis=0, tiled=True)


def in_hbm(*arrays):
    return tuple(pltpu.with_memory_space_constraint(array, pltpu.HBM) for array in arrays)


def shaped(shape, dtype):
    return jax.ShapeDtypeStruct(shape, dtype)


def swapped(shard, axis, first):
    peers = lax.axis_size(axis)
    pairs = [(at, (at + 1) % peers) for at in range(first, peers, 2)]
    return lax.ppermute(shard, axis, pairs + [(there, here) for here, there in pairs])


def on_device(
    node_feat,
    node_pos,
    node_cot,
    mesh_senders,
    edge_mask,
    halo_up,
    halo_down,
    contact_rows,
    contact_dst,
    contact_mask,
    w_one,
    b_one,
    w_dist,
    w_two,
    w_scal,
    w_vec,
    w_ten,
):
    f32, bf16 = jnp.float32, jnp.bfloat16
    node_count = node_feat.shape[1]
    contact_count = contact_rows.shape[0]
    device_count = lax.axis_size("dom") * lax.axis_size("sub")
    slot = contact_count // device_count
    chunks = contact_count // GATHER
    parts = LANES // slot
    height = -(-ROWS // (parts * 16)) * 16
    grad_scale = 1.0 / math.sqrt(device_count * node_count * DEGREE)
    table, requests = call(
        table_kernel,
        (
            shaped((ROWS, node_count), bf16),
            shaped((device_count, 1, slot), jnp.int32),
        ),
        (
            pltpu.VMEM((3, node_count), bf16),
            pltpu.VMEM((1, node_count), jnp.int32),
            pltpu.VMEM((1, node_count), jnp.int32),
            pltpu.VMEM((contact_count // LANES, LANES), jnp.int32),
            pltpu.SemaphoreType.DMA((5,)),
        ),
        in_specs=[IN_HBM] * 5,
        out_specs=(IN_VMEM, IN_VMEM),
    )(
        *in_hbm(
            node_feat,
            node_pos,
            halo_up[None],
            halo_down[None],
            contact_rows.reshape(contact_count // LANES, LANES),
        )
    )
    wanted = exchange(requests)
    wanted, table_late = lax.optimization_barrier((wanted, table))
    inner = swapped(table_late, "sub", 0)
    outer = swapped(table_late, "sub", 1)
    found = call(
        functools.partial(contact_gather_kernel, slot),
        pltpu.HBM((device_count, height, LANES), bf16),
        (
            pltpu.VMEM((device_count, height, LANES), bf16),
            pltpu.SemaphoreType.DMA((chunks,)),
        ),
        in_specs=[IN_VMEM, IN_VMEM],
        out_specs=IN_HBM,
    )(table, wanted)
    found, mesh_senders, edge_mask = lax.optimization_barrier((found, mesh_senders, edge_mask))
    replies = exchange(found)
    mesh_code = (
        jnp.where(edge_mask != 0, mesh_senders, -1)
        .reshape(node_count, DEGREE)
        .T.reshape(DEGREE, 1, node_count)
    )
    contact_dst = contact_dst.reshape(1, contact_count)
    contact_mask = contact_mask.reshape(1, contact_count)
    mesh_rows = HID + GATES
    recv_rows = FEAT + 16 + CS
    mesh_agg, mesh_grads, recv, contact_code, layers, rows = call(
        mesh_kernel,
        (
            pltpu.HBM((FEAT, node_count), f32),
            pltpu.HBM((mesh_rows, 2 * LANES), f32),
            shaped((recv_rows, contact_count), bf16),
            shaped((1, contact_count), jnp.int32),
            shaped((mesh_rows, HID), bf16),
            shaped((8, HID), f32),
        ),
        (
            pltpu.VMEM((FEAT, node_count), f32),
            pltpu.VMEM((mesh_rows, 2 * LANES), f32),
            pltpu.VMEM((recv_rows, node_count), bf16),
            pltpu.VMEM((ROWS, 3 * node_count), bf16),
            pltpu.VMEM((FEAT, FEAT), bf16),
            pltpu.SemaphoreType.DMA((2,)),
        ),
        in_specs=[IN_VMEM] * 14,
        out_specs=(IN_HBM,) * 2 + (IN_VMEM,) * 4,
        cost_estimate=pl.CostEstimate(
            flops=40_000_000_000, bytes_accessed=8_000_000, transcendentals=400_000
        ),
    )(
        table,
        inner,
        outer,
        mesh_code,
        node_cot,
        w_one,
        b_one[None],
        w_dist[None],
        w_two,
        w_scal,
        w_vec,
        w_ten,
        contact_dst,
        contact_mask,
    )
    packed_rows = mesh_rows + (CS * CS + CV * CV + CT * CT) // LANES + 2
    tiles = -(-packed_rows // (FINE * device_count))
    share = (device_count, tiles, FINE, LANES)
    agg_rows, packed = call(
        functools.partial(contact_kernel, slot, grad_scale),
        (shaped((FEAT, node_count), bf16), shaped(share, bf16)),
        (
            pltpu.VMEM((FEAT, node_count), f32),
            pltpu.VMEM((mesh_rows, 2 * LANES), f32),
            pltpu.VMEM((FEAT, node_count), bf16),
            pltpu.VMEM((ROWS, contact_count), bf16),
            pltpu.VMEM((packed_rows, LANES), f32),
            pltpu.SemaphoreType.DMA((3,)),
        ),
        in_specs=[IN_VMEM] * 5 + [IN_HBM] * 3,
        out_specs=(IN_VMEM, IN_VMEM),
    )(
        replies,
        recv,
        contact_code,
        layers,
        rows,
        *in_hbm(mesh_agg, mesh_grads, node_cot),
    )
    shares = call(sum_kernel, shaped(share, bf16))(exchange(packed))
    node_out, one, bias, dist, two, scal, vec, ten = call(
        finish_kernel,
        (
            shaped((FEAT, node_count), bf16),
            shaped((HID, 2 * CS), f32),
            shaped((1, HID), f32),
            shaped((1, HID), f32),
            shaped((GATES, HID), f32),
            shaped((CS, CS), f32),
            shaped((CV, CV), f32),
            shaped((CT, CT), f32),
        ),
        (pltpu.VMEM((FEAT, FEAT), bf16),),
    )(exchange(shares), table, agg_rows, w_scal, w_vec, w_ten)
    return node_out, one, bias[0], dist[0], two, scal, vec, ten


def solution(mesh):
    along = P(("dom", "sub"))
    columns = P(None, ("dom", "sub"))
    in_specs = (columns,) * 3 + (along,) * 7 + (P(),) * 7
    out_specs = (columns,) + (P(),) * 7
    return jax.shard_map(
        on_device, mesh=mesh, in_specs=in_specs, out_specs=out_specs, check_vma=False
    )
```

```python
import functools
import math

import jax
import jax.numpy as jnp
from jax import lax
from jax.experimental import pallas as pl
from jax.experimental.pallas import tpu as pltpu
from jax.sharding import PartitionSpec as P

CS = 64
CV = 32
CT = 16
HID = 128
DEGREE = 6
GATES = 144
FEAT = CS + 3 * CV + 9 * CT
ROWS = 320
LANES = 128
FINE = 2
CHUNK = 512
WIDE = 1024
VMEM_BYTES = 48 * 1024 * 1024


def dot(lhs, rhs, lhs_dim=1, rhs_dim=0):
    return lax.dot_general(
        lhs, rhs, (((lhs_dim,), (rhs_dim,)), ((), ())), preferred_element_type=jnp.float32
    )


def one_hot(code, width):
    rows = lax.broadcasted_iota(jnp.int16, (width, code.shape[1]), 0)
    return jnp.where(rows == code.astype(jnp.int16), jnp.bfloat16(1), jnp.bfloat16(0))


def join_index(table, row):
    pair = table[row : row + 2].astype(jnp.float32)
    return (pair[0:1] * 128.0 + pair[1:2]).astype(jnp.int32)


def table_kernel(
    feat_ref,
    pos_ref,
    up_ref,
    down_ref,
    rows_ref,
    table_ref,
    request_ref,
    pos_scr,
    up_scr,
    down_scr,
    rows_scr,
    sems,
):
    node_count = table_ref.shape[1]
    copies = [
        pltpu.make_async_copy(rows_ref, rows_scr, sems.at[0]),
        pltpu.make_async_copy(feat_ref, table_ref.at[:FEAT], sems.at[1]),
        pltpu.make_async_copy(pos_ref, pos_scr, sems.at[2]),
        pltpu.make_async_copy(up_ref, up_scr, sems.at[3]),
        pltpu.make_async_copy(down_ref, down_scr, sems.at[4]),
    ]
    for copy in copies:
        copy.start()
    copies[0].wait()
    slot = request_ref.shape[2]
    parts = LANES // slot
    for row in range(rows_scr.shape[0]):
        line = rows_scr[row : row + 1]
        for part in range(parts):
            request_ref[row * parts + part] = line[:, part * slot : (part + 1) * slot]
    for copy in copies[2:]:
        copy.wait()
    rows = lax.broadcasted_iota(jnp.int32, (ROWS - FEAT, node_count), 0)
    pos = pos_scr[...].astype(jnp.float32)
    tail = jnp.zeros((ROWS - FEAT, node_count), jnp.float32)
    for k in range(3):
        tail = jnp.where(rows == k, pos[k : k + 1], tail)
    for k, index_ref in ((3, up_scr), (5, down_scr)):
        index = index_ref[...]
        high = index >> 7
        tail = jnp.where(rows == k, high.astype(jnp.float32), tail)
        tail = jnp.where(rows == k + 1, (index - (high << 7)).astype(jnp.float32), tail)
    table_ref[FEAT:] = tail.astype(jnp.bfloat16)
    copies[1].wait()


def contact_gather_kernel(slot, table_ref, wanted_ref, out_hbm, out_ref, sems):
    node_count = table_ref.shape[1]
    parts = LANES // slot
    height = out_ref.shape[1]
    per_chunk = CHUNK // slot
    copies = []
    for chunk in range(wanted_ref.shape[0] // per_chunk):
        wanted = [wanted_ref[chunk * per_chunk + peer] for peer in range(per_chunk)]
        hot = one_hot(jnp.concatenate(wanted, 1), node_count)
        rows = dot(table_ref[...], hot).astype(jnp.bfloat16)
        if parts * height > ROWS:
            rows = jnp.concatenate(
                [rows, jnp.zeros((parts * height - ROWS, CHUNK), jnp.bfloat16)], 0
            )
        for peer in range(per_chunk):
            out_ref[chunk * per_chunk + peer] = jnp.concatenate(
                [
                    rows[part * height : (part + 1) * height, peer * slot : (peer + 1) * slot]
                    for part in range(parts)
                ],
                1,
            )
        done = pl.ds(chunk * per_chunk, per_chunk)
        copies.append(
            pltpu.make_async_copy(out_ref.at[done], out_hbm.at[done], sems.at[chunk])
        )
        copies[-1].start()
    for copy in copies:
        copy.wait()


def edge_math(src, base, first, inputs, pos_recv, back, live, weights):
    w_dist, w_two, w_two_t = weights
    edges = src.shape[1]
    offset = src[FEAT : FEAT + 3] - pos_recv
    if live is not None:
        offset = offset * live
    distance = jnp.sum(offset * offset, 0, keepdims=True)
    linear = base + first + w_dist * distance
    squashed = 0.5 * jnp.tanh(0.5 * linear) + 0.5
    hidden = (linear * squashed).astype(jnp.bfloat16)
    gates = dot(w_two, hidden)
    gate_vec = gates[CS : CS + CV]
    gate_dir = gates[CS + CV : CS + 2 * CV]
    gate_ten = gates[CS + 2 * CV :]
    message = [gates[:CS] * src[:CS]]
    vec_part = jnp.zeros((CV, edges), jnp.float32)
    dir_part = jnp.zeros((CV, edges), jnp.float32)
    for k in range(3):
        rows = slice(CS + k * CV, CS + (k + 1) * CV)
        message.append(gate_vec * src[rows] + gate_dir * offset[k : k + 1])
        vec_part = vec_part + back[rows] * src[rows]
        dir_part = dir_part + back[rows] * offset[k : k + 1]
    ten_part = jnp.zeros((CT, edges), jnp.float32)
    for m in range(9):
        rows = slice(CS + 3 * CV + m * CT, CS + 3 * CV + (m + 1) * CT)
        message.append(gate_ten * src[rows])
        ten_part = ten_part + back[rows] * src[rows]
    message = jnp.concatenate(message, 0)
    dgates = jnp.concatenate([back[:CS] * src[:CS], vec_part, dir_part, ten_part], 0).astype(
        jnp.bfloat16
    )
    hidden_grad = dot(w_two_t, dgates)
    linear_grad = (hidden_grad * squashed * (1.0 + linear * (1.0 - squashed))).astype(jnp.bfloat16)
    rows = lax.broadcasted_iota(jnp.int32, (16, edges), 0)
    coarse = distance.astype(jnp.bfloat16).astype(jnp.float32)
    extra = jnp.where(
        rows == 0, 1.0, jnp.where(rows == 1, coarse, jnp.where(rows == 2, distance - coarse, 0.0))
    ).astype(jnp.bfloat16)
    grads = (
        dot(linear_grad, jnp.concatenate([inputs, extra], 0), 1, 1),
        dot(dgates, hidden, 1, 1),
    )
    return message, grads


def as_columns(first_row, second_row):
    rows = lax.broadcasted_iota(jnp.int32, (LANES, LANES), 0)
    columns = jnp.where(rows == 0, first_row, jnp.where(rows == 1, second_row, 0.0)).T
    return columns[:, 0:1], columns[:, 1:2]


def add_grads(grads_ref, grads):
    grads_ref[:HID, : 2 * CS + 16] += grads[0]
    grads_ref[HID:, :HID] += grads[1]


def block_diagonal(block_ref, w_scal, w_vec, w_ten):
    block_ref[...] = jnp.zeros_like(block_ref)
    block_ref[:CS, :CS] = w_scal[...]
    for k in range(3):
        rows = slice(CS + k * CV, CS + (k + 1) * CV)
        block_ref[rows, rows] = w_vec[...]
    for m in range(9):
        rows = slice(CS + 3 * CV + m * CT, CS + 3 * CV + (m + 1) * CT)
        block_ref[rows, rows] = w_ten[...]


def mesh_kernel(
    table_ref,
    inner_ref,
    outer_ref,
    code_ref,
    cot_ref,
    w_one_ref,
    b_one_ref,
    w_dist_ref,
    w_two_ref,
    w_scal_ref,
    w_vec_ref,
    w_ten_ref,
    dst_ref,
    mask_ref,
    agg_out_ref,
    grads_out_ref,
    recv_out_ref,
    first_out_ref,
    code_out_ref,
    layers_out_ref,
    rows_out_ref,
    agg_ref,
    grads_ref,
    recv_ref,
    receive_ref,
    source_ref,
    block_ref,
    sems,
):
    node_count = table_ref.shape[1]
    source_ref[:, :node_count] = table_ref[...]
    even = lax.rem(lax.axis_index("sub"), 2) == 0
    low = lax.cond(even, lambda: outer_ref[...], lambda: inner_ref[...])
    high = lax.cond(even, lambda: inner_ref[...], lambda: outer_ref[...])
    source_ref[:, node_count : 2 * node_count] = dot(
        low, one_hot(join_index(low, FEAT + 3), node_count)
    ).astype(jnp.bfloat16)
    source_ref[:, 2 * node_count :] = dot(
        high, one_hot(join_index(high, FEAT + 5), node_count)
    ).astype(jnp.bfloat16)
    block_diagonal(block_ref, w_scal_ref, w_vec_ref, w_ten_ref)
    receive_ref[:FEAT] = dot(block_ref[...], cot_ref[...], 0, 0).astype(jnp.bfloat16)
    receive_ref[FEAT : FEAT + 16] = table_ref[FEAT:]
    receive_ref[FEAT + 16 :] = table_ref[:CS]
    w_one = w_one_ref[...]
    w_two = w_two_ref[...]
    b_column, dist_column = as_columns(b_one_ref[...], w_dist_ref[...])
    scal_recv = table_ref[:CS]
    recv_linear = dot(w_one[:, :CS], scal_recv) + b_column
    weights = (dist_column, w_two, w_two.T)
    pos_recv = table_ref[FEAT:].astype(jnp.float32)[:3]
    grads_ref[...] = jnp.zeros_like(grads_ref)
    agg_ref[...] = jnp.zeros_like(agg_ref)
    for step in range(DEGREE):
        code = code_ref[step]
        src = dot(source_ref[...], one_hot(code, 3 * node_count))
        live = jnp.where(code >= 0, 1.0, 0.0)
        back = receive_ref[:FEAT].astype(jnp.float32)
        scal_send = src[:CS].astype(jnp.bfloat16)
        inputs = jnp.concatenate([scal_recv, scal_send], 0)
        message, grads = edge_math(
            src, recv_linear, dot(w_one[:, CS:], scal_send), inputs, pos_recv, back, live, weights
        )
        agg_ref[...] += message
        add_grads(grads_ref, grads)
    code_out_ref[...] = jnp.where(mask_ref[...] != 0, dst_ref[...], -1)
    for chunk in range(code_out_ref.shape[0]):
        target = first_out_ref if chunk == 0 else recv_ref.at[chunk - 1]
        target[...] = dot(
            receive_ref[...], one_hot(code_out_ref[chunk], node_count)
        ).astype(jnp.bfloat16)
    layers_out_ref[:HID] = w_one
    layers_out_ref[HID:] = w_two
    rows = lax.broadcasted_iota(jnp.int32, (8, HID), 0)
    rows_out_ref[...] = jnp.where(rows == 0, b_one_ref[...], w_dist_ref[...])
    copies = [
        pltpu.make_async_copy(agg_ref, agg_out_ref, sems.at[0]),
        pltpu.make_async_copy(grads_ref, grads_out_ref, sems.at[1]),
        pltpu.make_async_copy(recv_ref, recv_out_ref, sems.at[2]),
    ]
    for copy in copies:
        copy.start()
    for copy in copies:
        copy.wait()


def contact_kernel(
    slot,
    grad_scale,
    reply_ref,
    first_ref,
    code_ref,
    layers_ref,
    rows_ref,
    recv_hbm,
    mesh_agg_hbm,
    mesh_grads_hbm,
    cot_hbm,
    agg_out_ref,
    packed_ref,
    recv_ref,
    agg_ref,
    grads_ref,
    cot_ref,
    src_scr,
    packed_scr,
    sems,
):
    chunks = code_ref.shape[0]
    sources = [
        (recv_hbm, recv_ref),
        (mesh_agg_hbm, agg_ref),
        (mesh_grads_hbm, grads_ref),
        (cot_hbm, cot_ref),
    ]
    copies = [
        pltpu.make_async_copy(source, target, sems.at[at])
        for at, (source, target) in enumerate(sources)
    ]
    for copy in copies:
        copy.start()
    node_count = cot_ref.shape[1]
    parts = LANES // slot
    per_chunk = WIDE // slot
    for chunk in range(chunks):
        blocks = [reply_ref[chunk * per_chunk + peer] for peer in range(per_chunk)]
        src_scr[chunk] = jnp.concatenate(
            [
                jnp.concatenate(
                    [block[:, part * slot : (part + 1) * slot] for block in blocks], 1
                )
                for part in range(parts)
            ],
            0,
        )[:ROWS]
    w_one = layers_ref[:HID]
    w_two = layers_ref[HID:]
    b_column, dist_column = as_columns(rows_ref[0:1], rows_ref[1:2])
    weights = (dist_column, w_two, w_two.T)
    for chunk in range(chunks):
        src_rows = src_scr[chunk]
        if chunk == 1:
            copies[0].wait()
        recv = first_ref[...] if chunk == 0 else recv_ref[chunk - 1]
        inputs = jnp.concatenate([recv[FEAT + 16 :], src_rows[:CS]], 0)
        message, grads = edge_math(
            src_rows.astype(jnp.float32),
            b_column,
            dot(w_one, inputs),
            inputs,
            recv[FEAT : FEAT + 16].astype(jnp.float32)[:3],
            recv[:FEAT].astype(jnp.float32),
            None,
            weights,
        )
        scattered = dot(message.astype(jnp.bfloat16), one_hot(code_ref[chunk], node_count), 1, 1)
        if chunk > 0:
            scattered = held[0] + scattered
            grads = [before + now for before, now in zip(held[1], grads)]
        held = (scattered, grads)
    for copy in copies[1:]:
        copy.wait()
    add_grads(grads_ref, held[1])
    agg_rows = (agg_ref[...] + held[0]).astype(jnp.bfloat16)
    agg_out_ref[...] = agg_rows
    cot = cot_ref[...]
    low = HID + GATES
    packed_scr[:low] = grads_ref[:, :LANES] * grad_scale
    scal = dot(cot[:CS], agg_rows[:CS], 1, 1) * grad_scale
    packed_scr[low : low + CS // 2] = jnp.concatenate([scal[: CS // 2], scal[CS // 2 :]], 1)
    low = low + CS // 2
    mixed = dot(cot[CS:], agg_rows[CS:], 1, 1)
    grad_vec = jnp.zeros((CV, CV), jnp.float32)
    for k in range(3):
        rows = slice(k * CV, (k + 1) * CV)
        grad_vec = grad_vec + mixed[rows, rows]
    each = CV * CV // LANES
    packed_scr[low : low + each] = grad_scale * jnp.concatenate(
        [grad_vec[at : at + each] for at in range(0, CV, each)], 1
    )
    low = low + each
    grad_ten = jnp.zeros((CT, CT), jnp.float32)
    for m in range(9):
        rows = slice(3 * CV + m * CT, 3 * CV + (m + 1) * CT)
        grad_ten = grad_ten + mixed[rows, rows]
    each = CT * CT // LANES
    packed_scr[low : low + each] = grad_scale * jnp.concatenate(
        [grad_ten[at : at + each] for at in range(0, CT, each)], 1
    )
    low = low + each
    extra = (grads_ref[:HID, LANES:] * grad_scale).T
    packed_scr[low : low + 1] = extra[0:1]
    packed_scr[low + 1 : low + 2] = extra[1:2] + extra[2:3]
    packed = packed_scr[...].astype(jnp.bfloat16)
    tiles = packed_ref.shape[1]
    for peer in range(packed_ref.shape[0]):
        for tile in range(tiles):
            at = (peer * tiles + tile) * FINE
            if at < packed.shape[0]:
                packed_ref[peer, tile] = packed[at : at + FINE]
            else:
                packed_ref[peer, tile] = jnp.zeros((FINE, LANES), jnp.bfloat16)


def sum_kernel(parts_ref, out_ref):
    total = parts_ref[0].astype(jnp.float32)
    for peer in range(1, parts_ref.shape[0]):
        total = total + parts_ref[peer].astype(jnp.float32)
    total = total.astype(jnp.bfloat16)
    for peer in range(out_ref.shape[0]):
        out_ref[peer] = total


def finish_kernel(
    blocks_ref,
    table_ref,
    agg_ref,
    w_scal_ref,
    w_vec_ref,
    w_ten_ref,
    out_ref,
    one_ref,
    bias_ref,
    dist_ref,
    two_ref,
    scal_ref,
    vec_ref,
    ten_ref,
    block_ref,
):
    block_diagonal(block_ref, w_scal_ref, w_vec_ref, w_ten_ref)
    out_ref[...] = (
        table_ref[:FEAT].astype(jnp.float32) + dot(block_ref[...], agg_ref[...])
    ).astype(jnp.bfloat16)

    tiles = blocks_ref.shape[1]

    def rows_of(at):
        peer, tile = divmod(at // FINE, tiles)
        return blocks_ref[peer, tile].astype(jnp.float32)

    for at in range(0, HID, FINE):
        one_ref[at : at + FINE] = rows_of(at)
    for at in range(0, GATES, FINE):
        two_ref[at : at + FINE] = rows_of(HID + at)
    low = HID + GATES
    for at in range(0, CS // 2, FINE):
        rows = rows_of(low + at)
        scal_ref[at : at + FINE] = rows[:, :CS]
        scal_ref[CS // 2 + at : CS // 2 + at + FINE] = rows[:, CS:]
    low = low + CS // 2
    for ref, width in ((vec_ref, CV), (ten_ref, CT)):
        each = width * width // LANES
        for at in range(0, each, FINE):
            rows = rows_of(low + at)
            for piece in range(width // each):
                to = piece * each + at
                ref[to : to + FINE] = rows[:, piece * width : (piece + 1) * width]
        low = low + each
    extra = rows_of(low)
    bias_ref[...] = extra[0:1]
    dist_ref[...] = extra[1:2]


def call(kernel, out_shape, scratch=(), in_specs=None, out_specs=None, cost_estimate=None):
    specs = {}
    if cost_estimate is not None:
        specs["cost_estimate"] = cost_estimate
    if in_specs is not None:
        specs["in_specs"] = in_specs
    if out_specs is not None:
        specs["out_specs"] = out_specs
    return pl.pallas_call(
        kernel,
        out_shape=out_shape,
        scratch_shapes=list(scratch),
        compiler_params=pltpu.CompilerParams(vmem_limit_bytes=VMEM_BYTES),
        **specs,
    )


IN_VMEM = pl.BlockSpec(memory_space=pltpu.VMEM)
IN_HBM = pl.BlockSpec(memory_space=pltpu.HBM)
ANYWHERE = pl.BlockSpec(memory_space=pl.ANY)


def exchange(blocks, axes=("dom", "sub")):
    return lax.all_to_all(blocks, axes, split_axis=0, concat_axis=0, tiled=True)


def in_hbm(*arrays):
    return tuple(pltpu.with_memory_space_constraint(array, pltpu.HBM) for array in arrays)


def shaped(shape, dtype):
    return jax.ShapeDtypeStruct(shape, dtype)


def swapped(shard, axis, first):
    peers = lax.axis_size(axis)
    pairs = [(at, (at + 1) % peers) for at in range(first, peers, 2)]
    return lax.ppermute(shard, axis, pairs + [(there, here) for here, there in pairs])


def on_device(
    node_feat,
    node_pos,
    node_cot,
    mesh_senders,
    edge_mask,
    halo_up,
    halo_down,
    contact_rows,
    contact_dst,
    contact_mask,
    w_one,
    b_one,
    w_dist,
    w_two,
    w_scal,
    w_vec,
    w_ten,
):
    f32, bf16 = jnp.float32, jnp.bfloat16
    node_count = node_feat.shape[1]
    contact_count = contact_rows.shape[0]
    device_count = lax.axis_size("dom") * lax.axis_size("sub")
    slot = contact_count // device_count
    chunks = contact_count // CHUNK
    wides = contact_count // WIDE
    parts = LANES // slot
    height = -(-ROWS // (parts * 16)) * 16
    grad_scale = 1.0 / math.sqrt(device_count * node_count * DEGREE)
    table, requests = call(
        table_kernel,
        (
            shaped((ROWS, node_count), bf16),
            shaped((device_count, 1, slot), jnp.int32),
        ),
        (
            pltpu.VMEM((3, node_count), bf16),
            pltpu.VMEM((1, node_count), jnp.int32),
            pltpu.VMEM((1, node_count), jnp.int32),
            pltpu.VMEM((contact_count // LANES, LANES), jnp.int32),
            pltpu.SemaphoreType.DMA((5,)),
        ),
        in_specs=[IN_HBM] * 5,
        out_specs=(IN_VMEM, IN_VMEM),
    )(
        *in_hbm(
            node_feat,
            node_pos,
            halo_up[None],
            halo_down[None],
            contact_rows.reshape(contact_count // LANES, LANES),
        )
    )
    wanted = exchange(requests)
    wanted, table_late = lax.optimization_barrier((wanted, table))
    inner = swapped(table_late, "sub", 0)
    outer = swapped(table_late, "sub", 1)
    found = call(
        functools.partial(contact_gather_kernel, slot),
        pltpu.HBM((device_count, height, LANES), bf16),
        (
            pltpu.VMEM((device_count, height, LANES), bf16),
            pltpu.SemaphoreType.DMA((chunks,)),
        ),
        in_specs=[IN_VMEM, IN_VMEM],
        out_specs=IN_HBM,
    )(table, wanted)
    found, mesh_senders, edge_mask = lax.optimization_barrier((found, mesh_senders, edge_mask))
    replies = exchange(found)
    mesh_code = (
        jnp.where(edge_mask != 0, mesh_senders, -1)
        .reshape(node_count, DEGREE)
        .T.reshape(DEGREE, 1, node_count)
    )
    contact_dst = contact_dst.reshape(wides, 1, WIDE)
    contact_mask = contact_mask.reshape(wides, 1, WIDE)
    mesh_rows = HID + GATES
    recv_rows = FEAT + 16 + CS
    mesh_agg, mesh_grads, recv, first, contact_code, layers, rows = call(
        mesh_kernel,
        (
            pltpu.HBM((FEAT, node_count), f32),
            pltpu.HBM((mesh_rows, 2 * LANES), f32),
            pltpu.HBM((wides - 1, recv_rows, WIDE), bf16),
            shaped((recv_rows, WIDE), bf16),
            shaped((wides, 1, WIDE), jnp.int32),
            shaped((mesh_rows, HID), bf16),
            shaped((8, HID), f32),
        ),
        (
            pltpu.VMEM((FEAT, node_count), f32),
            pltpu.VMEM((mesh_rows, 2 * LANES), f32),
            pltpu.VMEM((wides - 1, recv_rows, WIDE), bf16),
            pltpu.VMEM((recv_rows, node_count), bf16),
            pltpu.VMEM((ROWS, 3 * node_count), bf16),
            pltpu.VMEM((FEAT, FEAT), bf16),
            pltpu.SemaphoreType.DMA((3,)),
        ),
        in_specs=[IN_VMEM] * 14,
        out_specs=(IN_HBM,) * 3 + (IN_VMEM,) * 4,
        cost_estimate=pl.CostEstimate(
            flops=40_000_000_000, bytes_accessed=8_000_000, transcendentals=400_000
        ),
    )(
        table,
        inner,
        outer,
        mesh_code,
        node_cot,
        w_one,
        b_one[None],
        w_dist[None],
        w_two,
        w_scal,
        w_vec,
        w_ten,
        contact_dst,
        contact_mask,
    )
    packed_rows = mesh_rows + (CS * CS + CV * CV + CT * CT) // LANES + 2
    tiles = -(-packed_rows // (FINE * device_count))
    share = (device_count, tiles, FINE, LANES)
    agg_rows, packed = call(
        functools.partial(contact_kernel, slot, grad_scale),
        (shaped((FEAT, node_count), bf16), shaped(share, bf16)),
        (
            pltpu.VMEM((wides - 1, recv_rows, WIDE), bf16),
            pltpu.VMEM((FEAT, node_count), f32),
            pltpu.VMEM((mesh_rows, 2 * LANES), f32),
            pltpu.VMEM((FEAT, node_count), bf16),
            pltpu.VMEM((wides, ROWS, WIDE), bf16),
            pltpu.VMEM((packed_rows, LANES), f32),
            pltpu.SemaphoreType.DMA((4,)),
        ),
        in_specs=[IN_VMEM] * 5 + [IN_HBM] * 4,
        out_specs=(IN_VMEM, IN_VMEM),
    )(
        replies,
        first,
        contact_code,
        layers,
        rows,
        *in_hbm(recv, mesh_agg, mesh_grads, node_cot),
    )
    shares = call(sum_kernel, shaped(share, bf16))(exchange(packed))
    node_out, one, bias, dist, two, scal, vec, ten = call(
        finish_kernel,
        (
            shaped((FEAT, node_count), bf16),
            shaped((HID, 2 * CS), f32),
            shaped((1, HID), f32),
            shaped((1, HID), f32),
            shaped((GATES, HID), f32),
            shaped((CS, CS), f32),
            shaped((CV, CV), f32),
            shaped((CT, CT), f32),
        ),
        (pltpu.VMEM((FEAT, FEAT), bf16),),
    )(exchange(shares), table, agg_rows, w_scal, w_vec, w_ten)
    return node_out, one, bias[0], dist[0], two, scal, vec, ten


def solution(mesh):
    along = P(("dom", "sub"))
    columns = P(None, ("dom", "sub"))
    in_specs = (columns,) * 3 + (along,) * 7 + (P(),) * 7
    out_specs = (columns,) + (P(),) * 7
    return jax.shard_map(
        on_device, mesh=mesh, in_specs=in_specs, out_specs=out_specs, check_vma=False
    )
```
